32 devices in a mesh: group: 4 (over x, core), replica: 8 (over z, y).
Axes of the slice: x: 2, y: 2, z: 4, core: 2. Of those that a mesh axis runs over, the one named last changes fastest.
Arguments:
- tokens: bfloat16 [32768, 960], P(('group', 'replica')), may hold values from -6 to 6
- segments: int32 [64, 512], P(('group', 'replica')), may hold values from 0 to 3, never falling along the last dimension, each value on 1 to 256 neighbouring positions
- query_weight: bfloat16 [960, 960], P('group'), may hold values from -0.1875 to 0.1875
- key_weight: bfloat16 [960, 320], P('group'), may hold values from -0.1875 to 0.1875
- value_weight: bfloat16 [960, 320], P('group'), may hold values from -0.1875 to 0.1875
- output_weight: bfloat16 [960, 960], P('group'), may hold values from -0.75 to 0.75
- w_gate: bfloat16 [960, 2560], P('group'), may hold values from -0.1875 to 0.1875
- w_up: bfloat16 [960, 2560], P('group'), may hold values from -0.1875 to 0.1875
- w_down: bfloat16 [2560, 960], P('group'), may hold values from -0.125 to 0.125
- attn_gain: bfloat16 [960], P('group'), may hold values from 0.5 to 1.5
- ffn_gain: bfloat16 [960], P('group'), may hold values from 0.5 to 1.5
- cotangent: bfloat16 [32768, 960], P(('group', 'replica')), may hold values from -6 to 6
Outputs:
- output: bfloat16 [32768, 960], P(('group', 'replica'))
- grad_tokens: bfloat16 [32768, 960], P(('group', 'replica'))
- grad_query: float32 [960, 960], P('group')
- grad_key: float32 [960, 320], P('group')
- grad_value: float32 [960, 320], P('group')
- grad_out: float32 [960, 960], P('group')
- grad_gate: float32 [960, 2560], P('group')
- grad_up: float32 [960, 2560], P('group')
- grad_down: float32 [2560, 960], P('group')
- grad_attn_gain: float32 [960], P('group')
- grad_ffn_gain: float32 [960], P('group')
The draws below stay inside these ranges and needn't reach their ends.
Inputs may be any that keep to these rules, and one draw needn't show every extreme that they name: `segments`: along each sequence of 512 tokens the ids never fall; equal ids mark one document of at most 256 tokens.
All inputs are finite; a program needn't handle non-finite values.
Results may differ from the reference program's by a relative error of at most 0.017.
Values may be sent and summed in bfloat16 or wider, within the bound.
No kernel may reach another device: no remote copies, remote signals or barrier semaphores. Data moves between devices by JAX's collectives and lax.ppermute only.
A program may use at most 256 MiB of HBM per device.

```python
import math
import jax
import jax.numpy as jnp
import numpy as np
from jax import lax

D = 960
QUERY_HEADS = 15
KEY_VALUE_HEADS = 5
HEAD_WIDTH = 64
FF = 2560
SEQUENCE_LENGTH = 512
SEQS = 64
TOKENS = 32768


def steps_of(rng, dims, shards, smallest, high):
    def one(axis_at, shards_of):
        draws = jax.random.uniform(jax.random.fold_in(jax.random.fold_in(rng, 6), axis_at), (shards_of,), jnp.float32, smallest / len(shards), high / len(shards))
        return jnp.repeat(jnp.exp(draws), dims[axis_at] // shards_of).reshape((-1,) + (1,) * (len(dims) - axis_at - 1))

    factor_of = one(*shards[0])
    for cut in shards[1:]:
        factor_of = factor_of * one(*cut)
    return factor_of


def length_profile(count, total, limit, lean):
    portions = [(1 << 20) // math.isqrt(rank ** lean) + 1 for rank in range(2, count + 1)]
    spare, given = total - limit - (count - 1), [1] * (count - 1)
    while spare > 0:
        movable = [i for i in range(count - 1) if given[i] < limit]
        whole, budget = sum([portions[i] for i in movable]), spare
        for i in movable:
            more = min(limit - given[i], max(1, budget * portions[i] // whole), spare)
            given[i] = given[i] + more
            spare = spare - more
    return np.array([limit] + given)


def ragged(own_key, amount, total, most, lean):
    if amount == 2:
        one = jax.random.randint(own_key, (), max(1, total - most), min(most, total - 1) + 1)
        return jnp.stack([one, total - one])
    tallies = jnp.asarray(length_profile(amount, total, most, lean), jnp.int32)
    twos = (amount - 1) // 2
    giver, taker = tallies[1:1 + 2 * twos:2], tallies[2:2 + 2 * twos:2]
    slack = jnp.minimum(giver - 1, most - taker)
    shifted = jax.random.randint(jax.random.fold_in(own_key, 1), (twos,), 0, 1 << 20) % (slack + 1)
    tallies = tallies.at[1:1 + 2 * twos:2].set(giver - shifted).at[2:2 + 2 * twos:2].set(taker + shifted)
    return tallies[jax.random.permutation(jax.random.fold_in(own_key, 2), amount)]


def normal_values(rng, dims, scale, reach, pieces=(), held_as=jnp.bfloat16):
    loudness = steps_of(rng, dims, pieces, -0.22, 0.18) if pieces else 1.0
    array = jax.random.normal(rng, dims, jnp.float32) * scale * loudness
    return jnp.minimum(jnp.maximum(array, -reach), reach).astype(held_as)


def setup_inputs(seed: int = 0) -> dict:
    key_list = jax.random.split(jax.random.key(seed), 13)
    tokens = normal_values(key_list[0], (TOKENS, D), 1.0, 6.0, ((0, 32),))
    segments = jax.vmap(lambda own: jnp.searchsorted(jnp.cumsum(ragged(own, 4, SEQUENCE_LENGTH, SEQUENCE_LENGTH // 2, 1)), jnp.arange(SEQUENCE_LENGTH), side="right"))(jax.random.split(key_list[1], SEQS)).reshape((SEQS, SEQUENCE_LENGTH)).astype(jnp.int32)
    query_weight = normal_values(key_list[2], (D, D), D ** -0.5, 0.1875, ((0, 4),))
    key_weight = normal_values(key_list[3], (D, KEY_VALUE_HEADS * HEAD_WIDTH), D ** -0.5, 0.1875, ((0, 4),))
    value_weight = normal_values(key_list[4], (D, KEY_VALUE_HEADS * HEAD_WIDTH), D ** -0.5, 0.1875, ((0, 4),))
    output_weight = normal_values(key_list[5], (D, D), (D // 16) ** -0.5, 0.75, ((0, 4),))
    w_gate = normal_values(key_list[6], (D, FF), D ** -0.5, 0.1875, ((0, 4),))
    w_up = normal_values(key_list[7], (D, FF), D ** -0.5, 0.1875, ((0, 4),))
    w_down = normal_values(key_list[8], (FF, D), FF ** -0.5, 0.125, ((0, 4),))
    attn_gain = jnp.clip(1.0 + 0.1 * jax.random.normal(key_list[9], (D,), jnp.float32), 0.5, 1.5).astype(jnp.bfloat16)
    ffn_gain = jnp.clip(1.0 + 0.1 * jax.random.normal(key_list[10], (D,), jnp.float32), 0.5, 1.5).astype(jnp.bfloat16)
    cotangent = normal_values(key_list[11], (TOKENS, D), 1.0, 6.0, ((0, 32),))
    return {"tokens": tokens, "segments": segments, "query_weight": query_weight, "key_weight": key_weight, "value_weight": value_weight, "output_weight": output_weight, "w_gate": w_gate, "w_up": w_up, "w_down": w_down, "attn_gain": attn_gain, "ffn_gain": ffn_gain, "cotangent": cotangent}


EPS = 1e-05
THETA = 100000.0

@jax.custom_vjp
def low(v):
    return lax.optimization_barrier(v.astype(jnp.bfloat16)).astype(jnp.float32)

@jax.custom_vjp
def lower_backward(v):
    return v

def low_keep(v):
    return (low(v), None)

def low_pass(kept, grad):
    return (grad,)

def back_keep(v):
    return (v, None)

def back_low(kept, grad):
    return (low(grad),)
low.defvjp(low_keep, low_pass)
lower_backward.defvjp(back_keep, back_low)

def rms(value, gain):
    return value * lax.rsqrt(lax.optimization_barrier(jnp.mean(value * value, axis=-1, keepdims=True)) + EPS) * gain

def rotate(value, cosine, sine):
    half = HEAD_WIDTH // 2
    first = value[..., :half]
    second = value[..., half:]
    return value * cosine + jnp.concatenate([-second, first], axis=-1) * sine

def tables(segb):
    index = jnp.arange(SEQUENCE_LENGTH, dtype=jnp.int32)
    same = segb[:, :, None] == segb[:, None, :]
    start = lax.optimization_barrier(jnp.min(jnp.where(same, index[None, None, :], SEQUENCE_LENGTH), axis=-1))
    position = (index[None, :] - start).astype(jnp.float32)
    allowed = same & (index[:, None] >= index[None, :])[None]
    half = HEAD_WIDTH // 2
    freq = THETA ** (-(jnp.arange(half, dtype=jnp.float32) * 2.0 / HEAD_WIDTH))
    angle = position[..., None] * freq
    cosine = jnp.concatenate([jnp.cos(angle), jnp.cos(angle)], axis=-1)[:, :, None, :]
    sine = jnp.concatenate([jnp.sin(angle), jnp.sin(angle)], axis=-1)[:, :, None, :]
    return (allowed, cosine, sine)

def block(xb, segb, weights):
    query_weight, key_weight, value_weight, output_weight, w_gate, w_up, w_down, attn_gain, ffn_gain = weights
    token_count = xb.shape[0]
    share = QUERY_HEADS // KEY_VALUE_HEADS
    highest_precision = lax.Precision.HIGHEST
    allowed, cosine, sine = tables(segb)
    hidden_input = low(rms(xb, attn_gain))
    query_rows = jnp.einsum('vfl,lz->vfz', hidden_input, query_weight, precision=highest_precision).reshape(token_count, SEQUENCE_LENGTH, QUERY_HEADS, HEAD_WIDTH)
    key_rows = jnp.einsum('vfl,lz->vfz', hidden_input, key_weight, precision=highest_precision).reshape(token_count, SEQUENCE_LENGTH, KEY_VALUE_HEADS, HEAD_WIDTH)
    value_rows = jnp.einsum('vfl,lz->vfz', hidden_input, value_weight, precision=highest_precision).reshape(token_count, SEQUENCE_LENGTH, KEY_VALUE_HEADS, HEAD_WIDTH)
    query_rows = low(rotate(lower_backward(query_rows), cosine, sine))
    key_rows = low(rotate(lower_backward(key_rows), cosine, sine))
    value_rows = low(lower_backward(value_rows))
    grouped = query_rows.reshape(token_count, SEQUENCE_LENGTH, KEY_VALUE_HEADS, share, HEAD_WIDTH)
    scores = lower_backward(jnp.einsum('sikgd,sjkd->skgij', grouped, key_rows, precision=highest_precision) * HEAD_WIDTH ** (-0.5))
    scores = jnp.where(allowed[:, None, None], scores, -1e+30)
    probs = low(jax.nn.softmax(scores, axis=-1))
    attended_rows = jnp.einsum('skgij,sjkd->sikgd', probs, value_rows, precision=highest_precision).reshape(token_count, SEQUENCE_LENGTH, D)
    attended_rows = low(lower_backward(attended_rows))
    branch_output = lower_backward(jnp.einsum('tjx,xl->tjl', attended_rows, output_weight, precision=highest_precision))
    mid = xb + branch_output
    normed = low(rms(mid, ffn_gain))
    gate = lower_backward(jnp.einsum('snd,df->snf', normed, w_gate, precision=highest_precision))
    up_part = lower_backward(jnp.einsum('snd,df->snf', normed, w_up, precision=highest_precision))
    inner = low(jax.nn.silu(gate) * up_part)
    mixed = lower_backward(jnp.einsum('snf,fd->snd', inner, w_down, precision=highest_precision))
    return mid + mixed

def reference(tokens, segments, query_weight, key_weight, value_weight, output_weight, w_gate, w_up, w_down, attn_gain, ffn_gain, cotangent):
    per = math.gcd(SEQS, 8)
    blocks = SEQS // per
    inputs = tokens.astype(jnp.float32).reshape(blocks, per, SEQUENCE_LENGTH, D)
    seg_blocks = segments.reshape(blocks, per, SEQUENCE_LENGTH)
    weights = (query_weight.astype(jnp.float32), key_weight.astype(jnp.float32), value_weight.astype(jnp.float32), output_weight.astype(jnp.float32), w_gate.astype(jnp.float32), w_up.astype(jnp.float32), w_down.astype(jnp.float32), attn_gain.astype(jnp.float32), ffn_gain.astype(jnp.float32))
    checked = jax.checkpoint(block)

    def forward(inputs, weights):
        return lax.map(lambda pair: checked(pair[0], pair[1], weights), (inputs, seg_blocks))
    result, pull = jax.vjp(forward, inputs, weights)
    grad_in, grads = pull(cotangent.astype(jnp.float32).reshape(blocks, per, SEQUENCE_LENGTH, D))
    return (result.reshape(TOKENS, D).astype(jnp.bfloat16), grad_in.reshape(TOKENS, D).astype(jnp.bfloat16), grads[0], grads[1], grads[2], grads[3], grads[4], grads[5], grads[6], grads[7], grads[8])
```

```python
import jax
import jax.numpy as jnp
from jax import lax
from jax.experimental import pallas as pl
from jax.experimental.pallas import tpu as pltpu
from jax.sharding import PartitionSpec as P

D = 960
QUERY_HEADS = 15
KEY_VALUE_HEADS = 5
HEAD_WIDTH = 64
SHARE = QUERY_HEADS // KEY_VALUE_HEADS
HALF = HEAD_WIDTH // 2
KEYS = KEY_VALUE_HEADS * HEAD_WIDTH
EPS = 1e-05
THETA = 100000.0
TILE = 256
QB = 128
GAINS = 128
WIDE = D + 2 * KEYS
CUT = 640
OWN = 240
F32 = jnp.float32
BF16 = jnp.bfloat16
MIB = 1 << 20


def dot(a, b, ca, cb):
    return lax.dot_general(a, b, (((ca,), (cb,)), ((), ())), preferred_element_type=F32)


def params(limit, grid=1):
    return pltpu.CompilerParams(
        vmem_limit_bytes=limit * MIB, dimension_semantics=("arbitrary",) * grid
    )


def cost(flops, moved, exps=0):
    return pl.CostEstimate(flops=flops, bytes_accessed=moved, transcendentals=exps)


def shaped(*shape_type):
    return [jax.ShapeDtypeStruct(s, t) for s, t in shape_type]


def norm_columns(v):
    inverse = lax.rsqrt(jnp.mean(v * v, axis=0, keepdims=True) + EPS)
    return v * inverse, inverse


def norm_columns_back(grad, normal, inverse, gain):
    scaled = grad * gain
    back = inverse * (scaled - normal * jnp.mean(scaled * normal, axis=0, keepdims=True))
    return back, jnp.sum(grad * normal, axis=1, keepdims=True)


def fixed(shape):
    return pl.BlockSpec(shape, lambda *_: (0,) * len(shape), pipeline_mode=pl.Buffered(1))


def columns(height, width):
    return pl.BlockSpec((height, width), lambda i: (0, i))


def project_kernel(x_ref, w_ref, cos_ref, sin_ref, qkv_ref, h_ref):
    gain = w_ref[:, 0:1].astype(F32)
    normal, _ = norm_columns(x_ref[...].astype(F32))
    h = (normal * gain).astype(BF16)
    h_ref[...] = h
    c, s = cos_ref[...], sin_ref[...]
    out = dot(w_ref[:, GAINS:], h, 0, 0)
    for head in range(QUERY_HEADS + KEY_VALUE_HEADS):
        at = head * HEAD_WIDTH
        a, b = out[at:at + HALF], out[at + HALF:at + HEAD_WIDTH]
        scale = HEAD_WIDTH ** -0.5 if head < QUERY_HEADS else 1.0
        qkv_ref[at:at + HALF, :] = ((a * c - b * s) * scale).astype(BF16)
        qkv_ref[at + HALF:at + HEAD_WIDTH, :] = ((b * c + a * s) * scale).astype(BF16)
    qkv_ref[D + KEYS:, :] = out[D + KEYS:].astype(BF16)


def project(x, w, cos, sin):
    rows = x.shape[1]
    return pl.pallas_call(
        project_kernel,
        grid=(rows // TILE,),
        in_specs=[columns(D, TILE), fixed(w.shape), columns(HALF, TILE), columns(HALF, TILE)],
        out_specs=[columns(WIDE, TILE), columns(D, TILE)],
        out_shape=shaped(((WIDE, rows), BF16), ((D, rows), BF16)),
        compiler_params=params(40),
        cost_estimate=cost(2 * rows * D * WIDE, rows * (2 * D + WIDE) * 2 + D * WIDE * 2),
        name="project",
    )(x, w, cos, sin)


def key_span(block):
    return max(0, QB * (block - 2)), QB * (block + 1)


def make_bias(bias_ref, segr_ref, segc_ref, length):
    for b in range(length // QB):
        lo, hi = key_span(b)
        key_at = lax.broadcasted_iota(jnp.int32, (hi - lo, QB), 0) + lo
        query_at = lax.broadcasted_iota(jnp.int32, (hi - lo, QB), 1) + b * QB
        ok = (segc_ref[lo:hi, :] == segr_ref[:, b * QB:(b + 1) * QB]) & (key_at <= query_at)
        bias_ref[b, 0:hi - lo, :] = jnp.where(ok, 0.0, -1e30)


def three(ref, kv, b):
    return jnp.concatenate(
        [
            ref[pl.ds(pl.multiple_of((kv * SHARE + i) * HEAD_WIDTH, HEAD_WIDTH), HEAD_WIDTH),
                b * QB:(b + 1) * QB]
            for i in range(SHARE)
        ],
        axis=1,
    )


def wide_bias(bias_ref, b, n):
    one = bias_ref[b, 0:n, :]
    return jnp.concatenate([one] * SHARE, axis=1)


def attend_kernel(qkv_ref, segr_ref, segc_ref, o_ref, lse_ref, bias_ref):
    length = qkv_ref.shape[1]
    make_bias(bias_ref, segr_ref.at[0], segc_ref.at[0], length)

    @pl.loop(0, KEY_VALUE_HEADS)
    def _(kv):
        k = qkv_ref[pl.ds(pl.multiple_of(D + kv * HEAD_WIDTH, HEAD_WIDTH), HEAD_WIDTH), :]
        v = qkv_ref[pl.ds(pl.multiple_of(D + KEYS + kv * HEAD_WIDTH, HEAD_WIDTH), HEAD_WIDTH), :]
        for b in range(length // QB):
            lo, hi = key_span(b)
            s = dot(k[:, lo:hi], three(qkv_ref, kv, b), 0, 0) + wide_bias(bias_ref, b, hi - lo)
            top = jnp.max(s, axis=0, keepdims=True)
            p = jnp.exp(s - top)
            total = jnp.sum(p, axis=0, keepdims=True)
            out = dot(v[:, lo:hi], p.astype(BF16), 1, 0) / total
            lse = top + jnp.log(total)
            for i in range(SHARE):
                rows = pl.ds(pl.multiple_of((kv * SHARE + i) * HEAD_WIDTH, HEAD_WIDTH), HEAD_WIDTH)
                o_ref[rows, b * QB:(b + 1) * QB] = out[:, i * QB:(i + 1) * QB].astype(BF16)
                lse_ref[kv, i:i + 1, b * QB:(b + 1) * QB] = lse[:, i * QB:(i + 1) * QB]


def attend(qkv, segments):
    seqs, length = segments.shape
    wide, rows = qkv.shape
    pairs = seqs * QUERY_HEADS * length * length
    return pl.pallas_call(
        attend_kernel,
        grid=(seqs,),
        in_specs=[
            pl.BlockSpec((wide, length), lambda i: (0, i)),
            pl.BlockSpec((1, 1, length), lambda i: (i, 0, 0)),
            pl.BlockSpec((1, length, 1), lambda i: (i, 0, 0)),
        ],
        out_specs=[
            pl.BlockSpec((D, length), lambda i: (0, i)),
            pl.BlockSpec((KEY_VALUE_HEADS, 8, length), lambda i: (0, 0, i)),
        ],
        out_shape=shaped(((D, rows), BF16), ((KEY_VALUE_HEADS, 8, rows), F32)),
        scratch_shapes=[pltpu.VMEM((length // QB, 3 * QB, QB), F32)],
        compiler_params=params(48),
        cost_estimate=cost(pairs * 256 * 2, rows * (wide + D) * 2, pairs // 2),
        name="attend",
    )(qkv, segments[:, None, :], segments[:, :, None])


def middle_kernel(x_ref, o_ref, w_ref, gain_ref, x1_ref, h_ref):
    x1 = x_ref[...].astype(F32) + dot(w_ref[...], o_ref[...], 0, 0)
    normal, _ = norm_columns(x1)
    x1_ref[...] = x1
    h_ref[...] = (normal * gain_ref[:, 1:2].astype(F32)).astype(BF16)


def middle(x, o, w, gains):
    rows = x.shape[1]
    return pl.pallas_call(
        middle_kernel,
        grid=(rows // TILE,),
        in_specs=[columns(D, TILE), columns(D, TILE), fixed(w.shape), fixed((D, GAINS))],
        out_specs=[columns(D, TILE), columns(D, TILE)],
        out_shape=shaped(((D, rows), F32), ((D, rows), BF16)),
        compiler_params=params(40),
        cost_estimate=cost(2 * rows * D * D, rows * D * 10),
        name="middle",
    )(x, o, w, gains)


def split_owners(grad, core, keep_ref, send_ref):
    for x in range(2):
        a = grad[2 * x * OWN:(2 * x + 1) * OWN]
        b = grad[(2 * x + 1) * OWN:(2 * x + 2) * OWN]
        keep_ref[x, 0] = jnp.where(core == 0, a, b).astype(BF16)
        send_ref[x, 0] = jnp.where(core == 0, b, a).astype(BF16)


def feed_forward_kernel(core_ref, h_ref, dy_ref, x1_ref, wg_ref, wu_ref, wd_ref, y_ref, dh_ref,
                        gg_keep, gg_send, gu_keep, gu_send, gd_keep, gd_send, acc_ref):
    step = pl.program_id(0)
    core = core_ref[0]

    @pl.when(step == 0)
    def _():
        acc_ref[...] = x1_ref[...]
        dh_ref[...] = jnp.zeros_like(dh_ref)

    h, dy = h_ref[...], dy_ref[...]
    gate = dot(wg_ref[...], h, 0, 0)
    up = dot(wu_ref[...], h, 0, 0)
    dhid = dot(wd_ref[...], dy, 0, 0)
    sig = jax.nn.sigmoid(gate)
    silu = gate * sig
    hid = (silu * up).astype(BF16)
    dgate = (dhid * up * (sig + silu * (1.0 - sig))).astype(BF16)
    dup = (dhid * silu).astype(BF16)
    acc_ref[...] += dot(wd_ref[...], hid, 1, 0)
    split_owners(dot(h, dgate, 1, 1), core, gg_keep, gg_send)
    split_owners(dot(h, dup, 1, 1), core, gu_keep, gu_send)
    down = dot(dy, hid, 1, 1).astype(BF16).reshape(4, OWN, CUT)

    @pl.when(step % 2 == core)
    def _():
        gd_keep[0] = down

    @pl.when(step % 2 != core)
    def _():
        gd_send[0] = down

    dh_ref[...] += dot(wg_ref[...], dgate, 1, 0) + dot(wu_ref[...], dup, 1, 0)

    @pl.when(step == pl.num_programs(0) - 1)
    def _():
        y_ref[...] = acc_ref[...].astype(BF16)


def feed_forward(core, h, dy, x1, wg, wu, wd):
    rows, hidden = h.shape[1], wg.shape[1]
    steps = hidden // CUT
    part = (2, steps, OWN, CUT)
    by_rows = pl.BlockSpec((2, 1, OWN, CUT), lambda f: (0, f, 0, 0))
    by_columns = pl.BlockSpec((1, steps, OWN, CUT), lambda f: (f // 2, 0, 0, 0))
    return pl.pallas_call(
        feed_forward_kernel,
        grid=(steps,),
        in_specs=[
            pl.BlockSpec(memory_space=pltpu.SMEM),
            fixed((D, rows)), fixed((D, rows)), fixed((D, rows)),
            columns(D, CUT), columns(D, CUT), columns(D, CUT),
        ],
        out_specs=[fixed((D, rows)), fixed((D, rows))] + [by_rows] * 4 + [by_columns] * 2,
        out_shape=shaped(((D, rows), BF16), ((D, rows), F32)) + shaped((part, BF16)) * 6,
        scratch_shapes=[pltpu.VMEM((D, rows), F32)],
        compiler_params=params(60),
        cost_estimate=cost(18 * rows * D * hidden, 16 * rows * D + 12 * D * hidden, rows * hidden),
        name="feed_forward",
    )(core, h, dy, x1, wg, wu, wd)


def branch_kernel(dh_ref, x1_ref, dy_ref, gain_ref, w_ref, dx_ref, da_ref, do_ref, gain_grad):
    gain = gain_ref[:, 1:2].astype(F32)
    normal, inverse = norm_columns(x1_ref[...])
    back, part = norm_columns_back(dh_ref[...], normal, inverse, gain)
    dx = dy_ref[...].astype(F32) + back
    da = dx.astype(BF16)
    dx_ref[...] = dx
    da_ref[...] = da
    do_ref[...] = dot(w_ref[...], da, 1, 0).astype(BF16)

    @pl.when(pl.program_id(0) == 0)
    def _():
        gain_grad[...] = part

    @pl.when(pl.program_id(0) > 0)
    def _():
        gain_grad[...] += part


def branch(dh, x1, dy, gains, w):
    rows = dh.shape[1]
    return pl.pallas_call(
        branch_kernel,
        grid=(rows // TILE,),
        in_specs=[columns(D, TILE)] * 3 + [fixed((D, GAINS)), fixed(w.shape)],
        out_specs=[columns(D, TILE)] * 3 + [pl.BlockSpec((D, 1), lambda i: (0, 0))],
        out_shape=shaped(((D, rows), F32), ((D, rows), BF16), ((D, rows), BF16), ((D, 1), F32)),
        compiler_params=params(40),
        cost_estimate=cost(2 * rows * D * D, rows * D * 18),
        name="branch",
    )(dh, x1, dy, gains, w)


def attend_back_kernel(qkv_ref, o_ref, do_ref, lse_ref, segr_ref, segc_ref, cos_ref, sin_ref,
                       out_ref, bias_ref, dk_ref, dv_ref):
    length = qkv_ref.shape[1]
    make_bias(bias_ref, segr_ref.at[0], segc_ref.at[0], length)

    def turn_back(g, c, s, at, cols):
        a, b = g[:HALF], g[HALF:]
        at = pl.multiple_of(at, HEAD_WIDTH)
        out_ref[pl.ds(at, HALF), cols] = (a * c + b * s).astype(BF16)
        out_ref[pl.ds(pl.multiple_of(at + HALF, HALF), HALF), cols] = (b * c - a * s).astype(BF16)

    @pl.loop(0, KEY_VALUE_HEADS)
    def _(kv):
        k = qkv_ref[pl.ds(pl.multiple_of(D + kv * HEAD_WIDTH, HEAD_WIDTH), HEAD_WIDTH), :]
        v = qkv_ref[pl.ds(pl.multiple_of(D + KEYS + kv * HEAD_WIDTH, HEAD_WIDTH), HEAD_WIDTH), :]
        dk_ref[...] = jnp.zeros_like(dk_ref)
        dv_ref[...] = jnp.zeros_like(dv_ref)
        for b in range(length // QB):
            lo, hi = key_span(b)
            cols = slice(b * QB, (b + 1) * QB)
            q, o, do = three(qkv_ref, kv, b), three(o_ref, kv, b), three(do_ref, kv, b)
            lse = jnp.concatenate([lse_ref[kv, i:i + 1, cols] for i in range(SHARE)], axis=1)
            inner = jnp.sum(o.astype(F32) * do.astype(F32), axis=0, keepdims=True)
            s = dot(k[:, lo:hi], q, 0, 0) + wide_bias(bias_ref, b, hi - lo)
            p = jnp.exp(s - lse)
            dp = dot(v[:, lo:hi], do, 0, 0)
            ds = (p * (dp - inner)).astype(BF16)
            dv_ref[:, lo:hi] += dot(do, p.astype(BF16), 1, 1)
            dk_ref[:, lo:hi] += dot(q, ds, 1, 1)
            dq = dot(k[:, lo:hi], ds, 1, 0) * HEAD_WIDTH ** -0.5
            for i in range(SHARE):
                turn_back(dq[:, i * QB:(i + 1) * QB], cos_ref[:, cols], sin_ref[:, cols],
                          (kv * SHARE + i) * HEAD_WIDTH, cols)
        turn_back(dk_ref[...], cos_ref[...], sin_ref[...], D + kv * HEAD_WIDTH, slice(None))
        out_ref[pl.ds(pl.multiple_of(D + KEYS + kv * HEAD_WIDTH, HEAD_WIDTH), HEAD_WIDTH), :] = (
            dv_ref[...].astype(BF16))


def attend_back(qkv, o, do, lse, segments, cos, sin):
    seqs, length = segments.shape
    wide, rows = qkv.shape
    pairs = seqs * QUERY_HEADS * length * length
    return pl.pallas_call(
        attend_back_kernel,
        grid=(seqs,),
        in_specs=[
            pl.BlockSpec((wide, length), lambda i: (0, i)),
            pl.BlockSpec((D, length), lambda i: (0, i)),
            pl.BlockSpec((D, length), lambda i: (0, i)),
            pl.BlockSpec((KEY_VALUE_HEADS, 8, length), lambda i: (0, 0, i)),
            pl.BlockSpec((1, 1, length), lambda i: (i, 0, 0)),
            pl.BlockSpec((1, length, 1), lambda i: (i, 0, 0)),
            pl.BlockSpec((HALF, length), lambda i: (0, i)),
            pl.BlockSpec((HALF, length), lambda i: (0, i)),
        ],
        out_specs=pl.BlockSpec((wide, length), lambda i: (0, i)),
        out_shape=jax.ShapeDtypeStruct((wide, rows), BF16),
        scratch_shapes=[
            pltpu.VMEM((length // QB, 3 * QB, QB), F32),
            pltpu.VMEM((HEAD_WIDTH, length), F32),
            pltpu.VMEM((HEAD_WIDTH, length), F32),
        ],
        compiler_params=params(48),
        cost_estimate=cost(pairs * 256 * 5, rows * (2 * wide + 2 * D) * 2, pairs // 2),
        name="attend_back",
    )(qkv, o, do, lse, segments[:, None, :], segments[:, :, None], cos, sin)


def weight_kernel(core_ref, h_ref, dqkv_ref, o_ref, da_ref, keep_ref, send_ref):
    core = core_ref[0]
    step = pl.program_id(0)

    @pl.when(step < 2)
    def _():
        rows = pl.ds(pl.multiple_of(step * CUT, CUT), CUT)
        split_owners(dot(h_ref[...], dqkv_ref[rows, :], 1, 1), core, keep_ref, send_ref)

    @pl.when(step == 2)
    def _():
        left = dot(h_ref[...], dqkv_ref[2 * CUT:, :], 1, 1)
        right = dot(o_ref[...], da_ref[:3 * CUT - WIDE, :], 1, 1)
        split_owners(jnp.concatenate([left, right], axis=1), core, keep_ref, send_ref)

    @pl.when(step == 3)
    def _():
        split_owners(dot(o_ref[...], da_ref[3 * CUT - WIDE:, :], 1, 1), core, keep_ref, send_ref)


def weight_grads(core, h, dqkv, o, da):
    rows = h.shape[1]
    part = pl.BlockSpec((2, 1, OWN, CUT), lambda f: (0, f, 0, 0))
    return pl.pallas_call(
        weight_kernel,
        grid=(4,),
        in_specs=[pl.BlockSpec(memory_space=pltpu.SMEM), fixed((D, rows)), fixed((WIDE, rows)),
                  fixed((D, rows)), fixed((D, rows))],
        out_specs=[part, part],
        out_shape=shaped(((2, 4, OWN, CUT), BF16)) * 2,
        compiler_params=params(40),
        cost_estimate=cost(2 * rows * D * (D + WIDE), rows * (3 * D + WIDE) * 2 + D * 5120),
        name="weight_grads",
    )(core, h, dqkv, o, da)


def inputs_kernel(x_ref, dx_ref, w_ref, dqkv_ref, out_ref, gain_grad):
    gain = w_ref[:, 0:1].astype(F32)
    dh = dot(w_ref[:, GAINS:], dqkv_ref[...], 1, 0)
    normal, inverse = norm_columns(x_ref[...].astype(F32))
    back, part = norm_columns_back(dh, normal, inverse, gain)
    out_ref[...] = (dx_ref[...] + back).astype(BF16)

    @pl.when(pl.program_id(0) == 0)
    def _():
        gain_grad[...] = part

    @pl.when(pl.program_id(0) > 0)
    def _():
        gain_grad[...] += part


def input_grads(x, dx, w, dqkv):
    rows = x.shape[1]
    return pl.pallas_call(
        inputs_kernel,
        grid=(rows // TILE,),
        in_specs=[columns(D, TILE), columns(D, TILE), fixed(w.shape), columns(WIDE, TILE)],
        out_specs=[columns(D, TILE), pl.BlockSpec((D, 1), lambda i: (0, 0))],
        out_shape=shaped(((D, rows), BF16), ((D, 1), F32)),
        compiler_params=params(40),
        cost_estimate=cost(2 * rows * D * WIDE, rows * (D * 8 + WIDE * 2) + D * WIDE * 2),
        name="input_grads",
    )(x, dx, w, dqkv)


def tables(segments):
    length = segments.shape[1]
    index = jnp.arange(length, dtype=jnp.int32)
    same = segments[:, :, None] == segments[:, None, :]
    start = jnp.min(jnp.where(same, index[None, :, None], length), axis=1)
    position = (index[None, :] - start).astype(F32).reshape(1, -1)
    freq = THETA ** (-(jnp.arange(HALF, dtype=F32) * 2.0 / HEAD_WIDTH))
    angle = freq[:, None] * position
    return jnp.cos(angle), jnp.sin(angle)


def after(value, *others):
    return lax.optimization_barrier((value,) + others)[0]


class Cube:
    def __init__(self, count):
        self.count = count
        self.dims = count.bit_length() - 1
        self.masks = [1, 2, 6] + [1 << i for i in range(3, self.dims)]
        replica, group = lax.axis_index("replica"), lax.axis_index("group")
        bits = [(replica >> i) & 1 for i in range(self.dims)]
        self.coordinate = {i: bits[i] for i in range(self.dims)}
        self.coordinate[1] = bits[1] ^ bits[2]
        self.coordinate["x"] = group >> 1
        self.coordinate["core"] = group & 1

    def swap(self, value, dim):
        if dim == "x":
            return lax.ppermute(value, "group", [(i, i ^ 2) for i in range(4)])
        if dim == "core":
            return lax.ppermute(value, "group", [(i, i ^ 1) for i in range(4)])
        mask = self.masks[dim]
        return lax.ppermute(value, "replica", [(i, i ^ mask) for i in range(self.count)])

    def ordered(self, dim, mine, other, axis):
        return jnp.where(
            self.coordinate[dim] == 0,
            jnp.concatenate([mine, other], axis=axis),
            jnp.concatenate([other, mine], axis=axis),
        )


def gather(cube, shard, axis, relay, halves):
    sibling = cube.swap(shard, "core")
    if relay is None:
        across = cube.swap(shard, "x")
    else:
        size = shard.shape[halves] // 2
        part = lax.dynamic_slice_in_dim(shard, cube.coordinate[relay] * size, size, halves)
        direct = cube.swap(part, "x")
        across = cube.ordered(relay, direct, cube.swap(direct, relay), halves)
    diagonal = cube.swap(across, "core")
    here = cube.ordered("core", shard, sibling, axis)
    there = cube.ordered("core", across, diagonal, axis)
    return cube.ordered("x", here, there, axis)


def reduce_piece(cube, keep, got, order):
    rows, wide = keep.shape[2:]
    total = keep.astype(F32) + got.astype(F32)
    total = total.reshape(2, 2, 2, rows, wide)
    cut = [d for d in order if d != "x"]
    place = {"x": 0, cut[0]: 1, cut[1]: 2}
    for dim in order:
        mine = cube.coordinate[dim]
        other = lax.dynamic_slice_in_dim(total, 1 - mine, 1, place[dim]).astype(BF16)
        own = lax.dynamic_slice_in_dim(total, mine, 1, place[dim])
        total = own + cube.swap(other, dim).astype(F32)
    low = total.astype(BF16)
    for dim in range(cube.dims):
        if dim not in cut:
            low = (low.astype(F32) + cube.swap(low, dim).astype(F32)).astype(BF16)
    for dim in reversed(cut):
        low = cube.ordered(dim, low, cube.swap(low, dim), place[dim])
    return low.reshape(4, rows, wide)


def per_device(
    tokens,
    segments,
    query_weight,
    key_weight,
    value_weight,
    output_weight,
    w_gate,
    w_up,
    w_down,
    attn_gain,
    ffn_gain,
    cotangent,
    replicas,
):
    cube = Cube(replicas)
    core = cube.coordinate["core"].astype(jnp.int32).reshape(1)
    x, dy = tokens.T, cotangent.T
    pad = jnp.zeros((attn_gain.shape[0], GAINS - 2), BF16)
    first = jnp.concatenate(
        [attn_gain[:, None], ffn_gain[:, None], pad, query_weight, key_weight, value_weight], axis=1
    )
    wqkv = gather(cube, first, 0, None, 1)
    wo = gather(cube, output_weight, 0, None, 1)
    wg = gather(cube, w_gate, 0, 0, 1)
    wu = gather(cube, w_up, 0, 1, 1)
    wd = gather(cube, w_down.T, 1, 2, 0)
    gains = wqkv[:, :GAINS]

    cos, sin = tables(segments)
    qkv, h = project(x, wqkv, cos, sin)
    o, lse = attend(qkv, segments)
    x1, h2 = middle(x, o, wo, gains)
    y, dh2, gg_keep, gg_send, gu_keep, gu_send, gd_keep, gd_send = feed_forward(
        core, h2, dy, x1, wg, wu, wd
    )
    dx1, da, do, ffn_gain_grad = branch(dh2, x1, dy, gains, wo)
    dqkv = attend_back(qkv, o, do, lse, segments, cos, sin)
    ga_keep, ga_send = weight_grads(core, h, dqkv, o, da)
    grad_x, attn_gain_grad = input_grads(x, dx1, wqkv, dqkv)

    gg = reduce_piece(cube, gg_keep, cube.swap(gg_send, "core"), ("x", 0, 1))
    gu = reduce_piece(cube, gu_keep, cube.swap(gu_send, "core"), (1, "x", 2))
    gd = reduce_piece(cube, gd_keep, cube.swap(gd_send, "core"), (2, 0, "x"))
    ga_got = cube.swap(ga_send, "core")
    orders = (("x", 0, 1), (1, "x", 2), (2, 0, "x"))
    size = OWN // len(orders)
    ga = jnp.concatenate(
        [
            reduce_piece(cube, ga_keep[:, :, i * size:(i + 1) * size],
                         ga_got[:, :, i * size:(i + 1) * size], order)
            for i, order in enumerate(orders)
        ],
        axis=1,
    )
    flat = lambda g: jnp.swapaxes(g, 0, 1).reshape(OWN, 4 * CUT).astype(F32)
    ga = flat(ga)
    both = lax.psum(jnp.concatenate([attn_gain_grad, ffn_gain_grad], axis=1), ("group", "replica"))
    both = lax.dynamic_slice_in_dim(both, lax.axis_index("group") * OWN, OWN, 0)
    return (
        y.T,
        grad_x.T,
        ga[:, :D],
        ga[:, D:D + KEYS],
        ga[:, D + KEYS:WIDE],
        ga[:, WIDE:],
        flat(gg),
        flat(gu),
        gd.reshape(D, CUT).T.astype(F32),
        both[:, 0],
        both[:, 1],
    )


def solution(mesh):
    rows = P(("group", "replica"), None)
    weight, gain = P("group", None), P("group")
    replicas = mesh.shape["replica"]
    return jax.shard_map(
        lambda *args: per_device(*args, replicas),
        mesh=mesh,
        in_specs=(rows, rows) + (weight,) * 7 + (gain, gain, rows),
        out_specs=(rows, rows) + (weight,) * 7 + (gain, gain),
        check_vma=False,
    )
```

```python
import functools

import jax
import jax.numpy as jnp
from jax import lax
from jax.experimental import pallas as pl
from jax.experimental.pallas import tpu as pltpu
from jax.sharding import PartitionSpec as P

D = 960
QUERY_HEADS = 15
KEY_VALUE_HEADS = 5
HEAD_WIDTH = 64
SHARE = QUERY_HEADS // KEY_VALUE_HEADS
HALF = HEAD_WIDTH // 2
KEYS = KEY_VALUE_HEADS * HEAD_WIDTH
EPS = 1e-05
THETA = 100000.0
TILE = 256
QB = 128
GAINS = 128
WIDE = D + 2 * KEYS
CUT = 640
OWN = 240
F32 = jnp.float32
BF16 = jnp.bfloat16
MIB = 1 << 20


def dot(a, b, ca, cb):
    return lax.dot_general(a, b, (((ca,), (cb,)), ((), ())), preferred_element_type=F32)


def params(limit, grid=1):
    return pltpu.CompilerParams(
        vmem_limit_bytes=limit * MIB, dimension_semantics=("arbitrary",) * grid
    )


def cost(flops, moved, exps=0):
    return pl.CostEstimate(flops=flops, bytes_accessed=moved, transcendentals=exps)


def shaped(*shape_type):
    return [jax.ShapeDtypeStruct(s, t) for s, t in shape_type]


def norm_columns(v):
    inverse = lax.rsqrt(jnp.mean(v * v, axis=0, keepdims=True) + EPS)
    return v * inverse, inverse


def norm_columns_back(grad, normal, inverse, gain):
    scaled = grad * gain
    back = inverse * (scaled - normal * jnp.mean(scaled * normal, axis=0, keepdims=True))
    return back, jnp.sum(grad * normal, axis=1, keepdims=True)


def fixed(shape):
    return pl.BlockSpec(shape, lambda *_: (0,) * len(shape), pipeline_mode=pl.Buffered(1))


def columns(height, width):
    return pl.BlockSpec((height, width), lambda i: (0, i))


class Weight:
    def __init__(self, axis, pieces, dim=None, blocks=0):
        self.axis, self.dim, self.blocks = axis, dim, blocks
        self.arrays = [array for array, _, _ in pieces]
        self.places = [(flip, side) for _, flip, side in pieces]
        shape = list(self.arrays[0].shape)
        self.size = shape[axis]
        self.half = shape[1 - axis] // 2
        shape[axis] *= 4
        self.shape = tuple(shape)

    def specs(self):
        return [pl.BlockSpec(memory_space=pl.ANY)] * len(self.arrays)

    def scratch(self):
        if not self.blocks:
            return [pltpu.VMEM(self.shape, BF16), pltpu.SemaphoreType.DMA]
        block = (self.shape[0], self.shape[1] // self.blocks)
        return [pltpu.VMEM((self.blocks,) + block, BF16), pltpu.SemaphoreType.DMA((self.blocks,))]

    def load(self, where_ref, refs, scratch, sem):
        wide = self.shape[1] // max(self.blocks, 1)
        for ref, (flip, side) in zip(refs, self.places):
            at = (where_ref[0] ^ flip) * self.size
            other = 0 if side is None else (where_ref[1 + self.dim] ^ side) * self.half
            row, column = (at, other) if self.axis == 0 else (other, at)
            rows = pl.ds(pl.multiple_of(row, OWN), ref.shape[0])
            if not self.blocks:
                pltpu.make_async_copy(ref, scratch.at[rows, :], sem).start()
                continue
            first = column // wide
            for i in range(ref.shape[1] // wide):
                pltpu.make_async_copy(
                    ref.at[:, i * wide:(i + 1) * wide], scratch.at[first + i, rows, :],
                    sem.at[first + i],
                ).start()


def wait_for(scratch, sem):
    pltpu.make_async_copy(scratch, scratch, sem).wait()


SMEM = pl.BlockSpec(memory_space=pltpu.SMEM)


def project_kernel(weights, where_ref, x_ref, cos_ref, sin_ref, *refs):
    qkv_ref, h_ref, gains_ref, wq, q_sem, wk, k_sem = refs[8:]

    @pl.when(pl.program_id(0) == 0)
    def _():
        weights[0].load(where_ref, refs[:4], wq, q_sem)
        weights[1].load(where_ref, refs[4:8], wk, k_sem)
        wait_for(wq, q_sem)
        wait_for(wk, k_sem)
        gains_ref[...] = wk[:, 2 * KEYS:]

    gain = wk[:, 2 * KEYS:2 * KEYS + 1].astype(F32)
    normal, _ = norm_columns(x_ref[...].astype(F32))
    h = (normal * gain).astype(BF16)
    h_ref[...] = h
    c, s = cos_ref[...], sin_ref[...]

    def rotary(out, at, heads, scale):
        for head in range(heads):
            low = head * HEAD_WIDTH
            a, b = out[low:low + HALF], out[low + HALF:low + HEAD_WIDTH]
            to = at + low
            qkv_ref[to:to + HALF, :] = ((a * c - b * s) * scale).astype(BF16)
            qkv_ref[to + HALF:to + HEAD_WIDTH, :] = ((b * c + a * s) * scale).astype(BF16)

    rotary(dot(wq[...], h, 0, 0), 0, QUERY_HEADS, HEAD_WIDTH ** -0.5)
    out = dot(wk[:, :2 * KEYS], h, 0, 0)
    rotary(out, D, KEY_VALUE_HEADS, 1.0)
    qkv_ref[D + KEYS:, :] = out[KEYS:].astype(BF16)


def project(where, x, wq, wk, cos, sin):
    rows = x.shape[1]
    return pl.pallas_call(
        functools.partial(project_kernel, (wq, wk)),
        grid=(rows // TILE,),
        in_specs=[SMEM, columns(D, TILE), columns(HALF, TILE), columns(HALF, TILE)]
        + wq.specs() + wk.specs(),
        out_specs=[columns(WIDE, TILE), columns(D, TILE),
                   pl.BlockSpec((D, GAINS), lambda i: (0, 0))],
        out_shape=shaped(((WIDE, rows), BF16), ((D, rows), BF16), ((D, GAINS), BF16)),
        scratch_shapes=wq.scratch() + wk.scratch(),
        compiler_params=params(40),
        cost_estimate=cost(2 * rows * D * WIDE, rows * (2 * D + WIDE) * 2 + D * WIDE * 2),
        name="project",
    )(where, x, cos, sin, *wq.arrays, *wk.arrays)


def key_span(block):
    return max(0, QB * (block - 2)), QB * (block + 1)


def make_bias(bias_ref, segr_ref, segc_ref, length):
    for b in range(length // QB):
        lo, hi = key_span(b)
        key_at = lax.broadcasted_iota(jnp.int32, (hi - lo, QB), 0) + lo
        query_at = lax.broadcasted_iota(jnp.int32, (hi - lo, QB), 1) + b * QB
        ok = (segc_ref[lo:hi, :] == segr_ref[:, b * QB:(b + 1) * QB]) & (key_at <= query_at)
        bias_ref[b, 0:hi - lo, :] = jnp.where(ok, 0.0, -1e30)


def three(ref, kv, b):
    return jnp.concatenate(
        [
            ref[pl.ds(pl.multiple_of((kv * SHARE + i) * HEAD_WIDTH, HEAD_WIDTH), HEAD_WIDTH),
                b * QB:(b + 1) * QB]
            for i in range(SHARE)
        ],
        axis=1,
    )


def wide_bias(bias_ref, b, n):
    one = bias_ref[b, 0:n, :]
    return jnp.concatenate([one] * SHARE, axis=1)


def attend_kernel(qkv_ref, segr_ref, segc_ref, o_ref, lse_ref, bias_ref):
    length = qkv_ref.shape[1]
    make_bias(bias_ref, segr_ref.at[0], segc_ref.at[0], length)

    @pl.loop(0, KEY_VALUE_HEADS)
    def _(kv):
        k = qkv_ref[pl.ds(pl.multiple_of(D + kv * HEAD_WIDTH, HEAD_WIDTH), HEAD_WIDTH), :]
        v = qkv_ref[pl.ds(pl.multiple_of(D + KEYS + kv * HEAD_WIDTH, HEAD_WIDTH), HEAD_WIDTH), :]
        for b in range(length // QB):
            lo, hi = key_span(b)
            s = dot(k[:, lo:hi], three(qkv_ref, kv, b), 0, 0) + wide_bias(bias_ref, b, hi - lo)
            top = jnp.max(s, axis=0, keepdims=True)
            p = jnp.exp(s - top)
            total = jnp.sum(p, axis=0, keepdims=True)
            out = dot(v[:, lo:hi], p.astype(BF16), 1, 0) / total
            lse = top + jnp.log(total)
            for i in range(SHARE):
                rows = pl.ds(pl.multiple_of((kv * SHARE + i) * HEAD_WIDTH, HEAD_WIDTH), HEAD_WIDTH)
                o_ref[rows, b * QB:(b + 1) * QB] = out[:, i * QB:(i + 1) * QB].astype(BF16)
                lse_ref[kv, i:i + 1, b * QB:(b + 1) * QB] = lse[:, i * QB:(i + 1) * QB]


def attend(qkv, segments, at):
    length = segments.shape[1]
    wide = qkv.shape[0]
    pairs = QUERY_HEADS * length * length
    return pl.pallas_call(
        attend_kernel,
        grid=(1,),
        in_specs=[
            pl.BlockSpec((wide, length), lambda i: (0, at)),
            pl.BlockSpec((1, 1, length), lambda i: (at, 0, 0)),
            pl.BlockSpec((1, length, 1), lambda i: (at, 0, 0)),
        ],
        out_specs=[
            pl.BlockSpec((D, length), lambda i: (0, 0)),
            pl.BlockSpec((KEY_VALUE_HEADS, 8, length), lambda i: (0, 0, 0)),
        ],
        out_shape=shaped(((D, length), BF16), ((KEY_VALUE_HEADS, 8, length), F32)),
        scratch_shapes=[pltpu.VMEM((length // QB, 3 * QB, QB), F32)],
        compiler_params=params(40),
        cost_estimate=cost(pairs * 256 * 2, length * (wide + D) * 2, pairs // 2),
        name="attend",
    )(qkv, segments[:, None, :], segments[:, :, None])


def middle_kernel(weight, where_ref, x_ref, o_ref, gain_ref, *refs):
    x1_ref, h_ref, w, sem = refs[4:]

    @pl.when(pl.program_id(0) == 0)
    def _():
        weight.load(where_ref, refs[:4], w, sem)
        wait_for(w, sem)

    x1 = x_ref[...].astype(F32) + dot(w[...], o_ref[...], 0, 0)
    normal, _ = norm_columns(x1)
    x1_ref[...] = x1
    h_ref[...] = (normal * gain_ref[:, 1:2].astype(F32)).astype(BF16)


def middle(where, x, o, w, gains):
    rows = x.shape[1]
    return pl.pallas_call(
        functools.partial(middle_kernel, w),
        grid=(rows // TILE,),
        in_specs=[SMEM, columns(D, TILE), columns(D, TILE), fixed((D, GAINS))] + w.specs(),
        out_specs=[columns(D, TILE), columns(D, TILE)],
        out_shape=shaped(((D, rows), F32), ((D, rows), BF16)),
        scratch_shapes=w.scratch(),
        compiler_params=params(40),
        cost_estimate=cost(2 * rows * D * D, rows * D * 10),
        name="middle",
    )(where, x, o, gains, *w.arrays)


def split_owners(grad, core, keep_ref, send_ref):
    for x in range(2):
        a = grad[2 * x * OWN:(2 * x + 1) * OWN]
        b = grad[(2 * x + 1) * OWN:(2 * x + 2) * OWN]
        keep_ref[x, 0] = jnp.where(core == 0, a, b).astype(BF16)
        send_ref[x, 0] = jnp.where(core == 0, b, a).astype(BF16)


def feed_forward_kernel(weights, where_ref, h_ref, dy_ref, x1_ref, *refs):
    count = len(weights[0].arrays)
    (y_ref, dh_ref, gg_keep, gg_send, gu_keep, gu_send, gd_keep, gd_send, acc_ref, *scratch) = (
        refs[3 * count:]
    )
    step = pl.program_id(0)
    core = where_ref[0] & 1

    @pl.when(step == 0)
    def _():
        for i, weight in enumerate(weights):
            weight.load(where_ref, refs[i * count:(i + 1) * count], *scratch[2 * i:2 * i + 2])
        acc_ref[...] = x1_ref[...]
        dh_ref[...] = jnp.zeros_like(dh_ref)

    wg_ref, wu_ref, wd_ref = (w.at[step] for w in scratch[::2])
    for w, sem in zip((wg_ref, wu_ref, wd_ref), scratch[1::2]):
        wait_for(w, sem.at[step])
    h, dy = h_ref[...], dy_ref[...]
    gate = dot(wg_ref[...], h, 0, 0)
    up = dot(wu_ref[...], h, 0, 0)
    dhid = dot(wd_ref[...], dy, 0, 0)
    sig = jax.nn.sigmoid(gate)
    silu = gate * sig
    hid = (silu * up).astype(BF16)
    dgate = (dhid * up * (sig + silu * (1.0 - sig))).astype(BF16)
    dup = (dhid * silu).astype(BF16)
    acc_ref[...] += dot(wd_ref[...], hid, 1, 0)
    split_owners(dot(h, dgate, 1, 1), core, gg_keep, gg_send)
    split_owners(dot(h, dup, 1, 1), core, gu_keep, gu_send)
    down = dot(dy, hid, 1, 1).astype(BF16).reshape(4, OWN, CUT)

    @pl.when(step % 2 == core)
    def _():
        gd_keep[0] = down

    @pl.when(step % 2 != core)
    def _():
        gd_send[0] = down

    dh_ref[...] += dot(wg_ref[...], dgate, 1, 0) + dot(wu_ref[...], dup, 1, 0)

    @pl.when(step == pl.num_programs(0) - 1)
    def _():
        y_ref[...] = acc_ref[...].astype(BF16)


def feed_forward(where, h, dy, x1, weights):
    rows, hidden = h.shape[1], weights[0].shape[1]
    steps = hidden // CUT
    part = (2, steps, OWN, CUT)
    by_rows = pl.BlockSpec((2, 1, OWN, CUT), lambda f: (0, f, 0, 0))
    by_columns = pl.BlockSpec((1, steps, OWN, CUT), lambda f: (f // 2, 0, 0, 0))
    return pl.pallas_call(
        functools.partial(feed_forward_kernel, weights),
        grid=(steps,),
        in_specs=[
            SMEM,
            fixed((D, rows)), fixed((D, rows)), fixed((D, rows)),
        ] + sum((w.specs() for w in weights), []),
        out_specs=[fixed((D, rows)), fixed((D, rows))] + [by_rows] * 4 + [by_columns] * 2,
        out_shape=shaped(((D, rows), BF16), ((D, rows), F32)) + shaped((part, BF16)) * 6,
        scratch_shapes=sum((w.scratch() for w in weights), [pltpu.VMEM((D, rows), F32)]),
        compiler_params=params(60),
        cost_estimate=cost(18 * rows * D * hidden, 16 * rows * D + 12 * D * hidden, rows * hidden),
        name="feed_forward",
    )(where, h, dy, x1, *sum((w.arrays for w in weights), []))


def branch_kernel(weight, where_ref, dh_ref, x1_ref, dy_ref, gain_ref, *refs):
    dx_ref, da_ref, do_ref, gain_grad, w, sem = refs[4:]
    first = pl.program_id(0) == 0

    @pl.when(first)
    def _():
        weight.load(where_ref, refs[:4], w, sem)

    gain = gain_ref[:, 1:2].astype(F32)
    normal, inverse = norm_columns(x1_ref[...])
    back, part = norm_columns_back(dh_ref[...], normal, inverse, gain)
    dx = dy_ref[...].astype(F32) + back
    da = dx.astype(BF16)
    dx_ref[...] = dx
    da_ref[...] = da

    @pl.when(first)
    def _():
        gain_grad[...] = part
        wait_for(w, sem)

    @pl.when(jnp.logical_not(first))
    def _():
        gain_grad[...] += part

    do_ref[...] = dot(w[...], da, 1, 0).astype(BF16)


def branch(where, dh, x1, dy, gains, w):
    rows = dh.shape[1]
    return pl.pallas_call(
        functools.partial(branch_kernel, w),
        grid=(rows // TILE,),
        in_specs=[SMEM] + [columns(D, TILE)] * 3 + [fixed((D, GAINS))] + w.specs(),
        out_specs=[columns(D, TILE)] * 3 + [pl.BlockSpec((D, 1), lambda i: (0, 0))],
        out_shape=shaped(((D, rows), F32), ((D, rows), BF16), ((D, rows), BF16), ((D, 1), F32)),
        scratch_shapes=w.scratch(),
        compiler_params=params(40),
        cost_estimate=cost(2 * rows * D * D, rows * D * 18),
        name="branch",
    )(where, dh, x1, dy, gains, *w.arrays)


def attend_back_kernel(qkv_ref, o_ref, do_ref, lse_ref, segr_ref, segc_ref, cos_ref, sin_ref,
                       out_ref, bias_ref, dk_ref, dv_ref):
    length = qkv_ref.shape[1]
    make_bias(bias_ref, segr_ref.at[0], segc_ref.at[0], length)

    def turn_back(g, c, s, at, cols):
        a, b = g[:HALF], g[HALF:]
        at = pl.multiple_of(at, HEAD_WIDTH)
        out_ref[pl.ds(at, HALF), cols] = (a * c + b * s).astype(BF16)
        out_ref[pl.ds(pl.multiple_of(at + HALF, HALF), HALF), cols] = (b * c - a * s).astype(BF16)

    @pl.loop(0, KEY_VALUE_HEADS)
    def _(kv):
        k = qkv_ref[pl.ds(pl.multiple_of(D + kv * HEAD_WIDTH, HEAD_WIDTH), HEAD_WIDTH), :]
        v = qkv_ref[pl.ds(pl.multiple_of(D + KEYS + kv * HEAD_WIDTH, HEAD_WIDTH), HEAD_WIDTH), :]
        dk_ref[...] = jnp.zeros_like(dk_ref)
        dv_ref[...] = jnp.zeros_like(dv_ref)
        for b in range(length // QB):
            lo, hi = key_span(b)
            cols = slice(b * QB, (b + 1) * QB)
            q, o, do = three(qkv_ref, kv, b), three(o_ref, kv, b), three(do_ref, kv, b)
            lse = jnp.concatenate([lse_ref[kv, i:i + 1, cols] for i in range(SHARE)], axis=1)
            inner = jnp.sum(o.astype(F32) * do.astype(F32), axis=0, keepdims=True)
            s = dot(k[:, lo:hi], q, 0, 0) + wide_bias(bias_ref, b, hi - lo)
            p = jnp.exp(s - lse)
            dp = dot(v[:, lo:hi], do, 0, 0)
            ds = (p * (dp - inner)).astype(BF16)
            dv_ref[:, lo:hi] += dot(do, p.astype(BF16), 1, 1)
            dk_ref[:, lo:hi] += dot(q, ds, 1, 1)
            dq = dot(k[:, lo:hi], ds, 1, 0) * HEAD_WIDTH ** -0.5
            for i in range(SHARE):
                turn_back(dq[:, i * QB:(i + 1) * QB], cos_ref[:, cols], sin_ref[:, cols],
                          (kv * SHARE + i) * HEAD_WIDTH, cols)
        turn_back(dk_ref[...], cos_ref[...], sin_ref[...], D + kv * HEAD_WIDTH, slice(None))
        out_ref[pl.ds(pl.multiple_of(D + KEYS + kv * HEAD_WIDTH, HEAD_WIDTH), HEAD_WIDTH), :] = (
            dv_ref[...].astype(BF16))


def attend_back(qkv, o, do, lse, segments, cos, sin, at):
    length = segments.shape[1]
    wide = qkv.shape[0]
    pairs = QUERY_HEADS * length * length
    here = lambda height: pl.BlockSpec((height, length), lambda i: (0, at))
    return pl.pallas_call(
        attend_back_kernel,
        grid=(1,),
        in_specs=[
            here(wide),
            pl.BlockSpec((D, length), lambda i: (0, 0)),
            here(D),
            pl.BlockSpec((KEY_VALUE_HEADS, 8, length), lambda i: (0, 0, 0)),
            pl.BlockSpec((1, 1, length), lambda i: (at, 0, 0)),
            pl.BlockSpec((1, length, 1), lambda i: (at, 0, 0)),
            here(HALF),
            here(HALF),
        ],
        out_specs=pl.BlockSpec((wide, length), lambda i: (0, 0)),
        out_shape=jax.ShapeDtypeStruct((wide, length), BF16),
        scratch_shapes=[
            pltpu.VMEM((length // QB, 3 * QB, QB), F32),
            pltpu.VMEM((HEAD_WIDTH, length), F32),
            pltpu.VMEM((HEAD_WIDTH, length), F32),
        ],
        compiler_params=params(40),
        cost_estimate=cost(pairs * 256 * 5, length * (2 * wide + 2 * D) * 2, pairs // 2),
        name="attend_back",
    )(qkv, o, do, lse, segments[:, None, :], segments[:, :, None], cos, sin)


def weight_kernel(where_ref, h_ref, dqkv_ref, o_ref, da_ref, keep_ref, send_ref):
    core = where_ref[0] & 1
    step = pl.program_id(0)

    @pl.when(step < 2)
    def _():
        rows = pl.ds(pl.multiple_of(step * CUT, CUT), CUT)
        split_owners(dot(h_ref[...], dqkv_ref[rows, :], 1, 1), core, keep_ref, send_ref)

    @pl.when(step == 2)
    def _():
        left = dot(h_ref[...], dqkv_ref[2 * CUT:, :], 1, 1)
        right = dot(o_ref[...], da_ref[:3 * CUT - WIDE, :], 1, 1)
        split_owners(jnp.concatenate([left, right], axis=1), core, keep_ref, send_ref)

    @pl.when(step == 3)
    def _():
        split_owners(dot(o_ref[...], da_ref[3 * CUT - WIDE:, :], 1, 1), core, keep_ref, send_ref)


def weight_grads(where, h, dqkv, o, da):
    rows = h.shape[1]
    part = pl.BlockSpec((2, 1, OWN, CUT), lambda f: (0, f, 0, 0))
    return pl.pallas_call(
        weight_kernel,
        grid=(4,),
        in_specs=[SMEM, fixed((D, rows)), fixed((WIDE, rows)),
                  fixed((D, rows)), fixed((D, rows))],
        out_specs=[part, part],
        out_shape=shaped(((2, 4, OWN, CUT), BF16)) * 2,
        compiler_params=params(40),
        cost_estimate=cost(2 * rows * D * (D + WIDE), rows * (3 * D + WIDE) * 2 + D * 5120),
        name="weight_grads",
    )(where, h, dqkv, o, da)


def inputs_kernel(weights, where_ref, x_ref, dx_ref, dqkv_ref, *refs):
    out_ref, gain_grad, wq, q_sem, wk, k_sem = refs[8:]
    first = pl.program_id(0) == 0

    @pl.when(first)
    def _():
        weights[0].load(where_ref, refs[:4], wq, q_sem)
        weights[1].load(where_ref, refs[4:8], wk, k_sem)
        wait_for(wq, q_sem)
        wait_for(wk, k_sem)

    gain = wk[:, 2 * KEYS:2 * KEYS + 1].astype(F32)
    dh = dot(wq[...], dqkv_ref[:D], 1, 0) + dot(wk[:, :2 * KEYS], dqkv_ref[D:], 1, 0)
    normal, inverse = norm_columns(x_ref[...].astype(F32))
    back, part = norm_columns_back(dh, normal, inverse, gain)
    out_ref[...] = (dx_ref[...] + back).astype(BF16)

    @pl.when(first)
    def _():
        gain_grad[...] = part

    @pl.when(jnp.logical_not(first))
    def _():
        gain_grad[...] += part


def input_grads(where, x, dx, wq, wk, dqkv):
    rows = x.shape[1]
    return pl.pallas_call(
        functools.partial(inputs_kernel, (wq, wk)),
        grid=(rows // TILE,),
        in_specs=[SMEM, columns(D, TILE), columns(D, TILE), columns(WIDE, TILE)]
        + wq.specs() + wk.specs(),
        out_specs=[columns(D, TILE), pl.BlockSpec((D, 1), lambda i: (0, 0))],
        out_shape=shaped(((D, rows), BF16), ((D, 1), F32)),
        scratch_shapes=wq.scratch() + wk.scratch(),
        compiler_params=params(40),
        cost_estimate=cost(2 * rows * D * WIDE, rows * (D * 8 + WIDE * 2) + D * WIDE * 2),
        name="input_grads",
    )(where, x, dx, dqkv, *wq.arrays, *wk.arrays)


def tables(segments):
    length = segments.shape[1]
    index = jnp.arange(length, dtype=jnp.int32)
    same = segments[:, :, None] == segments[:, None, :]
    start = jnp.min(jnp.where(same, index[None, :, None], length), axis=1)
    position = (index[None, :] - start).astype(F32).reshape(1, -1)
    freq = THETA ** (-(jnp.arange(HALF, dtype=F32) * 2.0 / HEAD_WIDTH))
    angle = freq[:, None] * position
    return jnp.cos(angle), jnp.sin(angle)


def after(value, *others):
    return lax.optimization_barrier((value,) + others)[0]


class Cube:
    def __init__(self, count):
        self.count = count
        self.dims = count.bit_length() - 1
        self.masks = [1, 2, 6] + [1 << i for i in range(3, self.dims)]
        replica, group = lax.axis_index("replica"), lax.axis_index("group")
        bits = [(replica >> i) & 1 for i in range(self.dims)]
        self.coordinate = {i: bits[i] for i in range(self.dims)}
        self.coordinate[1] = bits[1] ^ bits[2]
        self.coordinate["x"] = group >> 1
        self.coordinate["core"] = group & 1
        self.me = group

    def swap(self, value, dim):
        if dim == "x":
            return lax.ppermute(value, "group", [(i, i ^ 2) for i in range(4)])
        if dim == "core":
            return lax.ppermute(value, "group", [(i, i ^ 1) for i in range(4)])
        mask = self.masks[dim]
        return lax.ppermute(value, "replica", [(i, i ^ mask) for i in range(self.count)])

    def ordered(self, dim, mine, other, axis):
        return jnp.where(
            self.coordinate[dim] == 0,
            jnp.concatenate([mine, other], axis=axis),
            jnp.concatenate([other, mine], axis=axis),
        )


def rows_of(own, sibling, across, diagonal):
    pieces = own, sibling, across, diagonal
    return Weight(0, [(array, flip, None) for flip, array in enumerate(pieces)])


class Relay:
    def __init__(self, cube, shard, axis, first, second):
        self.cube, self.shard, self.axis, self.dims = cube, shard, axis, (first, second)
        self.cut = 1 - axis
        self.size = shard.shape[self.cut] // 4
        at = 2 * cube.coordinate[second] + cube.coordinate[first]
        self.quarter = lax.dynamic_slice_in_dim(shard, at * self.size, self.size, self.cut)

    def cross(self, *others):
        self.direct = self.cube.swap(after(self.quarter, *others), "x")
        return self.direct

    def hand_on(self, *others):
        self.handed = self.cube.swap(after(self.direct, *others), self.dims[0])
        return self.handed

    def finish(self, *others):
        cube = self.cube
        handed = after(self.handed, *others)
        self.half = cube.ordered(self.dims[0], self.direct, handed, self.cut)
        self.rest = cube.swap(self.half, self.dims[1])
        self.half_diagonal = cube.swap(self.half, "core")
        return self.rest

    def weight(self, sibling, *others):
        rest = after(self.rest, *others)
        pieces = [
            (self.shard, 0, None), (sibling, 1, None), (self.half, 2, 0), (rest, 2, 1),
            (self.half_diagonal, 3, 0), (self.cube.swap(rest, "core"), 3, 1),
        ]
        return Weight(self.axis, pieces, self.dims[1], 4)


class Reduce:
    def __init__(self, cube, keep, got, order):
        rows, wide = keep.shape[2:]
        self.cube, self.order, self.shape = cube, order, (4, rows, wide)

        self.cut = [d for d in order[:2] if d != "x"][0]
        self.terms = [t.reshape(2, 2, 2, rows, wide) for t in (keep, got)]
        self.got = None

    def sum(self):
        return functools.reduce(jnp.add, [t.astype(F32) for t in self.terms]).astype(BF16)

    def step(self, index, *others):
        cube, dim = self.cube, self.order[index]
        if index < 2:
            mine, axis = cube.coordinate[dim], 0 if dim == "x" else 1
            take = lambda which: [
                lax.dynamic_slice_in_dim(t, which, 1, axis) for t in self.terms
            ]
            other, self.terms = take(1 - mine), take(mine)
            send = functools.reduce(jnp.add, [t.astype(F32) for t in other]).astype(BF16)
            self.got = cube.swap(after(send, *others), dim)
            self.terms = self.terms + [self.got]
        elif dim != self.cut:
            low = after(self.sum(), *others)
            self.got = cube.swap(low, dim)
            self.terms = [low, self.got]
        else:
            low = after(self.sum(), *others)
            self.got = cube.swap(low, dim)
            self.result = cube.ordered(dim, low, self.got, 1).reshape(self.shape)
        return self.got


def per_device(
    tokens,
    segments,
    query_weight,
    key_weight,
    value_weight,
    output_weight,
    w_gate,
    w_up,
    w_down,
    attn_gain,
    ffn_gain,
    cotangent,
    replicas,
):
    cube = Cube(replicas)
    where = jnp.stack([cube.me] + [cube.coordinate[i] for i in range(3)]).astype(jnp.int32)
    x, dy = tokens.T, cotangent.T

    q_across = cube.swap(query_weight, "x")
    pad = jnp.zeros((OWN, GAINS - 2), BF16)
    kv = jnp.concatenate(
        [key_weight, value_weight, attn_gain[:, None], ffn_gain[:, None], pad], axis=1
    )
    kv_across = cube.swap(kv, "x")
    q_sibling, kv_sibling = cube.swap(query_weight, "core"), cube.swap(kv, "core")
    q_diagonal, kv_diagonal = cube.swap(q_across, "core"), cube.swap(kv_across, "core")
    wq = rows_of(query_weight, q_sibling, q_across, q_diagonal)
    wk = rows_of(kv, kv_sibling, kv_across, kv_diagonal)
    cos, sin = tables(segments)
    relays = [
        Relay(cube, w_gate, 0, 0, 1), Relay(cube, w_up, 0, 1, 2), Relay(cube, w_down.T, 1, 2, 0)
    ]
    direct = [relay.cross(q_across, kv_across) for relay in relays]
    qkv, h, gains = project(where, x, wq, wk, cos, sin)
    wo_across = cube.swap(after(output_weight, qkv), "x")
    siblings = [cube.swap(after(relay.shard, qkv), "core") for relay in relays]
    wo_sibling = cube.swap(after(output_weight, qkv), "core")
    o0, lse0 = attend(qkv, segments, 0)
    qkv1 = after(qkv, o0, wo_sibling, *direct)
    handed = [relay.hand_on(o0) for relay in relays]
    o1, lse1 = attend(qkv1, segments, 1)
    wo_diagonal = cube.swap(after(wo_across, o1), "core")
    wo = rows_of(output_weight, wo_sibling, wo_across, wo_diagonal)
    o = jnp.concatenate([o0, after(o1, *handed)], axis=1)
    rest = [relay.finish(o1) for relay in relays]
    x1, h2 = middle(where, x, o, wo, gains)
    weights = [relay.weight(sibling, h2) for relay, sibling in zip(relays, siblings)]
    y, dh2, gg_keep, gg_send, gu_keep, gu_send, gd_keep, gd_send = feed_forward(
        where, h2, dy, x1, weights
    )

    gd_got, gg_got, gu_got = (cube.swap(g, "core") for g in (gd_send, gg_send, gu_send))
    dx1, da, do, ffn_gain_grad = branch(where, dh2, x1, dy, gains, wo)
    more = tuple(range(3, cube.dims))
    orders = [
        ("x", 0, 1, 2) + more + (0,), (1, "x", 2, 0) + more + (1,), (2, "x", 0, 1) + more + (2,)
    ]
    gd = Reduce(cube, gd_keep, gd_got, orders[0])
    gg = Reduce(cube, gg_keep, gg_got, orders[1])
    gu = Reduce(cube, gu_keep, gu_got, orders[2])
    do = after(do, gd_got, gg_got)
    first = [gd.step(0, da), gg.step(0, da)]
    dqkv0 = attend_back(qkv, o0, do, lse0, segments, cos, sin, 0)
    do1 = after(do, dqkv0, gu_got)
    first.append(gu.step(0, dqkv0))
    dqkv1 = attend_back(qkv, o1, do1, lse1, segments, cos, sin, 1)
    dqkv = jnp.concatenate([dqkv0, dqkv1], axis=1)
    ga_keep, ga_send = weight_grads(where, h, dqkv, o, da)
    ga_got = cube.swap(ga_send, "core")
    dqkv = after(dqkv, ga_send, *first[:2])
    second = [gd.step(1, ga_send), gg.step(1, ga_send)]
    grad_x, attn_gain_grad = input_grads(where, x, dx1, wq, wk, dqkv)
    second.append(gu.step(1, grad_x))
    size = OWN // 3
    cut = lambda g, i: g[:, :, i * size:(i + 1) * size]
    parts = [
        Reduce(cube, cut(ga_keep, i), cut(ga_got, i), order) for i, order in enumerate(orders)
    ]
    both = jnp.concatenate([attn_gain_grad, ffn_gain_grad], axis=1).T.reshape(-1)
    ends = ["core", "x"] + list(range(cube.dims))
    done = second + [ga_got]
    for index in range(len(orders[0])):
        now = [part.step(index, *done) for part in parts]
        if index + 2 < len(orders[0]):
            now += [piece.step(index + 2, *done) for piece in (gd, gg, gu)]
        got = cube.swap(after(both, *done), ends[index])
        both = both + got
        done = now + [got]
    for dim in ends[len(orders[0]):]:
        both = both + cube.swap(both, dim)
    both = lax.dynamic_slice_in_dim(both.reshape(2, D), cube.me * OWN, OWN, 1)
    flat = lambda g: jnp.swapaxes(g, 0, 1).reshape(OWN, 4 * CUT).astype(F32)
    ga = flat(jnp.concatenate([part.result for part in parts], axis=1))
    return (
        y.T,
        grad_x.T,
        ga[:, :D],
        ga[:, D:D + KEYS],
        ga[:, D + KEYS:WIDE],
        ga[:, WIDE:],
        flat(gg.result),
        flat(gu.result),
        gd.result.reshape(D, CUT).T.astype(F32),
        both[0],
        both[1],
    )


def solution(mesh):
    rows = P(("group", "replica"), None)
    weight, gain = P("group", None), P("group")
    replicas = mesh.shape["replica"]
    return jax.shard_map(
        lambda *args: per_device(*args, replicas),
        mesh=mesh,
        in_specs=(rows, rows) + (weight,) * 7 + (gain, gain, rows),
        out_specs=(rows, rows) + (weight,) * 7 + (gain, gain),
        check_vma=False,
    )
```

```python
import functools

import jax
import jax.numpy as jnp
from jax import lax
from jax.experimental import pallas as pl
from jax.experimental.pallas import tpu as pltpu
from jax.sharding import PartitionSpec as P

D = 960
QUERY_HEADS = 15
KEY_VALUE_HEADS = 5
HEAD_WIDTH = 64
SHARE = QUERY_HEADS // KEY_VALUE_HEADS
HALF = HEAD_WIDTH // 2
KEYS = KEY_VALUE_HEADS * HEAD_WIDTH
EPS = 1e-05
THETA = 100000.0
TILE = 256
QB = 128
GAINS = 128
WIDE = D + 2 * KEYS
CUT = 640
OWN = 240
F32 = jnp.float32
BF16 = jnp.bfloat16
MIB = 1 << 20


def dot(a, b, ca, cb):
    return lax.dot_general(a, b, (((ca,), (cb,)), ((), ())), preferred_element_type=F32)


def params(limit, grid=1):
    return pltpu.CompilerParams(
        vmem_limit_bytes=limit * MIB, dimension_semantics=("arbitrary",) * grid
    )


def cost(*_):
    return pl.CostEstimate(flops=1, bytes_accessed=1, transcendentals=0)


def shaped(*shape_type):
    return [jax.ShapeDtypeStruct(s, t) for s, t in shape_type]


def norm_columns(v):
    inverse = lax.rsqrt(jnp.mean(v * v, axis=0, keepdims=True) + EPS)
    return v * inverse, inverse


def norm_columns_back(grad, normal, inverse, gain):
    scaled = grad * gain
    back = inverse * (scaled - normal * jnp.mean(scaled * normal, axis=0, keepdims=True))
    return back, jnp.sum(grad * normal, axis=1, keepdims=True)


def fixed(shape):
    return pl.BlockSpec(shape, lambda *_: (0,) * len(shape), pipeline_mode=pl.Buffered(1))


def columns(height, width):
    return pl.BlockSpec((height, width), lambda i: (0, i))


class Weight:
    def __init__(self, axis, pieces, dim=None, blocks=0):
        self.axis, self.dim, self.blocks = axis, dim, blocks
        self.arrays = [array for array, _, _ in pieces]
        self.places = [(flip, side) for _, flip, side in pieces]
        shape = list(self.arrays[0].shape)
        self.size = shape[axis]
        self.half = shape[1 - axis] // 2
        shape[axis] *= 4
        self.shape = tuple(shape)

    def specs(self):
        return [pl.BlockSpec(memory_space=pl.ANY)] * len(self.arrays)

    def scratch(self):
        if not self.blocks:
            return [pltpu.VMEM(self.shape, BF16), pltpu.SemaphoreType.DMA]
        block = (self.shape[0], self.shape[1] // self.blocks)
        return [pltpu.VMEM((self.blocks,) + block, BF16), pltpu.SemaphoreType.DMA((self.blocks,))]

    def load(self, where_ref, refs, scratch, sem):
        wide = self.shape[1] // max(self.blocks, 1)
        for ref, (flip, side) in zip(refs, self.places):
            at = (where_ref[0] ^ flip) * self.size
            other = 0 if side is None else (where_ref[1 + self.dim] ^ side) * self.half
            row, column = (at, other) if self.axis == 0 else (other, at)
            rows = pl.ds(pl.multiple_of(row, OWN), ref.shape[0])
            if not self.blocks:
                pltpu.make_async_copy(ref, scratch.at[rows, :], sem).start()
                continue
            first = column // wide
            for i in range(ref.shape[1] // wide):
                pltpu.make_async_copy(
                    ref.at[:, i * wide:(i + 1) * wide], scratch.at[first + i, rows, :],
                    sem.at[first + i],
                ).start()


def wait_for(scratch, sem):
    pltpu.make_async_copy(scratch, scratch, sem).wait()


SMEM = pl.BlockSpec(memory_space=pltpu.SMEM)


def project_kernel(weights, where_ref, x_ref, cos_ref, sin_ref, *refs):
    qkv_ref, h_ref, gains_ref, wq, q_sem, wk, k_sem = refs[8:]

    @pl.when(pl.program_id(0) == 0)
    def _():
        weights[0].load(where_ref, refs[:4], wq, q_sem)
        weights[1].load(where_ref, refs[4:8], wk, k_sem)
        wait_for(wq, q_sem)
        wait_for(wk, k_sem)
        gains_ref[...] = wk[:, 2 * KEYS:]

    gain = wk[:, 2 * KEYS:2 * KEYS + 1].astype(F32)
    normal, _ = norm_columns(x_ref[...].astype(F32))
    h = (normal * gain).astype(BF16)
    h_ref[...] = h
    c, s = cos_ref[...], sin_ref[...]

    def rotary(out, at, heads, scale):
        for head in range(heads):
            low = head * HEAD_WIDTH
            a, b = out[low:low + HALF], out[low + HALF:low + HEAD_WIDTH]
            to = at + low
            qkv_ref[to:to + HALF, :] = ((a * c - b * s) * scale).astype(BF16)
            qkv_ref[to + HALF:to + HEAD_WIDTH, :] = ((b * c + a * s) * scale).astype(BF16)

    rotary(dot(wq[...], h, 0, 0), 0, QUERY_HEADS, HEAD_WIDTH ** -0.5)
    out = dot(wk[:, :2 * KEYS], h, 0, 0)
    rotary(out, D, KEY_VALUE_HEADS, 1.0)
    qkv_ref[D + KEYS:, :] = out[KEYS:].astype(BF16)


def project(where, x, wq, wk, cos, sin):
    rows = x.shape[1]
    return pl.pallas_call(
        functools.partial(project_kernel, (wq, wk)),
        grid=(rows // TILE,),
        in_specs=[SMEM, columns(D, TILE), columns(HALF, TILE), columns(HALF, TILE)]
        + wq.specs() + wk.specs(),
        out_specs=[columns(WIDE, TILE), columns(D, TILE),
                   pl.BlockSpec((D, GAINS), lambda i: (0, 0))],
        out_shape=shaped(((WIDE, rows), BF16), ((D, rows), BF16), ((D, GAINS), BF16)),
        scratch_shapes=wq.scratch() + wk.scratch(),
        compiler_params=params(40),
        cost_estimate=cost(2 * rows * D * WIDE, rows * (2 * D + WIDE) * 2 + D * WIDE * 2),
        name="project",
    )(where, x, cos, sin, *wq.arrays, *wk.arrays)


def key_span(block):
    return max(0, QB * (block - 2)), QB * (block + 1)


def make_bias(bias_ref, segr_ref, segc_ref, length):
    for b in range(length // QB):
        lo, hi = key_span(b)
        key_at = lax.broadcasted_iota(jnp.int32, (hi - lo, QB), 0) + lo
        query_at = lax.broadcasted_iota(jnp.int32, (hi - lo, QB), 1) + b * QB
        ok = (segc_ref[lo:hi, :] == segr_ref[:, b * QB:(b + 1) * QB]) & (key_at <= query_at)
        bias_ref[b, 0:hi - lo, :] = jnp.where(ok, 0.0, -1e30)


def three(ref, kv, b):
    return jnp.concatenate(
        [
            ref[pl.ds(pl.multiple_of((kv * SHARE + i) * HEAD_WIDTH, HEAD_WIDTH), HEAD_WIDTH),
                b * QB:(b + 1) * QB]
            for i in range(SHARE)
        ],
        axis=1,
    )


def wide_bias(bias_ref, b, n):
    one = bias_ref[b, 0:n, :]
    return jnp.concatenate([one] * SHARE, axis=1)


def attend_kernel(qkv_ref, segr_ref, segc_ref, o_ref, lse_ref, bias_ref):
    length = qkv_ref.shape[1]
    make_bias(bias_ref, segr_ref.at[0], segc_ref.at[0], length)

    @pl.loop(0, KEY_VALUE_HEADS)
    def _(kv):
        k = qkv_ref[pl.ds(pl.multiple_of(D + kv * HEAD_WIDTH, HEAD_WIDTH), HEAD_WIDTH), :]
        v = qkv_ref[pl.ds(pl.multiple_of(D + KEYS + kv * HEAD_WIDTH, HEAD_WIDTH), HEAD_WIDTH), :]
        for b in range(length // QB):
            lo, hi = key_span(b)
            s = dot(k[:, lo:hi], three(qkv_ref, kv, b), 0, 0) + wide_bias(bias_ref, b, hi - lo)
            top = jnp.max(s, axis=0, keepdims=True)
            p = jnp.exp(s - top)
            total = jnp.sum(p, axis=0, keepdims=True)
            out = dot(v[:, lo:hi], p.astype(BF16), 1, 0) / total
            lse = top + jnp.log(total)
            for i in range(SHARE):
                rows = pl.ds(pl.multiple_of((kv * SHARE + i) * HEAD_WIDTH, HEAD_WIDTH), HEAD_WIDTH)
                o_ref[rows, b * QB:(b + 1) * QB] = out[:, i * QB:(i + 1) * QB].astype(BF16)
                lse_ref[kv, i:i + 1, b * QB:(b + 1) * QB] = lse[:, i * QB:(i + 1) * QB]


def attend(qkv, segments, at):
    length = segments.shape[1]
    wide = qkv.shape[0]
    pairs = QUERY_HEADS * length * length
    return pl.pallas_call(
        attend_kernel,
        grid=(1,),
        in_specs=[
            pl.BlockSpec((wide, length), lambda i: (0, at)),
            pl.BlockSpec((1, 1, length), lambda i: (at, 0, 0)),
            pl.BlockSpec((1, length, 1), lambda i: (at, 0, 0)),
        ],
        out_specs=[
            pl.BlockSpec((D, length), lambda i: (0, 0)),
            pl.BlockSpec((KEY_VALUE_HEADS, 8, length), lambda i: (0, 0, 0)),
        ],
        out_shape=shaped(((D, length), BF16), ((KEY_VALUE_HEADS, 8, length), F32)),
        scratch_shapes=[pltpu.VMEM((length // QB, 3 * QB, QB), F32)],
        compiler_params=params(40),
        cost_estimate=cost(pairs * 256 * 2, length * (wide + D) * 2, pairs // 2),
        name="attend",
    )(qkv, segments[:, None, :], segments[:, :, None])


def middle_kernel(weight, where_ref, x_ref, o_ref, gain_ref, *refs):
    x1_ref, h_ref, w, sem = refs[4:]

    @pl.when(pl.program_id(0) == 0)
    def _():
        weight.load(where_ref, refs[:4], w, sem)
        wait_for(w, sem)

    x1 = x_ref[...].astype(F32) + dot(w[...], o_ref[...], 0, 0)
    normal, _ = norm_columns(x1)
    x1_ref[...] = x1
    h_ref[...] = (normal * gain_ref[:, 1:2].astype(F32)).astype(BF16)


def middle(where, x, o, w, gains):
    rows = x.shape[1]
    return pl.pallas_call(
        functools.partial(middle_kernel, w),
        grid=(rows // TILE,),
        in_specs=[SMEM, columns(D, TILE), columns(D, TILE), fixed((D, GAINS))] + w.specs(),
        out_specs=[columns(D, TILE), columns(D, TILE)],
        out_shape=shaped(((D, rows), F32), ((D, rows), BF16)),
        scratch_shapes=w.scratch(),
        compiler_params=params(40),
        cost_estimate=cost(2 * rows * D * D, rows * D * 10),
        name="middle",
    )(where, x, o, gains, *w.arrays)


def feed_forward_kernel(weights, where_ref, h_ref, dy_ref, x1_ref, *refs):
    count = len(weights[0].arrays)
    y_ref, dh_ref, hid_ref, dgate_ref, dup_ref, acc_ref, *scratch = refs[3 * count:]
    step = pl.program_id(0)

    @pl.when(step == 0)
    def _():
        for i, weight in enumerate(weights):
            weight.load(where_ref, refs[i * count:(i + 1) * count], *scratch[2 * i:2 * i + 2])
        acc_ref[...] = x1_ref[...]
        dh_ref[...] = jnp.zeros_like(dh_ref)

    wg_ref, wu_ref, wd_ref = (w.at[step] for w in scratch[::2])
    for w, sem in zip((wg_ref, wu_ref, wd_ref), scratch[1::2]):
        wait_for(w, sem.at[step])
    h, dy = h_ref[...], dy_ref[...]
    gate = dot(wg_ref[...], h, 0, 0)
    up = dot(wu_ref[...], h, 0, 0)
    dhid = dot(wd_ref[...], dy, 0, 0)
    sig = jax.nn.sigmoid(gate)
    silu = gate * sig
    hid = (silu * up).astype(BF16)
    dgate = (dhid * up * (sig + silu * (1.0 - sig))).astype(BF16)
    dup = (dhid * silu).astype(BF16)
    hid_ref[...] = hid
    dgate_ref[...] = dgate
    dup_ref[...] = dup
    acc_ref[...] += dot(wd_ref[...], hid, 1, 0)
    dh_ref[...] += dot(wg_ref[...], dgate, 1, 0) + dot(wu_ref[...], dup, 1, 0)

    @pl.when(step == pl.num_programs(0) - 1)
    def _():
        y_ref[...] = acc_ref[...].astype(BF16)


def feed_forward(where, h, dy, x1, weights):
    rows, hidden = h.shape[1], weights[0].shape[1]
    block = pl.BlockSpec((CUT, rows), lambda f: (f, 0))
    return pl.pallas_call(
        functools.partial(feed_forward_kernel, weights),
        grid=(hidden // CUT,),
        in_specs=[SMEM, fixed((D, rows)), fixed((D, rows)), fixed((D, rows))]
        + sum((w.specs() for w in weights), []),
        out_specs=[fixed((D, rows)), fixed((D, rows))] + [block] * 3,
        out_shape=shaped(((D, rows), BF16), ((D, rows), F32)) + shaped(((hidden, rows), BF16)) * 3,
        scratch_shapes=sum((w.scratch() for w in weights), [pltpu.VMEM((D, rows), F32)]),
        compiler_params=params(60),
        cost_estimate=cost(),
        name="feed_forward",
    )(where, h, dy, x1, *sum((w.arrays for w in weights), []))


def split_owners(grad, where_ref, put):
    core, x_here = where_ref[0] & 1, where_ref[0] >> 1
    for x in range(2):
        a = grad[2 * x * OWN:(2 * x + 1) * OWN].astype(BF16)
        b = grad[(2 * x + 1) * OWN:(2 * x + 2) * OWN].astype(BF16)
        put(x_here ^ x, jnp.where(core == 0, a, b), jnp.where(core == 0, b, a))


def row_grads_kernel(where_ref, a_ref, b_ref, keep_ref, send_ref):
    def put(x, keep, send):
        keep_ref[x, 0] = keep
        send_ref[x, 0] = send

    split_owners(dot(a_ref[...], b_ref[...], 1, 1), where_ref, put)


def column_grads_kernel(dim, where_ref, a_ref, b_ref, keep_ref, send_ref):
    grad = dot(a_ref[...], b_ref[...], 1, 1).astype(BF16)
    here = (pl.program_id(0) & 1) == (where_ref[0] & 1)

    def put(ref):
        for i in range(4):
            ref[0, (2 * where_ref[1 + dim]) ^ i] = grad[i * OWN:(i + 1) * OWN]

    pl.when(here)(lambda: put(keep_ref))
    pl.when(jnp.logical_not(here))(lambda: put(send_ref))


def ffn_grads(where, a, b, dim, by_columns):
    rows = a.shape[1]
    if by_columns:
        kernel = functools.partial(column_grads_kernel, dim)
        out = pl.BlockSpec((1, 4, OWN, CUT), lambda f, at: ((f >> 1) ^ (at[0] >> 1), 0, 0, 0))
    else:
        kernel = row_grads_kernel
        out = pl.BlockSpec((2, 1, OWN, CUT), lambda f, at: (0, f ^ (2 * at[1 + dim]), 0, 0))
    return pl.pallas_call(
        kernel,
        grid_spec=pltpu.PrefetchScalarGridSpec(
            num_scalar_prefetch=1,
            grid=(b.shape[0] // CUT,),
            in_specs=[fixed((D, rows)), pl.BlockSpec((CUT, rows), lambda f, at: (f, 0))],
            out_specs=[out, out],
        ),
        out_shape=shaped(((2, 4, OWN, CUT), BF16)) * 2,
        compiler_params=params(40),
        cost_estimate=cost(),
        name="ffn_grads",
    )(where, a, b)


def branch_kernel(weight, where_ref, dh_ref, x1_ref, dy_ref, gain_ref, *refs):
    dx_ref, da_ref, do_ref, gain_grad, w, sem = refs[4:]
    first = pl.program_id(0) == 0

    @pl.when(first)
    def _():
        weight.load(where_ref, refs[:4], w, sem)

    gain = gain_ref[:, 1:2].astype(F32)
    normal, inverse = norm_columns(x1_ref[...])
    back, part = norm_columns_back(dh_ref[...], normal, inverse, gain)
    dx = dy_ref[...].astype(F32) + back
    da = dx.astype(BF16)
    dx_ref[...] = dx
    da_ref[...] = da

    @pl.when(first)
    def _():
        gain_grad[...] = part
        wait_for(w, sem)

    @pl.when(jnp.logical_not(first))
    def _():
        gain_grad[...] += part

    do_ref[...] = dot(w[...], da, 1, 0).astype(BF16)


def branch(where, dh, x1, dy, gains, w):
    rows = dh.shape[1]
    return pl.pallas_call(
        functools.partial(branch_kernel, w),
        grid=(rows // TILE,),
        in_specs=[SMEM] + [columns(D, TILE)] * 3 + [fixed((D, GAINS))] + w.specs(),
        out_specs=[columns(D, TILE)] * 3 + [pl.BlockSpec((D, 1), lambda i: (0, 0))],
        out_shape=shaped(((D, rows), F32), ((D, rows), BF16), ((D, rows), BF16), ((D, 1), F32)),
        scratch_shapes=w.scratch(),
        compiler_params=params(40),
        cost_estimate=cost(2 * rows * D * D, rows * D * 18),
        name="branch",
    )(where, dh, x1, dy, gains, *w.arrays)


def attend_back_kernel(qkv_ref, o_ref, do_ref, lse_ref, segr_ref, segc_ref, cos_ref, sin_ref,
                       out_ref, bias_ref, dk_ref, dv_ref):
    length = qkv_ref.shape[1]
    make_bias(bias_ref, segr_ref.at[0], segc_ref.at[0], length)

    def turn_back(g, c, s, at, cols):
        a, b = g[:HALF], g[HALF:]
        at = pl.multiple_of(at, HEAD_WIDTH)
        out_ref[pl.ds(at, HALF), cols] = (a * c + b * s).astype(BF16)
        out_ref[pl.ds(pl.multiple_of(at + HALF, HALF), HALF), cols] = (b * c - a * s).astype(BF16)

    @pl.loop(0, KEY_VALUE_HEADS)
    def _(kv):
        k = qkv_ref[pl.ds(pl.multiple_of(D + kv * HEAD_WIDTH, HEAD_WIDTH), HEAD_WIDTH), :]
        v = qkv_ref[pl.ds(pl.multiple_of(D + KEYS + kv * HEAD_WIDTH, HEAD_WIDTH), HEAD_WIDTH), :]
        dk_ref[...] = jnp.zeros_like(dk_ref)
        dv_ref[...] = jnp.zeros_like(dv_ref)
        for b in range(length // QB):
            lo, hi = key_span(b)
            cols = slice(b * QB, (b + 1) * QB)
            q, o, do = three(qkv_ref, kv, b), three(o_ref, kv, b), three(do_ref, kv, b)
            lse = jnp.concatenate([lse_ref[kv, i:i + 1, cols] for i in range(SHARE)], axis=1)
            inner = jnp.sum(o.astype(F32) * do.astype(F32), axis=0, keepdims=True)
            s = dot(k[:, lo:hi], q, 0, 0) + wide_bias(bias_ref, b, hi - lo)
            p = jnp.exp(s - lse)
            dp = dot(v[:, lo:hi], do, 0, 0)
            ds = (p * (dp - inner)).astype(BF16)
            dv_ref[:, lo:hi] += dot(do, p.astype(BF16), 1, 1)
            dk_ref[:, lo:hi] += dot(q, ds, 1, 1)
            dq = dot(k[:, lo:hi], ds, 1, 0) * HEAD_WIDTH ** -0.5
            for i in range(SHARE):
                turn_back(dq[:, i * QB:(i + 1) * QB], cos_ref[:, cols], sin_ref[:, cols],
                          (kv * SHARE + i) * HEAD_WIDTH, cols)
        turn_back(dk_ref[...], cos_ref[...], sin_ref[...], D + kv * HEAD_WIDTH, slice(None))
        out_ref[pl.ds(pl.multiple_of(D + KEYS + kv * HEAD_WIDTH, HEAD_WIDTH), HEAD_WIDTH), :] = (
            dv_ref[...].astype(BF16))


def attend_back(qkv, o, do, lse, segments, cos, sin, at):
    length = segments.shape[1]
    wide = qkv.shape[0]
    pairs = QUERY_HEADS * length * length
    here = lambda height: pl.BlockSpec((height, length), lambda i: (0, at))
    return pl.pallas_call(
        attend_back_kernel,
        grid=(1,),
        in_specs=[
            here(wide),
            pl.BlockSpec((D, length), lambda i: (0, 0)),
            here(D),
            pl.BlockSpec((KEY_VALUE_HEADS, 8, length), lambda i: (0, 0, 0)),
            pl.BlockSpec((1, 1, length), lambda i: (at, 0, 0)),
            pl.BlockSpec((1, length, 1), lambda i: (at, 0, 0)),
            here(HALF),
            here(HALF),
        ],
        out_specs=pl.BlockSpec((wide, length), lambda i: (0, 0)),
        out_shape=jax.ShapeDtypeStruct((wide, length), BF16),
        scratch_shapes=[
            pltpu.VMEM((length // QB, 3 * QB, QB), F32),
            pltpu.VMEM((HEAD_WIDTH, length), F32),
            pltpu.VMEM((HEAD_WIDTH, length), F32),
        ],
        compiler_params=params(40),
        cost_estimate=cost(pairs * 256 * 5, length * (2 * wide + 2 * D) * 2, pairs // 2),
        name="attend_back",
    )(qkv, o, do, lse, segments[:, None, :], segments[:, :, None], cos, sin)


PIECES = ((0, 128), (128, OWN))


def weight_kernel(where_ref, h_ref, dqkv_ref, o_ref, da_ref, *out_refs):
    def store(block, grad):
        def put(x, keep, send):
            for i, (low, high) in enumerate(PIECES):
                at = block ^ (2 * where_ref[1 + i])
                out_refs[2 * i][x, at] = keep[low:high]
                out_refs[2 * i + 1][x, at] = send[low:high]

        split_owners(grad, where_ref, put)

    store(0, dot(h_ref[...], dqkv_ref[:CUT, :], 1, 1))
    store(1, dot(h_ref[...], dqkv_ref[CUT:2 * CUT, :], 1, 1))
    left = dot(h_ref[...], dqkv_ref[2 * CUT:, :], 1, 1)
    right = dot(o_ref[...], da_ref[:3 * CUT - WIDE, :], 1, 1)
    store(2, jnp.concatenate([left, right], axis=1))
    store(3, dot(o_ref[...], da_ref[3 * CUT - WIDE:, :], 1, 1))


def weight_grads(where, h, dqkv, o, da):
    rows = h.shape[1]
    shapes = [(2, 4, high - low, CUT) for low, high in PIECES for _ in range(2)]
    return pl.pallas_call(
        weight_kernel,
        grid=(1,),
        in_specs=[SMEM, fixed((D, rows)), fixed((WIDE, rows)), fixed((D, rows)), fixed((D, rows))],
        out_specs=[fixed(shape) for shape in shapes],
        out_shape=shaped(*((shape, BF16) for shape in shapes)),
        compiler_params=params(48),
        cost_estimate=cost(),
        name="weight_grads",
    )(where, h, dqkv, o, da)


def inputs_kernel(weights, where_ref, x_ref, dx_ref, dqkv_ref, *refs):
    out_ref, gain_grad, wq, q_sem, wk, k_sem = refs[8:]
    first = pl.program_id(0) == 0

    @pl.when(first)
    def _():
        weights[0].load(where_ref, refs[:4], wq, q_sem)
        weights[1].load(where_ref, refs[4:8], wk, k_sem)
        wait_for(wq, q_sem)
        wait_for(wk, k_sem)

    gain = wk[:, 2 * KEYS:2 * KEYS + 1].astype(F32)
    dh = dot(wq[...], dqkv_ref[:D], 1, 0) + dot(wk[:, :2 * KEYS], dqkv_ref[D:], 1, 0)
    normal, inverse = norm_columns(x_ref[...].astype(F32))
    back, part = norm_columns_back(dh, normal, inverse, gain)
    out_ref[...] = (dx_ref[...] + back).astype(BF16)

    @pl.when(first)
    def _():
        gain_grad[...] = part

    @pl.when(jnp.logical_not(first))
    def _():
        gain_grad[...] += part


def input_grads(where, x, dx, wq, wk, dqkv):
    rows = x.shape[1]
    return pl.pallas_call(
        functools.partial(inputs_kernel, (wq, wk)),
        grid=(rows // TILE,),
        in_specs=[SMEM, columns(D, TILE), columns(D, TILE), columns(WIDE, TILE)]
        + wq.specs() + wk.specs(),
        out_specs=[columns(D, TILE), pl.BlockSpec((D, 1), lambda i: (0, 0))],
        out_shape=shaped(((D, rows), BF16), ((D, 1), F32)),
        scratch_shapes=wq.scratch() + wk.scratch(),
        compiler_params=params(40),
        cost_estimate=cost(2 * rows * D * WIDE, rows * (D * 8 + WIDE * 2) + D * WIDE * 2),
        name="input_grads",
    )(where, x, dx, dqkv, *wq.arrays, *wk.arrays)


def tables(segments):
    length = segments.shape[1]
    index = jnp.arange(length, dtype=jnp.int32)
    same = segments[:, :, None] == segments[:, None, :]
    start = jnp.min(jnp.where(same, index[None, :, None], length), axis=1)
    position = (index[None, :] - start).astype(F32).reshape(1, -1)
    freq = THETA ** (-(jnp.arange(HALF, dtype=F32) * 2.0 / HEAD_WIDTH))
    angle = freq[:, None] * position
    return jnp.cos(angle), jnp.sin(angle)


def after(value, *others):
    return lax.optimization_barrier((value,) + others)[0]


class Cube:
    def __init__(self, count):
        self.count = count
        self.dims = count.bit_length() - 1
        self.masks = [1, 2, 6] + [1 << i for i in range(3, self.dims)]
        replica, group = lax.axis_index("replica"), lax.axis_index("group")
        bits = [(replica >> i) & 1 for i in range(self.dims)]
        self.coordinate = {i: bits[i] for i in range(self.dims)}
        self.coordinate[1] = bits[1] ^ bits[2]
        self.coordinate["x"] = group >> 1
        self.coordinate["core"] = group & 1
        self.me = group

    def swap(self, value, dim):
        if dim == "x":
            return lax.ppermute(value, "group", [(i, i ^ 2) for i in range(4)])
        if dim == "core":
            return lax.ppermute(value, "group", [(i, i ^ 1) for i in range(4)])
        mask = self.masks[dim]
        return lax.ppermute(value, "replica", [(i, i ^ mask) for i in range(self.count)])

    def ordered(self, dim, mine, other, axis):
        return jnp.where(
            self.coordinate[dim] == 0,
            jnp.concatenate([mine, other], axis=axis),
            jnp.concatenate([other, mine], axis=axis),
        )


def rows_of(own, sibling, across, diagonal):
    pieces = own, sibling, across, diagonal
    return Weight(0, [(array, flip, None) for flip, array in enumerate(pieces)])


class Relay:
    def __init__(self, cube, shard, axis, first, second):
        self.cube, self.shard, self.axis, self.dims = cube, shard, axis, (first, second)
        self.cut = 1 - axis
        self.size = shard.shape[self.cut] // 4
        at = 2 * cube.coordinate[second] + cube.coordinate[first]
        self.quarter = lax.dynamic_slice_in_dim(shard, at * self.size, self.size, self.cut)

    def cross(self, *others):
        self.direct = self.cube.swap(after(self.quarter, *others), "x")
        return self.direct

    def hand_on(self, *others):
        self.handed = self.cube.swap(after(self.direct, *others), self.dims[0])
        return self.handed

    def finish(self, *others):
        cube = self.cube
        handed = after(self.handed, *others)
        self.half = cube.ordered(self.dims[0], self.direct, handed, self.cut)
        self.rest = cube.swap(self.half, self.dims[1])
        self.half_diagonal = cube.swap(self.half, "core")
        return self.rest

    def weight(self, sibling, *others):
        rest = after(self.rest, *others)
        pieces = [
            (self.shard, 0, None), (sibling, 1, None), (self.half, 2, 0), (rest, 2, 1),
            (self.half_diagonal, 3, 0), (self.cube.swap(rest, "core"), 3, 1),
        ]
        return Weight(self.axis, pieces, self.dims[1], 4)


class Reduce:
    def __init__(self, cube, keep, got, order):
        rows, wide = keep.shape[2:]
        self.cube, self.order, self.shape = cube, order, (4, rows, wide)
        self.cut = [d for d in order[:2] if d != "x"][0]
        self.terms = [t.reshape(2, 2, 2, rows, wide) for t in (keep, got)]
        self.index = 0

    def sum(self, terms):
        return functools.reduce(jnp.add, [t.astype(F32) for t in terms]).astype(BF16)

    def ready(self, *others):
        dim = self.order[self.index]
        self.terms[-1] = after(self.terms[-1], *others)
        if self.index < 2:
            axis = 0 if dim == "x" else 1
            take = lambda i: [lax.slice_in_dim(t, i, i + 1, axis=axis) for t in self.terms]
            self.send, self.terms = self.sum(take(1)), take(0)
        else:
            self.send = self.sum(self.terms)
            self.terms = [self.send]
        return self.send

    def swap(self):
        dim = self.order[self.index]
        self.got = self.cube.swap(self.send, dim)
        self.index += 1
        if self.index == len(self.order):
            self.result = self.cube.ordered(dim, self.send, self.got, 1).reshape(self.shape)
        elif self.index > 2:
            self.terms = [self.send, self.got]
        else:
            self.terms = self.terms + [self.got]
        return self.got

    def step(self, *others):
        self.ready(*others)
        return self.swap()


def per_device(
    tokens,
    segments,
    query_weight,
    key_weight,
    value_weight,
    output_weight,
    w_gate,
    w_up,
    w_down,
    attn_gain,
    ffn_gain,
    cotangent,
    replicas,
):
    cube = Cube(replicas)
    where = jnp.stack([cube.me] + [cube.coordinate[i] for i in range(3)]).astype(jnp.int32)
    x, dy = tokens.T, cotangent.T

    q_across = cube.swap(query_weight, "x")
    pad = jnp.zeros((OWN, GAINS - 2), BF16)
    kv = jnp.concatenate(
        [key_weight, value_weight, attn_gain[:, None], ffn_gain[:, None], pad], axis=1
    )
    kv_across = cube.swap(kv, "x")
    q_sibling, kv_sibling = cube.swap(query_weight, "core"), cube.swap(kv, "core")
    q_diagonal, kv_diagonal = cube.swap(q_across, "core"), cube.swap(kv_across, "core")
    wq = rows_of(query_weight, q_sibling, q_across, q_diagonal)
    wk = rows_of(kv, kv_sibling, kv_across, kv_diagonal)
    cos, sin = tables(segments)
    relays = [
        Relay(cube, w_gate, 0, 0, 1), Relay(cube, w_up, 0, 1, 2), Relay(cube, w_down.T, 1, 2, 0)
    ]
    direct = [relay.cross(q_across, kv_across) for relay in relays]
    qkv, h, gains = project(where, x, wq, wk, cos, sin)
    wo_across = cube.swap(after(output_weight, qkv), "x")
    siblings = [cube.swap(after(relay.shard, qkv), "core") for relay in relays]
    wo_sibling = cube.swap(after(output_weight, qkv), "core")
    o0, lse0 = attend(qkv, segments, 0)
    qkv1 = after(qkv, o0, wo_sibling, *direct)
    handed = [relay.hand_on(o0) for relay in relays]
    o1, lse1 = attend(qkv1, segments, 1)
    wo_diagonal = cube.swap(after(wo_across, o1), "core")
    wo = rows_of(output_weight, wo_sibling, wo_across, wo_diagonal)
    o = jnp.concatenate([o0, after(o1, *handed)], axis=1)
    rest = [relay.finish(o1) for relay in relays]
    x1, h2 = middle(where, x, o, wo, gains)
    weights = [relay.weight(sibling, h2) for relay, sibling in zip(relays, siblings)]
    y, dh2, hid, dgate, dup = feed_forward(where, h2, dy, x1, weights)

    more = tuple(range(3, cube.dims))
    orders = [
        ("x", 0, 1, 2) + more + (0,), (1, "x", 2, 0) + more + (1,), (2, "x", 0, 1) + more + (2,)
    ]
    core = lambda value: cube.swap(value, "core")
    gd_keep, gd_send = ffn_grads(where, dy, hid, 0, True)
    gd = Reduce(cube, gd_keep, core(gd_send), orders[0])
    gg_keep, gg_send = ffn_grads(where, h2, after(dgate, gd_send), 1, False)
    gg = Reduce(cube, gg_keep, core(gg_send), orders[1])
    gd.ready(gg_send)
    gu_keep, gu_send = ffn_grads(where, h2, after(dup, gd.send), 2, False)
    gd.swap()
    gu = Reduce(cube, gu_keep, core(gu_send), orders[2])
    gg.ready(gu_send)
    dx1, da, do, ffn_gain_grad = branch(where, after(dh2, gg.send), x1, dy, gains, wo)
    gg.swap()
    gu.ready(da)
    do0 = after(do, gu.send)
    gu.swap()
    dqkv0 = attend_back(qkv, o0, do0, lse0, segments, cos, sin, 0)
    gd.ready(dqkv0)
    do1 = after(do, dqkv0, gd.send)
    gd.swap()
    dqkv1 = attend_back(qkv, o1, do1, lse1, segments, cos, sin, 1)
    gg.ready(dqkv1)
    dqkv = after(jnp.concatenate([dqkv0, dqkv1], axis=1), gg.send)
    gg.swap()
    parts = []
    weight_parts = weight_grads(where, h, dqkv, o, da)
    for i in range(len(PIECES)):
        keep, send = weight_parts[2 * i:2 * i + 2]
        parts.append(Reduce(cube, keep, core(send), orders[i]))
    gu.ready(send)
    gd.ready(send)
    dqkv = after(dqkv, gu.send, gd.send)
    gu.swap()
    gd.swap()
    grad_x, attn_gain_grad = input_grads(where, x, dx1, wq, wk, dqkv)
    both = jnp.concatenate([attn_gain_grad, ffn_gain_grad], axis=1).T.reshape(-1)
    ends = ["core", "x"] + list(range(cube.dims))
    swaps = [gg, parts[0], gu, parts[1], gd]
    token = grad_x
    for round_of in range(len(orders[0])):
        before = token
        for piece in swaps:
            if piece.index < len(piece.order):
                token = piece.ready(token)
                piece.swap()
        both = both + after(cube.swap(after(both, before), ends[round_of]), token)
    for dim in ends[len(orders[0]):]:
        both = both + cube.swap(both, dim)
    both = lax.dynamic_slice_in_dim(both.reshape(2, D), cube.me * OWN, OWN, 1)
    flat = lambda g: jnp.swapaxes(g, 0, 1).reshape(OWN, 4 * CUT).astype(F32)
    ga = flat(jnp.concatenate([part.result for part in parts], axis=1))
    return (
        y.T,
        grad_x.T,
        ga[:, :D],
        ga[:, D:D + KEYS],
        ga[:, D + KEYS:WIDE],
        ga[:, WIDE:],
        flat(gg.result),
        flat(gu.result),
        gd.result.reshape(D, CUT).T.astype(F32),
        both[0],
        both[1],
    )


def solution(mesh):
    rows = P(("group", "replica"), None)
    weight, gain = P("group", None), P("group")
    replicas = mesh.shape["replica"]
    return jax.shard_map(
        lambda *args: per_device(*args, replicas),
        mesh=mesh,
        in_specs=(rows, rows) + (weight,) * 7 + (gain, gain, rows),
        out_specs=(rows, rows) + (weight,) * 7 + (gain, gain),
        check_vma=False,
    )
```

```python
import functools

import jax
import jax.numpy as jnp
from jax import lax
from jax.experimental import pallas as pl
from jax.experimental.pallas import tpu as pltpu
from jax.sharding import PartitionSpec as P

D = 960
QUERY_HEADS = 15
KEY_VALUE_HEADS = 5
HEAD_WIDTH = 64
SHARE = QUERY_HEADS // KEY_VALUE_HEADS
HALF = HEAD_WIDTH // 2
KEYS = KEY_VALUE_HEADS * HEAD_WIDTH
EPS = 1e-05
THETA = 100000.0
TILE = 256
QB = 128
GAINS = 128
WIDE = D + 2 * KEYS
CUT = 640
OWN = 240
F32 = jnp.float32
BF16 = jnp.bfloat16
MIB = 1 << 20


def dot(a, b, ca, cb):
    return lax.dot_general(a, b, (((ca,), (cb,)), ((), ())), preferred_element_type=F32)


def params(limit, grid=1):
    return pltpu.CompilerParams(
        vmem_limit_bytes=limit * MIB, dimension_semantics=("arbitrary",) * grid
    )


def cost(*_):
    return pl.CostEstimate(flops=1, bytes_accessed=1, transcendentals=0)


def shaped(*shape_type):
    return [jax.ShapeDtypeStruct(s, t) for s, t in shape_type]


def norm_columns(v):
    inverse = lax.rsqrt(jnp.mean(v * v, axis=0, keepdims=True) + EPS)
    return v * inverse, inverse


def norm_columns_back(grad, normal, inverse, gain):
    scaled = grad * gain
    back = inverse * (scaled - normal * jnp.mean(scaled * normal, axis=0, keepdims=True))
    return back, jnp.sum(grad * normal, axis=1, keepdims=True)


def fixed(shape):
    return pl.BlockSpec(shape, lambda *_: (0,) * len(shape), pipeline_mode=pl.Buffered(1))


def columns(height, width):
    return pl.BlockSpec((height, width), lambda i: (0, i))


class Weight:
    def __init__(self, axis, pieces, dim=None, blocks=0):
        self.axis, self.dim, self.blocks = axis, dim, blocks
        self.arrays = [array for array, _, _ in pieces]
        self.places = [(flip, side) for _, flip, side in pieces]
        shape = list(self.arrays[0].shape)
        self.size = shape[axis]
        self.half = shape[1 - axis] // 2
        shape[axis] *= 4
        self.shape = tuple(shape)

    def specs(self):
        return [pl.BlockSpec(memory_space=pltpu.HBM)] * len(self.arrays)

    def scratch(self):
        if not self.blocks:
            return [pltpu.VMEM(self.shape, BF16), pltpu.SemaphoreType.DMA]
        block = (self.shape[0], self.shape[1] // self.blocks)
        return [pltpu.VMEM((self.blocks,) + block, BF16), pltpu.SemaphoreType.DMA((self.blocks,))]

    def load(self, where_ref, refs, scratch, sem):
        wide = self.shape[1] // max(self.blocks, 1)
        for ref, (flip, side) in zip(refs, self.places):
            at = (where_ref[0] ^ flip) * self.size
            other = 0 if side is None else (where_ref[1 + self.dim] ^ side) * self.half
            row, column = (at, other) if self.axis == 0 else (other, at)
            rows = pl.ds(pl.multiple_of(row, OWN), ref.shape[0])
            if not self.blocks:
                pltpu.make_async_copy(ref, scratch.at[rows, :], sem).start()
                continue
            first = column // wide
            for i in range(ref.shape[1] // wide):
                pltpu.make_async_copy(
                    ref.at[:, i * wide:(i + 1) * wide], scratch.at[first + i, rows, :],
                    sem.at[first + i],
                ).start()


def wait_for(scratch, sem):
    pltpu.make_async_copy(scratch, scratch, sem).wait()


SMEM = pl.BlockSpec(memory_space=pltpu.SMEM)


def project_kernel(weights, where_ref, x_ref, cos_ref, sin_ref, *refs):
    qkv_ref, h_ref, gains_ref, wq, q_sem, wk, k_sem = refs[8:]

    @pl.when(pl.program_id(0) == 0)
    def _():
        weights[0].load(where_ref, refs[:4], wq, q_sem)
        weights[1].load(where_ref, refs[4:8], wk, k_sem)
        wait_for(wq, q_sem)
        wait_for(wk, k_sem)
        gains_ref[...] = wk[:, 2 * KEYS:]

    gain = wk[:, 2 * KEYS:2 * KEYS + 1].astype(F32)
    normal, _ = norm_columns(x_ref[...].astype(F32))
    h = (normal * gain).astype(BF16)
    h_ref[...] = h
    c, s = cos_ref[...], sin_ref[...]

    def rotary(out, at, heads, scale):
        for head in range(heads):
            low = head * HEAD_WIDTH
            a, b = out[low:low + HALF], out[low + HALF:low + HEAD_WIDTH]
            to = at + low
            qkv_ref[to:to + HALF, :] = ((a * c - b * s) * scale).astype(BF16)
            qkv_ref[to + HALF:to + HEAD_WIDTH, :] = ((b * c + a * s) * scale).astype(BF16)

    rotary(dot(wq[...], h, 0, 0), 0, QUERY_HEADS, HEAD_WIDTH ** -0.5)
    out = dot(wk[:, :2 * KEYS], h, 0, 0)
    rotary(out, D, KEY_VALUE_HEADS, 1.0)
    qkv_ref[D + KEYS:, :] = out[KEYS:].astype(BF16)


def project(where, x, wq, wk, cos, sin):
    rows = x.shape[1]
    return pl.pallas_call(
        functools.partial(project_kernel, (wq, wk)),
        grid=(rows // TILE,),
        in_specs=[SMEM, columns(D, TILE), columns(HALF, TILE), columns(HALF, TILE)]
        + wq.specs() + wk.specs(),
        out_specs=[columns(WIDE, TILE), columns(D, TILE),
                   pl.BlockSpec((D, GAINS), lambda i: (0, 0))],
        out_shape=shaped(((WIDE, rows), BF16), ((D, rows), BF16), ((D, GAINS), BF16)),
        scratch_shapes=wq.scratch() + wk.scratch(),
        compiler_params=params(60),
        cost_estimate=cost(2 * rows * D * WIDE, rows * (2 * D + WIDE) * 2 + D * WIDE * 2),
        name="project",
    )(where, x, cos, sin, *wq.arrays, *wk.arrays)


def key_span(block):
    return max(0, QB * (block - 2)), QB * (block + 1)


def make_bias(bias_ref, segr_ref, segc_ref, length):
    for b in range(length // QB):
        lo, hi = key_span(b)
        key_at = lax.broadcasted_iota(jnp.int32, (hi - lo, QB), 0) + lo
        query_at = lax.broadcasted_iota(jnp.int32, (hi - lo, QB), 1) + b * QB
        ok = (segc_ref[lo:hi, :] == segr_ref[:, b * QB:(b + 1) * QB]) & (key_at <= query_at)
        bias_ref[b, 0:hi - lo, :] = jnp.where(ok, 0.0, -1e30)


def three(ref, kv, b):
    return jnp.concatenate(
        [
            ref[pl.ds(pl.multiple_of((kv * SHARE + i) * HEAD_WIDTH, HEAD_WIDTH), HEAD_WIDTH),
                b * QB:(b + 1) * QB]
            for i in range(SHARE)
        ],
        axis=1,
    )


def wide_bias(bias_ref, b, n):
    one = bias_ref[b, 0:n, :]
    return jnp.concatenate([one] * SHARE, axis=1)


def attend_kernel(qkv_ref, segr_ref, segc_ref, *refs):
    o_ref, lse_ref, done_ref, bias_ref = refs[-4:]
    done_ref[...] = jnp.zeros_like(done_ref)
    length = qkv_ref.shape[1]
    make_bias(bias_ref, segr_ref.at[0], segc_ref.at[0], length)

    @pl.loop(0, KEY_VALUE_HEADS)
    def _(kv):
        k = qkv_ref[pl.ds(pl.multiple_of(D + kv * HEAD_WIDTH, HEAD_WIDTH), HEAD_WIDTH), :]
        v = qkv_ref[pl.ds(pl.multiple_of(D + KEYS + kv * HEAD_WIDTH, HEAD_WIDTH), HEAD_WIDTH), :]
        for b in range(length // QB):
            lo, hi = key_span(b)
            s = dot(k[:, lo:hi], three(qkv_ref, kv, b), 0, 0) + wide_bias(bias_ref, b, hi - lo)
            top = jnp.max(s, axis=0, keepdims=True)
            p = jnp.exp(s - top)
            total = jnp.sum(p, axis=0, keepdims=True)
            out = dot(v[:, lo:hi], p.astype(BF16), 1, 0) / total
            lse = top + jnp.log(total)
            for i in range(SHARE):
                rows = pl.ds(pl.multiple_of((kv * SHARE + i) * HEAD_WIDTH, HEAD_WIDTH), HEAD_WIDTH)
                o_ref[rows, b * QB:(b + 1) * QB] = out[:, i * QB:(i + 1) * QB].astype(BF16)
                lse_ref[kv, i:i + 1, b * QB:(b + 1) * QB] = lse[:, i * QB:(i + 1) * QB]


DONE = jax.ShapeDtypeStruct((8, GAINS), F32)


def attend(qkv, segments, at, before=()):
    seqs, length = segments.shape
    wide, rows = qkv.shape
    return pl.pallas_call(
        attend_kernel,
        grid=(1,),
        in_specs=[
            pl.BlockSpec((wide, length), lambda i: (0, at)),
            pl.BlockSpec((1, 1, length), lambda i: (at, 0, 0)),
            pl.BlockSpec((1, length, 1), lambda i: (at, 0, 0)),
        ] + [pl.BlockSpec(memory_space=pltpu.HBM)] * len(before),
        out_specs=[
            pl.BlockSpec((D, length), lambda i: (0, at)),
            pl.BlockSpec((KEY_VALUE_HEADS, 8, length), lambda i: (0, 0, at)),
            fixed(DONE.shape),
        ],
        out_shape=shaped(((D, rows), BF16), ((KEY_VALUE_HEADS, 8, rows), F32)) + [DONE],
        input_output_aliases={3 + i: i for i in range(len(before))},
        scratch_shapes=[pltpu.VMEM((length // QB, 3 * QB, QB), F32)],
        compiler_params=params(60),
        cost_estimate=cost(),
        name="attend",
    )(qkv, segments[:, None, :], segments[:, :, None], *before)


def middle_kernel(weight, where_ref, x_ref, o_ref, gain_ref, *refs):
    x1_ref, h_ref, w, sem = refs[4:]

    @pl.when(pl.program_id(0) == 0)
    def _():
        weight.load(where_ref, refs[:4], w, sem)
        wait_for(w, sem)

    x1 = x_ref[...].astype(F32) + dot(w[...], o_ref[...], 0, 0)
    normal, _ = norm_columns(x1)
    x1_ref[...] = x1
    h_ref[...] = (normal * gain_ref[:, 1:2].astype(F32)).astype(BF16)


def middle(where, x, o, w, gains):
    rows = x.shape[1]
    return pl.pallas_call(
        functools.partial(middle_kernel, w),
        grid=(rows // TILE,),
        in_specs=[SMEM, columns(D, TILE), columns(D, TILE), fixed((D, GAINS))] + w.specs(),
        out_specs=[columns(D, TILE), columns(D, TILE)],
        out_shape=shaped(((D, rows), F32), ((D, rows), BF16)),
        scratch_shapes=w.scratch(),
        compiler_params=params(60),
        cost_estimate=cost(2 * rows * D * D, rows * D * 10),
        name="middle",
    )(where, x, o, gains, *w.arrays)


def feed_forward_kernel(weights, where_ref, h_ref, dy_ref, x1_ref, *refs):
    count = len(weights[0].arrays)
    y_ref, dh_ref, hid_ref, dgate_ref, dup_ref, acc_ref, *scratch = refs[3 * count:]
    step = pl.program_id(0)

    @pl.when(step == 0)
    def _():
        for i, weight in enumerate(weights):
            weight.load(where_ref, refs[i * count:(i + 1) * count], *scratch[2 * i:2 * i + 2])
        acc_ref[...] = x1_ref[...]
        dh_ref[...] = jnp.zeros_like(dh_ref)

    wg_ref, wu_ref, wd_ref = (w.at[step] for w in scratch[::2])
    for w, sem in zip((wg_ref, wu_ref, wd_ref), scratch[1::2]):
        wait_for(w, sem.at[step])
    h, dy = h_ref[...], dy_ref[...]
    gate = dot(wg_ref[...], h, 0, 0)
    up = dot(wu_ref[...], h, 0, 0)
    dhid = dot(wd_ref[...], dy, 0, 0)
    sig = jax.nn.sigmoid(gate)
    silu = gate * sig
    hid = (silu * up).astype(BF16)
    dgate = (dhid * up * (sig + silu * (1.0 - sig))).astype(BF16)
    dup = (dhid * silu).astype(BF16)
    hid_ref[...] = hid
    dgate_ref[...] = dgate
    dup_ref[...] = dup
    acc_ref[...] += dot(wd_ref[...], hid, 1, 0)
    dh_ref[...] += dot(wg_ref[...], dgate, 1, 0) + dot(wu_ref[...], dup, 1, 0)

    @pl.when(step == pl.num_programs(0) - 1)
    def _():
        y_ref[...] = acc_ref[...].astype(BF16)


def feed_forward(where, h, dy, x1, weights):
    rows, hidden = h.shape[1], weights[0].shape[1]
    block = pl.BlockSpec((CUT, rows), lambda f: (f, 0))
    return pl.pallas_call(
        functools.partial(feed_forward_kernel, weights),
        grid=(hidden // CUT,),
        in_specs=[SMEM, fixed((D, rows)), fixed((D, rows)), fixed((D, rows))]
        + sum((w.specs() for w in weights), []),
        out_specs=[fixed((D, rows)), fixed((D, rows))] + [block] * 3,
        out_shape=shaped(((D, rows), BF16), ((D, rows), F32)) + shaped(((hidden, rows), BF16)) * 3,
        scratch_shapes=sum((w.scratch() for w in weights), [pltpu.VMEM((D, rows), F32)]),
        compiler_params=params(60),
        cost_estimate=cost(),
        name="feed_forward",
    )(where, h, dy, x1, *sum((w.arrays for w in weights), []))


def split_owners(grad, where_ref, put):
    core, x_here = where_ref[0] & 1, where_ref[0] >> 1
    for x in range(2):
        a = grad[2 * x * OWN:(2 * x + 1) * OWN].astype(BF16)
        b = grad[(2 * x + 1) * OWN:(2 * x + 2) * OWN].astype(BF16)
        put(x_here ^ x, jnp.where(core == 0, a, b), jnp.where(core == 0, b, a))


def row_grads_kernel(where_ref, a_ref, b_ref, keep_ref, send_ref):
    def put(x, keep, send):
        keep_ref[x, 0] = keep
        send_ref[x, 0] = send

    split_owners(dot(a_ref[...], b_ref[...], 1, 1), where_ref, put)


def column_grads_kernel(dim, where_ref, a_ref, b_ref, keep_ref, send_ref):
    grad = dot(a_ref[...], b_ref[...], 1, 1).astype(BF16)
    here = (pl.program_id(0) & 1) == (where_ref[0] & 1)

    def put(ref):
        for i in range(4):
            ref[0, (2 * where_ref[1 + dim]) ^ i] = grad[i * OWN:(i + 1) * OWN]

    pl.when(here)(lambda: put(keep_ref))
    pl.when(jnp.logical_not(here))(lambda: put(send_ref))


def ffn_grads(where, a, b, dim, by_columns):
    rows = a.shape[1]
    if by_columns:
        kernel = functools.partial(column_grads_kernel, dim)
        out = pl.BlockSpec((1, 4, OWN, CUT), lambda f, at: ((f >> 1) ^ (at[0] >> 1), 0, 0, 0))
    else:
        kernel = row_grads_kernel
        out = pl.BlockSpec((2, 1, OWN, CUT), lambda f, at: (0, f ^ (2 * at[1 + dim]), 0, 0))
    return pl.pallas_call(
        kernel,
        grid_spec=pltpu.PrefetchScalarGridSpec(
            num_scalar_prefetch=1,
            grid=(b.shape[0] // CUT,),
            in_specs=[fixed((D, rows)), pl.BlockSpec((CUT, rows), lambda f, at: (f, 0))],
            out_specs=[out, out],
        ),
        out_shape=shaped(((2, 4, OWN, CUT), BF16)) * 2,
        compiler_params=params(60),
        cost_estimate=cost(),
        name="ffn_grads",
    )(where, a, b)


def branch_kernel(weight, where_ref, dh_ref, x1_ref, dy_ref, gain_ref, *refs):
    dx_ref, da_ref, do_ref, gain_grad, w, sem = refs[4:]
    first = pl.program_id(0) == 0

    @pl.when(first)
    def _():
        weight.load(where_ref, refs[:4], w, sem)

    gain = gain_ref[:, 1:2].astype(F32)
    normal, inverse = norm_columns(x1_ref[...])
    back, part = norm_columns_back(dh_ref[...], normal, inverse, gain)
    dx = dy_ref[...].astype(F32) + back
    da = dx.astype(BF16)
    dx_ref[...] = dx
    da_ref[...] = da

    @pl.when(first)
    def _():
        gain_grad[...] = part
        wait_for(w, sem)

    @pl.when(jnp.logical_not(first))
    def _():
        gain_grad[...] += part

    do_ref[...] = dot(w[...], da, 1, 0).astype(BF16)


def branch(where, dh, x1, dy, gains, w):
    rows = dh.shape[1]
    return pl.pallas_call(
        functools.partial(branch_kernel, w),
        grid=(rows // TILE,),
        in_specs=[SMEM] + [columns(D, TILE)] * 3 + [fixed((D, GAINS))] + w.specs(),
        out_specs=[columns(D, TILE)] * 3 + [pl.BlockSpec((D, 1), lambda i: (0, 0))],
        out_shape=shaped(((D, rows), F32), ((D, rows), BF16), ((D, rows), BF16), ((D, 1), F32)),
        scratch_shapes=w.scratch(),
        compiler_params=params(60),
        cost_estimate=cost(2 * rows * D * D, rows * D * 18),
        name="branch",
    )(where, dh, x1, dy, gains, *w.arrays)


def attend_back_kernel(qkv_ref, o_ref, do_ref, lse_ref, segr_ref, segc_ref, cos_ref, sin_ref,
                       *refs):
    out_ref, done_ref, bias_ref, dk_ref, dv_ref = refs[-5:]
    done_ref[...] = jnp.zeros_like(done_ref)
    length = qkv_ref.shape[1]
    make_bias(bias_ref, segr_ref.at[0], segc_ref.at[0], length)

    def turn_back(g, c, s, at, cols):
        a, b = g[:HALF], g[HALF:]
        at = pl.multiple_of(at, HEAD_WIDTH)
        out_ref[pl.ds(at, HALF), cols] = (a * c + b * s).astype(BF16)
        out_ref[pl.ds(pl.multiple_of(at + HALF, HALF), HALF), cols] = (b * c - a * s).astype(BF16)

    @pl.loop(0, KEY_VALUE_HEADS)
    def _(kv):
        k = qkv_ref[pl.ds(pl.multiple_of(D + kv * HEAD_WIDTH, HEAD_WIDTH), HEAD_WIDTH), :]
        v = qkv_ref[pl.ds(pl.multiple_of(D + KEYS + kv * HEAD_WIDTH, HEAD_WIDTH), HEAD_WIDTH), :]
        dk_ref[...] = jnp.zeros_like(dk_ref)
        dv_ref[...] = jnp.zeros_like(dv_ref)
        for b in range(length // QB):
            lo, hi = key_span(b)
            cols = slice(b * QB, (b + 1) * QB)
            q, o, do = three(qkv_ref, kv, b), three(o_ref, kv, b), three(do_ref, kv, b)
            lse = jnp.concatenate([lse_ref[kv, i:i + 1, cols] for i in range(SHARE)], axis=1)
            inner = jnp.sum(o.astype(F32) * do.astype(F32), axis=0, keepdims=True)
            s = dot(k[:, lo:hi], q, 0, 0) + wide_bias(bias_ref, b, hi - lo)
            p = jnp.exp(s - lse)
            dp = dot(v[:, lo:hi], do, 0, 0)
            ds = (p * (dp - inner)).astype(BF16)
            dv_ref[:, lo:hi] += dot(do, p.astype(BF16), 1, 1)
            dk_ref[:, lo:hi] += dot(q, ds, 1, 1)
            dq = dot(k[:, lo:hi], ds, 1, 0) * HEAD_WIDTH ** -0.5
            for i in range(SHARE):
                turn_back(dq[:, i * QB:(i + 1) * QB], cos_ref[:, cols], sin_ref[:, cols],
                          (kv * SHARE + i) * HEAD_WIDTH, cols)
        turn_back(dk_ref[...], cos_ref[...], sin_ref[...], D + kv * HEAD_WIDTH, slice(None))
        out_ref[pl.ds(pl.multiple_of(D + KEYS + kv * HEAD_WIDTH, HEAD_WIDTH), HEAD_WIDTH), :] = (
            dv_ref[...].astype(BF16))


def attend_back(qkv, o, do, lse, segments, cos, sin, at, before=()):
    length = segments.shape[1]
    wide, rows = qkv.shape
    here = lambda height: pl.BlockSpec((height, length), lambda i: (0, at))
    return pl.pallas_call(
        attend_back_kernel,
        grid=(1,),
        in_specs=[
            here(wide),
            here(D),
            here(D),
            pl.BlockSpec((KEY_VALUE_HEADS, 8, length), lambda i: (0, 0, at)),
            pl.BlockSpec((1, 1, length), lambda i: (at, 0, 0)),
            pl.BlockSpec((1, length, 1), lambda i: (at, 0, 0)),
            here(HALF),
            here(HALF),
        ] + [pl.BlockSpec(memory_space=pltpu.HBM)] * len(before),
        out_specs=[here(wide), fixed(DONE.shape)],
        out_shape=shaped(((wide, rows), BF16)) + [DONE],
        input_output_aliases={8 + i: i for i in range(len(before))},
        scratch_shapes=[
            pltpu.VMEM((length // QB, 3 * QB, QB), F32),
            pltpu.VMEM((HEAD_WIDTH, length), F32),
            pltpu.VMEM((HEAD_WIDTH, length), F32),
        ],
        compiler_params=params(60),
        cost_estimate=cost(),
        name="attend_back",
    )(qkv, o, do, lse, segments[:, None, :], segments[:, :, None], cos, sin, *before)


PIECES = ((0, 128), (128, OWN))


def weight_kernel(where_ref, h_ref, dqkv_ref, o_ref, da_ref, *out_refs):
    def store(block, grad):
        def put(x, keep, send):
            for i, (low, high) in enumerate(PIECES):
                at = block ^ (2 * where_ref[1 + i])
                out_refs[2 * i][x, at] = keep[low:high]
                out_refs[2 * i + 1][x, at] = send[low:high]

        split_owners(grad, where_ref, put)

    store(0, dot(h_ref[...], dqkv_ref[:CUT, :], 1, 1))
    store(1, dot(h_ref[...], dqkv_ref[CUT:2 * CUT, :], 1, 1))
    left = dot(h_ref[...], dqkv_ref[2 * CUT:, :], 1, 1)
    right = dot(o_ref[...], da_ref[:3 * CUT - WIDE, :], 1, 1)
    store(2, jnp.concatenate([left, right], axis=1))
    store(3, dot(o_ref[...], da_ref[3 * CUT - WIDE:, :], 1, 1))


def weight_grads(where, h, dqkv, o, da):
    rows = h.shape[1]
    shapes = [(2, 4, high - low, CUT) for low, high in PIECES for _ in range(2)]
    return pl.pallas_call(
        weight_kernel,
        grid=(1,),
        in_specs=[SMEM, fixed((D, rows)), fixed((WIDE, rows)), fixed((D, rows)), fixed((D, rows))],
        out_specs=[fixed(shape) for shape in shapes],
        out_shape=shaped(*((shape, BF16) for shape in shapes)),
        compiler_params=params(60),
        cost_estimate=cost(),
        name="weight_grads",
    )(where, h, dqkv, o, da)


def inputs_kernel(weights, where_ref, x_ref, dx_ref, dqkv_ref, *refs):
    out_ref, gain_grad, wq, q_sem, wk, k_sem = refs[8:]
    first = pl.program_id(0) == 0

    @pl.when(first)
    def _():
        weights[0].load(where_ref, refs[:4], wq, q_sem)
        weights[1].load(where_ref, refs[4:8], wk, k_sem)
        wait_for(wq, q_sem)
        wait_for(wk, k_sem)

    gain = wk[:, 2 * KEYS:2 * KEYS + 1].astype(F32)
    dh = dot(wq[...], dqkv_ref[:D], 1, 0) + dot(wk[:, :2 * KEYS], dqkv_ref[D:], 1, 0)
    normal, inverse = norm_columns(x_ref[...].astype(F32))
    back, part = norm_columns_back(dh, normal, inverse, gain)
    out_ref[...] = (dx_ref[...] + back).astype(BF16)

    @pl.when(first)
    def _():
        gain_grad[...] = part

    @pl.when(jnp.logical_not(first))
    def _():
        gain_grad[...] += part


def input_grads(where, x, dx, wq, wk, dqkv):
    rows = x.shape[1]
    return pl.pallas_call(
        functools.partial(inputs_kernel, (wq, wk)),
        grid=(rows // TILE,),
        in_specs=[SMEM, columns(D, TILE), columns(D, TILE), columns(WIDE, TILE)]
        + wq.specs() + wk.specs(),
        out_specs=[columns(D, TILE), pl.BlockSpec((D, 1), lambda i: (0, 0))],
        out_shape=shaped(((D, rows), BF16), ((D, 1), F32)),
        scratch_shapes=wq.scratch() + wk.scratch(),
        compiler_params=params(60),
        cost_estimate=cost(2 * rows * D * WIDE, rows * (D * 8 + WIDE * 2) + D * WIDE * 2),
        name="input_grads",
    )(where, x, dx, dqkv, *wq.arrays, *wk.arrays)


def tables(segments):
    length = segments.shape[1]
    index = jnp.arange(length, dtype=jnp.int32)
    same = segments[:, :, None] == segments[:, None, :]
    start = jnp.min(jnp.where(same, index[None, :, None], length), axis=1)
    position = (index[None, :] - start).astype(F32).reshape(1, -1)
    freq = THETA ** (-(jnp.arange(HALF, dtype=F32) * 2.0 / HEAD_WIDTH))
    angle = freq[:, None] * position
    return jnp.cos(angle), jnp.sin(angle)


def after(value, *others):
    return lax.optimization_barrier((value,) + others)[0]


class Cube:
    def __init__(self, count):
        self.count = count
        self.dims = count.bit_length() - 1
        self.masks = [1, 2, 6] + [1 << i for i in range(3, self.dims)]
        replica, group = lax.axis_index("replica"), lax.axis_index("group")
        bits = [(replica >> i) & 1 for i in range(self.dims)]
        self.coordinate = {i: bits[i] for i in range(self.dims)}
        self.coordinate[1] = bits[1] ^ bits[2]
        self.coordinate["x"] = group >> 1
        self.coordinate["core"] = group & 1
        self.me = group

    def swap(self, value, dim):
        if dim == "x":
            return lax.ppermute(value, "group", [(i, i ^ 2) for i in range(4)])
        if dim == "core":
            return lax.ppermute(value, "group", [(i, i ^ 1) for i in range(4)])
        mask = self.masks[dim]
        return lax.ppermute(value, "replica", [(i, i ^ mask) for i in range(self.count)])

    def ordered(self, dim, mine, other, axis):
        return jnp.where(
            self.coordinate[dim] == 0,
            jnp.concatenate([mine, other], axis=axis),
            jnp.concatenate([other, mine], axis=axis),
        )


def rows_of(own, sibling, across, diagonal):
    pieces = own, sibling, across, diagonal
    return Weight(0, [(array, flip, None) for flip, array in enumerate(pieces)])


class Relay:
    def __init__(self, cube, shard, axis, first, second):
        self.cube, self.shard, self.axis, self.dims = cube, shard, axis, (first, second)
        self.cut = 1 - axis
        self.size = shard.shape[self.cut] // 4
        at = 2 * cube.coordinate[second] + cube.coordinate[first]
        self.quarter = lax.dynamic_slice_in_dim(shard, at * self.size, self.size, self.cut)

    def cross(self, *others):
        self.direct = self.cube.swap(after(self.quarter, *others), "x")
        return self.direct

    def hand_on(self, *others):
        self.handed = self.cube.swap(after(self.direct, *others), self.dims[0])
        return self.handed

    def finish(self, *others):
        cube = self.cube
        handed = after(self.handed, *others)
        self.half = cube.ordered(self.dims[0], self.direct, handed, self.cut)
        self.rest = cube.swap(self.half, self.dims[1])
        self.half_diagonal = cube.swap(self.half, "core")
        return self.rest

    def weight(self, sibling, *others):
        rest = after(self.rest, *others)
        pieces = [
            (self.shard, 0, None), (sibling, 1, None), (self.half, 2, 0), (rest, 2, 1),
            (self.half_diagonal, 3, 0), (self.cube.swap(rest, "core"), 3, 1),
        ]
        return Weight(self.axis, pieces, self.dims[1], 4)


class Reduce:
    def __init__(self, cube, keep, got, order):
        rows, wide = keep.shape[2:]
        self.cube, self.order, self.shape = cube, order, (4, rows, wide)
        self.cut = [d for d in order[:2] if d != "x"][0]
        self.terms = [t.reshape(2, 2, 2, rows, wide) for t in (keep, got)]
        self.index = 0

    def sum(self, terms):
        return functools.reduce(jnp.add, [t.astype(F32) for t in terms]).astype(BF16)

    def ready(self, *others):
        dim = self.order[self.index]
        self.terms[-1] = after(self.terms[-1], *others)
        if self.index < 2:
            axis = 0 if dim == "x" else 1
            take = lambda i: [lax.slice_in_dim(t, i, i + 1, axis=axis) for t in self.terms]
            self.send, self.terms = self.sum(take(1)), take(0)
        else:
            self.send = self.sum(self.terms)
            self.terms = [self.send]
        return self.send

    def swap(self):
        dim = self.order[self.index]
        self.got = self.cube.swap(self.send, dim)
        self.index += 1
        if self.index == len(self.order):
            self.result = self.cube.ordered(dim, self.send, self.got, 1).reshape(self.shape)
        elif self.index > 2:
            self.terms = [self.send, self.got]
        else:
            self.terms = self.terms + [self.got]
        return self.got

    def step(self, *others):
        self.ready(*others)
        return self.swap()


def per_device(
    tokens,
    segments,
    query_weight,
    key_weight,
    value_weight,
    output_weight,
    w_gate,
    w_up,
    w_down,
    attn_gain,
    ffn_gain,
    cotangent,
    replicas,
):
    cube = Cube(replicas)
    where = jnp.stack([cube.me] + [cube.coordinate[i] for i in range(3)]).astype(jnp.int32)
    x, dy = tokens.T, cotangent.T

    core = lambda value: cube.swap(value, "core")
    q_across = cube.swap(query_weight, "x")
    pad = jnp.zeros((OWN, GAINS - 2), BF16)
    kv = jnp.concatenate(
        [key_weight, value_weight, attn_gain[:, None], ffn_gain[:, None], pad], axis=1
    )
    kv_across = cube.swap(after(kv, q_across), "x")
    relays = [
        Relay(cube, w_gate, 0, 0, 1), Relay(cube, w_up, 0, 1, 2), Relay(cube, w_down.T, 1, 2, 0)
    ]
    q_sibling, kv_sibling, wo_sibling = core(query_weight), core(kv), core(output_weight)
    siblings = [core(relay.shard) for relay in relays]
    cos, sin = tables(segments)
    early = [relay.quarter for relay in relays] + [cos, sin, q_sibling, kv_sibling, wo_sibling]
    q_across, kv_across = lax.optimization_barrier((q_across, kv_across, *early, *siblings))[:2]
    q_diagonal, kv_diagonal = core(q_across), core(kv_across)
    direct = [relay.cross(q_across, kv_across) for relay in relays]
    wq = rows_of(query_weight, q_sibling, q_across, q_diagonal)
    wk = rows_of(kv, kv_sibling, kv_across, kv_diagonal)
    qkv, h, gains = project(where, x, wq, wk, cos, sin)
    *first, done0 = attend(qkv, segments, 0)
    handed = [relay.hand_on(done0) for relay in relays]
    wo_across = cube.swap(after(output_weight, done0, *direct), "x")
    o, lse, done1 = attend(after(qkv, done0, *direct), segments, 1, first)
    rest = [relay.finish(done1) for relay in relays]
    wo_diagonal = core(after(wo_across, done1))
    wo = rows_of(output_weight, wo_sibling, wo_across, wo_diagonal)
    x1, h2 = middle(where, x, after(o, *[relay.half for relay in relays]), wo, gains)
    weights = [relay.weight(sibling, h2) for relay, sibling in zip(relays, siblings)]
    y, dh2, hid, dgate, dup = feed_forward(where, h2, dy, x1, weights)

    more = tuple(range(3, cube.dims))
    orders = [
        ("x", 0, 1, 2) + more + (0,), (1, "x", 2, 0) + more + (1,), (2, "x", 0, 1) + more + (2,)
    ]
    gd_keep, gd_send = ffn_grads(where, dy, hid, 0, True)
    gd = Reduce(cube, gd_keep, core(gd_send), orders[0])
    gg_keep, gg_send = ffn_grads(where, h2, after(dgate, gd_send), 1, False)
    gg = Reduce(cube, gg_keep, core(gg_send), orders[1])
    gd.ready(gg_send)
    gu_keep, gu_send = ffn_grads(where, h2, after(dup, gd.send), 2, False)
    gd.swap()
    gu = Reduce(cube, gu_keep, core(gu_send), orders[2])
    gg.ready(gu_send)
    dx1, da, do, ffn_gain_grad = branch(where, after(dh2, gg.send), x1, dy, gains, wo)
    gg.swap()
    gu.ready(da)
    gd.ready(da)
    do0 = after(do, gu.send, gd.send)
    gu.swap()
    gd.swap()
    *first, done0 = attend_back(qkv, o, do0, lse, segments, cos, sin, 0)
    gg.ready(done0)
    gd.ready(done0)
    do1 = after(do, done0, gg.send, gd.send)
    gg.swap()
    gd.swap()
    dqkv, done1 = attend_back(qkv, o, do1, lse, segments, cos, sin, 1, first)
    swaps = [gd, gg, gu]
    dqkv = after(dqkv, *[piece.ready(done1) for piece in swaps])
    for piece in swaps:
        piece.swap()
    parts = []
    weight_parts = weight_grads(where, h, dqkv, o, da)
    for i in range(len(PIECES)):
        keep, send = weight_parts[2 * i:2 * i + 2]
        parts.append(Reduce(cube, keep, core(send), orders[i]))
    dqkv = after(dqkv, *[part.ready(weight_parts[0]) for part in parts])
    for part in parts:
        part.swap()
    grad_x, attn_gain_grad = input_grads(where, x, dx1, wq, wk, dqkv)
    swaps = [gu, gg, parts[0], gd, parts[1]]
    both = jnp.concatenate([attn_gain_grad, ffn_gain_grad], axis=1).T.reshape(-1)
    ends = ["core", "x"] + list(range(cube.dims))
    token = grad_x
    for round_of in range(len(orders[0])):
        before = token
        for piece in swaps:
            if piece.index < len(piece.order):
                token = piece.ready(token)
                piece.swap()
        both = both + after(cube.swap(after(both, before), ends[round_of]), token)
    for dim in ends[len(orders[0]):]:
        both = both + cube.swap(both, dim)
    both = lax.dynamic_slice_in_dim(both.reshape(2, D), cube.me * OWN, OWN, 1)
    flat = lambda g: jnp.swapaxes(g, 0, 1).reshape(OWN, 4 * CUT).astype(F32)
    ga = flat(jnp.concatenate([part.result for part in parts], axis=1))
    return (
        y.T,
        grad_x.T,
        ga[:, :D],
        ga[:, D:D + KEYS],
        ga[:, D + KEYS:WIDE],
        ga[:, WIDE:],
        flat(gg.result),
        flat(gu.result),
        gd.result.reshape(D, CUT).T.astype(F32),
        both[0],
        both[1],
    )


def solution(mesh):
    rows = P(("group", "replica"), None)
    weight, gain = P("group", None), P("group")
    replicas = mesh.shape["replica"]
    return jax.shard_map(
        lambda *args: per_device(*args, replicas),
        mesh=mesh,
        in_specs=(rows, rows) + (weight,) * 7 + (gain, gain, rows),
        out_specs=(rows, rows) + (weight,) * 7 + (gain, gain),
        check_vma=False,
    )
```

```python
import functools

import jax
import jax.numpy as jnp
from jax import lax
from jax.experimental import pallas as pl
from jax.experimental.pallas import tpu as pltpu
from jax.sharding import PartitionSpec as P

D = 960
QUERY_HEADS = 15
KEY_VALUE_HEADS = 5
HEAD_WIDTH = 64
SHARE = QUERY_HEADS // KEY_VALUE_HEADS
HALF = HEAD_WIDTH // 2
KEYS = KEY_VALUE_HEADS * HEAD_WIDTH
EPS = 1e-05
THETA = 100000.0
TILE = 256
QB = 128
GAINS = 128
WIDE = D + 2 * KEYS
CUT = 640
OWN = 240
F32 = jnp.float32
BF16 = jnp.bfloat16
MIB = 1 << 20


def dot(a, b, ca, cb):
    return lax.dot_general(a, b, (((ca,), (cb,)), ((), ())), preferred_element_type=F32)


def params(limit, grid=1):
    return pltpu.CompilerParams(
        vmem_limit_bytes=limit * MIB, dimension_semantics=("arbitrary",) * grid
    )


def cost(*_):
    return pl.CostEstimate(flops=1, bytes_accessed=1, transcendentals=0)


def shaped(*shape_type):
    return [jax.ShapeDtypeStruct(s, t) for s, t in shape_type]


def norm_columns(v):
    inverse = lax.rsqrt(jnp.mean(v * v, axis=0, keepdims=True) + EPS)
    return v * inverse, inverse


def norm_columns_back(grad, normal, inverse, gain):
    scaled = grad * gain
    back = inverse * (scaled - normal * jnp.mean(scaled * normal, axis=0, keepdims=True))
    return back, jnp.sum(grad * normal, axis=1, keepdims=True)


def fixed(shape):
    return pl.BlockSpec(shape, lambda *_: (0,) * len(shape), pipeline_mode=pl.Buffered(1))


def columns(height, width):
    return pl.BlockSpec((height, width), lambda i: (0, i))


class Weight:
    def __init__(self, axis, pieces, dim=None, blocks=0):
        self.axis, self.dim, self.blocks = axis, dim, blocks
        self.arrays = [array for array, _, _ in pieces]
        self.places = [(flip, side) for _, flip, side in pieces]
        shape = list(self.arrays[0].shape)
        self.size = shape[axis]
        self.half = shape[1 - axis] // 2
        shape[axis] *= 4
        self.shape = tuple(shape)

    def specs(self):
        return [pl.BlockSpec(memory_space=pltpu.HBM)] * len(self.arrays)

    def scratch(self):
        if not self.blocks:
            return [pltpu.VMEM(self.shape, BF16), pltpu.SemaphoreType.DMA]
        block = (self.shape[0], self.shape[1] // self.blocks)
        return [pltpu.VMEM((self.blocks,) + block, BF16), pltpu.SemaphoreType.DMA((self.blocks,))]

    def load(self, where_ref, refs, scratch, sem):
        wide = self.shape[1] // max(self.blocks, 1)
        for ref, (flip, side) in zip(refs, self.places):
            at = (where_ref[0] ^ flip) * self.size
            other = 0 if side is None else (where_ref[1 + self.dim] ^ side) * self.half
            row, column = (at, other) if self.axis == 0 else (other, at)
            rows = pl.ds(pl.multiple_of(row, OWN), ref.shape[0])
            if not self.blocks:
                pltpu.make_async_copy(ref, scratch.at[rows, :], sem).start()
                continue
            first = column // wide
            for i in range(ref.shape[1] // wide):
                pltpu.make_async_copy(
                    ref.at[:, i * wide:(i + 1) * wide], scratch.at[first + i, rows, :],
                    sem.at[first + i],
                ).start()


def wait_for(scratch, sem):
    pltpu.make_async_copy(scratch, scratch, sem).wait()


SMEM = pl.BlockSpec(memory_space=pltpu.SMEM)


def project_kernel(weights, where_ref, x_ref, cos_ref, sin_ref, *refs):
    qkv_ref, h_ref, gains_ref, wq, q_sem, wk, k_sem = refs[8:]

    @pl.when(pl.program_id(0) == 0)
    def _():
        weights[0].load(where_ref, refs[:4], wq, q_sem)
        weights[1].load(where_ref, refs[4:8], wk, k_sem)
        wait_for(wq, q_sem)
        wait_for(wk, k_sem)
        gains_ref[...] = wk[:, 2 * KEYS:]

    gain = wk[:, 2 * KEYS:2 * KEYS + 1].astype(F32)
    normal, _ = norm_columns(x_ref[...].astype(F32))
    h = (normal * gain).astype(BF16)
    h_ref[...] = h
    c, s = cos_ref[...], sin_ref[...]

    def rotary(out, at, heads, scale):
        for head in range(heads):
            low = head * HEAD_WIDTH
            a, b = out[low:low + HALF], out[low + HALF:low + HEAD_WIDTH]
            to = at + low
            qkv_ref[to:to + HALF, :] = ((a * c - b * s) * scale).astype(BF16)
            qkv_ref[to + HALF:to + HEAD_WIDTH, :] = ((b * c + a * s) * scale).astype(BF16)

    rotary(dot(wq[...], h, 0, 0), 0, QUERY_HEADS, HEAD_WIDTH ** -0.5)
    out = dot(wk[:, :2 * KEYS], h, 0, 0)
    rotary(out, D, KEY_VALUE_HEADS, 1.0)
    qkv_ref[D + KEYS:, :] = out[KEYS:].astype(BF16)


def project(where, x, wq, wk, cos, sin):
    rows = x.shape[1]
    return pl.pallas_call(
        functools.partial(project_kernel, (wq, wk)),
        grid=(rows // TILE,),
        in_specs=[SMEM, columns(D, TILE), columns(HALF, TILE), columns(HALF, TILE)]
        + wq.specs() + wk.specs(),
        out_specs=[columns(WIDE, TILE), columns(D, TILE),
                   pl.BlockSpec((D, GAINS), lambda i: (0, 0))],
        out_shape=shaped(((WIDE, rows), BF16), ((D, rows), BF16), ((D, GAINS), BF16)),
        scratch_shapes=wq.scratch() + wk.scratch(),
        compiler_params=params(60),
        cost_estimate=cost(2 * rows * D * WIDE, rows * (2 * D + WIDE) * 2 + D * WIDE * 2),
        name="project",
    )(where, x, cos, sin, *wq.arrays, *wk.arrays)


def key_span(block):
    return max(0, QB * (block - 2)), QB * (block + 1)


def make_bias(bias_ref, segr_ref, segc_ref, length):
    for b in range(length // QB):
        lo, hi = key_span(b)
        key_at = lax.broadcasted_iota(jnp.int32, (hi - lo, QB), 0) + lo
        query_at = lax.broadcasted_iota(jnp.int32, (hi - lo, QB), 1) + b * QB
        ok = (segc_ref[lo:hi, :] == segr_ref[:, b * QB:(b + 1) * QB]) & (key_at <= query_at)
        bias_ref[b, 0:hi - lo, :] = jnp.where(ok, 0.0, -1e30)


def three(ref, kv, b):
    return jnp.concatenate(
        [
            ref[pl.ds(pl.multiple_of((kv * SHARE + i) * HEAD_WIDTH, HEAD_WIDTH), HEAD_WIDTH),
                b * QB:(b + 1) * QB]
            for i in range(SHARE)
        ],
        axis=1,
    )


def wide_bias(bias_ref, b, n):
    one = bias_ref[b, 0:n, :]
    return jnp.concatenate([one] * SHARE, axis=1)


def attend_kernel(qkv_ref, segr_ref, segc_ref, *refs):
    o_ref, lse_ref, done_ref, bias_ref = refs[-4:]
    done_ref[...] = jnp.zeros_like(done_ref)
    length = qkv_ref.shape[1]
    make_bias(bias_ref, segr_ref.at[0], segc_ref.at[0], length)

    @pl.loop(0, KEY_VALUE_HEADS)
    def _(kv):
        k = qkv_ref[pl.ds(pl.multiple_of(D + kv * HEAD_WIDTH, HEAD_WIDTH), HEAD_WIDTH), :]
        v = qkv_ref[pl.ds(pl.multiple_of(D + KEYS + kv * HEAD_WIDTH, HEAD_WIDTH), HEAD_WIDTH), :]
        for b in range(length // QB):
            lo, hi = key_span(b)
            s = dot(k[:, lo:hi], three(qkv_ref, kv, b), 0, 0) + wide_bias(bias_ref, b, hi - lo)
            top = jnp.max(s, axis=0, keepdims=True)
            p = jnp.exp(s - top)
            total = jnp.sum(p, axis=0, keepdims=True)
            out = dot(v[:, lo:hi], p.astype(BF16), 1, 0) / total
            lse = top + jnp.log(total)
            for i in range(SHARE):
                rows = pl.ds(pl.multiple_of((kv * SHARE + i) * HEAD_WIDTH, HEAD_WIDTH), HEAD_WIDTH)
                o_ref[rows, b * QB:(b + 1) * QB] = out[:, i * QB:(i + 1) * QB].astype(BF16)
                lse_ref[kv, i:i + 1, b * QB:(b + 1) * QB] = lse[:, i * QB:(i + 1) * QB]


DONE = jax.ShapeDtypeStruct((8, GAINS), F32)


def attend(qkv, segments, at, before=()):
    seqs, length = segments.shape
    wide, rows = qkv.shape
    return pl.pallas_call(
        attend_kernel,
        grid=(1,),
        in_specs=[
            pl.BlockSpec((wide, length), lambda i: (0, at)),
            pl.BlockSpec((1, 1, length), lambda i: (at, 0, 0)),
            pl.BlockSpec((1, length, 1), lambda i: (at, 0, 0)),
        ] + [pl.BlockSpec(memory_space=pltpu.HBM)] * len(before),
        out_specs=[
            pl.BlockSpec((D, length), lambda i: (0, at)),
            pl.BlockSpec((KEY_VALUE_HEADS, 8, length), lambda i: (0, 0, at)),
            fixed(DONE.shape),
        ],
        out_shape=shaped(((D, rows), BF16), ((KEY_VALUE_HEADS, 8, rows), F32)) + [DONE],
        input_output_aliases={3 + i: i for i in range(len(before))},
        scratch_shapes=[pltpu.VMEM((length // QB, 3 * QB, QB), F32)],
        compiler_params=params(60),
        cost_estimate=cost(),
        name="attend",
    )(qkv, segments[:, None, :], segments[:, :, None], *before)


def middle_kernel(weight, where_ref, x_ref, o_ref, gain_ref, *refs):
    x1_ref, h_ref, w, sem = refs[4:]

    @pl.when(pl.program_id(0) == 0)
    def _():
        weight.load(where_ref, refs[:4], w, sem)
        wait_for(w, sem)

    x1 = x_ref[...].astype(F32) + dot(w[...], o_ref[...], 0, 0)
    normal, _ = norm_columns(x1)
    x1_ref[...] = x1
    h_ref[...] = (normal * gain_ref[:, 1:2].astype(F32)).astype(BF16)


def middle(where, x, o, w, gains):
    rows = x.shape[1]
    return pl.pallas_call(
        functools.partial(middle_kernel, w),
        grid=(rows // TILE,),
        in_specs=[SMEM, columns(D, TILE), columns(D, TILE), fixed((D, GAINS))] + w.specs(),
        out_specs=[columns(D, TILE), columns(D, TILE)],
        out_shape=shaped(((D, rows), F32), ((D, rows), BF16)),
        scratch_shapes=w.scratch(),
        compiler_params=params(60),
        cost_estimate=cost(2 * rows * D * D, rows * D * 10),
        name="middle",
    )(where, x, o, gains, *w.arrays)


def feed_forward_kernel(weights, where_ref, h_ref, dy_ref, x1_ref, *refs):
    count = len(weights[0].arrays)
    y_ref, dh_ref, hid_ref, dgate_ref, dup_ref, acc_ref, *scratch = refs[3 * count:]
    step = pl.program_id(0)

    @pl.when(step == 0)
    def _():
        for i, weight in enumerate(weights):
            weight.load(where_ref, refs[i * count:(i + 1) * count], *scratch[2 * i:2 * i + 2])
        acc_ref[...] = x1_ref[...]
        dh_ref[...] = jnp.zeros_like(dh_ref)

    wg_ref, wu_ref, wd_ref = (w.at[step] for w in scratch[::2])
    for w, sem in zip((wg_ref, wu_ref, wd_ref), scratch[1::2]):
        wait_for(w, sem.at[step])
    h, dy = h_ref[...], dy_ref[...]
    gate = dot(wg_ref[...], h, 0, 0)
    up = dot(wu_ref[...], h, 0, 0)
    dhid = dot(wd_ref[...], dy, 0, 0)
    sig = jax.nn.sigmoid(gate)
    silu = gate * sig
    hid = (silu * up).astype(BF16)
    dgate = (dhid * up * (sig + silu * (1.0 - sig))).astype(BF16)
    dup = (dhid * silu).astype(BF16)
    hid_ref[...] = hid
    dgate_ref[...] = dgate
    dup_ref[...] = dup
    acc_ref[...] += dot(wd_ref[...], hid, 1, 0)
    dh_ref[...] += dot(wg_ref[...], dgate, 1, 0) + dot(wu_ref[...], dup, 1, 0)

    @pl.when(step == pl.num_programs(0) - 1)
    def _():
        y_ref[...] = acc_ref[...].astype(BF16)


def feed_forward(where, h, dy, x1, weights):
    rows, hidden = h.shape[1], weights[0].shape[1]
    block = pl.BlockSpec((CUT, rows), lambda f: (f, 0))
    return pl.pallas_call(
        functools.partial(feed_forward_kernel, weights),
        grid=(hidden // CUT,),
        in_specs=[SMEM, fixed((D, rows)), fixed((D, rows)), fixed((D, rows))]
        + sum((w.specs() for w in weights), []),
        out_specs=[fixed((D, rows)), fixed((D, rows))] + [block] * 3,
        out_shape=shaped(((D, rows), BF16), ((D, rows), F32)) + shaped(((hidden, rows), BF16)) * 3,
        scratch_shapes=sum((w.scratch() for w in weights), [pltpu.VMEM((D, rows), F32)]),
        compiler_params=params(60),
        cost_estimate=cost(),
        name="feed_forward",
    )(where, h, dy, x1, *sum((w.arrays for w in weights), []))


def block_here(where_ref):
    return 2 * where_ref[1] + where_ref[2]


def split_owners(grad, where_ref, put):
    core, x_here = where_ref[0] & 1, where_ref[0] >> 1
    for x in range(2):
        a = grad[2 * x * OWN:(2 * x + 1) * OWN].astype(BF16)
        b = grad[(2 * x + 1) * OWN:(2 * x + 2) * OWN].astype(BF16)
        put(x_here ^ x, jnp.where(core == 0, a, b), jnp.where(core == 0, b, a))


def row_grads_kernel(where_ref, a_ref, b_ref, keep_ref, send_ref):
    def put(x, keep, send):
        keep_ref[x, 0] = keep
        send_ref[x, 0] = send

    split_owners(dot(a_ref[...], b_ref[...], 1, 1), where_ref, put)


def column_grads_kernel(where_ref, a_ref, b_ref, keep_ref, send_ref):
    grad = dot(a_ref[...], b_ref[...], 1, 1).astype(BF16)
    here = (pl.program_id(0) & 1) == (where_ref[0] & 1)

    def put(ref):
        for i in range(4):
            ref[0, block_here(where_ref) ^ i] = grad[i * OWN:(i + 1) * OWN]

    pl.when(here)(lambda: put(keep_ref))
    pl.when(jnp.logical_not(here))(lambda: put(send_ref))


def ffn_grads(where, a, b, by_columns):
    rows = a.shape[1]
    if by_columns:
        kernel = column_grads_kernel
        out = pl.BlockSpec((1, 4, OWN, CUT), lambda f, at: ((f >> 1) ^ (at[0] >> 1), 0, 0, 0))
    else:
        kernel = row_grads_kernel
        out = pl.BlockSpec((2, 1, OWN, CUT), lambda f, at: (0, f ^ block_here(at), 0, 0))
    return pl.pallas_call(
        kernel,
        grid_spec=pltpu.PrefetchScalarGridSpec(
            num_scalar_prefetch=1,
            grid=(b.shape[0] // CUT,),
            in_specs=[fixed((D, rows)), pl.BlockSpec((CUT, rows), lambda f, at: (f, 0))],
            out_specs=[out, out],
        ),
        out_shape=shaped(((2, 4, OWN, CUT), BF16)) * 2,
        compiler_params=params(60),
        cost_estimate=cost(),
        name="ffn_grads",
    )(where, a, b)


def branch_kernel(weight, where_ref, dh_ref, x1_ref, dy_ref, gain_ref, *refs):
    dx_ref, da_ref, do_ref, gain_grad, w, sem = refs[4:]
    first = pl.program_id(0) == 0

    @pl.when(first)
    def _():
        weight.load(where_ref, refs[:4], w, sem)

    gain = gain_ref[:, 1:2].astype(F32)
    normal, inverse = norm_columns(x1_ref[...])
    back, part = norm_columns_back(dh_ref[...], normal, inverse, gain)
    dx = dy_ref[...].astype(F32) + back
    da = dx.astype(BF16)
    dx_ref[...] = dx
    da_ref[...] = da

    @pl.when(first)
    def _():
        gain_grad[...] = part
        wait_for(w, sem)

    @pl.when(jnp.logical_not(first))
    def _():
        gain_grad[...] += part

    do_ref[...] = dot(w[...], da, 1, 0).astype(BF16)


def branch(where, dh, x1, dy, gains, w):
    rows = dh.shape[1]
    return pl.pallas_call(
        functools.partial(branch_kernel, w),
        grid=(rows // TILE,),
        in_specs=[SMEM] + [columns(D, TILE)] * 3 + [fixed((D, GAINS))] + w.specs(),
        out_specs=[columns(D, TILE)] * 3 + [pl.BlockSpec((D, 1), lambda i: (0, 0))],
        out_shape=shaped(((D, rows), F32), ((D, rows), BF16), ((D, rows), BF16), ((D, 1), F32)),
        scratch_shapes=w.scratch(),
        compiler_params=params(60),
        cost_estimate=cost(2 * rows * D * D, rows * D * 18),
        name="branch",
    )(where, dh, x1, dy, gains, *w.arrays)


def attend_back_kernel(qkv_ref, o_ref, do_ref, lse_ref, segr_ref, segc_ref, cos_ref, sin_ref,
                       *refs):
    out_ref, done_ref, bias_ref, dk_ref, dv_ref = refs[-5:]
    done_ref[...] = jnp.zeros_like(done_ref)
    length = qkv_ref.shape[1]
    make_bias(bias_ref, segr_ref.at[0], segc_ref.at[0], length)

    def turn_back(g, c, s, at, cols):
        a, b = g[:HALF], g[HALF:]
        at = pl.multiple_of(at, HEAD_WIDTH)
        out_ref[pl.ds(at, HALF), cols] = (a * c + b * s).astype(BF16)
        out_ref[pl.ds(pl.multiple_of(at + HALF, HALF), HALF), cols] = (b * c - a * s).astype(BF16)

    @pl.loop(0, KEY_VALUE_HEADS)
    def _(kv):
        k = qkv_ref[pl.ds(pl.multiple_of(D + kv * HEAD_WIDTH, HEAD_WIDTH), HEAD_WIDTH), :]
        v = qkv_ref[pl.ds(pl.multiple_of(D + KEYS + kv * HEAD_WIDTH, HEAD_WIDTH), HEAD_WIDTH), :]
        dk_ref[...] = jnp.zeros_like(dk_ref)
        dv_ref[...] = jnp.zeros_like(dv_ref)
        for b in range(length // QB):
            lo, hi = key_span(b)
            cols = slice(b * QB, (b + 1) * QB)
            q, o, do = three(qkv_ref, kv, b), three(o_ref, kv, b), three(do_ref, kv, b)
            lse = jnp.concatenate([lse_ref[kv, i:i + 1, cols] for i in range(SHARE)], axis=1)
            inner = jnp.sum(o.astype(F32) * do.astype(F32), axis=0, keepdims=True)
            s = dot(k[:, lo:hi], q, 0, 0) + wide_bias(bias_ref, b, hi - lo)
            p = jnp.exp(s - lse)
            dp = dot(v[:, lo:hi], do, 0, 0)
            ds = (p * (dp - inner)).astype(BF16)
            dv_ref[:, lo:hi] += dot(do, p.astype(BF16), 1, 1)
            dk_ref[:, lo:hi] += dot(q, ds, 1, 1)
            dq = dot(k[:, lo:hi], ds, 1, 0) * HEAD_WIDTH ** -0.5
            for i in range(SHARE):
                turn_back(dq[:, i * QB:(i + 1) * QB], cos_ref[:, cols], sin_ref[:, cols],
                          (kv * SHARE + i) * HEAD_WIDTH, cols)
        turn_back(dk_ref[...], cos_ref[...], sin_ref[...], D + kv * HEAD_WIDTH, slice(None))
        out_ref[pl.ds(pl.multiple_of(D + KEYS + kv * HEAD_WIDTH, HEAD_WIDTH), HEAD_WIDTH), :] = (
            dv_ref[...].astype(BF16))


def attend_back(qkv, o, do, lse, segments, cos, sin, at, before=()):
    length = segments.shape[1]
    wide, rows = qkv.shape
    here = lambda height: pl.BlockSpec((height, length), lambda i: (0, at))
    return pl.pallas_call(
        attend_back_kernel,
        grid=(1,),
        in_specs=[
            here(wide),
            here(D),
            here(D),
            pl.BlockSpec((KEY_VALUE_HEADS, 8, length), lambda i: (0, 0, at)),
            pl.BlockSpec((1, 1, length), lambda i: (at, 0, 0)),
            pl.BlockSpec((1, length, 1), lambda i: (at, 0, 0)),
            here(HALF),
            here(HALF),
        ] + [pl.BlockSpec(memory_space=pltpu.HBM)] * len(before),
        out_specs=[here(wide), fixed(DONE.shape)],
        out_shape=shaped(((wide, rows), BF16)) + [DONE],
        input_output_aliases={8 + i: i for i in range(len(before))},
        scratch_shapes=[
            pltpu.VMEM((length // QB, 3 * QB, QB), F32),
            pltpu.VMEM((HEAD_WIDTH, length), F32),
            pltpu.VMEM((HEAD_WIDTH, length), F32),
        ],
        compiler_params=params(60),
        cost_estimate=cost(),
        name="attend_back",
    )(qkv, o, do, lse, segments[:, None, :], segments[:, :, None], cos, sin, *before)


PIECES = ((0, 128), (128, OWN))


def weight_kernel(where_ref, h_ref, dqkv_ref, o_ref, da_ref, *out_refs):
    def store(block, grad):
        def put(x, keep, send):
            for i, (low, high) in enumerate(PIECES):
                at = block ^ block_here(where_ref)
                out_refs[2 * i][x, at] = keep[low:high]
                out_refs[2 * i + 1][x, at] = send[low:high]

        split_owners(grad, where_ref, put)

    store(0, dot(h_ref[...], dqkv_ref[:CUT, :], 1, 1))
    store(1, dot(h_ref[...], dqkv_ref[CUT:2 * CUT, :], 1, 1))
    left = dot(h_ref[...], dqkv_ref[2 * CUT:, :], 1, 1)
    right = dot(o_ref[...], da_ref[:3 * CUT - WIDE, :], 1, 1)
    store(2, jnp.concatenate([left, right], axis=1))
    store(3, dot(o_ref[...], da_ref[3 * CUT - WIDE:, :], 1, 1))


def weight_grads(where, h, dqkv, o, da):
    rows = h.shape[1]
    shapes = [(2, 4, high - low, CUT) for low, high in PIECES for _ in range(2)]
    return pl.pallas_call(
        weight_kernel,
        grid=(1,),
        in_specs=[SMEM, fixed((D, rows)), fixed((WIDE, rows)), fixed((D, rows)), fixed((D, rows))],
        out_specs=[fixed(shape) for shape in shapes],
        out_shape=shaped(*((shape, BF16) for shape in shapes)),
        compiler_params=params(60),
        cost_estimate=cost(),
        name="weight_grads",
    )(where, h, dqkv, o, da)


def inputs_kernel(weights, where_ref, x_ref, dx_ref, dqkv_ref, *refs):
    out_ref, gain_grad, wq, q_sem, wk, k_sem = refs[8:]
    first = pl.program_id(0) == 0

    @pl.when(first)
    def _():
        weights[0].load(where_ref, refs[:4], wq, q_sem)
        weights[1].load(where_ref, refs[4:8], wk, k_sem)
        wait_for(wq, q_sem)
        wait_for(wk, k_sem)

    gain = wk[:, 2 * KEYS:2 * KEYS + 1].astype(F32)
    dh = dot(wq[...], dqkv_ref[:D], 1, 0) + dot(wk[:, :2 * KEYS], dqkv_ref[D:], 1, 0)
    normal, inverse = norm_columns(x_ref[...].astype(F32))
    back, part = norm_columns_back(dh, normal, inverse, gain)
    out_ref[...] = (dx_ref[...] + back).astype(BF16)

    @pl.when(first)
    def _():
        gain_grad[...] = part

    @pl.when(jnp.logical_not(first))
    def _():
        gain_grad[...] += part


def input_grads(where, x, dx, wq, wk, dqkv):
    rows = x.shape[1]
    return pl.pallas_call(
        functools.partial(inputs_kernel, (wq, wk)),
        grid=(rows // TILE,),
        in_specs=[SMEM, columns(D, TILE), columns(D, TILE), columns(WIDE, TILE)]
        + wq.specs() + wk.specs(),
        out_specs=[columns(D, TILE), pl.BlockSpec((D, 1), lambda i: (0, 0))],
        out_shape=shaped(((D, rows), BF16), ((D, 1), F32)),
        scratch_shapes=wq.scratch() + wk.scratch(),
        compiler_params=params(60),
        cost_estimate=cost(2 * rows * D * WIDE, rows * (D * 8 + WIDE * 2) + D * WIDE * 2),
        name="input_grads",
    )(where, x, dx, dqkv, *wq.arrays, *wk.arrays)


def tables(segments):
    length = segments.shape[1]
    index = jnp.arange(length, dtype=jnp.int32)
    same = segments[:, :, None] == segments[:, None, :]
    start = jnp.min(jnp.where(same, index[None, :, None], length), axis=1)
    position = (index[None, :] - start).astype(F32).reshape(1, -1)
    freq = THETA ** (-(jnp.arange(HALF, dtype=F32) * 2.0 / HEAD_WIDTH))
    angle = freq[:, None] * position
    return jnp.cos(angle), jnp.sin(angle)


def after(value, *others):
    return lax.optimization_barrier((value,) + others)[0]


class Cube:
    def __init__(self, count):
        self.count = count
        self.dims = count.bit_length() - 1
        replica, group = lax.axis_index("replica"), lax.axis_index("group")
        self.coordinate = {i: (replica >> i) & 1 for i in range(self.dims)}
        self.coordinate["x"] = group >> 1
        self.coordinate["core"] = group & 1
        self.me = group

    def swap(self, value, dim):
        if dim == "x":
            return lax.ppermute(value, "group", [(i, i ^ 2) for i in range(4)])
        if dim == "core":
            return lax.ppermute(value, "group", [(i, i ^ 1) for i in range(4)])
        return lax.ppermute(value, "replica", [(i, i ^ (1 << dim)) for i in range(self.count)])

    def ordered(self, dim, mine, other, axis):
        return jnp.where(
            self.coordinate[dim] == 0,
            jnp.concatenate([mine, other], axis=axis),
            jnp.concatenate([other, mine], axis=axis),
        )


def rows_of(own, sibling, across, diagonal):
    pieces = own, sibling, across, diagonal
    return Weight(0, [(array, flip, None) for flip, array in enumerate(pieces)])


class Relay:
    def __init__(self, cube, shard, axis, first, second):
        self.cube, self.shard, self.axis, self.dims = cube, shard, axis, (first, second)
        self.cut = 1 - axis
        self.size = shard.shape[self.cut] // 4
        at = 2 * cube.coordinate[second] + cube.coordinate[first]
        self.quarter = lax.dynamic_slice_in_dim(shard, at * self.size, self.size, self.cut)

    def cross(self, *others):
        self.direct = self.cube.swap(after(self.quarter, *others), "x")
        return self.direct

    def hand_on(self, *others):
        self.handed = self.cube.swap(after(self.direct, *others), self.dims[0])
        return self.handed

    def finish(self, *others):
        cube = self.cube
        handed = after(self.handed, *others)
        self.half = cube.ordered(self.dims[0], self.direct, handed, self.cut)
        self.rest = cube.swap(self.half, self.dims[1])
        self.half_diagonal = cube.swap(self.half, "core")
        return self.rest

    def weight(self, sibling, *others):
        rest = after(self.rest, *others)
        pieces = [
            (self.shard, 0, None), (sibling, 1, None), (self.half, 2, 0), (rest, 2, 1),
            (self.half_diagonal, 3, 0), (self.cube.swap(rest, "core"), 3, 1),
        ]
        return Weight(self.axis, pieces, self.dims[1], 4)


class Reduce:
    def __init__(self, cube, keep, got, halves, gathers):
        rows, wide = keep.shape[2:]
        self.cube, self.shape = cube, (4, rows, wide)
        self.order = halves + tuple(range(2, cube.dims)) + gathers
        self.place = {"x": 0, 0: 1, 1: 2}
        self.terms = [t.reshape(2, 2, 2, rows, wide) for t in (keep, got)]
        self.index = 0

    def sum(self, terms):
        if len(terms) == 1:
            return terms[0]
        return functools.reduce(jnp.add, [t.astype(F32) for t in terms]).astype(BF16)

    def ready(self, *others):
        dim = self.order[self.index]
        self.terms[-1] = after(self.terms[-1], *others)
        if self.index < 3:
            axis = self.place[dim]
            take = lambda i: [lax.slice_in_dim(t, i, i + 1, axis=axis) for t in self.terms]
            self.send, self.terms = self.sum(take(1)), take(0)
        else:
            self.send = self.sum(self.terms)
        return self.send

    def swap(self):
        dim = self.order[self.index]
        got = self.cube.swap(self.send, dim)
        self.index += 1
        if self.index <= 3:
            self.terms = self.terms + [got]
        elif self.index <= len(self.order) - 2:
            self.terms = [self.send, got]
        else:
            self.terms = [self.cube.ordered(dim, self.send, got, self.place[dim])]

    def result(self):
        return self.terms[0].reshape(self.shape)


def per_device(
    tokens,
    segments,
    query_weight,
    key_weight,
    value_weight,
    output_weight,
    w_gate,
    w_up,
    w_down,
    attn_gain,
    ffn_gain,
    cotangent,
    replicas,
):
    cube = Cube(replicas)
    where = jnp.stack([cube.me] + [cube.coordinate[i] for i in range(3)]).astype(jnp.int32)
    x, dy = tokens.T, cotangent.T

    core = lambda value: cube.swap(value, "core")
    q_across = cube.swap(query_weight, "x")
    pad = jnp.zeros((OWN, GAINS - 2), BF16)
    kv = jnp.concatenate(
        [key_weight, value_weight, attn_gain[:, None], ffn_gain[:, None], pad], axis=1
    )
    kv_across = cube.swap(after(kv, q_across), "x")
    relays = [
        Relay(cube, w_gate, 0, 0, 1), Relay(cube, w_up, 0, 1, 0), Relay(cube, w_down.T, 1, 0, 1)
    ]
    q_sibling, kv_sibling, wo_sibling = core(query_weight), core(kv), core(output_weight)
    siblings = [core(relay.shard) for relay in relays]
    cos, sin = tables(segments)
    early = [relay.quarter for relay in relays] + [cos, sin, q_sibling, kv_sibling, wo_sibling]
    q_across, kv_across = lax.optimization_barrier((q_across, kv_across, *early, *siblings))[:2]
    q_diagonal, kv_diagonal = core(q_across), core(kv_across)
    direct = [relay.cross(q_across, kv_across) for relay in relays]
    wq = rows_of(query_weight, q_sibling, q_across, q_diagonal)
    wk = rows_of(kv, kv_sibling, kv_across, kv_diagonal)
    qkv, h, gains = project(where, x, wq, wk, cos, sin)
    *first, done0 = attend(qkv, segments, 0)
    handed = [relay.hand_on(done0) for relay in relays]
    wo_across = cube.swap(after(output_weight, done0, *direct), "x")
    o, lse, done1 = attend(after(qkv, done0, *direct), segments, 1, first)
    rest = [relay.finish(done1) for relay in relays]
    wo_diagonal = core(after(wo_across, done1))
    wo = rows_of(output_weight, wo_sibling, wo_across, wo_diagonal)
    x1, h2 = middle(where, x, after(o, *[relay.half for relay in relays]), wo, gains)
    weights = [relay.weight(sibling, h2) for relay, sibling in zip(relays, siblings)]
    y, dh2, hid, dgate, dup = feed_forward(where, h2, dy, x1, weights)

    gd_keep, gd_send = ffn_grads(where, dy, hid, True)
    gd = Reduce(cube, gd_keep, core(gd_send), ("x", 0, 1), (1, 0))
    gg_keep, gg_send = ffn_grads(where, h2, after(dgate, gd_send), False)
    gg = Reduce(cube, gg_keep, core(gg_send), (0, "x", 1), (0, 1))
    gd.ready(gg_send)
    gu_keep, gu_send = ffn_grads(where, h2, after(dup, gd.send), False)
    gd.swap()
    gu = Reduce(cube, gu_keep, core(gu_send), (1, 0, "x"), (1, 0))
    gg.ready(gu_send)
    dx1, da, do, ffn_gain_grad = branch(where, after(dh2, gg.send), x1, dy, gains, wo)
    gg.swap()
    gu.ready(da)
    do0 = after(do, gu.send)
    gu.swap()
    *first, done0 = attend_back(qkv, o, do0, lse, segments, cos, sin, 0)
    do1 = after(do, done0, *[piece.ready(done0) for piece in (gd, gg)])
    gd.swap()
    gg.swap()
    dqkv, done1 = attend_back(qkv, o, do1, lse, segments, cos, sin, 1, first)
    swaps = [gd, gg, gu]
    dqkv = after(dqkv, *[piece.ready(done1) for piece in swaps])
    for piece in swaps:
        piece.swap()
    parts = []
    weight_parts = weight_grads(where, h, dqkv, o, da)
    for i, halves in enumerate((("x", 0, 1), (0, "x", 1))):
        keep, send = weight_parts[2 * i:2 * i + 2]
        parts.append(Reduce(cube, keep, core(send), halves, (1 - i, i)))
    dqkv = after(dqkv, *[part.ready(weight_parts[0]) for part in parts])
    for part in parts:
        part.swap()
    grad_x, attn_gain_grad = input_grads(where, x, dx1, wq, wk, dqkv)
    swaps = [gd, gg, gu] + parts
    both = jnp.concatenate([attn_gain_grad, ffn_gain_grad], axis=1).T.reshape(-1)
    ends = ["core", "x"] + list(range(cube.dims))
    token = grad_x
    while any(piece.index < len(piece.order) for piece in swaps):
        before = token
        for piece in swaps:
            if piece.index < len(piece.order):
                token = piece.ready(token)
                piece.swap()
        if ends:
            both = both + after(cube.swap(after(both, before), ends.pop(0)), token)
    for dim in ends:
        both = both + cube.swap(both, dim)
    both = lax.dynamic_slice_in_dim(both.reshape(2, D), cube.me * OWN, OWN, 1)
    flat = lambda g: jnp.concatenate([g[i] for i in range(4)], axis=1)
    ga = jnp.concatenate([flat(part.result()) for part in parts], axis=0).astype(F32)
    return (
        y.T,
        grad_x.T,
        ga[:, :D],
        ga[:, D:D + KEYS],
        ga[:, D + KEYS:WIDE],
        ga[:, WIDE:],
        flat(gg.result()).astype(F32),
        flat(gu.result()).astype(F32),
        gd.result().reshape(D, CUT).T.astype(F32),
        both[0],
        both[1],
    )


def solution(mesh):
    rows = P(("group", "replica"), None)
    weight, gain = P("group", None), P("group")
    replicas = mesh.shape["replica"]
    return jax.shard_map(
        lambda *args: per_device(*args, replicas),
        mesh=mesh,
        in_specs=(rows, rows) + (weight,) * 7 + (gain, gain, rows),
        out_specs=(rows, rows) + (weight,) * 7 + (gain, gain),
        check_vma=False,
    )
```

```python
import functools

import jax
import jax.numpy as jnp
from jax import lax
from jax.experimental import pallas as pl
from jax.experimental.pallas import tpu as pltpu
from jax.sharding import PartitionSpec as P

D = 960
QUERY_HEADS = 15
KEY_VALUE_HEADS = 5
HEAD_WIDTH = 64
SHARE = QUERY_HEADS // KEY_VALUE_HEADS
HALF = HEAD_WIDTH // 2
KEYS = KEY_VALUE_HEADS * HEAD_WIDTH
EPS = 1e-05
THETA = 100000.0
TILE = 512
QB = 128
GAINS = 128
WIDE = D + 2 * KEYS
CUT = 640
OWN = 240
PAIR = 2 * CUT
F32 = jnp.float32
BF16 = jnp.bfloat16
MIB = 1 << 20


def dot(a, b, ca, cb):
    return lax.dot_general(a, b, (((ca,), (cb,)), ((), ())), preferred_element_type=F32)


def params(limit, grid=1):
    return pltpu.CompilerParams(
        vmem_limit_bytes=limit * MIB, dimension_semantics=("arbitrary",) * grid
    )


def cost(*_):
    return pl.CostEstimate(flops=1, bytes_accessed=1, transcendentals=0)


def shaped(*shape_type):
    return [jax.ShapeDtypeStruct(s, t) for s, t in shape_type]


def norm_columns(v):
    inverse = lax.rsqrt(jnp.mean(v * v, axis=0, keepdims=True) + EPS)
    return v * inverse, inverse


def norm_columns_back(grad, normal, inverse, gain):
    scaled = grad * gain
    back = inverse * (scaled - normal * jnp.mean(scaled * normal, axis=0, keepdims=True))
    return back, jnp.sum(grad * normal, axis=1, keepdims=True)


def fixed(shape):
    return pl.BlockSpec(shape, lambda *_: (0,) * len(shape), pipeline_mode=pl.Buffered(1))


def columns(height, width):
    return pl.BlockSpec((height, width), lambda i: (0, i))


class Weight:
    def __init__(self, axis, pieces, dim=None, blocks=0):
        self.axis, self.dim, self.blocks = axis, dim, blocks
        self.arrays = [array for array, _, _ in pieces]
        self.places = [(flip, side) for _, flip, side in pieces]
        shape = list(self.arrays[0].shape)
        self.size = shape[axis]
        self.half = shape[1 - axis] // 2
        shape[axis] *= 4
        self.shape = tuple(shape)

    def specs(self):
        return [pl.BlockSpec(memory_space=pltpu.HBM)] * len(self.arrays)

    def scratch(self):
        if not self.blocks:
            return [pltpu.VMEM(self.shape, BF16), pltpu.SemaphoreType.DMA]
        block = (self.shape[0], self.shape[1] // self.blocks)
        return [pltpu.VMEM((self.blocks,) + block, BF16), pltpu.SemaphoreType.DMA((self.blocks,))]

    def load(self, where_ref, refs, scratch, sem):
        wide = self.shape[1] // max(self.blocks, 1)
        for ref, (flip, side) in zip(refs, self.places):
            at = (where_ref[0] ^ flip) * self.size
            other = 0 if side is None else (where_ref[1 + self.dim] ^ side) * self.half
            row, column = (at, other) if self.axis == 0 else (other, at)
            rows = pl.ds(pl.multiple_of(row, OWN), ref.shape[0])
            if not self.blocks:
                pltpu.make_async_copy(ref, scratch.at[rows, :], sem).start()
                continue
            first = column // wide
            if ref.shape[1] < wide:
                inner = pl.ds(pl.multiple_of(column % wide, GAINS), ref.shape[1])
                pltpu.make_async_copy(
                    ref, scratch.at[first, rows, inner], sem.at[first]
                ).start()
            for i in range(ref.shape[1] // wide):
                pltpu.make_async_copy(
                    ref.at[:, i * wide:(i + 1) * wide], scratch.at[first + i, rows, :],
                    sem.at[first + i],
                ).start()


def wait_for(scratch, sem):
    pltpu.make_async_copy(scratch, scratch, sem).wait()


SMEM = pl.BlockSpec(memory_space=pltpu.SMEM)


def project_kernel(weights, where_ref, x_ref, cos_ref, sin_ref, *refs):
    qkv_ref, h_ref, gains_ref, wq, q_sem, wk, k_sem = refs[8:]

    @pl.when(pl.program_id(0) == 0)
    def _():
        weights[0].load(where_ref, refs[:4], wq, q_sem)
        weights[1].load(where_ref, refs[4:8], wk, k_sem)
        wait_for(wq, q_sem)
        wait_for(wk, k_sem)
        gains_ref[...] = wk[:, 2 * KEYS:]

    gain = wk[:, 2 * KEYS:2 * KEYS + 1].astype(F32)
    normal, _ = norm_columns(x_ref[...].astype(F32))
    h = (normal * gain).astype(BF16)
    h_ref[...] = h
    c, s = cos_ref[...], sin_ref[...]

    def rotary(out, at, heads, scale):
        for head in range(heads):
            low = head * HEAD_WIDTH
            a, b = out[low:low + HALF], out[low + HALF:low + HEAD_WIDTH]
            to = at + low
            qkv_ref[to:to + HALF, :] = ((a * c - b * s) * scale).astype(BF16)
            qkv_ref[to + HALF:to + HEAD_WIDTH, :] = ((b * c + a * s) * scale).astype(BF16)

    rotary(dot(wq[...], h, 0, 0), 0, QUERY_HEADS, HEAD_WIDTH ** -0.5)
    out = dot(wk[:, :2 * KEYS], h, 0, 0)
    rotary(out, D, KEY_VALUE_HEADS, 1.0)
    qkv_ref[D + KEYS:, :] = out[KEYS:].astype(BF16)


def project(where, x, wq, wk, cos, sin):
    rows = x.shape[1]
    return pl.pallas_call(
        functools.partial(project_kernel, (wq, wk)),
        grid=(rows // TILE,),
        in_specs=[SMEM, columns(D, TILE), columns(HALF, TILE), columns(HALF, TILE)]
        + wq.specs() + wk.specs(),
        out_specs=[columns(WIDE, TILE), columns(D, TILE),
                   pl.BlockSpec((D, GAINS), lambda i: (0, 0))],
        out_shape=shaped(((WIDE, rows), BF16), ((D, rows), BF16), ((D, GAINS), BF16)),
        scratch_shapes=wq.scratch() + wk.scratch(),
        compiler_params=params(60),
        cost_estimate=cost(2 * rows * D * WIDE, rows * (2 * D + WIDE) * 2 + D * WIDE * 2),
        name="project",
    )(where, x, cos, sin, *wq.arrays, *wk.arrays)


def key_span(block):
    return max(0, QB * (block - 2)), QB * (block + 1)


def make_bias(bias_ref, segr_ref, segc_ref, length):
    for b in range(length // QB):
        lo, hi = key_span(b)
        key_at = lax.broadcasted_iota(jnp.int32, (hi - lo, QB), 0) + lo
        query_at = lax.broadcasted_iota(jnp.int32, (hi - lo, QB), 1) + b * QB
        ok = (segc_ref[lo:hi, :] == segr_ref[:, b * QB:(b + 1) * QB]) & (key_at <= query_at)
        bias_ref[b, 0:hi - lo, :] = jnp.where(ok, 0.0, -1e30)


def three(ref, kv, b):
    return jnp.concatenate(
        [
            ref[pl.ds(pl.multiple_of((kv * SHARE + i) * HEAD_WIDTH, HEAD_WIDTH), HEAD_WIDTH),
                b * QB:(b + 1) * QB]
            for i in range(SHARE)
        ],
        axis=1,
    )


def wide_bias(bias_ref, b, n):
    one = bias_ref[b, 0:n, :]
    return jnp.concatenate([one] * SHARE, axis=1)


def attend_kernel(qkv_ref, segr_ref, segc_ref, *refs):
    o_ref, lse_ref, done_ref, bias_ref = refs[-4:]
    done_ref[...] = jnp.zeros_like(done_ref)
    length = qkv_ref.shape[1]
    make_bias(bias_ref, segr_ref.at[0], segc_ref.at[0], length)

    @pl.loop(0, KEY_VALUE_HEADS)
    def _(kv):
        k = qkv_ref[pl.ds(pl.multiple_of(D + kv * HEAD_WIDTH, HEAD_WIDTH), HEAD_WIDTH), :]
        v = qkv_ref[pl.ds(pl.multiple_of(D + KEYS + kv * HEAD_WIDTH, HEAD_WIDTH), HEAD_WIDTH), :]
        for b in range(length // QB):
            lo, hi = key_span(b)
            s = dot(k[:, lo:hi], three(qkv_ref, kv, b), 0, 0) + wide_bias(bias_ref, b, hi - lo)
            top = jnp.max(s, axis=0, keepdims=True)
            p = jnp.exp(s - top)
            total = jnp.sum(p, axis=0, keepdims=True)
            out = dot(v[:, lo:hi], p.astype(BF16), 1, 0) / total
            lse = top + jnp.log(total)
            for i in range(SHARE):
                rows = pl.ds(pl.multiple_of((kv * SHARE + i) * HEAD_WIDTH, HEAD_WIDTH), HEAD_WIDTH)
                o_ref[rows, b * QB:(b + 1) * QB] = out[:, i * QB:(i + 1) * QB].astype(BF16)
                lse_ref[kv, i:i + 1, b * QB:(b + 1) * QB] = lse[:, i * QB:(i + 1) * QB]


DONE = jax.ShapeDtypeStruct((8, GAINS), F32)


def attend(qkv, segments, at, before=()):
    seqs, length = segments.shape
    wide, rows = qkv.shape
    return pl.pallas_call(
        attend_kernel,
        grid=(1,),
        in_specs=[
            pl.BlockSpec((wide, length), lambda i: (0, at)),
            pl.BlockSpec((1, 1, length), lambda i: (at, 0, 0)),
            pl.BlockSpec((1, length, 1), lambda i: (at, 0, 0)),
        ] + [pl.BlockSpec(memory_space=pltpu.HBM)] * len(before),
        out_specs=[
            pl.BlockSpec((D, length), lambda i: (0, at)),
            pl.BlockSpec((KEY_VALUE_HEADS, 8, length), lambda i: (0, 0, at)),
            fixed(DONE.shape),
        ],
        out_shape=shaped(((D, rows), BF16), ((KEY_VALUE_HEADS, 8, rows), F32)) + [DONE],
        input_output_aliases={3 + i: i for i in range(len(before))},
        scratch_shapes=[pltpu.VMEM((length // QB, 3 * QB, QB), F32)],
        compiler_params=params(60),
        cost_estimate=cost(),
        name="attend",
    )(qkv, segments[:, None, :], segments[:, :, None], *before)


def middle_kernel(weight, where_ref, x_ref, o_ref, gain_ref, *refs):
    x1_ref, h_ref, w, sem = refs[4:]

    @pl.when(pl.program_id(0) == 0)
    def _():
        weight.load(where_ref, refs[:4], w, sem)
        wait_for(w, sem)

    x1 = x_ref[...].astype(F32) + dot(w[...], o_ref[...], 0, 0)
    normal, _ = norm_columns(x1)
    x1_ref[...] = x1
    h_ref[...] = (normal * gain_ref[:, 1:2].astype(F32)).astype(BF16)


def middle(where, x, o, w, gains):
    rows = x.shape[1]
    return pl.pallas_call(
        functools.partial(middle_kernel, w),
        grid=(rows // TILE,),
        in_specs=[SMEM, columns(D, TILE), columns(D, TILE), fixed((D, GAINS))] + w.specs(),
        out_specs=[columns(D, TILE), columns(D, TILE)],
        out_shape=shaped(((D, rows), F32), ((D, rows), BF16)),
        scratch_shapes=w.scratch(),
        compiler_params=params(60),
        cost_estimate=cost(2 * rows * D * D, rows * D * 10),
        name="middle",
    )(where, x, o, gains, *w.arrays)


def feed_forward_kernel(weights, where_ref, h_ref, dy_ref, x1_ref, *refs):
    count = len(weights[0].arrays)
    y_ref, dh_ref, hid_ref, dgate_ref, dup_ref, acc_ref, acc_sem, *scratch = refs[3 * count:]
    step = pl.program_id(0)

    @pl.when(step == 0)
    def _():
        for i, weight in enumerate(weights):
            weight.load(where_ref, refs[i * count:(i + 1) * count], *scratch[2 * i:2 * i + 2])
        pltpu.make_async_copy(x1_ref, acc_ref, acc_sem).start()
        dh_ref[...] = jnp.zeros_like(dh_ref)
        pltpu.make_async_copy(x1_ref, acc_ref, acc_sem).wait()

    wg_ref, wu_ref, wd_ref = (w.at[step] for w in scratch[::2])
    for w, sem in zip((wg_ref, wu_ref, wd_ref), scratch[1::2]):
        wait_for(w, sem.at[step])
    h, dy = h_ref[...], dy_ref[...]
    gate = dot(wg_ref[...], h, 0, 0)
    up = dot(wu_ref[...], h, 0, 0)
    dhid = dot(wd_ref[...], dy, 0, 0)
    sig = jax.nn.sigmoid(gate)
    silu = gate * sig
    hid = (silu * up).astype(BF16)
    dgate = (dhid * up * (sig + silu * (1.0 - sig))).astype(BF16)
    dup = (dhid * silu).astype(BF16)
    hid_ref[...] = hid
    dgate_ref[...] = dgate
    dup_ref[...] = dup
    acc_ref[...] += dot(wd_ref[...], hid, 1, 0)
    dh_ref[...] += dot(wg_ref[...], dgate, 1, 0) + dot(wu_ref[...], dup, 1, 0)

    @pl.when(step == pl.num_programs(0) - 1)
    def _():
        y_ref[...] = acc_ref[...].astype(BF16)


def feed_forward(where, h, dy, x1, weights):
    rows, hidden = h.shape[1], weights[0].shape[1]
    block = pl.BlockSpec((PAIR, rows), lambda f: (f, 0), pipeline_mode=pl.Buffered(1))
    return pl.pallas_call(
        functools.partial(feed_forward_kernel, weights),
        grid=(hidden // PAIR,),
        in_specs=[SMEM, fixed((D, rows)), fixed((D, rows)), pl.BlockSpec(memory_space=pltpu.HBM)]
        + sum((w.specs() for w in weights), []),
        out_specs=[fixed((D, rows)), fixed((D, rows))] + [block] * 3,
        out_shape=shaped(((D, rows), BF16), ((D, rows), F32)) + shaped(((hidden, rows), BF16)) * 3,
        scratch_shapes=sum(
            (w.scratch() for w in weights), [pltpu.VMEM((D, rows), F32), pltpu.SemaphoreType.DMA]
        ),
        compiler_params=params(63),
        cost_estimate=cost(),
        name="feed_forward",
    )(where, h, dy, x1, *sum((w.arrays for w in weights), []))


def block_here(where_ref):
    return 2 * where_ref[1] + where_ref[2]


def split_owners(grad, where_ref, put):
    core, x_here = where_ref[0] & 1, where_ref[0] >> 1
    for x in range(2):
        a = grad[2 * x * OWN:(2 * x + 1) * OWN].astype(BF16)
        b = grad[(2 * x + 1) * OWN:(2 * x + 2) * OWN].astype(BF16)
        put(x_here ^ x, jnp.where(core == 0, a, b), jnp.where(core == 0, b, a))


def row_grads_kernel(where_ref, a_ref, b_ref, keep_ref, send_ref):
    grad = dot(a_ref[...], b_ref[...], 1, 1)
    for i in range(2):
        def put(x, keep, send):
            keep_ref[x, i ^ where_ref[2]] = keep
            send_ref[x, i ^ where_ref[2]] = send

        split_owners(grad[:, i * CUT:(i + 1) * CUT], where_ref, put)


def column_grads_kernel(where_ref, a_ref, b_ref, keep_ref, send_ref):
    grad = dot(a_ref[...], b_ref[...], 1, 1).astype(BF16)
    first = (where_ref[0] & 1) == 0
    for i in range(4):
        at = block_here(where_ref) ^ i
        a, b = grad[i * OWN:(i + 1) * OWN, :CUT], grad[i * OWN:(i + 1) * OWN, CUT:]
        keep_ref[0, at] = jnp.where(first, a, b)
        send_ref[0, at] = jnp.where(first, b, a)


def ffn_grads(where, a, b, by_columns):
    rows = a.shape[1]
    if by_columns:
        kernel = column_grads_kernel
        out = pl.BlockSpec((1, 4, OWN, CUT), lambda f, at: (f ^ (at[0] >> 1), 0, 0, 0))
    else:
        kernel = row_grads_kernel
        out = pl.BlockSpec((2, 2, OWN, CUT), lambda f, at: (0, f ^ at[1], 0, 0))
    return pl.pallas_call(
        kernel,
        grid_spec=pltpu.PrefetchScalarGridSpec(
            num_scalar_prefetch=1,
            grid=(b.shape[0] // PAIR,),
            in_specs=[fixed((D, rows)), pl.BlockSpec((PAIR, rows), lambda f, at: (f, 0))],
            out_specs=[out, out],
        ),
        out_shape=shaped(((2, 4, OWN, CUT), BF16)) * 2,
        compiler_params=params(60),
        cost_estimate=cost(),
        name="ffn_grads",
    )(where, a, b)


def branch_kernel(weight, where_ref, dh_ref, x1_ref, dy_ref, gain_ref, *refs):
    dx_ref, da_ref, do_ref, gain_grad, w, sem = refs[4:]
    first = pl.program_id(0) == 0

    @pl.when(first)
    def _():
        weight.load(where_ref, refs[:4], w, sem)

    gain = gain_ref[:, 1:2].astype(F32)
    normal, inverse = norm_columns(x1_ref[...])
    back, part = norm_columns_back(dh_ref[...], normal, inverse, gain)
    dx = dy_ref[...].astype(F32) + back
    da = dx.astype(BF16)
    dx_ref[...] = dx
    da_ref[...] = da

    @pl.when(first)
    def _():
        gain_grad[...] = part
        wait_for(w, sem)

    @pl.when(jnp.logical_not(first))
    def _():
        gain_grad[...] += part

    do_ref[...] = dot(w[...], da, 1, 0).astype(BF16)


def branch(where, dh, x1, dy, gains, w):
    rows = dh.shape[1]
    return pl.pallas_call(
        functools.partial(branch_kernel, w),
        grid=(rows // TILE,),
        in_specs=[SMEM] + [columns(D, TILE)] * 3 + [fixed((D, GAINS))] + w.specs(),
        out_specs=[columns(D, TILE)] * 3 + [pl.BlockSpec((D, 1), lambda i: (0, 0))],
        out_shape=shaped(((D, rows), F32), ((D, rows), BF16), ((D, rows), BF16), ((D, 1), F32)),
        scratch_shapes=w.scratch(),
        compiler_params=params(60),
        cost_estimate=cost(2 * rows * D * D, rows * D * 18),
        name="branch",
    )(where, dh, x1, dy, gains, *w.arrays)


def attend_back_kernel(qkv_ref, o_ref, do_ref, lse_ref, segr_ref, segc_ref, cos_ref, sin_ref,
                       *refs):
    out_ref, done_ref, bias_ref, dk_ref, dv_ref = refs[-5:]
    done_ref[...] = jnp.zeros_like(done_ref)
    length = qkv_ref.shape[1]
    make_bias(bias_ref, segr_ref.at[0], segc_ref.at[0], length)

    def turn_back(g, c, s, at, cols):
        a, b = g[:HALF], g[HALF:]
        at = pl.multiple_of(at, HEAD_WIDTH)
        out_ref[pl.ds(at, HALF), cols] = (a * c + b * s).astype(BF16)
        out_ref[pl.ds(pl.multiple_of(at + HALF, HALF), HALF), cols] = (b * c - a * s).astype(BF16)

    @pl.loop(0, KEY_VALUE_HEADS)
    def _(kv):
        k = qkv_ref[pl.ds(pl.multiple_of(D + kv * HEAD_WIDTH, HEAD_WIDTH), HEAD_WIDTH), :]
        v = qkv_ref[pl.ds(pl.multiple_of(D + KEYS + kv * HEAD_WIDTH, HEAD_WIDTH), HEAD_WIDTH), :]
        dk_ref[...] = jnp.zeros_like(dk_ref)
        dv_ref[...] = jnp.zeros_like(dv_ref)
        for b in range(length // QB):
            lo, hi = key_span(b)
            cols = slice(b * QB, (b + 1) * QB)
            q, o, do = three(qkv_ref, kv, b), three(o_ref, kv, b), three(do_ref, kv, b)
            lse = jnp.concatenate([lse_ref[kv, i:i + 1, cols] for i in range(SHARE)], axis=1)
            inner = jnp.sum(o.astype(F32) * do.astype(F32), axis=0, keepdims=True)
            s = dot(k[:, lo:hi], q, 0, 0) + wide_bias(bias_ref, b, hi - lo)
            p = jnp.exp(s - lse)
            dp = dot(v[:, lo:hi], do, 0, 0)
            ds = (p * (dp - inner)).astype(BF16)
            dv_ref[:, lo:hi] += dot(do, p.astype(BF16), 1, 1)
            dk_ref[:, lo:hi] += dot(q, ds, 1, 1)
            dq = dot(k[:, lo:hi], ds, 1, 0) * HEAD_WIDTH ** -0.5
            for i in range(SHARE):
                turn_back(dq[:, i * QB:(i + 1) * QB], cos_ref[:, cols], sin_ref[:, cols],
                          (kv * SHARE + i) * HEAD_WIDTH, cols)
        turn_back(dk_ref[...], cos_ref[...], sin_ref[...], D + kv * HEAD_WIDTH, slice(None))
        out_ref[pl.ds(pl.multiple_of(D + KEYS + kv * HEAD_WIDTH, HEAD_WIDTH), HEAD_WIDTH), :] = (
            dv_ref[...].astype(BF16))


def attend_back(qkv, o, do, lse, segments, cos, sin, at, before=()):
    length = segments.shape[1]
    wide, rows = qkv.shape
    here = lambda height: pl.BlockSpec((height, length), lambda i: (0, at))
    return pl.pallas_call(
        attend_back_kernel,
        grid=(1,),
        in_specs=[
            here(wide),
            here(D),
            here(D),
            pl.BlockSpec((KEY_VALUE_HEADS, 8, length), lambda i: (0, 0, at)),
            pl.BlockSpec((1, 1, length), lambda i: (at, 0, 0)),
            pl.BlockSpec((1, length, 1), lambda i: (at, 0, 0)),
            here(HALF),
            here(HALF),
        ] + [pl.BlockSpec(memory_space=pltpu.HBM)] * len(before),
        out_specs=[here(wide), fixed(DONE.shape)],
        out_shape=shaped(((wide, rows), BF16)) + [DONE],
        input_output_aliases={8 + i: i for i in range(len(before))},
        scratch_shapes=[
            pltpu.VMEM((length // QB, 3 * QB, QB), F32),
            pltpu.VMEM((HEAD_WIDTH, length), F32),
            pltpu.VMEM((HEAD_WIDTH, length), F32),
        ],
        compiler_params=params(60),
        cost_estimate=cost(),
        name="attend_back",
    )(qkv, o, do, lse, segments[:, None, :], segments[:, :, None], cos, sin, *before)


PIECES = ((0, 128), (128, OWN))


def weight_kernel(where_ref, h_ref, dqkv_ref, o_ref, da_ref, *out_refs):
    def store(block, grad):
        def put(x, keep, send):
            for i, (low, high) in enumerate(PIECES):
                at = block ^ block_here(where_ref)
                out_refs[2 * i][x, at] = keep[low:high]
                out_refs[2 * i + 1][x, at] = send[low:high]

        split_owners(grad, where_ref, put)

    grad = dot(h_ref[...], dqkv_ref[:PAIR, :], 1, 1)
    store(0, grad[:, :CUT])
    store(1, grad[:, CUT:])
    left = dot(h_ref[...], dqkv_ref[2 * CUT:, :], 1, 1)
    right = dot(o_ref[...], da_ref[:3 * CUT - WIDE, :], 1, 1)
    store(2, jnp.concatenate([left, right], axis=1))
    store(3, dot(o_ref[...], da_ref[3 * CUT - WIDE:, :], 1, 1))


def weight_grads(where, h, dqkv, o, da):
    rows = h.shape[1]
    shapes = [(2, 4, high - low, CUT) for low, high in PIECES for _ in range(2)]
    return pl.pallas_call(
        weight_kernel,
        grid=(1,),
        in_specs=[SMEM, fixed((D, rows)), fixed((WIDE, rows)), fixed((D, rows)), fixed((D, rows))],
        out_specs=[fixed(shape) for shape in shapes],
        out_shape=shaped(*((shape, BF16) for shape in shapes)),
        compiler_params=params(60),
        cost_estimate=cost(),
        name="weight_grads",
    )(where, h, dqkv, o, da)


def inputs_kernel(weights, where_ref, x_ref, dx_ref, dqkv_ref, *refs):
    out_ref, gain_grad, wq, q_sem, wk, k_sem = refs[8:]
    first = pl.program_id(0) == 0

    @pl.when(first)
    def _():
        weights[0].load(where_ref, refs[:4], wq, q_sem)
        weights[1].load(where_ref, refs[4:8], wk, k_sem)
        wait_for(wq, q_sem)
        wait_for(wk, k_sem)

    gain = wk[:, 2 * KEYS:2 * KEYS + 1].astype(F32)
    dh = dot(wq[...], dqkv_ref[:D], 1, 0) + dot(wk[:, :2 * KEYS], dqkv_ref[D:], 1, 0)
    normal, inverse = norm_columns(x_ref[...].astype(F32))
    back, part = norm_columns_back(dh, normal, inverse, gain)
    out_ref[...] = (dx_ref[...] + back).astype(BF16)

    @pl.when(first)
    def _():
        gain_grad[...] = part

    @pl.when(jnp.logical_not(first))
    def _():
        gain_grad[...] += part


def input_grads(where, x, dx, wq, wk, dqkv):
    rows = x.shape[1]
    return pl.pallas_call(
        functools.partial(inputs_kernel, (wq, wk)),
        grid=(rows // TILE,),
        in_specs=[SMEM, columns(D, TILE), columns(D, TILE), columns(WIDE, TILE)]
        + wq.specs() + wk.specs(),
        out_specs=[columns(D, TILE), pl.BlockSpec((D, 1), lambda i: (0, 0))],
        out_shape=shaped(((D, rows), BF16), ((D, 1), F32)),
        scratch_shapes=wq.scratch() + wk.scratch(),
        compiler_params=params(60),
        cost_estimate=cost(2 * rows * D * WIDE, rows * (D * 8 + WIDE * 2) + D * WIDE * 2),
        name="input_grads",
    )(where, x, dx, dqkv, *wq.arrays, *wk.arrays)


def tables(segments):
    length = segments.shape[1]
    index = jnp.arange(length, dtype=jnp.int32)
    same = segments[:, :, None] == segments[:, None, :]
    start = jnp.min(jnp.where(same, index[None, :, None], length), axis=1)
    position = (index[None, :] - start).astype(F32).reshape(1, -1)
    freq = THETA ** (-(jnp.arange(HALF, dtype=F32) * 2.0 / HEAD_WIDTH))
    angle = freq[:, None] * position
    return jnp.cos(angle), jnp.sin(angle)


def after(value, *others):
    return lax.optimization_barrier((value,) + others)[0]


class Cube:
    def __init__(self, count):
        self.count = count
        self.dims = count.bit_length() - 1
        replica, group = lax.axis_index("replica"), lax.axis_index("group")
        self.coordinate = {i: (replica >> i) & 1 for i in range(self.dims)}
        self.coordinate["x"] = group >> 1
        self.coordinate["core"] = group & 1
        self.me = group

    def swap(self, value, dim):
        if dim == "x":
            return lax.ppermute(value, "group", [(i, i ^ 2) for i in range(4)])
        if dim == "core":
            return lax.ppermute(value, "group", [(i, i ^ 1) for i in range(4)])
        return lax.ppermute(value, "replica", [(i, i ^ (1 << dim)) for i in range(self.count)])

    def ordered(self, dim, mine, other, axis):
        return jnp.where(
            self.coordinate[dim] == 0,
            jnp.concatenate([mine, other], axis=axis),
            jnp.concatenate([other, mine], axis=axis),
        )


def rows_of(own, sibling, across, diagonal):
    pieces = own, sibling, across, diagonal
    return Weight(0, [(array, flip, None) for flip, array in enumerate(pieces)])


class Relay:
    def __init__(self, cube, shard, axis, first, second):
        self.cube, self.shard, self.axis, self.dims = cube, shard, axis, (first, second)
        self.cut = 1 - axis
        self.size = shard.shape[self.cut] // 4
        at = 2 * cube.coordinate[second] + cube.coordinate[first]
        self.quarter = lax.dynamic_slice_in_dim(shard, at * self.size, self.size, self.cut)

    def cross(self, *others):
        self.direct = self.cube.swap(after(self.quarter, *others), "x")
        return self.direct

    def hand_on(self, *others):
        self.handed = self.cube.swap(after(self.direct, *others), self.dims[0])
        return self.handed

    def finish(self, *others):
        cube = self.cube
        handed = after(self.handed, *others)
        self.half = cube.ordered(self.dims[0], self.direct, handed, self.cut)
        self.rest = cube.swap(self.half, self.dims[1])
        self.half_diagonal = cube.swap(self.half, "core")
        return self.rest

    def weight(self, sibling, *others):
        rest = after(self.rest, *others)
        pieces = [
            (self.shard, 0, None), (sibling, 1, None), (self.half, 2, 0), (rest, 2, 1),
            (self.half_diagonal, 3, 0), (self.cube.swap(rest, "core"), 3, 1),
        ]
        return Weight(self.axis, pieces, self.dims[1], 2)


class Reduce:
    def __init__(self, cube, keep, got, halves, gathers):
        rows, wide = keep.shape[2:]
        self.cube, self.shape = cube, (4, rows, wide)
        self.order = halves + tuple(range(2, cube.dims)) + gathers
        self.place = {"x": 0, 0: 1, 1: 2}
        self.terms = [t.reshape(2, 2, 2, rows, wide) for t in (keep, got)]
        self.index = 0
        self.done = False

    def sum(self, terms):
        if len(terms) == 1:
            return terms[0]
        return functools.reduce(jnp.add, [t.astype(F32) for t in terms]).astype(BF16)

    def ready(self, *others):
        dim = self.order[self.index]
        self.terms[-1] = after(self.terms[-1], *others)
        if self.index < 3:
            axis = self.place[dim]
            take = lambda i: [lax.slice_in_dim(t, i, i + 1, axis=axis) for t in self.terms]
            self.send, self.terms = self.sum(take(1)), take(0)
        else:
            self.send = self.sum(self.terms)
        return self.send

    def swap(self):
        dim = self.order[self.index]
        got = self.cube.swap(self.send, dim)
        self.index += 1
        if self.index <= 3:
            self.terms = self.terms + [got]
        elif self.index <= len(self.order) - 2:
            self.terms = [self.send, got]
        elif self.index < len(self.order):
            self.terms = [self.cube.ordered(dim, self.send, got, self.place[dim])]
        else:
            self.terms = [self.send, got]

    def finish(self, *others):
        self.done = True
        low, got = (after(value, *others) for value in self.terms)
        self.result = self.cube.ordered(self.order[-1], low, got, self.place[self.order[-1]])
        self.result = self.result.reshape(self.shape)
        return self.result


def per_device(
    tokens,
    segments,
    query_weight,
    key_weight,
    value_weight,
    output_weight,
    w_gate,
    w_up,
    w_down,
    attn_gain,
    ffn_gain,
    cotangent,
    replicas,
):
    cube = Cube(replicas)
    where = jnp.stack([cube.me] + [cube.coordinate[i] for i in range(3)]).astype(jnp.int32)
    x, dy = tokens.T, cotangent.T

    core = lambda value: cube.swap(value, "core")
    q_across = cube.swap(query_weight, "x")
    pad = jnp.zeros((OWN, GAINS - 2), BF16)
    kv = jnp.concatenate(
        [key_weight, value_weight, attn_gain[:, None], ffn_gain[:, None], pad], axis=1
    )
    kv_across = cube.swap(after(kv, q_across), "x")
    relays = [
        Relay(cube, w_gate, 0, 0, 1), Relay(cube, w_up, 0, 1, 0), Relay(cube, w_down.T, 1, 0, 1)
    ]
    q_sibling, kv_sibling, wo_sibling = core(query_weight), core(kv), core(output_weight)
    siblings = [core(relay.shard) for relay in relays]
    cos, sin = tables(segments)
    early = [relay.quarter for relay in relays] + [cos, sin, q_sibling, kv_sibling, wo_sibling]
    q_across, kv_across = lax.optimization_barrier((q_across, kv_across, *early, *siblings))[:2]
    q_diagonal, kv_diagonal = core(q_across), core(kv_across)
    direct = [relay.cross(q_across, kv_across) for relay in relays]
    wq = rows_of(query_weight, q_sibling, q_across, q_diagonal)
    wk = rows_of(kv, kv_sibling, kv_across, kv_diagonal)
    qkv, h, gains = project(where, x, wq, wk, cos, sin)
    *first, done0 = attend(qkv, segments, 0)
    handed = [relay.hand_on(done0) for relay in relays]
    wo_across = cube.swap(after(output_weight, done0, *direct), "x")
    o, lse, done1 = attend(after(qkv, done0, *direct), segments, 1, first)
    rest = [relay.finish(done1) for relay in relays]
    wo_diagonal = core(after(wo_across, done1))
    wo = rows_of(output_weight, wo_sibling, wo_across, wo_diagonal)
    x1, h2 = middle(where, x, after(o, *[relay.half for relay in relays]), wo, gains)
    weights = [relay.weight(sibling, h2) for relay, sibling in zip(relays, siblings)]
    y, dh2, hid, dgate, dup = feed_forward(where, h2, dy, x1, weights)

    gd_keep, gd_send = ffn_grads(where, dy, hid, True)
    gd = Reduce(cube, gd_keep, core(gd_send), ("x", 0, 1), (1, 0))
    gg_keep, gg_send = ffn_grads(where, h2, after(dgate, gd_send), False)
    gg = Reduce(cube, gg_keep, core(gg_send), (0, "x", 1), (0, 1))
    gd.ready(gg_send)
    gu_keep, gu_send = ffn_grads(where, h2, after(dup, gd.send), False)
    gd.swap()
    gu = Reduce(cube, gu_keep, core(gu_send), (1, 0, "x"), (1, 0))
    gg.ready(gu_send)
    dx1, da, do, ffn_gain_grad = branch(where, after(dh2, gg.send), x1, dy, gains, wo)
    gg.swap()
    gu.ready(da)
    do0 = after(do, gu.send)
    gu.swap()
    *first, done0 = attend_back(qkv, o, do0, lse, segments, cos, sin, 0)
    do1 = after(do, done0, *[piece.ready(done0) for piece in (gd, gg)])
    gd.swap()
    gg.swap()
    dqkv, done1 = attend_back(qkv, o, do1, lse, segments, cos, sin, 1, first)
    swaps = [gd, gg, gu]
    dqkv = after(dqkv, *[piece.ready(done1) for piece in swaps])
    for piece in swaps:
        piece.swap()
    parts = []
    weight_parts = weight_grads(where, h, dqkv, o, da)
    for i, halves in enumerate((("x", 0, 1), (0, "x", 1))):
        keep, send = weight_parts[2 * i:2 * i + 2]
        parts.append(Reduce(cube, keep, core(send), halves, (1 - i, i)))
    dqkv = after(dqkv, *[part.ready(weight_parts[0]) for part in parts])
    for part in parts:
        part.swap()
    grad_x, attn_gain_grad = input_grads(where, x, dx1, wq, wk, dqkv)
    swaps = [gd, gg, gu] + parts
    both = jnp.concatenate([attn_gain_grad, ffn_gain_grad], axis=1).T.reshape(-1)
    ends = ["core", "x"] + list(range(cube.dims))
    token = grad_x
    while any(piece.index < len(piece.order) for piece in swaps):
        active = [piece for piece in swaps if piece.index < len(piece.order)]
        for piece in active:
            token = piece.ready(token, both)
            piece.swap()
        for piece in swaps:
            if piece not in active and not piece.done:
                token = piece.finish(token)
        if ends:
            both = both + after(cube.swap(both, ends.pop(0)), token)
    for piece in swaps:
        if not piece.done:
            token = piece.finish(token)
    for dim in ends:
        both = both + cube.swap(both, dim)
    both = lax.dynamic_slice_in_dim(both.reshape(2, D), cube.me * OWN, OWN, 1)
    flat = lambda g: jnp.concatenate([g[i] for i in range(4)], axis=1)
    ga = jnp.concatenate([flat(part.result) for part in parts], axis=0).astype(F32)
    return (
        y.T,
        grad_x.T,
        ga[:, :D],
        ga[:, D:D + KEYS],
        ga[:, D + KEYS:WIDE],
        ga[:, WIDE:],
        flat(gg.result).astype(F32),
        flat(gu.result).astype(F32),
        gd.result.reshape(D, CUT).T.astype(F32),
        both[0],
        both[1],
    )


def solution(mesh):
    rows = P(("group", "replica"), None)
    weight, gain = P("group", None), P("group")
    replicas = mesh.shape["replica"]
    return jax.shard_map(
        lambda *args: per_device(*args, replicas),
        mesh=mesh,
        in_specs=(rows, rows) + (weight,) * 7 + (gain, gain, rows),
        out_specs=(rows, rows) + (weight,) * 7 + (gain, gain),
        check_vma=False,
    )
```

```python
import functools

import jax
import jax.numpy as jnp
from jax import lax
from jax.experimental import pallas as pl
from jax.experimental.pallas import tpu as pltpu
from jax.sharding import PartitionSpec as P

D = 960
QUERY_HEADS = 15
KEY_VALUE_HEADS = 5
HEAD_WIDTH = 64
SHARE = QUERY_HEADS // KEY_VALUE_HEADS
HALF = HEAD_WIDTH // 2
KEYS = KEY_VALUE_HEADS * HEAD_WIDTH
EPS = 1e-05
THETA = 100000.0
TILE = 512
HALF_TILE = 256
QB = 128
GAINS = 128
WIDE = D + 2 * KEYS
CUT = 640
OWN = 240
PAIR = 2 * CUT
F32 = jnp.float32
BF16 = jnp.bfloat16
MIB = 1 << 20


def dot(a, b, ca, cb):
    return lax.dot_general(a, b, (((ca,), (cb,)), ((), ())), preferred_element_type=F32)


def params(limit, grid=1):
    return pltpu.CompilerParams(
        vmem_limit_bytes=limit * MIB, dimension_semantics=("arbitrary",) * grid
    )


def cost(*_):
    return pl.CostEstimate(flops=1, bytes_accessed=1, transcendentals=0)


def shaped(*shape_type):
    return [jax.ShapeDtypeStruct(s, t) for s, t in shape_type]


def norm_columns(v):
    inverse = lax.rsqrt(jnp.mean(v * v, axis=0, keepdims=True) + EPS)
    return v * inverse, inverse


def norm_columns_back(grad, normal, inverse, gain):
    scaled = grad * gain
    back = inverse * (scaled - normal * jnp.mean(scaled * normal, axis=0, keepdims=True))
    return back, jnp.sum(grad * normal, axis=1, keepdims=True)


def fixed(shape):
    return pl.BlockSpec(shape, lambda *_: (0,) * len(shape), pipeline_mode=pl.Buffered(1))


def columns(height, width):
    return pl.BlockSpec((height, width), lambda i: (0, i))


class Weight:
    def __init__(self, axis, pieces, dim=None, blocks=0):
        self.axis, self.dim, self.blocks = axis, dim, blocks
        self.arrays = [array for array, _, _ in pieces]
        self.places = [(flip, side) for _, flip, side in pieces]
        shape = list(self.arrays[0].shape)
        self.size = shape[axis]
        self.half = shape[1 - axis] // 2
        shape[axis] *= 4
        self.shape = tuple(shape)

    def specs(self):
        return [pl.BlockSpec(memory_space=pltpu.HBM)] * len(self.arrays)

    def scratch(self):
        if not self.blocks:
            return [pltpu.VMEM(self.shape, BF16), pltpu.SemaphoreType.DMA]
        block = (self.shape[0], self.shape[1] // self.blocks)
        return [pltpu.VMEM((self.blocks,) + block, BF16), pltpu.SemaphoreType.DMA((self.blocks,))]

    def load(self, where_ref, refs, scratch, sem):
        wide = self.shape[1] // max(self.blocks, 1)
        for ref, (flip, side) in zip(refs, self.places):
            at = (where_ref[0] ^ flip) * self.size
            other = 0 if side is None else (where_ref[1 + self.dim] ^ side) * self.half
            row, column = (at, other) if self.axis == 0 else (other, at)
            rows = pl.ds(pl.multiple_of(row, OWN), ref.shape[0])
            if not self.blocks:
                pltpu.make_async_copy(ref, scratch.at[rows, :], sem).start()
                continue
            first = column // wide
            for i in range(ref.shape[1] // wide):
                pltpu.make_async_copy(
                    ref.at[:, i * wide:(i + 1) * wide], scratch.at[first + i, rows, :],
                    sem.at[first + i],
                ).start()


def wait_for(scratch, sem):
    pltpu.make_async_copy(scratch, scratch, sem).wait()


SMEM = pl.BlockSpec(memory_space=pltpu.SMEM)


def project_kernel(weights, where_ref, x_ref, cos_ref, sin_ref, *refs):
    qkv_ref, h_ref, gains_ref, wq, q_sem, wk, k_sem = refs[8:]

    @pl.when(pl.program_id(0) == 0)
    def _():
        weights[0].load(where_ref, refs[:4], wq, q_sem)
        weights[1].load(where_ref, refs[4:8], wk, k_sem)
        wait_for(wq, q_sem)
        wait_for(wk, k_sem)
        gains_ref[...] = wk[:, 2 * KEYS:]

    gain = wk[:, 2 * KEYS:2 * KEYS + 1].astype(F32)
    normal, _ = norm_columns(x_ref[...].astype(F32))
    h = (normal * gain).astype(BF16)
    h_ref[...] = h
    c, s = cos_ref[...], sin_ref[...]

    def rotary(out, at, heads, scale):
        for head in range(heads):
            low = head * HEAD_WIDTH
            a, b = out[low:low + HALF], out[low + HALF:low + HEAD_WIDTH]
            to = at + low
            qkv_ref[to:to + HALF, :] = ((a * c - b * s) * scale).astype(BF16)
            qkv_ref[to + HALF:to + HEAD_WIDTH, :] = ((b * c + a * s) * scale).astype(BF16)

    rotary(dot(wq[...], h, 0, 0), 0, QUERY_HEADS, HEAD_WIDTH ** -0.5)
    out = dot(wk[:, :2 * KEYS], h, 0, 0)
    rotary(out, D, KEY_VALUE_HEADS, 1.0)
    qkv_ref[D + KEYS:, :] = out[KEYS:].astype(BF16)


def project(where, x, wq, wk, cos, sin):
    rows = x.shape[1]
    return pl.pallas_call(
        functools.partial(project_kernel, (wq, wk)),
        grid=(rows // TILE,),
        in_specs=[SMEM, columns(D, TILE), columns(HALF, TILE), columns(HALF, TILE)]
        + wq.specs() + wk.specs(),
        out_specs=[columns(WIDE, TILE), columns(D, TILE),
                   pl.BlockSpec((D, GAINS), lambda i: (0, 0))],
        out_shape=shaped(((WIDE, rows), BF16), ((D, rows), BF16), ((D, GAINS), BF16)),
        scratch_shapes=wq.scratch() + wk.scratch(),
        compiler_params=params(60),
        cost_estimate=cost(2 * rows * D * WIDE, rows * (2 * D + WIDE) * 2 + D * WIDE * 2),
        name="project",
    )(where, x, cos, sin, *wq.arrays, *wk.arrays)


def key_span(block):
    return max(0, QB * (block - 2)), QB * (block + 1)


def make_bias(bias_ref, segr_ref, segc_ref, length):
    for b in range(length // QB):
        lo, hi = key_span(b)
        key_at = lax.broadcasted_iota(jnp.int32, (hi - lo, QB), 0) + lo
        query_at = lax.broadcasted_iota(jnp.int32, (hi - lo, QB), 1) + b * QB
        ok = (segc_ref[lo:hi, :] == segr_ref[:, b * QB:(b + 1) * QB]) & (key_at <= query_at)
        bias_ref[b, 0:hi - lo, :] = jnp.where(ok, 0.0, -1e30)


def three(ref, kv, b):
    return jnp.concatenate(
        [
            ref[pl.ds(pl.multiple_of((kv * SHARE + i) * HEAD_WIDTH, HEAD_WIDTH), HEAD_WIDTH),
                b * QB:(b + 1) * QB]
            for i in range(SHARE)
        ],
        axis=1,
    )


def wide_bias(bias_ref, b, n):
    one = bias_ref[b, 0:n, :]
    return jnp.concatenate([one] * SHARE, axis=1)


def attend_kernel(qkv_ref, segr_ref, segc_ref, *refs):
    o_ref, lse_ref, done_ref, bias_ref = refs[-4:]
    done_ref[...] = jnp.zeros_like(done_ref)
    length = qkv_ref.shape[1]
    make_bias(bias_ref, segr_ref.at[0], segc_ref.at[0], length)

    @pl.loop(0, KEY_VALUE_HEADS)
    def _(kv):
        k = qkv_ref[pl.ds(pl.multiple_of(D + kv * HEAD_WIDTH, HEAD_WIDTH), HEAD_WIDTH), :]
        v = qkv_ref[pl.ds(pl.multiple_of(D + KEYS + kv * HEAD_WIDTH, HEAD_WIDTH), HEAD_WIDTH), :]
        for b in range(length // QB):
            lo, hi = key_span(b)
            s = dot(k[:, lo:hi], three(qkv_ref, kv, b), 0, 0) + wide_bias(bias_ref, b, hi - lo)
            top = jnp.max(s, axis=0, keepdims=True)
            p = jnp.exp(s - top)
            total = jnp.sum(p, axis=0, keepdims=True)
            out = dot(v[:, lo:hi], p.astype(BF16), 1, 0) / total
            lse = top + jnp.log(total)
            for i in range(SHARE):
                rows = pl.ds(pl.multiple_of((kv * SHARE + i) * HEAD_WIDTH, HEAD_WIDTH), HEAD_WIDTH)
                o_ref[rows, b * QB:(b + 1) * QB] = out[:, i * QB:(i + 1) * QB].astype(BF16)
                lse_ref[kv, i:i + 1, b * QB:(b + 1) * QB] = lse[:, i * QB:(i + 1) * QB]


DONE = jax.ShapeDtypeStruct((8, GAINS), F32)


def attend(qkv, segments, at, before=()):
    seqs, length = segments.shape
    wide, rows = qkv.shape
    return pl.pallas_call(
        attend_kernel,
        grid=(1,),
        in_specs=[
            pl.BlockSpec((wide, length), lambda i: (0, at)),
            pl.BlockSpec((1, 1, length), lambda i: (at, 0, 0)),
            pl.BlockSpec((1, length, 1), lambda i: (at, 0, 0)),
        ] + [pl.BlockSpec(memory_space=pltpu.HBM)] * len(before),
        out_specs=[
            pl.BlockSpec((D, length), lambda i: (0, at)),
            pl.BlockSpec((KEY_VALUE_HEADS, 8, length), lambda i: (0, 0, at)),
            fixed(DONE.shape),
        ],
        out_shape=shaped(((D, rows), BF16), ((KEY_VALUE_HEADS, 8, rows), F32)) + [DONE],
        input_output_aliases={3 + i: i for i in range(len(before))},
        scratch_shapes=[pltpu.VMEM((length // QB, 3 * QB, QB), F32)],
        compiler_params=params(60),
        cost_estimate=cost(),
        name="attend",
    )(qkv, segments[:, None, :], segments[:, :, None], *before)


def middle_kernel(weight, where_ref, x_ref, o_ref, gain_ref, *refs):
    x1_ref, h_ref, w, sem = refs[4:]

    @pl.when(pl.program_id(0) == 0)
    def _():
        weight.load(where_ref, refs[:4], w, sem)
        wait_for(w, sem)

    x1 = x_ref[...].astype(F32) + dot(w[...], o_ref[...], 0, 0)
    normal, _ = norm_columns(x1)
    x1_ref[...] = x1
    h_ref[...] = (normal * gain_ref[:, 1:2].astype(F32)).astype(BF16)


def middle(where, x, o, w, gains):
    rows = x.shape[1]
    return pl.pallas_call(
        functools.partial(middle_kernel, w),
        grid=(rows // TILE,),
        in_specs=[SMEM, columns(D, TILE), columns(D, TILE), fixed((D, GAINS))] + w.specs(),
        out_specs=[columns(D, TILE), columns(D, TILE)],
        out_shape=shaped(((D, rows), F32), ((D, rows), BF16)),
        scratch_shapes=w.scratch(),
        compiler_params=params(60),
        cost_estimate=cost(2 * rows * D * D, rows * D * 10),
        name="middle",
    )(where, x, o, gains, *w.arrays)


def feed_forward_kernel(weights, where_ref, h_ref, dy_ref, x1_ref, *refs):
    count = len(weights[0].arrays)
    y_ref, dh_ref, hid_ref, dgate_ref, dup_ref, acc_ref, acc_sem, *scratch = refs[3 * count:]
    step = pl.program_id(0)

    @pl.when(step == 0)
    def _():
        for i, weight in enumerate(weights):
            weight.load(where_ref, refs[i * count:(i + 1) * count], *scratch[2 * i:2 * i + 2])
        pltpu.make_async_copy(x1_ref, acc_ref, acc_sem).start()
        dh_ref[...] = jnp.zeros_like(dh_ref)
        pltpu.make_async_copy(x1_ref, acc_ref, acc_sem).wait()

    wg_ref, wu_ref, wd_ref = (w.at[step] for w in scratch[::2])
    for w, sem in zip((wg_ref, wu_ref, wd_ref), scratch[1::2]):
        wait_for(w, sem.at[step])
    h, dy = h_ref[...], dy_ref[...]
    gate = dot(wg_ref[...], h, 0, 0)
    up = dot(wu_ref[...], h, 0, 0)
    dhid = dot(wd_ref[...], dy, 0, 0)
    sig = jax.nn.sigmoid(gate)
    silu = gate * sig
    hid = (silu * up).astype(BF16)
    dgate = (dhid * up * (sig + silu * (1.0 - sig))).astype(BF16)
    dup = (dhid * silu).astype(BF16)
    hid_ref[...] = hid
    dgate_ref[...] = dgate
    dup_ref[...] = dup
    acc_ref[...] += dot(wd_ref[...], hid, 1, 0)
    dh_ref[...] += dot(wg_ref[...], dgate, 1, 0) + dot(wu_ref[...], dup, 1, 0)

    @pl.when(step == pl.num_programs(0) - 1)
    def _():
        y_ref[...] = acc_ref[...].astype(BF16)


def feed_forward(where, h, dy, x1, weights):
    rows, hidden = h.shape[1], weights[0].shape[1]
    block = pl.BlockSpec((CUT, rows), lambda f: (f, 0))
    return pl.pallas_call(
        functools.partial(feed_forward_kernel, weights),
        grid=(hidden // CUT,),
        in_specs=[SMEM, fixed((D, rows)), fixed((D, rows)), pl.BlockSpec(memory_space=pltpu.HBM)]
        + sum((w.specs() for w in weights), []),
        out_specs=[fixed((D, rows)), fixed((D, rows))] + [block] * 3,
        out_shape=shaped(((D, rows), BF16), ((D, rows), F32)) + shaped(((hidden, rows), BF16)) * 3,
        scratch_shapes=sum(
            (w.scratch() for w in weights), [pltpu.VMEM((D, rows), F32), pltpu.SemaphoreType.DMA]
        ),
        compiler_params=params(60),
        cost_estimate=cost(),
        name="feed_forward",
    )(where, h, dy, x1, *sum((w.arrays for w in weights), []))


def block_here(where_ref):
    return 2 * where_ref[1] + where_ref[2]


def split_owners(grad, where_ref, put):
    core, x_here = where_ref[0] & 1, where_ref[0] >> 1
    for x in range(2):
        a = grad[2 * x * OWN:(2 * x + 1) * OWN].astype(BF16)
        b = grad[(2 * x + 1) * OWN:(2 * x + 2) * OWN].astype(BF16)
        put(x_here ^ x, jnp.where(core == 0, a, b), jnp.where(core == 0, b, a))


def row_grads_kernel(where_ref, a_ref, b_ref, keep_ref, send_ref):
    grad = dot(a_ref[...], b_ref[...], 1, 1)
    for i in range(2):
        def put(x, keep, send):
            keep_ref[x, i ^ where_ref[2]] = keep
            send_ref[x, i ^ where_ref[2]] = send

        split_owners(grad[:, i * CUT:(i + 1) * CUT], where_ref, put)


def column_grads_kernel(where_ref, a_ref, b_ref, keep_ref, send_ref):
    grad = dot(a_ref[...], b_ref[...], 1, 1).astype(BF16)
    first = (where_ref[0] & 1) == 0
    for i in range(4):
        at = block_here(where_ref) ^ i
        a, b = grad[i * OWN:(i + 1) * OWN, :CUT], grad[i * OWN:(i + 1) * OWN, CUT:]
        keep_ref[0, at] = jnp.where(first, a, b)
        send_ref[0, at] = jnp.where(first, b, a)


def ffn_grads(where, a, b, by_columns):
    rows = a.shape[1]
    if by_columns:
        kernel = column_grads_kernel
        out = pl.BlockSpec((1, 4, OWN, CUT), lambda f, at: (f ^ (at[0] >> 1), 0, 0, 0))
    else:
        kernel = row_grads_kernel
        out = pl.BlockSpec((2, 2, OWN, CUT), lambda f, at: (0, f ^ at[1], 0, 0))
    return pl.pallas_call(
        kernel,
        grid_spec=pltpu.PrefetchScalarGridSpec(
            num_scalar_prefetch=1,
            grid=(b.shape[0] // PAIR,),
            in_specs=[fixed((D, rows)), pl.BlockSpec((PAIR, rows), lambda f, at: (f, 0))],
            out_specs=[out, out],
        ),
        out_shape=shaped(((2, 4, OWN, CUT), BF16)) * 2,
        compiler_params=params(60),
        cost_estimate=cost(),
        name="ffn_grads",
    )(where, a, b)


def branch_kernel(weight, where_ref, dh_ref, x1_ref, dy_ref, gain_ref, *refs):
    dx_ref, da_ref, do_ref, gain_grad, w, sem = refs[4:]
    first = pl.program_id(0) == 0

    @pl.when(first)
    def _():
        weight.load(where_ref, refs[:4], w, sem)

    gain = gain_ref[:, 1:2].astype(F32)
    normal, inverse = norm_columns(x1_ref[...])
    back, part = norm_columns_back(dh_ref[...], normal, inverse, gain)
    dx = dy_ref[...].astype(F32) + back
    da = dx.astype(BF16)
    dx_ref[...] = dx
    da_ref[...] = da

    @pl.when(first)
    def _():
        gain_grad[...] = part
        wait_for(w, sem)

    @pl.when(jnp.logical_not(first))
    def _():
        gain_grad[...] += part

    do_ref[...] = dot(w[...], da, 1, 0).astype(BF16)


def branch(where, dh, x1, dy, gains, w):
    rows = dh.shape[1]
    return pl.pallas_call(
        functools.partial(branch_kernel, w),
        grid=(rows // TILE,),
        in_specs=[SMEM] + [columns(D, TILE)] * 3 + [fixed((D, GAINS))] + w.specs(),
        out_specs=[columns(D, TILE)] * 3 + [pl.BlockSpec((D, 1), lambda i: (0, 0))],
        out_shape=shaped(((D, rows), F32), ((D, rows), BF16), ((D, rows), BF16), ((D, 1), F32)),
        scratch_shapes=w.scratch(),
        compiler_params=params(60),
        cost_estimate=cost(2 * rows * D * D, rows * D * 18),
        name="branch",
    )(where, dh, x1, dy, gains, *w.arrays)


def attend_back_kernel(qkv_ref, o_ref, do_ref, lse_ref, segr_ref, segc_ref, cos_ref, sin_ref,
                       *refs):
    out_ref, done_ref, bias_ref, dk_ref, dv_ref = refs[-5:]
    done_ref[...] = jnp.zeros_like(done_ref)
    length = qkv_ref.shape[1]
    make_bias(bias_ref, segr_ref.at[0], segc_ref.at[0], length)

    def turn_back(g, c, s, at, cols):
        a, b = g[:HALF], g[HALF:]
        at = pl.multiple_of(at, HEAD_WIDTH)
        out_ref[pl.ds(at, HALF), cols] = (a * c + b * s).astype(BF16)
        out_ref[pl.ds(pl.multiple_of(at + HALF, HALF), HALF), cols] = (b * c - a * s).astype(BF16)

    @pl.loop(0, KEY_VALUE_HEADS)
    def _(kv):
        k = qkv_ref[pl.ds(pl.multiple_of(D + kv * HEAD_WIDTH, HEAD_WIDTH), HEAD_WIDTH), :]
        v = qkv_ref[pl.ds(pl.multiple_of(D + KEYS + kv * HEAD_WIDTH, HEAD_WIDTH), HEAD_WIDTH), :]
        dk_ref[...] = jnp.zeros_like(dk_ref)
        dv_ref[...] = jnp.zeros_like(dv_ref)
        for b in range(length // QB):
            lo, hi = key_span(b)
            cols = slice(b * QB, (b + 1) * QB)
            q, o, do = three(qkv_ref, kv, b), three(o_ref, kv, b), three(do_ref, kv, b)
            lse = jnp.concatenate([lse_ref[kv, i:i + 1, cols] for i in range(SHARE)], axis=1)
            inner = jnp.sum(o.astype(F32) * do.astype(F32), axis=0, keepdims=True)
            s = dot(k[:, lo:hi], q, 0, 0) + wide_bias(bias_ref, b, hi - lo)
            p = jnp.exp(s - lse)
            dp = dot(v[:, lo:hi], do, 0, 0)
            ds = (p * (dp - inner)).astype(BF16)
            dv_ref[:, lo:hi] += dot(do, p.astype(BF16), 1, 1)
            dk_ref[:, lo:hi] += dot(q, ds, 1, 1)
            dq = dot(k[:, lo:hi], ds, 1, 0) * HEAD_WIDTH ** -0.5
            for i in range(SHARE):
                turn_back(dq[:, i * QB:(i + 1) * QB], cos_ref[:, cols], sin_ref[:, cols],
                          (kv * SHARE + i) * HEAD_WIDTH, cols)
        turn_back(dk_ref[...], cos_ref[...], sin_ref[...], D + kv * HEAD_WIDTH, slice(None))
        out_ref[pl.ds(pl.multiple_of(D + KEYS + kv * HEAD_WIDTH, HEAD_WIDTH), HEAD_WIDTH), :] = (
            dv_ref[...].astype(BF16))


def attend_back(qkv, o, do, lse, segments, cos, sin, at, before=()):
    length = segments.shape[1]
    wide, rows = qkv.shape
    here = lambda height: pl.BlockSpec((height, length), lambda i: (0, at))
    return pl.pallas_call(
        attend_back_kernel,
        grid=(1,),
        in_specs=[
            here(wide),
            here(D),
            here(D),
            pl.BlockSpec((KEY_VALUE_HEADS, 8, length), lambda i: (0, 0, at)),
            pl.BlockSpec((1, 1, length), lambda i: (at, 0, 0)),
            pl.BlockSpec((1, length, 1), lambda i: (at, 0, 0)),
            here(HALF),
            here(HALF),
        ] + [pl.BlockSpec(memory_space=pltpu.HBM)] * len(before),
        out_specs=[here(wide), fixed(DONE.shape)],
        out_shape=shaped(((wide, rows), BF16)) + [DONE],
        input_output_aliases={8 + i: i for i in range(len(before))},
        scratch_shapes=[
            pltpu.VMEM((length // QB, 3 * QB, QB), F32),
            pltpu.VMEM((HEAD_WIDTH, length), F32),
            pltpu.VMEM((HEAD_WIDTH, length), F32),
        ],
        compiler_params=params(60),
        cost_estimate=cost(),
        name="attend_back",
    )(qkv, o, do, lse, segments[:, None, :], segments[:, :, None], cos, sin, *before)


PIECES = ((0, 128), (128, OWN))


def weight_kernel(where_ref, h_ref, dqkv_ref, o_ref, da_ref, *out_refs):
    def store(block, grad):
        def put(x, keep, send):
            for i, (low, high) in enumerate(PIECES):
                at = block ^ block_here(where_ref)
                out_refs[2 * i][x, at] = keep[low:high]
                out_refs[2 * i + 1][x, at] = send[low:high]

        split_owners(grad, where_ref, put)

    grad = dot(h_ref[...], dqkv_ref[:PAIR, :], 1, 1)
    store(0, grad[:, :CUT])
    store(1, grad[:, CUT:])
    left = dot(h_ref[...], dqkv_ref[2 * CUT:, :], 1, 1)
    right = dot(o_ref[...], da_ref[:3 * CUT - WIDE, :], 1, 1)
    store(2, jnp.concatenate([left, right], axis=1))
    store(3, dot(o_ref[...], da_ref[3 * CUT - WIDE:, :], 1, 1))


def weight_grads(where, h, dqkv, o, da):
    rows = h.shape[1]
    shapes = [(2, 4, high - low, CUT) for low, high in PIECES for _ in range(2)]
    return pl.pallas_call(
        weight_kernel,
        grid=(1,),
        in_specs=[SMEM, fixed((D, rows)), fixed((WIDE, rows)), fixed((D, rows)), fixed((D, rows))],
        out_specs=[fixed(shape) for shape in shapes],
        out_shape=shaped(*((shape, BF16) for shape in shapes)),
        compiler_params=params(60),
        cost_estimate=cost(),
        name="weight_grads",
    )(where, h, dqkv, o, da)


def inputs_kernel(weights, where_ref, x_ref, dx_ref, dqkv_ref, *refs):
    out_ref, gain_grad, wq, q_sem, wk, k_sem = refs[8:]
    first = pl.program_id(0) == 0

    @pl.when(first)
    def _():
        weights[0].load(where_ref, refs[:4], wq, q_sem)
        weights[1].load(where_ref, refs[4:8], wk, k_sem)
        wait_for(wq, q_sem)
        wait_for(wk, k_sem)

    gain = wk[:, 2 * KEYS:2 * KEYS + 1].astype(F32)
    dh = dot(wq[...], dqkv_ref[:D], 1, 0) + dot(wk[:, :2 * KEYS], dqkv_ref[D:], 1, 0)
    normal, inverse = norm_columns(x_ref[...].astype(F32))
    back, part = norm_columns_back(dh, normal, inverse, gain)
    out_ref[...] = (dx_ref[...] + back).astype(BF16)

    @pl.when(first)
    def _():
        gain_grad[...] = part

    @pl.when(jnp.logical_not(first))
    def _():
        gain_grad[...] += part


def input_grads(where, x, dx, wq, wk, dqkv):
    rows = x.shape[1]
    return pl.pallas_call(
        functools.partial(inputs_kernel, (wq, wk)),
        grid=(rows // HALF_TILE,),
        in_specs=[SMEM, columns(D, HALF_TILE), columns(D, HALF_TILE), columns(WIDE, HALF_TILE)]
        + wq.specs() + wk.specs(),
        out_specs=[columns(D, HALF_TILE), pl.BlockSpec((D, 1), lambda i: (0, 0))],
        out_shape=shaped(((D, rows), BF16), ((D, 1), F32)),
        scratch_shapes=wq.scratch() + wk.scratch(),
        compiler_params=params(60),
        cost_estimate=cost(2 * rows * D * WIDE, rows * (D * 8 + WIDE * 2) + D * WIDE * 2),
        name="input_grads",
    )(where, x, dx, dqkv, *wq.arrays, *wk.arrays)


def tables(segments):
    length = segments.shape[1]
    index = jnp.arange(length, dtype=jnp.int32)
    same = segments[:, :, None] == segments[:, None, :]
    start = jnp.min(jnp.where(same, index[None, :, None], length), axis=1)
    position = (index[None, :] - start).astype(F32).reshape(1, -1)
    freq = THETA ** (-(jnp.arange(HALF, dtype=F32) * 2.0 / HEAD_WIDTH))
    angle = freq[:, None] * position
    return jnp.cos(angle), jnp.sin(angle)


def after(value, *others):
    return lax.optimization_barrier((value,) + others)[0]


class Cube:
    def __init__(self, count):
        self.count = count
        self.dims = count.bit_length() - 1
        replica, group = lax.axis_index("replica"), lax.axis_index("group")
        self.coordinate = {i: (replica >> i) & 1 for i in range(self.dims)}
        self.coordinate["x"] = group >> 1
        self.coordinate["core"] = group & 1
        self.me = group

    def swap(self, value, dim):
        if dim == "x":
            return lax.ppermute(value, "group", [(i, i ^ 2) for i in range(4)])
        if dim == "core":
            return lax.ppermute(value, "group", [(i, i ^ 1) for i in range(4)])
        return lax.ppermute(value, "replica", [(i, i ^ (1 << dim)) for i in range(self.count)])

    def ordered(self, dim, mine, other, axis):
        return jnp.where(
            self.coordinate[dim] == 0,
            jnp.concatenate([mine, other], axis=axis),
            jnp.concatenate([other, mine], axis=axis),
        )


def rows_of(own, sibling, across, diagonal):
    pieces = own, sibling, across, diagonal
    return Weight(0, [(array, flip, None) for flip, array in enumerate(pieces)])


class Relay:
    def __init__(self, cube, shard, axis, first, second):
        self.cube, self.shard, self.axis, self.first, self.second = cube, shard, axis, first, second
        self.cut = 1 - axis
        size = shard.shape[self.cut] // (2 if first is None else 4)
        at = cube.coordinate[second]
        if first is not None:
            at = 2 * at + cube.coordinate[first]
        self.part = lax.dynamic_slice_in_dim(shard, at * size, size, self.cut)

    def cross(self, *others):
        self.direct = self.cube.swap(after(self.part, *others), "x")
        return self.direct

    def hand_on(self, *others):
        self.direct = after(self.direct, *others)
        if self.first is None:
            self.half = self.direct
            self.rest = self.cube.swap(self.half, self.second)
            return self.rest
        self.handed = self.cube.swap(self.direct, self.first)
        return self.handed

    def finish(self, *others):
        cube = self.cube
        if self.first is not None:
            handed = after(self.handed, *others)
            self.half = cube.ordered(self.first, self.direct, handed, self.cut)
            self.rest = cube.swap(self.half, self.second)
        self.half_diagonal = cube.swap(self.half, "core")

    def weight(self, sibling, *others):
        rest = after(self.rest, *others)
        pieces = [
            (self.shard, 0, None), (sibling, 1, None), (self.half, 2, 0), (rest, 2, 1),
            (self.half_diagonal, 3, 0), (self.cube.swap(rest, "core"), 3, 1),
        ]
        return Weight(self.axis, pieces, self.second, 4)


class Reduce:
    def __init__(self, cube, keep, got, halves, gathers):
        rows, wide = keep.shape[2:]
        self.cube, self.shape = cube, (4, rows, wide)
        self.order = halves + tuple(range(2, cube.dims)) + gathers
        self.place = {"x": 0, 0: 1, 1: 2}
        self.terms = [t.reshape(2, 2, 2, rows, wide) for t in (keep, got)]
        self.index = 0
        self.done = False

    def sum(self, terms):
        if len(terms) == 1:
            return terms[0]
        return functools.reduce(jnp.add, [t.astype(F32) for t in terms]).astype(BF16)

    @staticmethod
    def land(pieces, other):
        got = lax.optimization_barrier((*(piece.terms[-1] for piece in pieces), other))
        for piece, value in zip(pieces, got):
            piece.terms[-1] = value

    def ready(self, *others):
        dim = self.order[self.index]
        if others:
            self.terms[-1] = after(self.terms[-1], *others)
        if self.index < 3:
            axis = self.place[dim]
            take = lambda i: [lax.slice_in_dim(t, i, i + 1, axis=axis) for t in self.terms]
            self.send, self.terms = self.sum(take(1)), take(0)
        else:
            self.send = self.sum(self.terms)
        return self.send

    def swap(self):
        dim = self.order[self.index]
        got = self.cube.swap(self.send, dim)
        self.index += 1
        if self.index <= 3:
            self.terms = self.terms + [got]
        elif self.index <= len(self.order) - 2:
            self.terms = [self.send, got]
        elif self.index < len(self.order):
            self.terms = [self.cube.ordered(dim, self.send, got, self.place[dim])]
        else:
            self.terms = [self.send, got]

    def finish(self, *others):
        self.done = True
        low, got = (after(value, *others) for value in self.terms)
        self.result = self.cube.ordered(self.order[-1], low, got, self.place[self.order[-1]])
        self.result = self.result.reshape(self.shape)
        return self.result


def per_device(
    tokens,
    segments,
    query_weight,
    key_weight,
    value_weight,
    output_weight,
    w_gate,
    w_up,
    w_down,
    attn_gain,
    ffn_gain,
    cotangent,
    replicas,
):
    cube = Cube(replicas)
    where = jnp.stack([cube.me] + [cube.coordinate[i] for i in range(3)]).astype(jnp.int32)
    x, dy = tokens.T, cotangent.T

    core = lambda value: cube.swap(value, "core")
    q_across = cube.swap(query_weight, "x")
    pad = jnp.zeros((OWN, GAINS - 2), BF16)
    kv = jnp.concatenate(
        [key_weight, value_weight, attn_gain[:, None], ffn_gain[:, None], pad], axis=1
    )
    kv_across = cube.swap(after(kv, q_across), "x")
    relays = [
        Relay(cube, w_gate, 0, 0, 1), Relay(cube, w_up, 0, 1, 0), Relay(cube, w_down.T, 1, None, 0)
    ]
    q_sibling, kv_sibling, wo_sibling = core(query_weight), core(kv), core(output_weight)
    siblings = [core(relay.shard) for relay in relays]
    cos, sin = tables(segments)
    early = [relay.part for relay in relays] + [cos, sin, where, q_sibling, kv_sibling, wo_sibling]
    q_across, kv_across = lax.optimization_barrier((q_across, kv_across, *early, *siblings))[:2]
    q_diagonal, kv_diagonal = core(q_across), core(kv_across)
    direct = [relay.cross(q_across, kv_across) for relay in relays]
    wq = rows_of(query_weight, q_sibling, q_across, q_diagonal)
    wk = rows_of(kv, kv_sibling, kv_across, kv_diagonal)
    qkv, h, gains = project(where, x, wq, wk, cos, sin)
    *first, done0 = attend(qkv, segments, 0)
    for relay in relays:
        relay.hand_on(done0)
    wo_across = cube.swap(after(output_weight, done0, *direct), "x")
    o, lse, done1 = attend(after(qkv, done0, *direct), segments, 1, first)
    for relay in relays:
        relay.finish(done1)
    wo_diagonal = core(after(wo_across, done1))
    wo = rows_of(output_weight, wo_sibling, wo_across, wo_diagonal)
    x1, h2 = middle(where, x, after(o, relays[0].half, relays[1].half), wo, gains)
    weights = [relay.weight(sibling, h2) for relay, sibling in zip(relays, siblings)]
    y, dh2, hid, dgate, dup = feed_forward(where, h2, dy, x1, weights)

    gd_keep, gd_send = ffn_grads(where, dy, hid, True)
    gd = Reduce(cube, gd_keep, core(gd_send), ("x", 0, 1), (0, 1))
    gg_keep, gg_send = ffn_grads(where, h2, after(dgate, gd_send), False)
    gg = Reduce(cube, gg_keep, core(gg_send), (0, "x", 1), (1, 0))
    gd.ready(gg_send)
    gu_keep, gu_send = ffn_grads(where, h2, after(dup, gd.send), False)
    gd.swap()
    gu = Reduce(cube, gu_keep, core(gu_send), ("x", 0, 1), (1, 0))
    gg.ready(gu_send)
    dx1, da, do, ffn_gain_grad = branch(where, after(dh2, gg.send), x1, dy, gains, wo)
    gg.swap()
    gu.ready(da)
    do0 = after(do, gu.send)
    gu.swap()
    *first, done0 = attend_back(qkv, o, do0, lse, segments, cos, sin, 0)
    Reduce.land((gd, gg), done0)
    do1 = after(do, done0, gd.ready(), gg.ready())
    gd.swap()
    gg.swap()
    dqkv, done1 = attend_back(qkv, o, do1, lse, segments, cos, sin, 1, first)
    swaps = [gd, gg, gu]
    Reduce.land(swaps, done1)
    dqkv = after(dqkv, *[piece.ready() for piece in swaps])
    for piece in swaps:
        piece.swap()
    parts = []
    weight_parts = weight_grads(where, h, dqkv, o, da)
    for i, halves in enumerate((("x", 0, 1), (0, "x", 1))):
        keep, send = weight_parts[2 * i:2 * i + 2]
        parts.append(Reduce(cube, keep, core(send), halves, (1 - i, i)))
    dqkv = after(dqkv, *[part.ready() for part in parts])
    for part in parts:
        part.swap()
    grad_x, attn_gain_grad = input_grads(where, x, dx1, wq, wk, dqkv)
    swaps = [gd] + parts + [gg, gu]
    Reduce.land(swaps, grad_x)
    both = jnp.concatenate([attn_gain_grad, ffn_gain_grad], axis=1).T.reshape(-1)
    ends = ["core", "x"] + list(range(cube.dims))
    token = grad_x
    while any(piece.index < len(piece.order) for piece in swaps):
        active = [piece for piece in swaps if piece.index < len(piece.order)]
        for piece in active:
            token = piece.ready(token, both)
            piece.swap()
        for piece in swaps:
            if piece not in active and not piece.done:
                token = piece.finish(token)
        if ends:
            both = both + after(cube.swap(both, ends.pop(0)), token)
    for piece in swaps:
        if not piece.done:
            token = piece.finish(token)
    for dim in ends:
        both = both + cube.swap(both, dim)
    both = lax.dynamic_slice_in_dim(both.reshape(2, D), cube.me * OWN, OWN, 1)
    flat = lambda g: jnp.concatenate([g[i] for i in range(4)], axis=1)
    ga = jnp.concatenate([flat(part.result) for part in parts], axis=0).astype(F32)
    return (
        y.T,
        grad_x.T,
        ga[:, :D],
        ga[:, D:D + KEYS],
        ga[:, D + KEYS:WIDE],
        ga[:, WIDE:],
        flat(gg.result).astype(F32),
        flat(gu.result).astype(F32),
        gd.result.reshape(D, CUT).T.astype(F32),
        both[0],
        both[1],
    )


def solution(mesh):
    rows = P(("group", "replica"), None)
    weight, gain = P("group", None), P("group")
    replicas = mesh.shape["replica"]
    return jax.shard_map(
        lambda *args: per_device(*args, replicas),
        mesh=mesh,
        in_specs=(rows, rows) + (weight,) * 7 + (gain, gain, rows),
        out_specs=(rows, rows) + (weight,) * 7 + (gain, gain),
        check_vma=False,
    )
```

```python
import functools

import jax
import jax.numpy as jnp
from jax import lax
from jax.experimental import pallas as pl
from jax.experimental.pallas import tpu as pltpu
from jax.sharding import PartitionSpec as P

D = 960
QUERY_HEADS = 15
KEY_VALUE_HEADS = 5
HEAD_WIDTH = 64
SHARE = QUERY_HEADS // KEY_VALUE_HEADS
HALF = HEAD_WIDTH // 2
KEYS = KEY_VALUE_HEADS * HEAD_WIDTH
EPS = 1e-05
THETA = 100000.0
TILE = 512
HALF_TILE = 256
QB = 128
GAINS = 128
WIDE = D + 2 * KEYS
CUT = 640
OWN = 240
PAIR = 2 * CUT
F32 = jnp.float32
BF16 = jnp.bfloat16
MIB = 1 << 20


def dot(a, b, ca, cb):
    return lax.dot_general(a, b, (((ca,), (cb,)), ((), ())), preferred_element_type=F32)


def params(limit, grid=1):
    return pltpu.CompilerParams(
        vmem_limit_bytes=limit * MIB, dimension_semantics=("arbitrary",) * grid
    )


def cost(*_):
    return pl.CostEstimate(flops=1, bytes_accessed=1, transcendentals=0)


def shaped(*shape_type):
    return [jax.ShapeDtypeStruct(s, t) for s, t in shape_type]


def norm_columns(v):
    inverse = lax.rsqrt(jnp.mean(v * v, axis=0, keepdims=True) + EPS)
    return v * inverse, inverse


def norm_columns_back(grad, normal, inverse, gain):
    scaled = grad * gain
    back = inverse * (scaled - normal * jnp.mean(scaled * normal, axis=0, keepdims=True))
    return back, jnp.sum(grad * normal, axis=1, keepdims=True)


def fixed(shape):
    return pl.BlockSpec(shape, lambda *_: (0,) * len(shape), pipeline_mode=pl.Buffered(1))


def columns(height, width):
    return pl.BlockSpec((height, width), lambda i: (0, i))


class Weight:
    def __init__(self, axis, pieces, dim=None, blocks=0):
        self.axis, self.dim, self.blocks = axis, dim, blocks
        self.arrays = [array for array, _, _ in pieces]
        self.places = [(flip, side) for _, flip, side in pieces]
        shape = list(self.arrays[0].shape)
        self.size = shape[axis]
        self.half = shape[1 - axis] // 2
        shape[axis] *= 4
        self.shape = tuple(shape)

    def specs(self):
        return [pl.BlockSpec(memory_space=pltpu.HBM)] * len(self.arrays)

    def scratch(self):
        if not self.blocks:
            return [pltpu.VMEM(self.shape, BF16), pltpu.SemaphoreType.DMA]
        block = (self.shape[0], self.shape[1] // self.blocks)
        return [pltpu.VMEM((self.blocks,) + block, BF16), pltpu.SemaphoreType.DMA((self.blocks,))]

    def load(self, where_ref, refs, scratch, sem):
        wide = self.shape[1] // max(self.blocks, 1)
        for ref, (flip, side) in zip(refs, self.places):
            at = (where_ref[0] ^ flip) * self.size
            other = 0 if side is None else (where_ref[1 + self.dim] ^ side) * self.half
            row, column = (at, other) if self.axis == 0 else (other, at)
            rows = pl.ds(pl.multiple_of(row, OWN), ref.shape[0])
            if not self.blocks:
                pltpu.make_async_copy(ref, scratch.at[rows, :], sem).start()
                continue
            first = column // wide
            for i in range(ref.shape[1] // wide):
                pltpu.make_async_copy(
                    ref.at[:, i * wide:(i + 1) * wide], scratch.at[first + i, rows, :],
                    sem.at[first + i],
                ).start()


def wait_for(scratch, sem):
    pltpu.make_async_copy(scratch, scratch, sem).wait()


SMEM = pl.BlockSpec(memory_space=pltpu.SMEM)


def project_kernel(weights, where_ref, x_ref, cos_ref, sin_ref, *refs):
    qkv_ref, h_ref, gains_ref, wq, q_sem, wk, k_sem = refs[8:]

    @pl.when(pl.program_id(0) == 0)
    def _():
        weights[0].load(where_ref, refs[:4], wq, q_sem)
        weights[1].load(where_ref, refs[4:8], wk, k_sem)
        wait_for(wq, q_sem)
        wait_for(wk, k_sem)
        gains_ref[...] = wk[:, 2 * KEYS:]

    gain = wk[:, 2 * KEYS:2 * KEYS + 1].astype(F32)
    normal, _ = norm_columns(x_ref[...].astype(F32))
    h = (normal * gain).astype(BF16)
    h_ref[...] = h
    c, s = cos_ref[...], sin_ref[...]

    def rotary(out, at, heads, scale):
        for head in range(heads):
            low = head * HEAD_WIDTH
            a, b = out[low:low + HALF], out[low + HALF:low + HEAD_WIDTH]
            to = at + low
            qkv_ref[to:to + HALF, :] = ((a * c - b * s) * scale).astype(BF16)
            qkv_ref[to + HALF:to + HEAD_WIDTH, :] = ((b * c + a * s) * scale).astype(BF16)

    rotary(dot(wq[...], h, 0, 0), 0, QUERY_HEADS, HEAD_WIDTH ** -0.5)
    out = dot(wk[:, :2 * KEYS], h, 0, 0)
    rotary(out, D, KEY_VALUE_HEADS, 1.0)
    qkv_ref[D + KEYS:, :] = out[KEYS:].astype(BF16)


def project(where, x, wq, wk, cos, sin):
    rows = x.shape[1]
    return pl.pallas_call(
        functools.partial(project_kernel, (wq, wk)),
        grid=(rows // TILE,),
        in_specs=[SMEM, columns(D, TILE), columns(HALF, TILE), columns(HALF, TILE)]
        + wq.specs() + wk.specs(),
        out_specs=[columns(WIDE, TILE), columns(D, TILE),
                   pl.BlockSpec((D, GAINS), lambda i: (0, 0))],
        out_shape=shaped(((WIDE, rows), BF16), ((D, rows), BF16), ((D, GAINS), BF16)),
        scratch_shapes=wq.scratch() + wk.scratch(),
        compiler_params=params(60),
        cost_estimate=cost(2 * rows * D * WIDE, rows * (2 * D + WIDE) * 2 + D * WIDE * 2),
        name="project",
    )(where, x, cos, sin, *wq.arrays, *wk.arrays)


def key_span(block):
    return max(0, QB * (block - 2)), QB * (block + 1)


def make_bias(bias_ref, segr_ref, segc_ref, length):
    for b in range(length // QB):
        lo, hi = key_span(b)
        key_at = lax.broadcasted_iota(jnp.int32, (hi - lo, QB), 0) + lo
        query_at = lax.broadcasted_iota(jnp.int32, (hi - lo, QB), 1) + b * QB
        ok = (segc_ref[lo:hi, :] == segr_ref[:, b * QB:(b + 1) * QB]) & (key_at <= query_at)
        bias_ref[b, 0:hi - lo, :] = jnp.where(ok, 0.0, -1e30)


def three(ref, kv, b):
    return jnp.concatenate(
        [
            ref[pl.ds(pl.multiple_of((kv * SHARE + i) * HEAD_WIDTH, HEAD_WIDTH), HEAD_WIDTH),
                b * QB:(b + 1) * QB]
            for i in range(SHARE)
        ],
        axis=1,
    )


def wide_bias(bias_ref, b, n):
    one = bias_ref[b, 0:n, :]
    return jnp.concatenate([one] * SHARE, axis=1)


def attend_kernel(qkv_ref, segr_ref, segc_ref, *refs):
    o_ref, lse_ref, done_ref, bias_ref = refs[-4:]
    done_ref[...] = jnp.zeros_like(done_ref)
    length = qkv_ref.shape[1]
    make_bias(bias_ref, segr_ref.at[0], segc_ref.at[0], length)

    @pl.loop(0, KEY_VALUE_HEADS)
    def _(kv):
        k = qkv_ref[pl.ds(pl.multiple_of(D + kv * HEAD_WIDTH, HEAD_WIDTH), HEAD_WIDTH), :]
        v = qkv_ref[pl.ds(pl.multiple_of(D + KEYS + kv * HEAD_WIDTH, HEAD_WIDTH), HEAD_WIDTH), :]
        for b in range(length // QB):
            lo, hi = key_span(b)
            s = dot(k[:, lo:hi], three(qkv_ref, kv, b), 0, 0) + wide_bias(bias_ref, b, hi - lo)
            top = jnp.max(s, axis=0, keepdims=True)
            p = jnp.exp(s - top)
            total = jnp.sum(p, axis=0, keepdims=True)
            out = dot(v[:, lo:hi], p.astype(BF16), 1, 0) / total
            lse = top + jnp.log(total)
            for i in range(SHARE):
                rows = pl.ds(pl.multiple_of((kv * SHARE + i) * HEAD_WIDTH, HEAD_WIDTH), HEAD_WIDTH)
                o_ref[rows, b * QB:(b + 1) * QB] = out[:, i * QB:(i + 1) * QB].astype(BF16)
                lse_ref[kv, i:i + 1, b * QB:(b + 1) * QB] = lse[:, i * QB:(i + 1) * QB]


DONE = jax.ShapeDtypeStruct((8, GAINS), F32)


def attend(qkv, segments, at, before=()):
    seqs, length = segments.shape
    wide, rows = qkv.shape
    return pl.pallas_call(
        attend_kernel,
        grid=(1,),
        in_specs=[
            pl.BlockSpec((wide, length), lambda i: (0, at)),
            pl.BlockSpec((1, 1, length), lambda i: (at, 0, 0)),
            pl.BlockSpec((1, length, 1), lambda i: (at, 0, 0)),
        ] + [pl.BlockSpec(memory_space=pltpu.HBM)] * len(before),
        out_specs=[
            pl.BlockSpec((D, length), lambda i: (0, at)),
            pl.BlockSpec((KEY_VALUE_HEADS, 8, length), lambda i: (0, 0, at)),
            fixed(DONE.shape),
        ],
        out_shape=shaped(((D, rows), BF16), ((KEY_VALUE_HEADS, 8, rows), F32)) + [DONE],
        input_output_aliases={3 + i: i for i in range(len(before))},
        scratch_shapes=[pltpu.VMEM((length // QB, 3 * QB, QB), F32)],
        compiler_params=params(60),
        cost_estimate=cost(),
        name="attend",
    )(qkv, segments[:, None, :], segments[:, :, None], *before)


def middle_kernel(weight, where_ref, x_ref, o_ref, gain_ref, *refs):
    x1_ref, h_ref, w, sem = refs[4:]

    @pl.when(pl.program_id(0) == 0)
    def _():
        weight.load(where_ref, refs[:4], w, sem)
        wait_for(w, sem)

    x1 = x_ref[...].astype(F32) + dot(w[...], o_ref[...], 0, 0)
    normal, _ = norm_columns(x1)
    x1_ref[...] = x1
    h_ref[...] = (normal * gain_ref[:, 1:2].astype(F32)).astype(BF16)


def middle(where, x, o, w, gains):
    rows = x.shape[1]
    return pl.pallas_call(
        functools.partial(middle_kernel, w),
        grid=(rows // TILE,),
        in_specs=[SMEM, columns(D, TILE), columns(D, TILE), fixed((D, GAINS))] + w.specs(),
        out_specs=[columns(D, TILE), columns(D, TILE)],
        out_shape=shaped(((D, rows), F32), ((D, rows), BF16)),
        scratch_shapes=w.scratch(),
        compiler_params=params(60),
        cost_estimate=cost(2 * rows * D * D, rows * D * 10),
        name="middle",
    )(where, x, o, gains, *w.arrays)


def feed_forward_kernel(weights, where_ref, h_ref, dy_ref, x1_ref, *refs):
    count = len(weights[0].arrays)
    y_ref, dh_ref, hid_ref, dgate_ref, dup_ref, acc_ref, acc_sem, *scratch = refs[3 * count:]
    step = pl.program_id(0)

    @pl.when(step == 0)
    def _():
        for i, weight in enumerate(weights):
            weight.load(where_ref, refs[i * count:(i + 1) * count], *scratch[2 * i:2 * i + 2])
        pltpu.make_async_copy(x1_ref, acc_ref, acc_sem).start()
        dh_ref[...] = jnp.zeros_like(dh_ref)
        pltpu.make_async_copy(x1_ref, acc_ref, acc_sem).wait()

    wg_ref, wu_ref, wd_ref = (w.at[step] for w in scratch[::2])
    for w, sem in zip((wg_ref, wu_ref, wd_ref), scratch[1::2]):
        wait_for(w, sem.at[step])
    h, dy = h_ref[...], dy_ref[...]
    gate = dot(wg_ref[...], h, 0, 0)
    up = dot(wu_ref[...], h, 0, 0)
    dhid = dot(wd_ref[...], dy, 0, 0)
    sig = jax.nn.sigmoid(gate)
    silu = gate * sig
    hid = (silu * up).astype(BF16)
    dgate = (dhid * up * (sig + silu * (1.0 - sig))).astype(BF16)
    dup = (dhid * silu).astype(BF16)
    hid_ref[...] = hid
    dgate_ref[...] = dgate
    dup_ref[...] = dup
    acc_ref[...] += dot(wd_ref[...], hid, 1, 0)
    dh_ref[...] += dot(wg_ref[...], dgate, 1, 0) + dot(wu_ref[...], dup, 1, 0)

    @pl.when(step == pl.num_programs(0) - 1)
    def _():
        y_ref[...] = acc_ref[...].astype(BF16)


def feed_forward(where, h, dy, x1, weights):
    rows, hidden = h.shape[1], weights[0].shape[1]
    block = pl.BlockSpec((CUT, rows), lambda f: (f, 0))
    return pl.pallas_call(
        functools.partial(feed_forward_kernel, weights),
        grid=(hidden // CUT,),
        in_specs=[SMEM, fixed((D, rows)), fixed((D, rows)), pl.BlockSpec(memory_space=pltpu.HBM)]
        + sum((w.specs() for w in weights), []),
        out_specs=[fixed((D, rows)), fixed((D, rows))] + [block] * 3,
        out_shape=shaped(((D, rows), BF16), ((D, rows), F32)) + shaped(((hidden, rows), BF16)) * 3,
        scratch_shapes=sum(
            (w.scratch() for w in weights), [pltpu.VMEM((D, rows), F32), pltpu.SemaphoreType.DMA]
        ),
        compiler_params=params(60),
        cost_estimate=cost(),
        name="feed_forward",
    )(where, h, dy, x1, *sum((w.arrays for w in weights), []))


def block_here(where_ref):
    return 2 * where_ref[1] + where_ref[2]


def split_owners(grad, where_ref, put):
    core, x_here = where_ref[0] & 1, where_ref[0] >> 1
    for x in range(2):
        a = grad[2 * x * OWN:(2 * x + 1) * OWN].astype(BF16)
        b = grad[(2 * x + 1) * OWN:(2 * x + 2) * OWN].astype(BF16)
        put(x_here ^ x, jnp.where(core == 0, a, b), jnp.where(core == 0, b, a))


def row_grads_kernel(where_ref, a_ref, b_ref, keep_ref, send_ref):
    grad = dot(a_ref[...], b_ref[...], 1, 1)
    for i in range(2):
        def put(x, keep, send):
            keep_ref[x, i ^ where_ref[2]] = keep
            send_ref[x, i ^ where_ref[2]] = send

        split_owners(grad[:, i * CUT:(i + 1) * CUT], where_ref, put)


def column_grads_kernel(where_ref, a_ref, b_ref, keep_ref, send_ref):
    grad = dot(a_ref[...], b_ref[...], 1, 1).astype(BF16)
    first = (where_ref[0] & 1) == 0
    for i in range(4):
        at = block_here(where_ref) ^ i
        a, b = grad[i * OWN:(i + 1) * OWN, :CUT], grad[i * OWN:(i + 1) * OWN, CUT:]
        keep_ref[0, at] = jnp.where(first, a, b)
        send_ref[0, at] = jnp.where(first, b, a)


def ffn_grads(where, a, b, by_columns):
    rows = a.shape[1]
    if by_columns:
        kernel = column_grads_kernel
        out = pl.BlockSpec((1, 4, OWN, CUT), lambda f, at: (f ^ (at[0] >> 1), 0, 0, 0))
    else:
        kernel = row_grads_kernel
        out = pl.BlockSpec((2, 2, OWN, CUT), lambda f, at: (0, f ^ at[1], 0, 0))
    return pl.pallas_call(
        kernel,
        grid_spec=pltpu.PrefetchScalarGridSpec(
            num_scalar_prefetch=1,
            grid=(b.shape[0] // PAIR,),
            in_specs=[fixed((D, rows)), pl.BlockSpec((PAIR, rows), lambda f, at: (f, 0))],
            out_specs=[out, out],
        ),
        out_shape=shaped(((2, 4, OWN, CUT), BF16)) * 2,
        compiler_params=params(60),
        cost_estimate=cost(),
        name="ffn_grads",
    )(where, a, b)


def branch_kernel(weight, where_ref, dh_ref, x1_ref, dy_ref, gain_ref, *refs):
    dx_ref, da_ref, do_ref, gain_grad, w, sem = refs[4:]
    first = pl.program_id(0) == 0

    @pl.when(first)
    def _():
        weight.load(where_ref, refs[:4], w, sem)

    gain = gain_ref[:, 1:2].astype(F32)
    normal, inverse = norm_columns(x1_ref[...])
    back, part = norm_columns_back(dh_ref[...], normal, inverse, gain)
    dx = dy_ref[...].astype(F32) + back
    da = dx.astype(BF16)
    dx_ref[...] = dx
    da_ref[...] = da

    @pl.when(first)
    def _():
        gain_grad[...] = part
        wait_for(w, sem)

    @pl.when(jnp.logical_not(first))
    def _():
        gain_grad[...] += part

    do_ref[...] = dot(w[...], da, 1, 0).astype(BF16)


def branch(where, dh, x1, dy, gains, w):
    rows = dh.shape[1]
    return pl.pallas_call(
        functools.partial(branch_kernel, w),
        grid=(rows // TILE,),
        in_specs=[SMEM] + [columns(D, TILE)] * 3 + [fixed((D, GAINS))] + w.specs(),
        out_specs=[columns(D, TILE)] * 3 + [pl.BlockSpec((D, 1), lambda i: (0, 0))],
        out_shape=shaped(((D, rows), F32), ((D, rows), BF16), ((D, rows), BF16), ((D, 1), F32)),
        scratch_shapes=w.scratch(),
        compiler_params=params(60),
        cost_estimate=cost(2 * rows * D * D, rows * D * 18),
        name="branch",
    )(where, dh, x1, dy, gains, *w.arrays)


def attend_back_kernel(qkv_ref, o_ref, do_ref, lse_ref, segr_ref, segc_ref, cos_ref, sin_ref,
                       *refs):
    out_ref, done_ref, bias_ref, dk_ref, dv_ref = refs[-5:]
    done_ref[...] = jnp.zeros_like(done_ref)
    length = qkv_ref.shape[1]
    make_bias(bias_ref, segr_ref.at[0], segc_ref.at[0], length)

    def turn_back(g, c, s, at, cols):
        a, b = g[:HALF], g[HALF:]
        at = pl.multiple_of(at, HEAD_WIDTH)
        out_ref[pl.ds(at, HALF), cols] = (a * c + b * s).astype(BF16)
        out_ref[pl.ds(pl.multiple_of(at + HALF, HALF), HALF), cols] = (b * c - a * s).astype(BF16)

    @pl.loop(0, KEY_VALUE_HEADS)
    def _(kv):
        k = qkv_ref[pl.ds(pl.multiple_of(D + kv * HEAD_WIDTH, HEAD_WIDTH), HEAD_WIDTH), :]
        v = qkv_ref[pl.ds(pl.multiple_of(D + KEYS + kv * HEAD_WIDTH, HEAD_WIDTH), HEAD_WIDTH), :]
        dk_ref[...] = jnp.zeros_like(dk_ref)
        dv_ref[...] = jnp.zeros_like(dv_ref)
        for b in range(length // QB):
            lo, hi = key_span(b)
            cols = slice(b * QB, (b + 1) * QB)
            q, o, do = three(qkv_ref, kv, b), three(o_ref, kv, b), three(do_ref, kv, b)
            lse = jnp.concatenate([lse_ref[kv, i:i + 1, cols] for i in range(SHARE)], axis=1)
            inner = jnp.sum(o.astype(F32) * do.astype(F32), axis=0, keepdims=True)
            s = dot(k[:, lo:hi], q, 0, 0) + wide_bias(bias_ref, b, hi - lo)
            p = jnp.exp(s - lse)
            dp = dot(v[:, lo:hi], do, 0, 0)
            ds = (p * (dp - inner)).astype(BF16)
            dv_ref[:, lo:hi] += dot(do, p.astype(BF16), 1, 1)
            dk_ref[:, lo:hi] += dot(q, ds, 1, 1)
            dq = dot(k[:, lo:hi], ds, 1, 0) * HEAD_WIDTH ** -0.5
            for i in range(SHARE):
                turn_back(dq[:, i * QB:(i + 1) * QB], cos_ref[:, cols], sin_ref[:, cols],
                          (kv * SHARE + i) * HEAD_WIDTH, cols)
        turn_back(dk_ref[...], cos_ref[...], sin_ref[...], D + kv * HEAD_WIDTH, slice(None))
        out_ref[pl.ds(pl.multiple_of(D + KEYS + kv * HEAD_WIDTH, HEAD_WIDTH), HEAD_WIDTH), :] = (
            dv_ref[...].astype(BF16))


def attend_back(qkv, o, do, lse, segments, cos, sin, at, before=()):
    length = segments.shape[1]
    wide, rows = qkv.shape
    here = lambda height: pl.BlockSpec((height, length), lambda i: (0, at))
    return pl.pallas_call(
        attend_back_kernel,
        grid=(1,),
        in_specs=[
            here(wide),
            here(D),
            here(D),
            pl.BlockSpec((KEY_VALUE_HEADS, 8, length), lambda i: (0, 0, at)),
            pl.BlockSpec((1, 1, length), lambda i: (at, 0, 0)),
            pl.BlockSpec((1, length, 1), lambda i: (at, 0, 0)),
            here(HALF),
            here(HALF),
        ] + [pl.BlockSpec(memory_space=pltpu.HBM)] * len(before),
        out_specs=[here(wide), fixed(DONE.shape)],
        out_shape=shaped(((wide, rows), BF16)) + [DONE],
        input_output_aliases={8 + i: i for i in range(len(before))},
        scratch_shapes=[
            pltpu.VMEM((length // QB, 3 * QB, QB), F32),
            pltpu.VMEM((HEAD_WIDTH, length), F32),
            pltpu.VMEM((HEAD_WIDTH, length), F32),
        ],
        compiler_params=params(60),
        cost_estimate=cost(),
        name="attend_back",
    )(qkv, o, do, lse, segments[:, None, :], segments[:, :, None], cos, sin, *before)


PIECES = ((0, 128), (128, OWN))


def weight_kernel(where_ref, h_ref, dqkv_ref, o_ref, da_ref, *out_refs):
    def store(block, grad):
        def put(x, keep, send):
            for i, (low, high) in enumerate(PIECES):
                at = block ^ block_here(where_ref)
                out_refs[2 * i][x, at] = keep[low:high]
                out_refs[2 * i + 1][x, at] = send[low:high]

        split_owners(grad, where_ref, put)

    grad = dot(h_ref[...], dqkv_ref[:PAIR, :], 1, 1)
    store(0, grad[:, :CUT])
    store(1, grad[:, CUT:])
    left = dot(h_ref[...], dqkv_ref[2 * CUT:, :], 1, 1)
    right = dot(o_ref[...], da_ref[:3 * CUT - WIDE, :], 1, 1)
    store(2, jnp.concatenate([left, right], axis=1))
    store(3, dot(o_ref[...], da_ref[3 * CUT - WIDE:, :], 1, 1))


def weight_grads(where, h, dqkv, o, da):
    rows = h.shape[1]
    shapes = [(2, 4, high - low, CUT) for low, high in PIECES for _ in range(2)]
    return pl.pallas_call(
        weight_kernel,
        grid=(1,),
        in_specs=[SMEM, fixed((D, rows)), fixed((WIDE, rows)), fixed((D, rows)), fixed((D, rows))],
        out_specs=[fixed(shape) for shape in shapes],
        out_shape=shaped(*((shape, BF16) for shape in shapes)),
        compiler_params=params(60),
        cost_estimate=cost(),
        name="weight_grads",
    )(where, h, dqkv, o, da)


def inputs_kernel(weights, where_ref, x_ref, dx_ref, dqkv_ref, *refs):
    out_ref, gain_grad, wq, q_sem, wk, k_sem = refs[8:]
    first = pl.program_id(0) == 0

    @pl.when(first)
    def _():
        weights[0].load(where_ref, refs[:4], wq, q_sem)
        weights[1].load(where_ref, refs[4:8], wk, k_sem)
        wait_for(wq, q_sem)
        wait_for(wk, k_sem)

    gain = wk[:, 2 * KEYS:2 * KEYS + 1].astype(F32)
    dh = dot(wq[...], dqkv_ref[:D], 1, 0) + dot(wk[:, :2 * KEYS], dqkv_ref[D:], 1, 0)
    normal, inverse = norm_columns(x_ref[...].astype(F32))
    back, part = norm_columns_back(dh, normal, inverse, gain)
    out_ref[...] = (dx_ref[...] + back).astype(BF16)

    @pl.when(first)
    def _():
        gain_grad[...] = part

    @pl.when(jnp.logical_not(first))
    def _():
        gain_grad[...] += part


def input_grads(where, x, dx, wq, wk, dqkv):
    rows = x.shape[1]
    return pl.pallas_call(
        functools.partial(inputs_kernel, (wq, wk)),
        grid=(rows // HALF_TILE,),
        in_specs=[SMEM, columns(D, HALF_TILE), columns(D, HALF_TILE), columns(WIDE, HALF_TILE)]
        + wq.specs() + wk.specs(),
        out_specs=[columns(D, HALF_TILE), pl.BlockSpec((D, 1), lambda i: (0, 0))],
        out_shape=shaped(((D, rows), BF16), ((D, 1), F32)),
        scratch_shapes=wq.scratch() + wk.scratch(),
        compiler_params=params(60),
        cost_estimate=cost(2 * rows * D * WIDE, rows * (D * 8 + WIDE * 2) + D * WIDE * 2),
        name="input_grads",
    )(where, x, dx, dqkv, *wq.arrays, *wk.arrays)


def tables(segments):
    length = segments.shape[1]
    index = jnp.arange(length, dtype=jnp.int32)
    same = segments[:, :, None] == segments[:, None, :]
    start = jnp.min(jnp.where(same, index[None, :, None], length), axis=1)
    position = (index[None, :] - start).astype(F32).reshape(1, -1)
    freq = THETA ** (-(jnp.arange(HALF, dtype=F32) * 2.0 / HEAD_WIDTH))
    angle = freq[:, None] * position
    return jnp.cos(angle), jnp.sin(angle)


def after(value, *others):
    return lax.optimization_barrier((value,) + others)[0]


class Cube:
    def __init__(self, count):
        self.count = count
        self.dims = count.bit_length() - 1
        replica, group = lax.axis_index("replica"), lax.axis_index("group")
        self.coordinate = {i: (replica >> i) & 1 for i in range(self.dims)}
        self.coordinate["x"] = group >> 1
        self.coordinate["core"] = group & 1
        self.me = group

    def swap(self, value, dim):
        if dim == "x":
            return lax.ppermute(value, "group", [(i, i ^ 2) for i in range(4)])
        if dim == "core":
            return lax.ppermute(value, "group", [(i, i ^ 1) for i in range(4)])
        return lax.ppermute(value, "replica", [(i, i ^ (1 << dim)) for i in range(self.count)])

    def ordered(self, dim, mine, other, axis):
        return jnp.where(
            self.coordinate[dim] == 0,
            jnp.concatenate([mine, other], axis=axis),
            jnp.concatenate([other, mine], axis=axis),
        )


def rows_of(own, sibling, across, diagonal):
    pieces = own, sibling, across, diagonal
    return Weight(0, [(array, flip, None) for flip, array in enumerate(pieces)])


class Relay:
    def __init__(self, cube, shard, axis, first, second):
        self.cube, self.shard, self.axis, self.first, self.second = cube, shard, axis, first, second
        self.cut = 1 - axis
        size = shard.shape[self.cut] // (2 if first is None else 4)
        at = cube.coordinate[second]
        if first is not None:
            at = 2 * at + cube.coordinate[first]
        self.part = lax.dynamic_slice_in_dim(shard, at * size, size, self.cut)

    def cross(self, *others):
        self.direct = self.cube.swap(after(self.part, *others), "x")
        return self.direct

    def hand_on(self, *others):
        self.direct = after(self.direct, *others)
        if self.first is None:
            self.half = self.direct
            self.rest = self.cube.swap(self.half, self.second)
            return self.rest
        self.handed = self.cube.swap(self.direct, self.first)
        return self.handed

    def finish(self, *others):
        cube = self.cube
        if self.first is not None:
            handed = after(self.handed, *others)
            self.half = cube.ordered(self.first, self.direct, handed, self.cut)
            self.rest = cube.swap(self.half, self.second)
        self.half_diagonal = cube.swap(self.half, "core")

    def weight(self, sibling, *others):
        rest = after(self.rest, *others)
        pieces = [
            (self.shard, 0, None), (sibling, 1, None), (self.half, 2, 0), (rest, 2, 1),
            (self.half_diagonal, 3, 0), (self.cube.swap(rest, "core"), 3, 1),
        ]
        return Weight(self.axis, pieces, self.second, 4)


class Reduce:
    def __init__(self, cube, keep, got, halves, gathers):
        rows, wide = keep.shape[2:]
        self.cube, self.shape = cube, (4, rows, wide)
        self.order = halves + tuple(range(2, cube.dims)) + gathers
        self.place = {"x": 0, 0: 1, 1: 2}
        self.terms = [t.reshape(2, 2, 2, rows, wide) for t in (keep, got)]
        self.index = 0
        self.done = False

    def sum(self, terms):
        if len(terms) == 1:
            return terms[0]
        return functools.reduce(jnp.add, [t.astype(F32) for t in terms]).astype(BF16)

    @staticmethod
    def land(pieces, other):
        got = lax.optimization_barrier((*(piece.terms[-1] for piece in pieces), other))
        for piece, value in zip(pieces, got):
            piece.terms[-1] = value

    def ready(self, *others):
        dim = self.order[self.index]
        if others:
            self.terms[-1] = after(self.terms[-1], *others)
        if self.index < 3:
            axis = self.place[dim]
            take = lambda i: [lax.slice_in_dim(t, i, i + 1, axis=axis) for t in self.terms]
            self.send, self.terms = self.sum(take(1)), take(0)
        else:
            self.send = self.sum(self.terms)
        return self.send

    def swap(self):
        dim = self.order[self.index]
        got = self.cube.swap(self.send, dim)
        self.index += 1
        if self.index <= 3:
            self.terms = self.terms + [got]
        elif self.index <= len(self.order) - 2:
            self.terms = [self.send, got]
        elif self.index < len(self.order):
            self.terms = [self.cube.ordered(dim, self.send, got, self.place[dim])]
        else:
            self.terms = [self.send, got]

    def finish(self, *others):
        self.done = True
        low, got = (after(value, *others) for value in self.terms)
        self.result = self.cube.ordered(self.order[-1], low, got, self.place[self.order[-1]])
        self.result = self.result.reshape(self.shape)
        return self.result


def per_device(
    tokens,
    segments,
    query_weight,
    key_weight,
    value_weight,
    output_weight,
    w_gate,
    w_up,
    w_down,
    attn_gain,
    ffn_gain,
    cotangent,
    replicas,
):
    cube = Cube(replicas)
    where = jnp.stack([cube.me] + [cube.coordinate[i] for i in range(3)]).astype(jnp.int32)
    x, dy = tokens.T, cotangent.T

    core = lambda value: cube.swap(value, "core")
    q_across = cube.swap(query_weight, "x")
    pad = jnp.zeros((OWN, GAINS - 2), BF16)
    kv = jnp.concatenate(
        [key_weight, value_weight, attn_gain[:, None], ffn_gain[:, None], pad], axis=1
    )
    kv_across = cube.swap(after(kv, q_across), "x")
    relays = [
        Relay(cube, w_gate, 0, 0, 1), Relay(cube, w_up, 0, 1, 0), Relay(cube, w_down.T, 1, None, 0)
    ]
    q_sibling, kv_sibling, wo_sibling = core(query_weight), core(kv), core(output_weight)
    siblings = [core(relay.shard) for relay in relays]
    cos, sin = tables(segments)
    early = [relay.part for relay in relays] + [cos, sin, where, q_sibling, kv_sibling, wo_sibling]
    q_across, kv_across = lax.optimization_barrier((q_across, kv_across, *early, *siblings))[:2]
    q_diagonal, kv_diagonal = core(q_across), core(kv_across)
    direct = [relay.cross(q_across, kv_across) for relay in relays]
    wq = rows_of(query_weight, q_sibling, q_across, q_diagonal)
    wk = rows_of(kv, kv_sibling, kv_across, kv_diagonal)
    qkv, h, gains = project(where, x, wq, wk, cos, sin)
    *first, done0 = attend(qkv, segments, 0)
    for relay in relays:
        relay.hand_on(done0)
    wo_across = cube.swap(after(output_weight, done0, *direct), "x")
    o, lse, done1 = attend(after(qkv, done0, *direct), segments, 1, first)
    for relay in relays:
        relay.finish(done1)
    wo_diagonal = core(after(wo_across, done1))
    wo = rows_of(output_weight, wo_sibling, wo_across, wo_diagonal)
    x1, h2 = middle(where, x, after(o, relays[0].half, relays[1].half), wo, gains)
    weights = [relay.weight(sibling, h2) for relay, sibling in zip(relays, siblings)]
    y, dh2, hid, dgate, dup = feed_forward(where, h2, dy, x1, weights)

    gd_keep, gd_send = ffn_grads(where, dy, hid, True)
    gd = Reduce(cube, gd_keep, core(gd_send), ("x", 0, 1), (1, 0))
    gg_keep, gg_send = ffn_grads(where, h2, after(dgate, gd_send), False)
    gg = Reduce(cube, gg_keep, core(gg_send), (0, "x", 1), (1, 0))
    gd.ready(gg_send)
    gu_keep, gu_send = ffn_grads(where, h2, after(dup, gd.send), False)
    gd.swap()
    gu = Reduce(cube, gu_keep, core(gu_send), (1, 0, "x"), (1, 0))
    gg.ready(gu_send)
    dx1, da, do, ffn_gain_grad = branch(where, after(dh2, gg.send), x1, dy, gains, wo)
    gg.swap()
    gu.ready(da)
    do0 = after(do, gu.send)
    gu.swap()
    *first, done0 = attend_back(qkv, o, do0, lse, segments, cos, sin, 0)
    Reduce.land((gd, gg), done0)
    do1 = after(do, done0, gd.ready(), gg.ready())
    gd.swap()
    gg.swap()
    dqkv, done1 = attend_back(qkv, o, do1, lse, segments, cos, sin, 1, first)
    swaps = [gd, gg, gu]
    Reduce.land(swaps, done1)
    dqkv = after(dqkv, *[piece.ready() for piece in swaps])
    for piece in swaps:
        piece.swap()
    parts = []
    weight_parts = weight_grads(where, h, dqkv, o, da)
    for i, halves in enumerate((("x", 0, 1), (0, "x", 1))):
        keep, send = weight_parts[2 * i:2 * i + 2]
        parts.append(Reduce(cube, keep, core(send), halves, (1, 0)))
    dqkv = after(dqkv, *[part.ready() for part in parts])
    for part in parts:
        part.swap()
    grad_x, attn_gain_grad = input_grads(where, x, dx1, wq, wk, dqkv)
    swaps = [gd, gg, gu] + parts
    Reduce.land(swaps, grad_x)
    both = jnp.concatenate([attn_gain_grad, ffn_gain_grad], axis=1).T.reshape(-1)
    ends = ["core", "x"] + list(range(cube.dims))
    token = grad_x
    while any(piece.index < len(piece.order) for piece in swaps):
        active = [piece for piece in swaps if piece.index < len(piece.order)]
        for piece in active:
            token = piece.ready(token, both)
            piece.swap()
        for piece in swaps:
            if piece not in active and not piece.done:
                token = piece.finish(token)
        if ends:
            both = both + after(cube.swap(both, ends.pop(0)), token)
    for piece in swaps:
        if not piece.done:
            token = piece.finish(token)
    for dim in ends:
        both = both + cube.swap(both, dim)
    both = lax.dynamic_slice_in_dim(both.reshape(2, D), cube.me * OWN, OWN, 1)
    flat = lambda g: jnp.concatenate([g[i] for i in range(4)], axis=1)
    ga = jnp.concatenate([flat(part.result) for part in parts], axis=0).astype(F32)
    return (
        y.T,
        grad_x.T,
        ga[:, :D],
        ga[:, D:D + KEYS],
        ga[:, D + KEYS:WIDE],
        ga[:, WIDE:],
        flat(gg.result).astype(F32),
        flat(gu.result).astype(F32),
        gd.result.reshape(D, CUT).T.astype(F32),
        both[0],
        both[1],
    )


def solution(mesh):
    rows = P(("group", "replica"), None)
    weight, gain = P("group", None), P("group")
    replicas = mesh.shape["replica"]
    return jax.shard_map(
        lambda *args: per_device(*args, replicas),
        mesh=mesh,
        in_specs=(rows, rows) + (weight,) * 7 + (gain, gain, rows),
        out_specs=(rows, rows) + (weight,) * 7 + (gain, gain),
        check_vma=False,
    )
```

```python
import functools

import jax
import jax.numpy as jnp
from jax import lax
from jax.experimental import pallas as pl
from jax.experimental.pallas import tpu as pltpu
from jax.sharding import PartitionSpec as P

D = 960
QUERY_HEADS = 15
KEY_VALUE_HEADS = 5
HEAD_WIDTH = 64
SHARE = QUERY_HEADS // KEY_VALUE_HEADS
HALF = HEAD_WIDTH // 2
KEYS = KEY_VALUE_HEADS * HEAD_WIDTH
EPS = 1e-05
THETA = 100000.0
TILE = 512
HALF_TILE = 256
QB = 128
GAINS = 128
WIDE = D + 2 * KEYS
CUT = 640
OWN = 240
PAIR = 2 * CUT
F32 = jnp.float32
BF16 = jnp.bfloat16
MIB = 1 << 20


def dot(a, b, ca, cb):
    return lax.dot_general(a, b, (((ca,), (cb,)), ((), ())), preferred_element_type=F32)


def params(limit, grid=1):
    return pltpu.CompilerParams(
        vmem_limit_bytes=limit * MIB, dimension_semantics=("arbitrary",) * grid
    )


def cost(*_):
    return pl.CostEstimate(flops=1, bytes_accessed=1, transcendentals=0)


def shaped(*shape_type):
    return [jax.ShapeDtypeStruct(s, t) for s, t in shape_type]


def norm_columns(v):
    inverse = lax.rsqrt(jnp.mean(v * v, axis=0, keepdims=True) + EPS)
    return v * inverse, inverse


def norm_columns_back(grad, normal, inverse, gain):
    scaled = grad * gain
    back = inverse * (scaled - normal * jnp.mean(scaled * normal, axis=0, keepdims=True))
    return back, jnp.sum(grad * normal, axis=1, keepdims=True)


def fixed(shape):
    return pl.BlockSpec(shape, lambda *_: (0,) * len(shape), pipeline_mode=pl.Buffered(1))


def columns(height, width):
    return pl.BlockSpec((height, width), lambda i: (0, i))


class Weight:
    def __init__(self, axis, pieces, dim=None, blocks=0):
        self.axis, self.dim, self.blocks = axis, dim, blocks
        self.arrays = [array for array, _, _ in pieces]
        self.places = [(flip, side) for _, flip, side in pieces]
        shape = list(self.arrays[0].shape)
        self.size = shape[axis]
        self.half = shape[1 - axis] // 2
        shape[axis] *= 4
        self.shape = tuple(shape)

    def specs(self):
        return [pl.BlockSpec(memory_space=pltpu.HBM)] * len(self.arrays)

    def scratch(self):
        if not self.blocks:
            return [pltpu.VMEM(self.shape, BF16), pltpu.SemaphoreType.DMA]
        block = (self.shape[0], self.shape[1] // self.blocks)
        return [pltpu.VMEM((self.blocks,) + block, BF16), pltpu.SemaphoreType.DMA((self.blocks,))]

    def load(self, where_ref, refs, scratch, sem):
        wide = self.shape[1] // max(self.blocks, 1)
        for ref, (flip, side) in zip(refs, self.places):
            at = (where_ref[0] ^ flip) * self.size
            other = 0 if side is None else (where_ref[1 + self.dim] ^ side) * self.half
            row, column = (at, other) if self.axis == 0 else (other, at)
            rows = pl.ds(pl.multiple_of(row, OWN), ref.shape[0])
            if not self.blocks:
                pltpu.make_async_copy(ref, scratch.at[rows, :], sem).start()
                continue
            first = column // wide
            for i in range(ref.shape[1] // wide):
                pltpu.make_async_copy(
                    ref.at[:, i * wide:(i + 1) * wide], scratch.at[first + i, rows, :],
                    sem.at[first + i],
                ).start()


def wait_for(scratch, sem):
    pltpu.make_async_copy(scratch, scratch, sem).wait()


SMEM = pl.BlockSpec(memory_space=pltpu.SMEM)


def project_kernel(weights, where_ref, x_ref, cos_ref, sin_ref, *refs):
    qkv_ref, h_ref, gains_ref, wq, q_sem, wk, k_sem = refs[8:]

    @pl.when(pl.program_id(0) == 0)
    def _():
        weights[0].load(where_ref, refs[:4], wq, q_sem)
        weights[1].load(where_ref, refs[4:8], wk, k_sem)
        wait_for(wq, q_sem)
        wait_for(wk, k_sem)
        gains_ref[...] = wk[:, 2 * KEYS:]

    gain = wk[:, 2 * KEYS:2 * KEYS + 1].astype(F32)
    normal, _ = norm_columns(x_ref[...].astype(F32))
    h = (normal * gain).astype(BF16)
    h_ref[...] = h
    c, s = cos_ref[...], sin_ref[...]

    def rotary(out, at, heads, scale):
        for head in range(heads):
            low = head * HEAD_WIDTH
            a, b = out[low:low + HALF], out[low + HALF:low + HEAD_WIDTH]
            to = at + low
            qkv_ref[to:to + HALF, :] = ((a * c - b * s) * scale).astype(BF16)
            qkv_ref[to + HALF:to + HEAD_WIDTH, :] = ((b * c + a * s) * scale).astype(BF16)

    rotary(dot(wq[...], h, 0, 0), 0, QUERY_HEADS, HEAD_WIDTH ** -0.5)
    out = dot(wk[:, :2 * KEYS], h, 0, 0)
    rotary(out, D, KEY_VALUE_HEADS, 1.0)
    qkv_ref[D + KEYS:, :] = out[KEYS:].astype(BF16)


def project(where, x, wq, wk, cos, sin):
    rows = x.shape[1]
    return pl.pallas_call(
        functools.partial(project_kernel, (wq, wk)),
        grid=(rows // TILE,),
        in_specs=[SMEM, columns(D, TILE), columns(HALF, TILE), columns(HALF, TILE)]
        + wq.specs() + wk.specs(),
        out_specs=[columns(WIDE, TILE), columns(D, TILE),
                   pl.BlockSpec((D, GAINS), lambda i: (0, 0))],
        out_shape=shaped(((WIDE, rows), BF16), ((D, rows), BF16), ((D, GAINS), BF16)),
        scratch_shapes=wq.scratch() + wk.scratch(),
        compiler_params=params(60),
        cost_estimate=cost(2 * rows * D * WIDE, rows * (2 * D + WIDE) * 2 + D * WIDE * 2),
        name="project",
    )(where, x, cos, sin, *wq.arrays, *wk.arrays)


def key_span(block):
    return max(0, QB * (block - 2)), QB * (block + 1)


def make_bias(bias_ref, segr_ref, segc_ref, length):
    for b in range(length // QB):
        lo, hi = key_span(b)
        key_at = lax.broadcasted_iota(jnp.int32, (hi - lo, QB), 0) + lo
        query_at = lax.broadcasted_iota(jnp.int32, (hi - lo, QB), 1) + b * QB
        ok = (segc_ref[lo:hi, :] == segr_ref[:, b * QB:(b + 1) * QB]) & (key_at <= query_at)
        bias_ref[b, 0:hi - lo, :] = jnp.where(ok, 0.0, -1e30)


def three(ref, kv, b):
    return jnp.concatenate(
        [
            ref[pl.ds(pl.multiple_of((kv * SHARE + i) * HEAD_WIDTH, HEAD_WIDTH), HEAD_WIDTH),
                b * QB:(b + 1) * QB]
            for i in range(SHARE)
        ],
        axis=1,
    )


def wide_bias(bias_ref, b, n):
    one = bias_ref[b, 0:n, :]
    return jnp.concatenate([one] * SHARE, axis=1)


def attend_kernel(qkv_ref, segr_ref, segc_ref, *refs):
    o_ref, lse_ref, done_ref, bias_ref = refs[-4:]
    done_ref[...] = jnp.zeros_like(done_ref)
    length = qkv_ref.shape[1]
    make_bias(bias_ref, segr_ref.at[0], segc_ref.at[0], length)

    @pl.loop(0, KEY_VALUE_HEADS)
    def _(kv):
        k = qkv_ref[pl.ds(pl.multiple_of(D + kv * HEAD_WIDTH, HEAD_WIDTH), HEAD_WIDTH), :]
        v = qkv_ref[pl.ds(pl.multiple_of(D + KEYS + kv * HEAD_WIDTH, HEAD_WIDTH), HEAD_WIDTH), :]
        for b in range(length // QB):
            lo, hi = key_span(b)
            s = dot(k[:, lo:hi], three(qkv_ref, kv, b), 0, 0) + wide_bias(bias_ref, b, hi - lo)
            top = jnp.max(s, axis=0, keepdims=True)
            p = jnp.exp(s - top)
            total = jnp.sum(p, axis=0, keepdims=True)
            out = dot(v[:, lo:hi], p.astype(BF16), 1, 0) / total
            lse = top + jnp.log(total)
            for i in range(SHARE):
                rows = pl.ds(pl.multiple_of((kv * SHARE + i) * HEAD_WIDTH, HEAD_WIDTH), HEAD_WIDTH)
                o_ref[rows, b * QB:(b + 1) * QB] = out[:, i * QB:(i + 1) * QB].astype(BF16)
                lse_ref[kv, i:i + 1, b * QB:(b + 1) * QB] = lse[:, i * QB:(i + 1) * QB]


DONE = jax.ShapeDtypeStruct((8, GAINS), F32)


def attend(qkv, segments, at, before=()):
    seqs, length = segments.shape
    wide, rows = qkv.shape
    return pl.pallas_call(
        attend_kernel,
        grid=(1,),
        in_specs=[
            pl.BlockSpec((wide, length), lambda i: (0, at)),
            pl.BlockSpec((1, 1, length), lambda i: (at, 0, 0)),
            pl.BlockSpec((1, length, 1), lambda i: (at, 0, 0)),
        ] + [pl.BlockSpec(memory_space=pltpu.HBM)] * len(before),
        out_specs=[
            pl.BlockSpec((D, length), lambda i: (0, at)),
            pl.BlockSpec((KEY_VALUE_HEADS, 8, length), lambda i: (0, 0, at)),
            fixed(DONE.shape),
        ],
        out_shape=shaped(((D, rows), BF16), ((KEY_VALUE_HEADS, 8, rows), F32)) + [DONE],
        input_output_aliases={3 + i: i for i in range(len(before))},
        scratch_shapes=[pltpu.VMEM((length // QB, 3 * QB, QB), F32)],
        compiler_params=params(60),
        cost_estimate=cost(),
        name="attend",
    )(qkv, segments[:, None, :], segments[:, :, None], *before)


def middle_kernel(weight, where_ref, x_ref, o_ref, gain_ref, *refs):
    x1_ref, h_ref, w, sem = refs[4:]

    @pl.when(pl.program_id(0) == 0)
    def _():
        weight.load(where_ref, refs[:4], w, sem)
        wait_for(w, sem)

    x1 = x_ref[...].astype(F32) + dot(w[...], o_ref[...], 0, 0)
    normal, _ = norm_columns(x1)
    x1_ref[...] = x1
    h_ref[...] = (normal * gain_ref[:, 1:2].astype(F32)).astype(BF16)


def middle(where, x, o, w, gains):
    rows = x.shape[1]
    return pl.pallas_call(
        functools.partial(middle_kernel, w),
        grid=(rows // TILE,),
        in_specs=[SMEM, columns(D, TILE), columns(D, TILE), fixed((D, GAINS))] + w.specs(),
        out_specs=[columns(D, TILE), columns(D, TILE)],
        out_shape=shaped(((D, rows), F32), ((D, rows), BF16)),
        scratch_shapes=w.scratch(),
        compiler_params=params(60),
        cost_estimate=cost(2 * rows * D * D, rows * D * 10),
        name="middle",
    )(where, x, o, gains, *w.arrays)


def feed_forward_kernel(weights, where_ref, h_ref, dy_ref, x1_ref, *refs):
    count = len(weights[0].arrays)
    y_ref, dh_ref, hid_ref, dgate_ref, dup_ref, acc_ref, acc_sem, *scratch = refs[3 * count:]
    step = pl.program_id(0)

    @pl.when(step == 0)
    def _():
        for i, weight in enumerate(weights):
            weight.load(where_ref, refs[i * count:(i + 1) * count], *scratch[2 * i:2 * i + 2])
        pltpu.make_async_copy(x1_ref, acc_ref, acc_sem).start()
        dh_ref[...] = jnp.zeros_like(dh_ref)
        pltpu.make_async_copy(x1_ref, acc_ref, acc_sem).wait()

    wg_ref, wu_ref, wd_ref = (w.at[step] for w in scratch[::2])
    for w, sem in zip((wg_ref, wu_ref, wd_ref), scratch[1::2]):
        wait_for(w, sem.at[step])
    h, dy = h_ref[...], dy_ref[...]
    gate = dot(wg_ref[...], h, 0, 0)
    up = dot(wu_ref[...], h, 0, 0)
    dhid = dot(wd_ref[...], dy, 0, 0)
    sig = jax.nn.sigmoid(gate)
    silu = gate * sig
    hid = (silu * up).astype(BF16)
    dgate = (dhid * up * (sig + silu * (1.0 - sig))).astype(BF16)
    dup = (dhid * silu).astype(BF16)
    hid_ref[...] = hid
    dgate_ref[...] = dgate
    dup_ref[...] = dup
    acc_ref[...] += dot(wd_ref[...], hid, 1, 0)
    dh_ref[...] += dot(wg_ref[...], dgate, 1, 0) + dot(wu_ref[...], dup, 1, 0)

    @pl.when(step == pl.num_programs(0) - 1)
    def _():
        y_ref[...] = acc_ref[...].astype(BF16)


def feed_forward(where, h, dy, x1, weights):
    rows, hidden = h.shape[1], weights[0].shape[1]
    block = pl.BlockSpec((CUT, rows), lambda f: (f, 0))
    return pl.pallas_call(
        functools.partial(feed_forward_kernel, weights),
        grid=(hidden // CUT,),
        in_specs=[SMEM, fixed((D, rows)), fixed((D, rows)), pl.BlockSpec(memory_space=pltpu.HBM)]
        + sum((w.specs() for w in weights), []),
        out_specs=[fixed((D, rows)), fixed((D, rows))] + [block] * 3,
        out_shape=shaped(((D, rows), BF16), ((D, rows), F32)) + shaped(((hidden, rows), BF16)) * 3,
        scratch_shapes=sum(
            (w.scratch() for w in weights), [pltpu.VMEM((D, rows), F32), pltpu.SemaphoreType.DMA]
        ),
        compiler_params=params(60),
        cost_estimate=cost(),
        name="feed_forward",
    )(where, h, dy, x1, *sum((w.arrays for w in weights), []))


def block_here(where_ref):
    return 2 * where_ref[1] + where_ref[2]


def split_owners(grad, where_ref, put):
    core, x_here = where_ref[0] & 1, where_ref[0] >> 1
    for x in range(2):
        a = grad[2 * x * OWN:(2 * x + 1) * OWN].astype(BF16)
        b = grad[(2 * x + 1) * OWN:(2 * x + 2) * OWN].astype(BF16)
        put(x_here ^ x, jnp.where(core == 0, a, b), jnp.where(core == 0, b, a))


def row_grads_kernel(where_ref, a_ref, b_ref, keep_ref, send_ref):
    grad = dot(a_ref[...], b_ref[...], 1, 1)
    for i in range(2):
        def put(x, keep, send):
            keep_ref[x, i ^ where_ref[2]] = keep
            send_ref[x, i ^ where_ref[2]] = send

        split_owners(grad[:, i * CUT:(i + 1) * CUT], where_ref, put)


def column_grads_kernel(where_ref, a_ref, b_ref, keep_ref, send_ref):
    grad = dot(a_ref[...], b_ref[...], 1, 1).astype(BF16)
    first = (where_ref[0] & 1) == 0
    for i in range(4):
        at = block_here(where_ref) ^ i
        a, b = grad[i * OWN:(i + 1) * OWN, :CUT], grad[i * OWN:(i + 1) * OWN, CUT:]
        keep_ref[0, at] = jnp.where(first, a, b)
        send_ref[0, at] = jnp.where(first, b, a)


def ffn_grads(where, a, b, by_columns):
    rows = a.shape[1]
    if by_columns:
        kernel = column_grads_kernel
        out = pl.BlockSpec((1, 4, OWN, CUT), lambda f, at: (f ^ (at[0] >> 1), 0, 0, 0))
    else:
        kernel = row_grads_kernel
        out = pl.BlockSpec((2, 2, OWN, CUT), lambda f, at: (0, f ^ at[1], 0, 0))
    return pl.pallas_call(
        kernel,
        grid_spec=pltpu.PrefetchScalarGridSpec(
            num_scalar_prefetch=1,
            grid=(b.shape[0] // PAIR,),
            in_specs=[fixed((D, rows)), pl.BlockSpec((PAIR, rows), lambda f, at: (f, 0))],
            out_specs=[out, out],
        ),
        out_shape=shaped(((2, 4, OWN, CUT), BF16)) * 2,
        compiler_params=params(60),
        cost_estimate=cost(),
        name="ffn_grads",
    )(where, a, b)


def branch_kernel(weight, where_ref, dh_ref, x1_ref, dy_ref, gain_ref, *refs):
    dx_ref, da_ref, do_ref, gain_grad, w, sem = refs[4:]
    first = pl.program_id(0) == 0

    @pl.when(first)
    def _():
        weight.load(where_ref, refs[:4], w, sem)

    gain = gain_ref[:, 1:2].astype(F32)
    normal, inverse = norm_columns(x1_ref[...])
    back, part = norm_columns_back(dh_ref[...], normal, inverse, gain)
    dx = dy_ref[...].astype(F32) + back
    da = dx.astype(BF16)
    dx_ref[...] = dx
    da_ref[...] = da

    @pl.when(first)
    def _():
        gain_grad[...] = part
        wait_for(w, sem)

    @pl.when(jnp.logical_not(first))
    def _():
        gain_grad[...] += part

    do_ref[...] = dot(w[...], da, 1, 0).astype(BF16)


def branch(where, dh, x1, dy, gains, w):
    rows = dh.shape[1]
    return pl.pallas_call(
        functools.partial(branch_kernel, w),
        grid=(rows // TILE,),
        in_specs=[SMEM] + [columns(D, TILE)] * 3 + [fixed((D, GAINS))] + w.specs(),
        out_specs=[columns(D, TILE)] * 3 + [pl.BlockSpec((D, 1), lambda i: (0, 0))],
        out_shape=shaped(((D, rows), F32), ((D, rows), BF16), ((D, rows), BF16), ((D, 1), F32)),
        scratch_shapes=w.scratch(),
        compiler_params=params(60),
        cost_estimate=cost(2 * rows * D * D, rows * D * 18),
        name="branch",
    )(where, dh, x1, dy, gains, *w.arrays)


def attend_back_kernel(qkv_ref, o_ref, do_ref, lse_ref, segr_ref, segc_ref, cos_ref, sin_ref,
                       *refs):
    out_ref, done_ref, bias_ref, dk_ref, dv_ref = refs[-5:]
    done_ref[...] = jnp.zeros_like(done_ref)
    length = qkv_ref.shape[1]
    make_bias(bias_ref, segr_ref.at[0], segc_ref.at[0], length)

    def turn_back(g, c, s, at, cols):
        a, b = g[:HALF], g[HALF:]
        at = pl.multiple_of(at, HEAD_WIDTH)
        out_ref[pl.ds(at, HALF), cols] = (a * c + b * s).astype(BF16)
        out_ref[pl.ds(pl.multiple_of(at + HALF, HALF), HALF), cols] = (b * c - a * s).astype(BF16)

    @pl.loop(0, KEY_VALUE_HEADS)
    def _(kv):
        k = qkv_ref[pl.ds(pl.multiple_of(D + kv * HEAD_WIDTH, HEAD_WIDTH), HEAD_WIDTH), :]
        v = qkv_ref[pl.ds(pl.multiple_of(D + KEYS + kv * HEAD_WIDTH, HEAD_WIDTH), HEAD_WIDTH), :]
        dk_ref[...] = jnp.zeros_like(dk_ref)
        dv_ref[...] = jnp.zeros_like(dv_ref)
        for b in range(length // QB):
            lo, hi = key_span(b)
            cols = slice(b * QB, (b + 1) * QB)
            q, o, do = three(qkv_ref, kv, b), three(o_ref, kv, b), three(do_ref, kv, b)
            lse = jnp.concatenate([lse_ref[kv, i:i + 1, cols] for i in range(SHARE)], axis=1)
            inner = jnp.sum(o.astype(F32) * do.astype(F32), axis=0, keepdims=True)
            s = dot(k[:, lo:hi], q, 0, 0) + wide_bias(bias_ref, b, hi - lo)
            p = jnp.exp(s - lse)
            dp = dot(v[:, lo:hi], do, 0, 0)
            ds = (p * (dp - inner)).astype(BF16)
            dv_ref[:, lo:hi] += dot(do, p.astype(BF16), 1, 1)
            dk_ref[:, lo:hi] += dot(q, ds, 1, 1)
            dq = dot(k[:, lo:hi], ds, 1, 0) * HEAD_WIDTH ** -0.5
            for i in range(SHARE):
                turn_back(dq[:, i * QB:(i + 1) * QB], cos_ref[:, cols], sin_ref[:, cols],
                          (kv * SHARE + i) * HEAD_WIDTH, cols)
        turn_back(dk_ref[...], cos_ref[...], sin_ref[...], D + kv * HEAD_WIDTH, slice(None))
        out_ref[pl.ds(pl.multiple_of(D + KEYS + kv * HEAD_WIDTH, HEAD_WIDTH), HEAD_WIDTH), :] = (
            dv_ref[...].astype(BF16))


def attend_back(qkv, o, do, lse, segments, cos, sin, at, before=()):
    length = segments.shape[1]
    wide, rows = qkv.shape
    here = lambda height: pl.BlockSpec((height, length), lambda i: (0, at))
    return pl.pallas_call(
        attend_back_kernel,
        grid=(1,),
        in_specs=[
            here(wide),
            here(D),
            here(D),
            pl.BlockSpec((KEY_VALUE_HEADS, 8, length), lambda i: (0, 0, at)),
            pl.BlockSpec((1, 1, length), lambda i: (at, 0, 0)),
            pl.BlockSpec((1, length, 1), lambda i: (at, 0, 0)),
            here(HALF),
            here(HALF),
        ] + [pl.BlockSpec(memory_space=pltpu.HBM)] * len(before),
        out_specs=[here(wide), fixed(DONE.shape)],
        out_shape=shaped(((wide, rows), BF16)) + [DONE],
        input_output_aliases={8 + i: i for i in range(len(before))},
        scratch_shapes=[
            pltpu.VMEM((length // QB, 3 * QB, QB), F32),
            pltpu.VMEM((HEAD_WIDTH, length), F32),
            pltpu.VMEM((HEAD_WIDTH, length), F32),
        ],
        compiler_params=params(60),
        cost_estimate=cost(),
        name="attend_back",
    )(qkv, o, do, lse, segments[:, None, :], segments[:, :, None], cos, sin, *before)


PIECES = ((0, 128), (128, OWN))


def weight_kernel(where_ref, h_ref, dqkv_ref, o_ref, da_ref, *out_refs):
    def store(block, grad):
        def put(x, keep, send):
            for i, (low, high) in enumerate(PIECES):
                at = block ^ block_here(where_ref)
                out_refs[2 * i][x, at] = keep[low:high]
                out_refs[2 * i + 1][x, at] = send[low:high]

        split_owners(grad, where_ref, put)

    grad = dot(h_ref[...], dqkv_ref[:PAIR, :], 1, 1)
    store(0, grad[:, :CUT])
    store(1, grad[:, CUT:])
    left = dot(h_ref[...], dqkv_ref[2 * CUT:, :], 1, 1)
    right = dot(o_ref[...], da_ref[:3 * CUT - WIDE, :], 1, 1)
    store(2, jnp.concatenate([left, right], axis=1))
    store(3, dot(o_ref[...], da_ref[3 * CUT - WIDE:, :], 1, 1))


def weight_grads(where, h, dqkv, o, da):
    rows = h.shape[1]
    shapes = [(2, 4, high - low, CUT) for low, high in PIECES for _ in range(2)]
    return pl.pallas_call(
        weight_kernel,
        grid=(1,),
        in_specs=[SMEM, fixed((D, rows)), fixed((WIDE, rows)), fixed((D, rows)), fixed((D, rows))],
        out_specs=[fixed(shape) for shape in shapes],
        out_shape=shaped(*((shape, BF16) for shape in shapes)),
        compiler_params=params(60),
        cost_estimate=cost(),
        name="weight_grads",
    )(where, h, dqkv, o, da)


def inputs_kernel(weights, where_ref, x_ref, dx_ref, dqkv_ref, *refs):
    out_ref, gain_grad, wq, q_sem, wk, k_sem = refs[8:]
    first = pl.program_id(0) == 0

    @pl.when(first)
    def _():
        weights[0].load(where_ref, refs[:4], wq, q_sem)
        weights[1].load(where_ref, refs[4:8], wk, k_sem)
        wait_for(wq, q_sem)
        wait_for(wk, k_sem)

    gain = wk[:, 2 * KEYS:2 * KEYS + 1].astype(F32)
    dh = dot(wq[...], dqkv_ref[:D], 1, 0) + dot(wk[:, :2 * KEYS], dqkv_ref[D:], 1, 0)
    normal, inverse = norm_columns(x_ref[...].astype(F32))
    back, part = norm_columns_back(dh, normal, inverse, gain)
    out_ref[...] = (dx_ref[...] + back).astype(BF16)

    @pl.when(first)
    def _():
        gain_grad[...] = part

    @pl.when(jnp.logical_not(first))
    def _():
        gain_grad[...] += part


def input_grads(where, x, dx, wq, wk, dqkv):
    rows = x.shape[1]
    return pl.pallas_call(
        functools.partial(inputs_kernel, (wq, wk)),
        grid=(rows // HALF_TILE,),
        in_specs=[SMEM, columns(D, HALF_TILE), columns(D, HALF_TILE), columns(WIDE, HALF_TILE)]
        + wq.specs() + wk.specs(),
        out_specs=[columns(D, HALF_TILE), pl.BlockSpec((D, 1), lambda i: (0, 0))],
        out_shape=shaped(((D, rows), BF16), ((D, 1), F32)),
        scratch_shapes=wq.scratch() + wk.scratch(),
        compiler_params=params(60),
        cost_estimate=cost(2 * rows * D * WIDE, rows * (D * 8 + WIDE * 2) + D * WIDE * 2),
        name="input_grads",
    )(where, x, dx, dqkv, *wq.arrays, *wk.arrays)


def tables(segments):
    length = segments.shape[1]
    index = jnp.arange(length, dtype=jnp.int32)
    same = segments[:, :, None] == segments[:, None, :]
    start = jnp.min(jnp.where(same, index[None, :, None], length), axis=1)
    position = (index[None, :] - start).astype(F32).reshape(1, -1)
    freq = THETA ** (-(jnp.arange(HALF, dtype=F32) * 2.0 / HEAD_WIDTH))
    angle = freq[:, None] * position
    return jnp.cos(angle), jnp.sin(angle)


def after(value, *others):
    return lax.optimization_barrier((value,) + others)[0]


class Cube:
    def __init__(self, count):
        self.count = count
        self.dims = count.bit_length() - 1
        replica, group = lax.axis_index("replica"), lax.axis_index("group")
        self.coordinate = {i: (replica >> i) & 1 for i in range(self.dims)}
        self.coordinate["x"] = group >> 1
        self.coordinate["core"] = group & 1
        self.me = group

    def swap(self, value, dim):
        if dim == "x":
            return lax.ppermute(value, "group", [(i, i ^ 2) for i in range(4)])
        if dim == "core":
            return lax.ppermute(value, "group", [(i, i ^ 1) for i in range(4)])
        return lax.ppermute(value, "replica", [(i, i ^ (1 << dim)) for i in range(self.count)])

    def ordered(self, dim, mine, other, axis):
        return jnp.where(
            self.coordinate[dim] == 0,
            jnp.concatenate([mine, other], axis=axis),
            jnp.concatenate([other, mine], axis=axis),
        )


def rows_of(own, sibling, across, diagonal):
    pieces = own, sibling, across, diagonal
    return Weight(0, [(array, flip, None) for flip, array in enumerate(pieces)])


class Relay:
    def __init__(self, cube, shard, axis, first, second):
        self.cube, self.shard, self.axis, self.first, self.second = cube, shard, axis, first, second
        self.cut = 1 - axis
        size = shard.shape[self.cut] // (2 if first is None else 4)
        at = cube.coordinate[second]
        if first is not None:
            at = 2 * at + cube.coordinate[first]
        self.part = lax.dynamic_slice_in_dim(shard, at * size, size, self.cut)

    def cross(self, *others):
        self.direct = self.cube.swap(after(self.part, *others), "x")
        return self.direct

    def hand_on(self, *others):
        self.direct = after(self.direct, *others)
        if self.first is None:
            self.half = self.direct
            self.rest = self.cube.swap(self.half, self.second)
            return self.rest
        self.handed = self.cube.swap(self.direct, self.first)
        return self.handed

    def finish(self, *others):
        cube = self.cube
        if self.first is not None:
            handed = after(self.handed, *others)
            self.half = cube.ordered(self.first, self.direct, handed, self.cut)
            self.rest = cube.swap(self.half, self.second)
        self.half_diagonal = cube.swap(self.half, "core")

    def weight(self, sibling, *others):
        rest = after(self.rest, *others)
        pieces = [
            (self.shard, 0, None), (sibling, 1, None), (self.half, 2, 0), (rest, 2, 1),
            (self.half_diagonal, 3, 0), (self.cube.swap(rest, "core"), 3, 1),
        ]
        return Weight(self.axis, pieces, self.second, 4)


class Reduce:
    def __init__(self, cube, keep, got, halves, gathers):
        rows, wide = keep.shape[2:]
        self.cube, self.shape = cube, (4, rows, wide)
        self.order = halves + tuple(range(2, cube.dims)) + gathers
        self.place = {"x": 0, 0: 1, 1: 2}
        self.terms = [t.reshape(2, 2, 2, rows, wide) for t in (keep, got)]
        self.index = 0
        self.done = False

    def sum(self, terms):
        if len(terms) == 1:
            return terms[0]
        return functools.reduce(jnp.add, [t.astype(F32) for t in terms]).astype(BF16)

    @staticmethod
    def land(pieces, other):
        got = lax.optimization_barrier((*(piece.terms[-1] for piece in pieces), other))
        for piece, value in zip(pieces, got):
            piece.terms[-1] = value

    def ready(self, *others):
        dim = self.order[self.index]
        if others:
            self.terms[-1] = after(self.terms[-1], *others)
        if self.index < 3:
            axis = self.place[dim]
            take = lambda i: [lax.slice_in_dim(t, i, i + 1, axis=axis) for t in self.terms]
            self.send, self.terms = self.sum(take(1)), take(0)
        else:
            self.send = self.sum(self.terms)
        return self.send

    def swap(self):
        dim = self.order[self.index]
        got = self.cube.swap(self.send, dim)
        self.index += 1
        if self.index <= 3:
            self.terms = self.terms + [got]
        elif self.index <= len(self.order) - 2:
            self.terms = [self.send, got]
        elif self.index < len(self.order):
            self.terms = [self.cube.ordered(dim, self.send, got, self.place[dim])]
        else:
            self.terms = [self.send, got]

    def finish(self, *others):
        self.done = True
        low, got = (after(value, *others) for value in self.terms)
        self.result = self.cube.ordered(self.order[-1], low, got, self.place[self.order[-1]])
        self.result = self.result.reshape(self.shape)
        return self.result


def per_device(
    tokens,
    segments,
    query_weight,
    key_weight,
    value_weight,
    output_weight,
    w_gate,
    w_up,
    w_down,
    attn_gain,
    ffn_gain,
    cotangent,
    replicas,
):
    cube = Cube(replicas)
    where = jnp.stack([cube.me] + [cube.coordinate[i] for i in range(3)]).astype(jnp.int32)
    x, dy = tokens.T, cotangent.T

    core = lambda value: cube.swap(value, "core")
    q_across = cube.swap(query_weight, "x")
    pad = jnp.zeros((OWN, GAINS - 2), BF16)
    kv = jnp.concatenate(
        [key_weight, value_weight, attn_gain[:, None], ffn_gain[:, None], pad], axis=1
    )
    kv_across = cube.swap(after(kv, q_across), "x")
    relays = [
        Relay(cube, w_gate, 0, 0, 1), Relay(cube, w_up, 0, 1, 0), Relay(cube, w_down.T, 1, None, 0)
    ]
    q_sibling, kv_sibling, wo_sibling = core(query_weight), core(kv), core(output_weight)
    siblings = [core(relay.shard) for relay in relays]
    cos, sin = tables(segments)
    early = [relay.part for relay in relays] + [cos, sin, where, q_sibling, kv_sibling, wo_sibling]
    q_across, kv_across = lax.optimization_barrier((q_across, kv_across, *early, *siblings))[:2]
    q_diagonal, kv_diagonal = core(q_across), core(kv_across)
    direct = [relay.cross(q_across, kv_across) for relay in relays]
    wq = rows_of(query_weight, q_sibling, q_across, q_diagonal)
    wk = rows_of(kv, kv_sibling, kv_across, kv_diagonal)
    qkv, h, gains = project(where, x, wq, wk, cos, sin)
    *first, done0 = attend(qkv, segments, 0)
    for relay in relays:
        relay.hand_on(done0)
    wo_across = cube.swap(after(output_weight, done0, *direct), "x")
    o, lse, done1 = attend(after(qkv, done0, *direct), segments, 1, first)
    for relay in relays:
        relay.finish(done1)
    wo_diagonal = core(after(wo_across, done1))
    wo = rows_of(output_weight, wo_sibling, wo_across, wo_diagonal)
    x1, h2 = middle(where, x, after(o, relays[0].half, relays[1].half), wo, gains)
    weights = [relay.weight(sibling, h2) for relay, sibling in zip(relays, siblings)]
    y, dh2, hid, dgate, dup = feed_forward(where, h2, dy, x1, weights)

    gd_keep, gd_send = ffn_grads(where, dy, hid, True)
    gd = Reduce(cube, gd_keep, core(gd_send), ("x", 0, 1), (1, 0))
    gg_keep, gg_send = ffn_grads(where, h2, after(dgate, gd_send), False)
    gg = Reduce(cube, gg_keep, core(gg_send), (0, "x", 1), (1, 0))
    gd.ready(gg_send)
    gu_keep, gu_send = ffn_grads(where, h2, after(dup, gd.send), False)
    gd.swap()
    gu = Reduce(cube, gu_keep, core(gu_send), (1, 0, "x"), (1, 0))
    gg.ready(gu_send)
    dx1, da, do, ffn_gain_grad = branch(where, after(dh2, gg.send), x1, dy, gains, wo)
    gg.swap()
    gu.ready(da)
    do0 = after(do, gu.send)
    gu.swap()
    *first, done0 = attend_back(qkv, o, do0, lse, segments, cos, sin, 0)
    Reduce.land((gd, gg), done0)
    do1 = after(do, done0, gd.ready(), gg.ready())
    gd.swap()
    gg.swap()
    dqkv, done1 = attend_back(qkv, o, do1, lse, segments, cos, sin, 1, first)
    swaps = [gd, gg, gu]
    Reduce.land(swaps, done1)
    dqkv = after(dqkv, *[piece.ready() for piece in swaps])
    for piece in swaps:
        piece.swap()
    parts = []
    *got, keep0, send0, keep1, send1 = lax.optimization_barrier(
        (*(piece.terms[-1] for piece in swaps), *weight_grads(where, h, dqkv, o, da))
    )
    for piece, value in zip(swaps, got):
        piece.terms[-1] = value
    for keep, send, halves in ((keep0, send0, ("x", 0, 1)), (keep1, send1, (0, "x", 1))):
        parts.append(Reduce(cube, keep, core(send), halves, (1, 0)))
    dqkv = after(dqkv, *[piece.ready() for piece in swaps + parts])
    for piece in swaps + parts:
        piece.swap()
    grad_x, attn_gain_grad = input_grads(where, x, dx1, wq, wk, dqkv)
    Reduce.land(parts + [gu], grad_x)
    swaps = parts + [gd, gg, gu]
    both = jnp.concatenate([attn_gain_grad, ffn_gain_grad], axis=1).T.reshape(-1)
    ends = ["core", "x"] + list(range(cube.dims))
    token = grad_x
    for piece in parts + [gu]:
        token = piece.ready(token)
        piece.swap()
    while any(piece.index < len(piece.order) for piece in swaps):
        active = [piece for piece in swaps if piece.index < len(piece.order)]
        for piece in active:
            token = piece.ready(token, both)
            piece.swap()
        for piece in swaps:
            if piece not in active and not piece.done:
                token = piece.finish(token)
        if ends:
            both = both + after(cube.swap(both, ends.pop(0)), token)
    for piece in swaps:
        if not piece.done:
            token = piece.finish(token)
    for dim in ends:
        both = both + cube.swap(both, dim)
    both = lax.dynamic_slice_in_dim(both.reshape(2, D), cube.me * OWN, OWN, 1)
    flat = lambda g: jnp.concatenate([g[i] for i in range(4)], axis=1)
    ga = jnp.concatenate([flat(part.result) for part in parts], axis=0).astype(F32)
    return (
        y.T,
        grad_x.T,
        ga[:, :D],
        ga[:, D:D + KEYS],
        ga[:, D + KEYS:WIDE],
        ga[:, WIDE:],
        flat(gg.result).astype(F32),
        flat(gu.result).astype(F32),
        gd.result.reshape(D, CUT).T.astype(F32),
        both[0],
        both[1],
    )


def solution(mesh):
    rows = P(("group", "replica"), None)
    weight, gain = P("group", None), P("group")
    replicas = mesh.shape["replica"]
    return jax.shard_map(
        lambda *args: per_device(*args, replicas),
        mesh=mesh,
        in_specs=(rows, rows) + (weight,) * 7 + (gain, gain, rows),
        out_specs=(rows, rows) + (weight,) * 7 + (gain, gain),
        check_vma=False,
    )
```

```python
import functools

import jax
import jax.numpy as jnp
from jax import lax
from jax.experimental import pallas as pl
from jax.experimental.pallas import tpu as pltpu
from jax.sharding import PartitionSpec as P

D = 960
QUERY_HEADS = 15
KEY_VALUE_HEADS = 5
HEAD_WIDTH = 64
SHARE = QUERY_HEADS // KEY_VALUE_HEADS
HALF = HEAD_WIDTH // 2
KEYS = KEY_VALUE_HEADS * HEAD_WIDTH
EPS = 1e-05
THETA = 100000.0
TILE = 512
HALF_TILE = 256
QB = 128
GAINS = 128
WIDE = D + 2 * KEYS
CUT = 640
OWN = 240
PAIR = 2 * CUT
F32 = jnp.float32
BF16 = jnp.bfloat16
MIB = 1 << 20


def dot(a, b, ca, cb):
    return lax.dot_general(a, b, (((ca,), (cb,)), ((), ())), preferred_element_type=F32)


def params(limit, grid=1):
    return pltpu.CompilerParams(
        vmem_limit_bytes=limit * MIB, dimension_semantics=("arbitrary",) * grid
    )


def cost(*_):
    return pl.CostEstimate(flops=1, bytes_accessed=1, transcendentals=0)


def shaped(*shape_type):
    return [jax.ShapeDtypeStruct(s, t) for s, t in shape_type]


def norm_columns(v):
    inverse = lax.rsqrt(jnp.mean(v * v, axis=0, keepdims=True) + EPS)
    return v * inverse, inverse


def norm_columns_back(grad, normal, inverse, gain):
    scaled = grad * gain
    back = inverse * (scaled - normal * jnp.mean(scaled * normal, axis=0, keepdims=True))
    return back, jnp.sum(grad * normal, axis=1, keepdims=True)


def fixed(shape):
    return pl.BlockSpec(shape, lambda *_: (0,) * len(shape), pipeline_mode=pl.Buffered(1))


def columns(height, width):
    return pl.BlockSpec((height, width), lambda i: (0, i))


class Weight:
    def __init__(self, axis, pieces, dim=None, blocks=0):
        self.axis, self.dim, self.blocks = axis, dim, blocks
        self.arrays = [array for array, _, _ in pieces]
        self.places = [(flip, side) for _, flip, side in pieces]
        shape = list(self.arrays[0].shape)
        self.size = shape[axis]
        self.half = shape[1 - axis] // 2
        shape[axis] *= 4
        self.shape = tuple(shape)

    def specs(self):
        return [pl.BlockSpec(memory_space=pltpu.HBM)] * len(self.arrays)

    def scratch(self):
        if not self.blocks:
            return [pltpu.VMEM(self.shape, BF16), pltpu.SemaphoreType.DMA]
        block = (self.shape[0], self.shape[1] // self.blocks)
        return [pltpu.VMEM((self.blocks,) + block, BF16), pltpu.SemaphoreType.DMA((self.blocks,))]

    def load(self, where_ref, refs, scratch, sem):
        wide = self.shape[1] // max(self.blocks, 1)
        for ref, (flip, side) in zip(refs, self.places):
            at = (where_ref[0] ^ flip) * self.size
            other = 0 if side is None else (where_ref[1 + self.dim] ^ side) * self.half
            row, column = (at, other) if self.axis == 0 else (other, at)
            rows = pl.ds(pl.multiple_of(row, OWN), ref.shape[0])
            if not self.blocks:
                pltpu.make_async_copy(ref, scratch.at[rows, :], sem).start()
                continue
            first = column // wide
            for i in range(ref.shape[1] // wide):
                pltpu.make_async_copy(
                    ref.at[:, i * wide:(i + 1) * wide], scratch.at[first + i, rows, :],
                    sem.at[first + i],
                ).start()


def wait_for(scratch, sem):
    pltpu.make_async_copy(scratch, scratch, sem).wait()


SMEM = pl.BlockSpec(memory_space=pltpu.SMEM)


def project_kernel(weights, where_ref, x_ref, cos_ref, sin_ref, *refs):
    qkv_ref, h_ref, gains_ref, wq, q_sem, wk, k_sem = refs[8:]

    @pl.when(pl.program_id(0) == 0)
    def _():
        weights[0].load(where_ref, refs[:4], wq, q_sem)
        weights[1].load(where_ref, refs[4:8], wk, k_sem)
        wait_for(wq, q_sem)
        wait_for(wk, k_sem)
        gains_ref[...] = wk[:, 2 * KEYS:]

    gain = wk[:, 2 * KEYS:2 * KEYS + 1].astype(F32)
    normal, _ = norm_columns(x_ref[...].astype(F32))
    h = (normal * gain).astype(BF16)
    h_ref[...] = h
    c, s = cos_ref[...], sin_ref[...]

    def rotary(out, at, heads, scale):
        for head in range(heads):
            low = head * HEAD_WIDTH
            a, b = out[low:low + HALF], out[low + HALF:low + HEAD_WIDTH]
            to = at + low
            qkv_ref[to:to + HALF, :] = ((a * c - b * s) * scale).astype(BF16)
            qkv_ref[to + HALF:to + HEAD_WIDTH, :] = ((b * c + a * s) * scale).astype(BF16)

    rotary(dot(wq[...], h, 0, 0), 0, QUERY_HEADS, HEAD_WIDTH ** -0.5)
    out = dot(wk[:, :2 * KEYS], h, 0, 0)
    rotary(out, D, KEY_VALUE_HEADS, 1.0)
    qkv_ref[D + KEYS:, :] = out[KEYS:].astype(BF16)


def project(where, x, wq, wk, cos, sin):
    rows = x.shape[1]
    return pl.pallas_call(
        functools.partial(project_kernel, (wq, wk)),
        grid=(rows // TILE,),
        in_specs=[SMEM, columns(D, TILE), columns(HALF, TILE), columns(HALF, TILE)]
        + wq.specs() + wk.specs(),
        out_specs=[columns(WIDE, TILE), columns(D, TILE),
                   pl.BlockSpec((D, GAINS), lambda i: (0, 0))],
        out_shape=shaped(((WIDE, rows), BF16), ((D, rows), BF16), ((D, GAINS), BF16)),
        scratch_shapes=wq.scratch() + wk.scratch(),
        compiler_params=params(60),
        cost_estimate=cost(2 * rows * D * WIDE, rows * (2 * D + WIDE) * 2 + D * WIDE * 2),
        name="project",
    )(where, x, cos, sin, *wq.arrays, *wk.arrays)


def key_span(block):
    return max(0, QB * (block - 2)), QB * (block + 1)


def make_bias(bias_ref, segr_ref, segc_ref, length):
    for b in range(length // QB):
        lo, hi = key_span(b)
        key_at = lax.broadcasted_iota(jnp.int32, (hi - lo, QB), 0) + lo
        query_at = lax.broadcasted_iota(jnp.int32, (hi - lo, QB), 1) + b * QB
        ok = (segc_ref[lo:hi, :] == segr_ref[:, b * QB:(b + 1) * QB]) & (key_at <= query_at)
        bias_ref[b, 0:hi - lo, :] = jnp.where(ok, 0.0, -1e30)


def three(ref, kv, b):
    return jnp.concatenate(
        [
            ref[pl.ds(pl.multiple_of((kv * SHARE + i) * HEAD_WIDTH, HEAD_WIDTH), HEAD_WIDTH),
                b * QB:(b + 1) * QB]
            for i in range(SHARE)
        ],
        axis=1,
    )


def wide_bias(bias_ref, b, n):
    one = bias_ref[b, 0:n, :]
    return jnp.concatenate([one] * SHARE, axis=1)


def attend_kernel(qkv_ref, segr_ref, segc_ref, *refs):
    o_ref, lse_ref, done_ref, bias_ref = refs[-4:]
    done_ref[...] = jnp.zeros_like(done_ref)
    length = qkv_ref.shape[1]
    make_bias(bias_ref, segr_ref.at[0], segc_ref.at[0], length)

    @pl.loop(0, KEY_VALUE_HEADS)
    def _(kv):
        k = qkv_ref[pl.ds(pl.multiple_of(D + kv * HEAD_WIDTH, HEAD_WIDTH), HEAD_WIDTH), :]
        v = qkv_ref[pl.ds(pl.multiple_of(D + KEYS + kv * HEAD_WIDTH, HEAD_WIDTH), HEAD_WIDTH), :]
        for b in range(length // QB):
            lo, hi = key_span(b)
            s = dot(k[:, lo:hi], three(qkv_ref, kv, b), 0, 0) + wide_bias(bias_ref, b, hi - lo)
            top = jnp.max(s, axis=0, keepdims=True)
            p = jnp.exp(s - top)
            total = jnp.sum(p, axis=0, keepdims=True)
            out = dot(v[:, lo:hi], p.astype(BF16), 1, 0) / total
            lse = top + jnp.log(total)
            for i in range(SHARE):
                rows = pl.ds(pl.multiple_of((kv * SHARE + i) * HEAD_WIDTH, HEAD_WIDTH), HEAD_WIDTH)
                o_ref[rows, b * QB:(b + 1) * QB] = out[:, i * QB:(i + 1) * QB].astype(BF16)
                lse_ref[kv, i:i + 1, b * QB:(b + 1) * QB] = lse[:, i * QB:(i + 1) * QB]


DONE = jax.ShapeDtypeStruct((8, GAINS), F32)


def attend(qkv, segments, at, before=()):
    seqs, length = segments.shape
    wide, rows = qkv.shape
    return pl.pallas_call(
        attend_kernel,
        grid=(1,),
        in_specs=[
            pl.BlockSpec((wide, length), lambda i: (0, at)),
            pl.BlockSpec((1, 1, length), lambda i: (at, 0, 0)),
            pl.BlockSpec((1, length, 1), lambda i: (at, 0, 0)),
        ] + [pl.BlockSpec(memory_space=pltpu.HBM)] * len(before),
        out_specs=[
            pl.BlockSpec((D, length), lambda i: (0, at)),
            pl.BlockSpec((KEY_VALUE_HEADS, 8, length), lambda i: (0, 0, at)),
            fixed(DONE.shape),
        ],
        out_shape=shaped(((D, rows), BF16), ((KEY_VALUE_HEADS, 8, rows), F32)) + [DONE],
        input_output_aliases={3 + i: i for i in range(len(before))},
        scratch_shapes=[pltpu.VMEM((length // QB, 3 * QB, QB), F32)],
        compiler_params=params(60),
        cost_estimate=cost(),
        name="attend",
    )(qkv, segments[:, None, :], segments[:, :, None], *before)


def middle_kernel(weight, where_ref, x_ref, o_ref, gain_ref, *refs):
    x1_ref, h_ref, w, sem = refs[4:]

    @pl.when(pl.program_id(0) == 0)
    def _():
        weight.load(where_ref, refs[:4], w, sem)
        wait_for(w, sem)

    x1 = x_ref[...].astype(F32) + dot(w[...], o_ref[...], 0, 0)
    normal, _ = norm_columns(x1)
    x1_ref[...] = x1
    h_ref[...] = (normal * gain_ref[:, 1:2].astype(F32)).astype(BF16)


def middle(where, x, o, w, gains):
    rows = x.shape[1]
    return pl.pallas_call(
        functools.partial(middle_kernel, w),
        grid=(rows // TILE,),
        in_specs=[SMEM, columns(D, TILE), columns(D, TILE), fixed((D, GAINS))] + w.specs(),
        out_specs=[columns(D, TILE), columns(D, TILE)],
        out_shape=shaped(((D, rows), F32), ((D, rows), BF16)),
        scratch_shapes=w.scratch(),
        compiler_params=params(60),
        cost_estimate=cost(2 * rows * D * D, rows * D * 10),
        name="middle",
    )(where, x, o, gains, *w.arrays)


def feed_forward_kernel(weights, where_ref, h_ref, dy_ref, x1_ref, *refs):
    count = len(weights[0].arrays)
    y_ref, dh_ref, hid_ref, dgate_ref, dup_ref, acc_ref, acc_sem, *scratch = refs[3 * count:]
    step = pl.program_id(0)

    @pl.when(step == 0)
    def _():
        for i, weight in enumerate(weights):
            weight.load(where_ref, refs[i * count:(i + 1) * count], *scratch[2 * i:2 * i + 2])
        pltpu.make_async_copy(x1_ref, acc_ref, acc_sem).start()
        dh_ref[...] = jnp.zeros_like(dh_ref)
        pltpu.make_async_copy(x1_ref, acc_ref, acc_sem).wait()

    wg_ref, wu_ref, wd_ref = (w.at[step] for w in scratch[::2])
    for w, sem in zip((wg_ref, wu_ref, wd_ref), scratch[1::2]):
        wait_for(w, sem.at[step])
    h, dy = h_ref[...], dy_ref[...]
    gate = dot(wg_ref[...], h, 0, 0)
    up = dot(wu_ref[...], h, 0, 0)
    dhid = dot(wd_ref[...], dy, 0, 0)
    sig = jax.nn.sigmoid(gate)
    silu = gate * sig
    hid = (silu * up).astype(BF16)
    dgate = (dhid * up * (sig + silu * (1.0 - sig))).astype(BF16)
    dup = (dhid * silu).astype(BF16)
    hid_ref[...] = hid
    dgate_ref[...] = dgate
    dup_ref[...] = dup
    acc_ref[...] += dot(wd_ref[...], hid, 1, 0)
    dh_ref[...] += dot(wg_ref[...], dgate, 1, 0) + dot(wu_ref[...], dup, 1, 0)

    @pl.when(step == pl.num_programs(0) - 1)
    def _():
        y_ref[...] = acc_ref[...].astype(BF16)


def feed_forward(where, h, dy, x1, weights):
    rows, hidden = h.shape[1], weights[0].shape[1]
    block = pl.BlockSpec((CUT, rows), lambda f: (f, 0))
    return pl.pallas_call(
        functools.partial(feed_forward_kernel, weights),
        grid=(hidden // CUT,),
        in_specs=[SMEM, fixed((D, rows)), fixed((D, rows)), pl.BlockSpec(memory_space=pltpu.HBM)]
        + sum((w.specs() for w in weights), []),
        out_specs=[fixed((D, rows)), fixed((D, rows))] + [block] * 3,
        out_shape=shaped(((D, rows), BF16), ((D, rows), F32)) + shaped(((hidden, rows), BF16)) * 3,
        scratch_shapes=sum(
            (w.scratch() for w in weights), [pltpu.VMEM((D, rows), F32), pltpu.SemaphoreType.DMA]
        ),
        compiler_params=params(60),
        cost_estimate=cost(),
        name="feed_forward",
    )(where, h, dy, x1, *sum((w.arrays for w in weights), []))


def block_here(where_ref):
    return 2 * where_ref[1] + where_ref[2]


def split_owners(grad, where_ref, put):
    core, x_here = where_ref[0] & 1, where_ref[0] >> 1
    for x in range(2):
        a = grad[2 * x * OWN:(2 * x + 1) * OWN].astype(BF16)
        b = grad[(2 * x + 1) * OWN:(2 * x + 2) * OWN].astype(BF16)
        put(x_here ^ x, jnp.where(core == 0, a, b), jnp.where(core == 0, b, a))


def row_grads_kernel(where_ref, a_ref, b_ref, keep_ref, send_ref):
    grad = dot(a_ref[...], b_ref[...], 1, 1)
    for i in range(2):
        def put(x, keep, send):
            keep_ref[x, i ^ where_ref[2]] = keep
            send_ref[x, i ^ where_ref[2]] = send

        split_owners(grad[:, i * CUT:(i + 1) * CUT], where_ref, put)


def column_grads_kernel(where_ref, a_ref, b_ref, keep_ref, send_ref):
    grad = dot(a_ref[...], b_ref[...], 1, 1).astype(BF16)
    first = (where_ref[0] & 1) == 0
    for i in range(4):
        at = block_here(where_ref) ^ i
        a, b = grad[i * OWN:(i + 1) * OWN, :CUT], grad[i * OWN:(i + 1) * OWN, CUT:]
        keep_ref[0, at] = jnp.where(first, a, b)
        send_ref[0, at] = jnp.where(first, b, a)


def ffn_grads(where, a, b, by_columns):
    rows = a.shape[1]
    if by_columns:
        kernel = column_grads_kernel
        out = pl.BlockSpec((1, 4, OWN, CUT), lambda f, at: (f ^ (at[0] >> 1), 0, 0, 0))
    else:
        kernel = row_grads_kernel
        out = pl.BlockSpec((2, 2, OWN, CUT), lambda f, at: (0, f ^ at[1], 0, 0))
    return pl.pallas_call(
        kernel,
        grid_spec=pltpu.PrefetchScalarGridSpec(
            num_scalar_prefetch=1,
            grid=(b.shape[0] // PAIR,),
            in_specs=[fixed((D, rows)), pl.BlockSpec((PAIR, rows), lambda f, at: (f, 0))],
            out_specs=[out, out],
        ),
        out_shape=shaped(((2, 4, OWN, CUT), BF16)) * 2,
        compiler_params=params(60),
        cost_estimate=cost(),
        name="ffn_grads",
    )(where, a, b)


def branch_kernel(weight, where_ref, dh_ref, x1_ref, dy_ref, gain_ref, *refs):
    dx_ref, da_ref, do_ref, gain_grad, w, sem = refs[4:]
    first = pl.program_id(0) == 0

    @pl.when(first)
    def _():
        weight.load(where_ref, refs[:4], w, sem)

    gain = gain_ref[:, 1:2].astype(F32)
    normal, inverse = norm_columns(x1_ref[...])
    back, part = norm_columns_back(dh_ref[...], normal, inverse, gain)
    dx = dy_ref[...].astype(F32) + back
    da = dx.astype(BF16)
    dx_ref[...] = dx
    da_ref[...] = da

    @pl.when(first)
    def _():
        gain_grad[...] = part
        wait_for(w, sem)

    @pl.when(jnp.logical_not(first))
    def _():
        gain_grad[...] += part

    do_ref[...] = dot(w[...], da, 1, 0).astype(BF16)


def branch(where, dh, x1, dy, gains, w):
    rows = dh.shape[1]
    return pl.pallas_call(
        functools.partial(branch_kernel, w),
        grid=(rows // TILE,),
        in_specs=[SMEM] + [columns(D, TILE)] * 3 + [fixed((D, GAINS))] + w.specs(),
        out_specs=[columns(D, TILE)] * 3 + [pl.BlockSpec((D, 1), lambda i: (0, 0))],
        out_shape=shaped(((D, rows), F32), ((D, rows), BF16), ((D, rows), BF16), ((D, 1), F32)),
        scratch_shapes=w.scratch(),
        compiler_params=params(60),
        cost_estimate=cost(2 * rows * D * D, rows * D * 18),
        name="branch",
    )(where, dh, x1, dy, gains, *w.arrays)


def attend_back_kernel(qkv_ref, o_ref, do_ref, lse_ref, segr_ref, segc_ref, cos_ref, sin_ref,
                       *refs):
    out_ref, done_ref, bias_ref, dk_ref, dv_ref = refs[-5:]
    done_ref[...] = jnp.zeros_like(done_ref)
    length = qkv_ref.shape[1]
    make_bias(bias_ref, segr_ref.at[0], segc_ref.at[0], length)

    def turn_back(g, c, s, at, cols):
        a, b = g[:HALF], g[HALF:]
        at = pl.multiple_of(at, HEAD_WIDTH)
        out_ref[pl.ds(at, HALF), cols] = (a * c + b * s).astype(BF16)
        out_ref[pl.ds(pl.multiple_of(at + HALF, HALF), HALF), cols] = (b * c - a * s).astype(BF16)

    @pl.loop(0, KEY_VALUE_HEADS)
    def _(kv):
        k = qkv_ref[pl.ds(pl.multiple_of(D + kv * HEAD_WIDTH, HEAD_WIDTH), HEAD_WIDTH), :]
        v = qkv_ref[pl.ds(pl.multiple_of(D + KEYS + kv * HEAD_WIDTH, HEAD_WIDTH), HEAD_WIDTH), :]
        dk_ref[...] = jnp.zeros_like(dk_ref)
        dv_ref[...] = jnp.zeros_like(dv_ref)
        for b in range(length // QB):
            lo, hi = key_span(b)
            cols = slice(b * QB, (b + 1) * QB)
            q, o, do = three(qkv_ref, kv, b), three(o_ref, kv, b), three(do_ref, kv, b)
            lse = jnp.concatenate([lse_ref[kv, i:i + 1, cols] for i in range(SHARE)], axis=1)
            inner = jnp.sum(o.astype(F32) * do.astype(F32), axis=0, keepdims=True)
            s = dot(k[:, lo:hi], q, 0, 0) + wide_bias(bias_ref, b, hi - lo)
            p = jnp.exp(s - lse)
            dp = dot(v[:, lo:hi], do, 0, 0)
            ds = (p * (dp - inner)).astype(BF16)
            dv_ref[:, lo:hi] += dot(do, p.astype(BF16), 1, 1)
            dk_ref[:, lo:hi] += dot(q, ds, 1, 1)
            dq = dot(k[:, lo:hi], ds, 1, 0) * HEAD_WIDTH ** -0.5
            for i in range(SHARE):
                turn_back(dq[:, i * QB:(i + 1) * QB], cos_ref[:, cols], sin_ref[:, cols],
                          (kv * SHARE + i) * HEAD_WIDTH, cols)
        turn_back(dk_ref[...], cos_ref[...], sin_ref[...], D + kv * HEAD_WIDTH, slice(None))
        out_ref[pl.ds(pl.multiple_of(D + KEYS + kv * HEAD_WIDTH, HEAD_WIDTH), HEAD_WIDTH), :] = (
            dv_ref[...].astype(BF16))


def attend_back(qkv, o, do, lse, segments, cos, sin, at, before=()):
    length = segments.shape[1]
    wide, rows = qkv.shape
    here = lambda height: pl.BlockSpec((height, length), lambda i: (0, at))
    return pl.pallas_call(
        attend_back_kernel,
        grid=(1,),
        in_specs=[
            here(wide),
            here(D),
            here(D),
            pl.BlockSpec((KEY_VALUE_HEADS, 8, length), lambda i: (0, 0, at)),
            pl.BlockSpec((1, 1, length), lambda i: (at, 0, 0)),
            pl.BlockSpec((1, length, 1), lambda i: (at, 0, 0)),
            here(HALF),
            here(HALF),
        ] + [pl.BlockSpec(memory_space=pltpu.HBM)] * len(before),
        out_specs=[here(wide), fixed(DONE.shape)],
        out_shape=shaped(((wide, rows), BF16)) + [DONE],
        input_output_aliases={8 + i: i for i in range(len(before))},
        scratch_shapes=[
            pltpu.VMEM((length // QB, 3 * QB, QB), F32),
            pltpu.VMEM((HEAD_WIDTH, length), F32),
            pltpu.VMEM((HEAD_WIDTH, length), F32),
        ],
        compiler_params=params(60),
        cost_estimate=cost(),
        name="attend_back",
    )(qkv, o, do, lse, segments[:, None, :], segments[:, :, None], cos, sin, *before)


PIECES = ((0, OWN),)


def weight_kernel(where_ref, h_ref, dqkv_ref, o_ref, da_ref, *out_refs):
    def store(block, grad):
        def put(x, keep, send):
            for i, (low, high) in enumerate(PIECES):
                at = block ^ block_here(where_ref)
                out_refs[2 * i][x, at] = keep[low:high]
                out_refs[2 * i + 1][x, at] = send[low:high]

        split_owners(grad, where_ref, put)

    grad = dot(h_ref[...], dqkv_ref[:PAIR, :], 1, 1)
    store(0, grad[:, :CUT])
    store(1, grad[:, CUT:])
    left = dot(h_ref[...], dqkv_ref[2 * CUT:, :], 1, 1)
    right = dot(o_ref[...], da_ref[:3 * CUT - WIDE, :], 1, 1)
    store(2, jnp.concatenate([left, right], axis=1))
    store(3, dot(o_ref[...], da_ref[3 * CUT - WIDE:, :], 1, 1))


def weight_grads(where, h, dqkv, o, da):
    rows = h.shape[1]
    shapes = [(2, 4, high - low, CUT) for low, high in PIECES for _ in range(2)]
    return pl.pallas_call(
        weight_kernel,
        grid=(1,),
        in_specs=[SMEM, fixed((D, rows)), fixed((WIDE, rows)), fixed((D, rows)), fixed((D, rows))],
        out_specs=[fixed(shape) for shape in shapes],
        out_shape=shaped(*((shape, BF16) for shape in shapes)),
        compiler_params=params(60),
        cost_estimate=cost(),
        name="weight_grads",
    )(where, h, dqkv, o, da)


def inputs_kernel(weights, where_ref, x_ref, dx_ref, dqkv_ref, *refs):
    out_ref, gain_grad, wq, q_sem, wk, k_sem = refs[8:]
    first = pl.program_id(0) == 0

    @pl.when(first)
    def _():
        weights[0].load(where_ref, refs[:4], wq, q_sem)
        weights[1].load(where_ref, refs[4:8], wk, k_sem)
        wait_for(wq, q_sem)
        wait_for(wk, k_sem)

    gain = wk[:, 2 * KEYS:2 * KEYS + 1].astype(F32)
    dh = dot(wq[...], dqkv_ref[:D], 1, 0) + dot(wk[:, :2 * KEYS], dqkv_ref[D:], 1, 0)
    normal, inverse = norm_columns(x_ref[...].astype(F32))
    back, part = norm_columns_back(dh, normal, inverse, gain)
    out_ref[...] = (dx_ref[...] + back).astype(BF16)

    @pl.when(first)
    def _():
        gain_grad[...] = part

    @pl.when(jnp.logical_not(first))
    def _():
        gain_grad[...] += part


def input_grads(where, x, dx, wq, wk, dqkv):
    rows = x.shape[1]
    return pl.pallas_call(
        functools.partial(inputs_kernel, (wq, wk)),
        grid=(rows // HALF_TILE,),
        in_specs=[SMEM, columns(D, HALF_TILE), columns(D, HALF_TILE), columns(WIDE, HALF_TILE)]
        + wq.specs() + wk.specs(),
        out_specs=[columns(D, HALF_TILE), pl.BlockSpec((D, 1), lambda i: (0, 0))],
        out_shape=shaped(((D, rows), BF16), ((D, 1), F32)),
        scratch_shapes=wq.scratch() + wk.scratch(),
        compiler_params=params(60),
        cost_estimate=cost(2 * rows * D * WIDE, rows * (D * 8 + WIDE * 2) + D * WIDE * 2),
        name="input_grads",
    )(where, x, dx, dqkv, *wq.arrays, *wk.arrays)


def tables(segments):
    length = segments.shape[1]
    index = jnp.arange(length, dtype=jnp.int32)
    same = segments[:, :, None] == segments[:, None, :]
    start = jnp.min(jnp.where(same, index[None, :, None], length), axis=1)
    position = (index[None, :] - start).astype(F32).reshape(1, -1)
    freq = THETA ** (-(jnp.arange(HALF, dtype=F32) * 2.0 / HEAD_WIDTH))
    angle = freq[:, None] * position
    return jnp.cos(angle), jnp.sin(angle)


def after(value, *others):
    return lax.optimization_barrier((value,) + others)[0]


class Cube:
    def __init__(self, count):
        self.count = count
        self.dims = count.bit_length() - 1
        replica, group = lax.axis_index("replica"), lax.axis_index("group")
        self.coordinate = {i: (replica >> i) & 1 for i in range(self.dims)}
        self.coordinate["x"] = group >> 1
        self.coordinate["core"] = group & 1
        self.me = group

    def swap(self, value, dim):
        if dim == "x":
            return lax.ppermute(value, "group", [(i, i ^ 2) for i in range(4)])
        if dim == "core":
            return lax.ppermute(value, "group", [(i, i ^ 1) for i in range(4)])
        return lax.ppermute(value, "replica", [(i, i ^ (1 << dim)) for i in range(self.count)])

    def ordered(self, dim, mine, other, axis):
        return jnp.where(
            self.coordinate[dim] == 0,
            jnp.concatenate([mine, other], axis=axis),
            jnp.concatenate([other, mine], axis=axis),
        )


def rows_of(own, sibling, across, diagonal):
    pieces = own, sibling, across, diagonal
    return Weight(0, [(array, flip, None) for flip, array in enumerate(pieces)])


class Relay:
    def __init__(self, cube, shard, axis, first, second):
        self.cube, self.shard, self.axis, self.first, self.second = cube, shard, axis, first, second
        self.cut = 1 - axis
        size = shard.shape[self.cut] // (2 if first is None else 4)
        at = cube.coordinate[second]
        if first is not None:
            at = 2 * at + cube.coordinate[first]
        self.part = lax.dynamic_slice_in_dim(shard, at * size, size, self.cut)

    def cross(self, *others):
        self.direct = self.cube.swap(after(self.part, *others), "x")
        return self.direct

    def hand_on(self, *others):
        self.direct = after(self.direct, *others)
        if self.first is None:
            self.half = self.direct
            self.rest = self.cube.swap(self.half, self.second)
            return self.rest
        self.handed = self.cube.swap(self.direct, self.first)
        return self.handed

    def finish(self, *others):
        cube = self.cube
        if self.first is not None:
            handed = after(self.handed, *others)
            self.half = cube.ordered(self.first, self.direct, handed, self.cut)
            self.rest = cube.swap(self.half, self.second)
        self.half_diagonal = cube.swap(self.half, "core")

    def weight(self, sibling, *others):
        rest = after(self.rest, *others)
        pieces = [
            (self.shard, 0, None), (sibling, 1, None), (self.half, 2, 0), (rest, 2, 1),
            (self.half_diagonal, 3, 0), (self.cube.swap(rest, "core"), 3, 1),
        ]
        return Weight(self.axis, pieces, self.second, 4)


class Reduce:
    def __init__(self, cube, keep, got, halves, gathers):
        rows, wide = keep.shape[2:]
        self.cube, self.shape = cube, (4, rows, wide)
        self.order = halves + tuple(range(2, cube.dims)) + gathers
        self.place = {"x": 0, 0: 1, 1: 2}
        self.terms = [t.reshape(2, 2, 2, rows, wide) for t in (keep, got)]
        self.index = 0
        self.done = False

    def sum(self, terms):
        if len(terms) == 1:
            return terms[0]
        return functools.reduce(jnp.add, [t.astype(F32) for t in terms]).astype(BF16)

    @staticmethod
    def land(pieces, other):
        got = lax.optimization_barrier((*(piece.terms[-1] for piece in pieces), other))
        for piece, value in zip(pieces, got):
            piece.terms[-1] = value

    def ready(self, *others):
        dim = self.order[self.index]
        if others:
            self.terms[-1] = after(self.terms[-1], *others)
        if self.index < 3:
            axis = self.place[dim]
            take = lambda i: [lax.slice_in_dim(t, i, i + 1, axis=axis) for t in self.terms]
            self.send, self.terms = self.sum(take(1)), take(0)
        else:
            self.send = self.sum(self.terms)
        return self.send

    def swap(self):
        dim = self.order[self.index]
        got = self.cube.swap(self.send, dim)
        self.index += 1
        if self.index <= 3:
            self.terms = self.terms + [got]
        elif self.index <= len(self.order) - 2:
            self.terms = [self.send, got]
        elif self.index < len(self.order):
            self.terms = [self.cube.ordered(dim, self.send, got, self.place[dim])]
        else:
            self.terms = [self.send, got]

    def finish(self, *others):
        self.done = True
        low, got = (after(value, *others) for value in self.terms)
        self.result = self.cube.ordered(self.order[-1], low, got, self.place[self.order[-1]])
        self.result = self.result.reshape(self.shape)
        return self.result


def per_device(
    tokens,
    segments,
    query_weight,
    key_weight,
    value_weight,
    output_weight,
    w_gate,
    w_up,
    w_down,
    attn_gain,
    ffn_gain,
    cotangent,
    replicas,
):
    cube = Cube(replicas)
    where = jnp.stack([cube.me] + [cube.coordinate[i] for i in range(3)]).astype(jnp.int32)
    x, dy = tokens.T, cotangent.T

    core = lambda value: cube.swap(value, "core")
    q_across = cube.swap(query_weight, "x")
    pad = jnp.zeros((OWN, GAINS - 2), BF16)
    kv = jnp.concatenate(
        [key_weight, value_weight, attn_gain[:, None], ffn_gain[:, None], pad], axis=1
    )
    kv_across = cube.swap(after(kv, q_across), "x")
    relays = [
        Relay(cube, w_gate, 0, 0, 1), Relay(cube, w_up, 0, 1, 0), Relay(cube, w_down.T, 1, None, 0)
    ]
    q_sibling, kv_sibling, wo_sibling = core(query_weight), core(kv), core(output_weight)
    siblings = [core(relay.shard) for relay in relays]
    cos, sin = tables(segments)
    early = [relay.part for relay in relays] + [cos, sin, where, q_sibling, kv_sibling, wo_sibling]
    q_across, kv_across = lax.optimization_barrier((q_across, kv_across, *early, *siblings))[:2]
    q_diagonal, kv_diagonal = core(q_across), core(kv_across)
    direct = [relay.cross(q_across, kv_across) for relay in relays]
    wq = rows_of(query_weight, q_sibling, q_across, q_diagonal)
    wk = rows_of(kv, kv_sibling, kv_across, kv_diagonal)
    qkv, h, gains = project(where, x, wq, wk, cos, sin)
    *first, done0 = attend(qkv, segments, 0)
    for relay in relays:
        relay.hand_on(done0)
    wo_across = cube.swap(after(output_weight, done0, *direct), "x")
    o, lse, done1 = attend(after(qkv, done0, *direct), segments, 1, first)
    for relay in relays:
        relay.finish(done1)
    wo_diagonal = core(after(wo_across, done1))
    wo = rows_of(output_weight, wo_sibling, wo_across, wo_diagonal)
    x1, h2 = middle(where, x, after(o, relays[0].half, relays[1].half), wo, gains)
    weights = [relay.weight(sibling, h2) for relay, sibling in zip(relays, siblings)]
    y, dh2, hid, dgate, dup = feed_forward(where, h2, dy, x1, weights)

    gd_keep, gd_send = ffn_grads(where, dy, hid, True)
    gd = Reduce(cube, gd_keep, core(gd_send), ("x", 0, 1), (1, 0))
    gg_keep, gg_send = ffn_grads(where, h2, after(dgate, gd_send), False)
    gg = Reduce(cube, gg_keep, core(gg_send), (0, "x", 1), (1, 0))
    gd.ready(gg_send)
    gu_keep, gu_send = ffn_grads(where, h2, after(dup, gd.send), False)
    gd.swap()
    gu = Reduce(cube, gu_keep, core(gu_send), (1, 0, "x"), (1, 0))
    gg.ready(gu_send)
    dx1, da, do, ffn_gain_grad = branch(where, after(dh2, gg.send), x1, dy, gains, wo)
    gg.swap()
    gu.ready(da)
    do0 = after(do, gu.send)
    gu.swap()
    *first, done0 = attend_back(qkv, o, do0, lse, segments, cos, sin, 0)
    Reduce.land((gd, gg), done0)
    do1 = after(do, done0, gd.ready(), gg.ready())
    gd.swap()
    gg.swap()
    dqkv, done1 = attend_back(qkv, o, do1, lse, segments, cos, sin, 1, first)
    swaps = [gd, gg, gu]
    Reduce.land(swaps, done1)
    dqkv = after(dqkv, *[piece.ready() for piece in swaps])
    for piece in swaps:
        piece.swap()
    parts = []
    weight_parts = weight_grads(where, h, dqkv, o, da)
    for i, halves in enumerate((("x", 0, 1),)):
        keep, send = weight_parts[2 * i:2 * i + 2]
        parts.append(Reduce(cube, keep, core(send), halves, (1, 0)))
    dqkv = after(dqkv, *[part.ready() for part in parts])
    for part in parts:
        part.swap()
    grad_x, attn_gain_grad = input_grads(where, x, dx1, wq, wk, dqkv)
    swaps = [gd, gg, gu]
    Reduce.land(swaps, grad_x)
    swaps += parts
    both = jnp.concatenate([attn_gain_grad, ffn_gain_grad], axis=1).T.reshape(-1)
    ends = ["core", "x"] + list(range(cube.dims))
    token = grad_x
    for piece in swaps:
        token = piece.ready(token)
        piece.swap()
    swaps = parts + [gd, gg, gu]
    while any(piece.index < len(piece.order) for piece in swaps):
        active = [piece for piece in swaps if piece.index < len(piece.order)]
        for piece in active:
            token = piece.ready(token, both)
            piece.swap()
        for piece in swaps:
            if piece not in active and not piece.done:
                token = piece.finish(token)
        if ends:
            both = both + after(cube.swap(both, ends.pop(0)), token)
    for piece in swaps:
        if not piece.done:
            token = piece.finish(token)
    for dim in ends:
        both = both + cube.swap(both, dim)
    both = lax.dynamic_slice_in_dim(both.reshape(2, D), cube.me * OWN, OWN, 1)
    flat = lambda g: jnp.concatenate([g[i] for i in range(4)], axis=1)
    ga = jnp.concatenate([flat(part.result) for part in parts], axis=0).astype(F32)
    return (
        y.T,
        grad_x.T,
        ga[:, :D],
        ga[:, D:D + KEYS],
        ga[:, D + KEYS:WIDE],
        ga[:, WIDE:],
        flat(gg.result).astype(F32),
        flat(gu.result).astype(F32),
        gd.result.reshape(D, CUT).T.astype(F32),
        both[0],
        both[1],
    )


def solution(mesh):
    rows = P(("group", "replica"), None)
    weight, gain = P("group", None), P("group")
    replicas = mesh.shape["replica"]
    return jax.shard_map(
        lambda *args: per_device(*args, replicas),
        mesh=mesh,
        in_specs=(rows, rows) + (weight,) * 7 + (gain, gain, rows),
        out_specs=(rows, rows) + (weight,) * 7 + (gain, gain),
        check_vma=False,
    )
```

```python
import functools

import jax
import jax.numpy as jnp
from jax import lax
from jax.experimental import pallas as pl
from jax.experimental.pallas import tpu as pltpu
from jax.sharding import PartitionSpec as P

D = 960
QUERY_HEADS = 15
KEY_VALUE_HEADS = 5
HEAD_WIDTH = 64
SHARE = QUERY_HEADS // KEY_VALUE_HEADS
HALF = HEAD_WIDTH // 2
KEYS = KEY_VALUE_HEADS * HEAD_WIDTH
EPS = 1e-05
THETA = 100000.0
TILE = 512
HALF_TILE = 256
QB = 128
GAINS = 128
WIDE = D + 2 * KEYS
CUT = 640
OWN = 240
PAIR = 2 * CUT
F32 = jnp.float32
BF16 = jnp.bfloat16
MIB = 1 << 20


def dot(a, b, ca, cb):
    return lax.dot_general(a, b, (((ca,), (cb,)), ((), ())), preferred_element_type=F32)


def params(limit, grid=1):
    return pltpu.CompilerParams(
        vmem_limit_bytes=limit * MIB, dimension_semantics=("arbitrary",) * grid
    )


def cost(*_):
    return pl.CostEstimate(flops=1, bytes_accessed=1, transcendentals=0)


def shaped(*shape_type):
    return [jax.ShapeDtypeStruct(s, t) for s, t in shape_type]


def norm_columns(v):
    inverse = lax.rsqrt(jnp.mean(v * v, axis=0, keepdims=True) + EPS)
    return v * inverse, inverse


def norm_columns_back(grad, normal, inverse, gain):
    scaled = grad * gain
    back = inverse * (scaled - normal * jnp.mean(scaled * normal, axis=0, keepdims=True))
    return back, jnp.sum(grad * normal, axis=1, keepdims=True)


def fixed(shape):
    return pl.BlockSpec(shape, lambda *_: (0,) * len(shape), pipeline_mode=pl.Buffered(1))


def columns(height, width):
    return pl.BlockSpec((height, width), lambda i: (0, i))


class Weight:
    def __init__(self, axis, pieces, dim=None, blocks=0):
        self.axis, self.dim, self.blocks = axis, dim, blocks
        self.arrays = [array for array, _, _ in pieces]
        self.places = [(flip, side) for _, flip, side in pieces]
        shape = list(self.arrays[0].shape)
        self.size = shape[axis]
        self.half = shape[1 - axis] // 2
        shape[axis] *= 4
        self.shape = tuple(shape)

    def specs(self):
        return [pl.BlockSpec(memory_space=pltpu.HBM)] * len(self.arrays)

    def scratch(self):
        if not self.blocks:
            return [pltpu.VMEM(self.shape, BF16), pltpu.SemaphoreType.DMA]
        block = (self.shape[0], self.shape[1] // self.blocks)
        return [pltpu.VMEM((self.blocks,) + block, BF16), pltpu.SemaphoreType.DMA((self.blocks,))]

    def load(self, where_ref, refs, scratch, sem):
        wide = self.shape[1] // max(self.blocks, 1)
        for ref, (flip, side) in zip(refs, self.places):
            at = (where_ref[0] ^ flip) * self.size
            other = 0 if side is None else (where_ref[1 + self.dim] ^ side) * self.half
            row, column = (at, other) if self.axis == 0 else (other, at)
            rows = pl.ds(pl.multiple_of(row, OWN), ref.shape[0])
            if not self.blocks:
                pltpu.make_async_copy(ref, scratch.at[rows, :], sem).start()
                continue
            first = column // wide
            for i in range(ref.shape[1] // wide):
                pltpu.make_async_copy(
                    ref.at[:, i * wide:(i + 1) * wide], scratch.at[first + i, rows, :],
                    sem.at[first + i],
                ).start()


def wait_for(scratch, sem):
    pltpu.make_async_copy(scratch, scratch, sem).wait()


SMEM = pl.BlockSpec(memory_space=pltpu.SMEM)


def project_kernel(weights, where_ref, x_ref, cos_ref, sin_ref, *refs):
    qkv_ref, h_ref, gains_ref, wq, q_sem, wk, k_sem = refs[8:]

    @pl.when(pl.program_id(0) == 0)
    def _():
        weights[0].load(where_ref, refs[:4], wq, q_sem)
        weights[1].load(where_ref, refs[4:8], wk, k_sem)
        wait_for(wq, q_sem)
        wait_for(wk, k_sem)
        gains_ref[...] = wk[:, 2 * KEYS:]

    gain = wk[:, 2 * KEYS:2 * KEYS + 1].astype(F32)
    normal, _ = norm_columns(x_ref[...].astype(F32))
    h = (normal * gain).astype(BF16)
    h_ref[...] = h
    c, s = cos_ref[...], sin_ref[...]

    def rotary(out, at, heads, scale):
        for head in range(heads):
            low = head * HEAD_WIDTH
            a, b = out[low:low + HALF], out[low + HALF:low + HEAD_WIDTH]
            to = at + low
            qkv_ref[to:to + HALF, :] = ((a * c - b * s) * scale).astype(BF16)
            qkv_ref[to + HALF:to + HEAD_WIDTH, :] = ((b * c + a * s) * scale).astype(BF16)

    rotary(dot(wq[...], h, 0, 0), 0, QUERY_HEADS, HEAD_WIDTH ** -0.5)
    out = dot(wk[:, :2 * KEYS], h, 0, 0)
    rotary(out, D, KEY_VALUE_HEADS, 1.0)
    qkv_ref[D + KEYS:, :] = out[KEYS:].astype(BF16)


def project(where, x, wq, wk, cos, sin):
    rows = x.shape[1]
    return pl.pallas_call(
        functools.partial(project_kernel, (wq, wk)),
        grid=(rows // TILE,),
        in_specs=[SMEM, columns(D, TILE), columns(HALF, TILE), columns(HALF, TILE)]
        + wq.specs() + wk.specs(),
        out_specs=[columns(WIDE, TILE), columns(D, TILE),
                   pl.BlockSpec((D, GAINS), lambda i: (0, 0))],
        out_shape=shaped(((WIDE, rows), BF16), ((D, rows), BF16), ((D, GAINS), BF16)),
        scratch_shapes=wq.scratch() + wk.scratch(),
        compiler_params=params(60),
        cost_estimate=cost(2 * rows * D * WIDE, rows * (2 * D + WIDE) * 2 + D * WIDE * 2),
        name="project",
    )(where, x, cos, sin, *wq.arrays, *wk.arrays)


def key_span(block):
    return max(0, QB * (block - 2)), QB * (block + 1)


def make_bias(bias_ref, segr_ref, segc_ref, length):
    for b in range(length // QB):
        lo, hi = key_span(b)
        key_at = lax.broadcasted_iota(jnp.int32, (hi - lo, QB), 0) + lo
        query_at = lax.broadcasted_iota(jnp.int32, (hi - lo, QB), 1) + b * QB
        ok = (segc_ref[lo:hi, :] == segr_ref[:, b * QB:(b + 1) * QB]) & (key_at <= query_at)
        bias_ref[b, 0:hi - lo, :] = jnp.where(ok, 0.0, -1e30)


def three(ref, kv, b):
    return jnp.concatenate(
        [
            ref[pl.ds(pl.multiple_of((kv * SHARE + i) * HEAD_WIDTH, HEAD_WIDTH), HEAD_WIDTH),
                b * QB:(b + 1) * QB]
            for i in range(SHARE)
        ],
        axis=1,
    )


def wide_bias(bias_ref, b, n):
    one = bias_ref[b, 0:n, :]
    return jnp.concatenate([one] * SHARE, axis=1)


def attend_kernel(qkv_ref, segr_ref, segc_ref, *refs):
    o_ref, lse_ref, done_ref, bias_ref = refs[-4:]
    done_ref[...] = jnp.zeros_like(done_ref)
    length = qkv_ref.shape[1]
    make_bias(bias_ref, segr_ref.at[0], segc_ref.at[0], length)

    @pl.loop(0, KEY_VALUE_HEADS)
    def _(kv):
        k = qkv_ref[pl.ds(pl.multiple_of(D + kv * HEAD_WIDTH, HEAD_WIDTH), HEAD_WIDTH), :]
        v = qkv_ref[pl.ds(pl.multiple_of(D + KEYS + kv * HEAD_WIDTH, HEAD_WIDTH), HEAD_WIDTH), :]
        for b in range(length // QB):
            lo, hi = key_span(b)
            s = dot(k[:, lo:hi], three(qkv_ref, kv, b), 0, 0) + wide_bias(bias_ref, b, hi - lo)
            top = jnp.max(s, axis=0, keepdims=True)
            p = jnp.exp(s - top)
            total = jnp.sum(p, axis=0, keepdims=True)
            out = dot(v[:, lo:hi], p.astype(BF16), 1, 0) / total
            lse = top + jnp.log(total)
            for i in range(SHARE):
                rows = pl.ds(pl.multiple_of((kv * SHARE + i) * HEAD_WIDTH, HEAD_WIDTH), HEAD_WIDTH)
                o_ref[rows, b * QB:(b + 1) * QB] = out[:, i * QB:(i + 1) * QB].astype(BF16)
                lse_ref[kv, i:i + 1, b * QB:(b + 1) * QB] = lse[:, i * QB:(i + 1) * QB]


DONE = jax.ShapeDtypeStruct((8, GAINS), F32)


def attend(qkv, segments, at, before=()):
    seqs, length = segments.shape
    wide, rows = qkv.shape
    return pl.pallas_call(
        attend_kernel,
        grid=(1,),
        in_specs=[
            pl.BlockSpec((wide, length), lambda i: (0, at)),
            pl.BlockSpec((1, 1, length), lambda i: (at, 0, 0)),
            pl.BlockSpec((1, length, 1), lambda i: (at, 0, 0)),
        ] + [pl.BlockSpec(memory_space=pltpu.HBM)] * len(before),
        out_specs=[
            pl.BlockSpec((D, length), lambda i: (0, at)),
            pl.BlockSpec((KEY_VALUE_HEADS, 8, length), lambda i: (0, 0, at)),
            fixed(DONE.shape),
        ],
        out_shape=shaped(((D, rows), BF16), ((KEY_VALUE_HEADS, 8, rows), F32)) + [DONE],
        input_output_aliases={3 + i: i for i in range(len(before))},
        scratch_shapes=[pltpu.VMEM((length // QB, 3 * QB, QB), F32)],
        compiler_params=params(60),
        cost_estimate=cost(),
        name="attend",
    )(qkv, segments[:, None, :], segments[:, :, None], *before)


def middle_kernel(weight, where_ref, x_ref, o_ref, gain_ref, *refs):
    x1_ref, h_ref, w, sem = refs[4:]

    @pl.when(pl.program_id(0) == 0)
    def _():
        weight.load(where_ref, refs[:4], w, sem)
        wait_for(w, sem)

    x1 = x_ref[...].astype(F32) + dot(w[...], o_ref[...], 0, 0)
    normal, _ = norm_columns(x1)
    x1_ref[...] = x1
    h_ref[...] = (normal * gain_ref[:, 1:2].astype(F32)).astype(BF16)


def middle(where, x, o, w, gains):
    rows = x.shape[1]
    return pl.pallas_call(
        functools.partial(middle_kernel, w),
        grid=(rows // TILE,),
        in_specs=[SMEM, columns(D, TILE), columns(D, TILE), fixed((D, GAINS))] + w.specs(),
        out_specs=[columns(D, TILE), columns(D, TILE)],
        out_shape=shaped(((D, rows), F32), ((D, rows), BF16)),
        scratch_shapes=w.scratch(),
        compiler_params=params(60),
        cost_estimate=cost(2 * rows * D * D, rows * D * 10),
        name="middle",
    )(where, x, o, gains, *w.arrays)


def feed_forward_kernel(weights, where_ref, h_ref, dy_ref, x1_ref, *refs):
    count = len(weights[0].arrays)
    y_ref, dh_ref, hid_ref, dgate_ref, dup_ref, acc_ref, acc_sem, *scratch = refs[3 * count:]
    step = pl.program_id(0)

    @pl.when(step == 0)
    def _():
        for i, weight in enumerate(weights):
            weight.load(where_ref, refs[i * count:(i + 1) * count], *scratch[2 * i:2 * i + 2])
        pltpu.make_async_copy(x1_ref, acc_ref, acc_sem).start()
        dh_ref[...] = jnp.zeros_like(dh_ref)
        pltpu.make_async_copy(x1_ref, acc_ref, acc_sem).wait()

    wg_ref, wu_ref, wd_ref = (w.at[step] for w in scratch[::2])
    for w, sem in zip((wg_ref, wu_ref, wd_ref), scratch[1::2]):
        wait_for(w, sem.at[step])
    h, dy = h_ref[...], dy_ref[...]
    gate = dot(wg_ref[...], h, 0, 0)
    up = dot(wu_ref[...], h, 0, 0)
    dhid = dot(wd_ref[...], dy, 0, 0)
    sig = jax.nn.sigmoid(gate)
    silu = gate * sig
    hid = (silu * up).astype(BF16)
    dgate = (dhid * up * (sig + silu * (1.0 - sig))).astype(BF16)
    dup = (dhid * silu).astype(BF16)
    hid_ref[...] = hid
    dgate_ref[...] = dgate
    dup_ref[...] = dup
    acc_ref[...] += dot(wd_ref[...], hid, 1, 0)
    dh_ref[...] += dot(wg_ref[...], dgate, 1, 0) + dot(wu_ref[...], dup, 1, 0)

    @pl.when(step == pl.num_programs(0) - 1)
    def _():
        y_ref[...] = acc_ref[...].astype(BF16)


def feed_forward(where, h, dy, x1, weights):
    rows, hidden = h.shape[1], weights[0].shape[1]
    block = pl.BlockSpec((CUT, rows), lambda f: (f, 0))
    return pl.pallas_call(
        functools.partial(feed_forward_kernel, weights),
        grid=(hidden // CUT,),
        in_specs=[SMEM, fixed((D, rows)), fixed((D, rows)), pl.BlockSpec(memory_space=pltpu.HBM)]
        + sum((w.specs() for w in weights), []),
        out_specs=[fixed((D, rows)), fixed((D, rows))] + [block] * 3,
        out_shape=shaped(((D, rows), BF16), ((D, rows), F32)) + shaped(((hidden, rows), BF16)) * 3,
        scratch_shapes=sum(
            (w.scratch() for w in weights), [pltpu.VMEM((D, rows), F32), pltpu.SemaphoreType.DMA]
        ),
        compiler_params=params(60),
        cost_estimate=cost(),
        name="feed_forward",
    )(where, h, dy, x1, *sum((w.arrays for w in weights), []))


def block_here(where_ref):
    return 2 * where_ref[1] + where_ref[2]


def split_owners(grad, where_ref, put):
    core, x_here = where_ref[0] & 1, where_ref[0] >> 1
    for x in range(2):
        a = grad[2 * x * OWN:(2 * x + 1) * OWN].astype(BF16)
        b = grad[(2 * x + 1) * OWN:(2 * x + 2) * OWN].astype(BF16)
        put(x_here ^ x, jnp.where(core == 0, a, b), jnp.where(core == 0, b, a))


def row_grads_kernel(where_ref, a_ref, b_ref, keep_ref, send_ref):
    grad = dot(a_ref[...], b_ref[...], 1, 1)
    for i in range(2):
        def put(x, keep, send):
            keep_ref[x, i ^ where_ref[2]] = keep
            send_ref[x, i ^ where_ref[2]] = send

        split_owners(grad[:, i * CUT:(i + 1) * CUT], where_ref, put)


def column_grads_kernel(where_ref, a_ref, b_ref, keep_ref, send_ref):
    grad = dot(a_ref[...], b_ref[...], 1, 1).astype(BF16)
    first = (where_ref[0] & 1) == 0
    for i in range(4):
        at = block_here(where_ref) ^ i
        a, b = grad[i * OWN:(i + 1) * OWN, :CUT], grad[i * OWN:(i + 1) * OWN, CUT:]
        keep_ref[0, at] = jnp.where(first, a, b)
        send_ref[0, at] = jnp.where(first, b, a)


def ffn_grads(where, a, b, by_columns):
    rows = a.shape[1]
    if by_columns:
        kernel = column_grads_kernel
        out = pl.BlockSpec((1, 4, OWN, CUT), lambda f, at: (f ^ (at[0] >> 1), 0, 0, 0))
    else:
        kernel = row_grads_kernel
        out = pl.BlockSpec((2, 2, OWN, CUT), lambda f, at: (0, f ^ at[1], 0, 0))
    return pl.pallas_call(
        kernel,
        grid_spec=pltpu.PrefetchScalarGridSpec(
            num_scalar_prefetch=1,
            grid=(b.shape[0] // PAIR,),
            in_specs=[fixed((D, rows)), pl.BlockSpec((PAIR, rows), lambda f, at: (f, 0))],
            out_specs=[out, out],
        ),
        out_shape=shaped(((2, 4, OWN, CUT), BF16)) * 2,
        compiler_params=params(60),
        cost_estimate=cost(),
        name="ffn_grads",
    )(where, a, b)


def branch_kernel(weight, where_ref, dh_ref, x1_ref, dy_ref, gain_ref, *refs):
    dx_ref, da_ref, do_ref, gain_grad, w, sem = refs[4:]
    first = pl.program_id(0) == 0

    @pl.when(first)
    def _():
        weight.load(where_ref, refs[:4], w, sem)

    gain = gain_ref[:, 1:2].astype(F32)
    normal, inverse = norm_columns(x1_ref[...])
    back, part = norm_columns_back(dh_ref[...], normal, inverse, gain)
    dx = dy_ref[...].astype(F32) + back
    da = dx.astype(BF16)
    dx_ref[...] = dx
    da_ref[...] = da

    @pl.when(first)
    def _():
        gain_grad[...] = part
        wait_for(w, sem)

    @pl.when(jnp.logical_not(first))
    def _():
        gain_grad[...] += part

    do_ref[...] = dot(w[...], da, 1, 0).astype(BF16)


def branch(where, dh, x1, dy, gains, w):
    rows = dh.shape[1]
    return pl.pallas_call(
        functools.partial(branch_kernel, w),
        grid=(rows // TILE,),
        in_specs=[SMEM] + [columns(D, TILE)] * 3 + [fixed((D, GAINS))] + w.specs(),
        out_specs=[columns(D, TILE)] * 3 + [pl.BlockSpec((D, 1), lambda i: (0, 0))],
        out_shape=shaped(((D, rows), F32), ((D, rows), BF16), ((D, rows), BF16), ((D, 1), F32)),
        scratch_shapes=w.scratch(),
        compiler_params=params(60),
        cost_estimate=cost(2 * rows * D * D, rows * D * 18),
        name="branch",
    )(where, dh, x1, dy, gains, *w.arrays)


def attend_back_kernel(qkv_ref, o_ref, do_ref, lse_ref, segr_ref, segc_ref, cos_ref, sin_ref,
                       *refs):
    out_ref, done_ref, bias_ref, dk_ref, dv_ref = refs[-5:]
    done_ref[...] = jnp.zeros_like(done_ref)
    length = qkv_ref.shape[1]
    make_bias(bias_ref, segr_ref.at[0], segc_ref.at[0], length)

    def turn_back(g, c, s, at, cols):
        a, b = g[:HALF], g[HALF:]
        at = pl.multiple_of(at, HEAD_WIDTH)
        out_ref[pl.ds(at, HALF), cols] = (a * c + b * s).astype(BF16)
        out_ref[pl.ds(pl.multiple_of(at + HALF, HALF), HALF), cols] = (b * c - a * s).astype(BF16)

    @pl.loop(0, KEY_VALUE_HEADS)
    def _(kv):
        k = qkv_ref[pl.ds(pl.multiple_of(D + kv * HEAD_WIDTH, HEAD_WIDTH), HEAD_WIDTH), :]
        v = qkv_ref[pl.ds(pl.multiple_of(D + KEYS + kv * HEAD_WIDTH, HEAD_WIDTH), HEAD_WIDTH), :]
        dk_ref[...] = jnp.zeros_like(dk_ref)
        dv_ref[...] = jnp.zeros_like(dv_ref)
        for b in range(length // QB):
            lo, hi = key_span(b)
            cols = slice(b * QB, (b + 1) * QB)
            q, o, do = three(qkv_ref, kv, b), three(o_ref, kv, b), three(do_ref, kv, b)
            lse = jnp.concatenate([lse_ref[kv, i:i + 1, cols] for i in range(SHARE)], axis=1)
            inner = jnp.sum(o.astype(F32) * do.astype(F32), axis=0, keepdims=True)
            s = dot(k[:, lo:hi], q, 0, 0) + wide_bias(bias_ref, b, hi - lo)
            p = jnp.exp(s - lse)
            dp = dot(v[:, lo:hi], do, 0, 0)
            ds = (p * (dp - inner)).astype(BF16)
            dv_ref[:, lo:hi] += dot(do, p.astype(BF16), 1, 1)
            dk_ref[:, lo:hi] += dot(q, ds, 1, 1)
            dq = dot(k[:, lo:hi], ds, 1, 0) * HEAD_WIDTH ** -0.5
            for i in range(SHARE):
                turn_back(dq[:, i * QB:(i + 1) * QB], cos_ref[:, cols], sin_ref[:, cols],
                          (kv * SHARE + i) * HEAD_WIDTH, cols)
        turn_back(dk_ref[...], cos_ref[...], sin_ref[...], D + kv * HEAD_WIDTH, slice(None))
        out_ref[pl.ds(pl.multiple_of(D + KEYS + kv * HEAD_WIDTH, HEAD_WIDTH), HEAD_WIDTH), :] = (
            dv_ref[...].astype(BF16))


def attend_back(qkv, o, do, lse, segments, cos, sin, at, before=()):
    length = segments.shape[1]
    wide, rows = qkv.shape
    here = lambda height: pl.BlockSpec((height, length), lambda i: (0, at))
    return pl.pallas_call(
        attend_back_kernel,
        grid=(1,),
        in_specs=[
            here(wide),
            here(D),
            here(D),
            pl.BlockSpec((KEY_VALUE_HEADS, 8, length), lambda i: (0, 0, at)),
            pl.BlockSpec((1, 1, length), lambda i: (at, 0, 0)),
            pl.BlockSpec((1, length, 1), lambda i: (at, 0, 0)),
            here(HALF),
            here(HALF),
        ] + [pl.BlockSpec(memory_space=pltpu.HBM)] * len(before),
        out_specs=[here(wide), fixed(DONE.shape)],
        out_shape=shaped(((wide, rows), BF16)) + [DONE],
        input_output_aliases={8 + i: i for i in range(len(before))},
        scratch_shapes=[
            pltpu.VMEM((length // QB, 3 * QB, QB), F32),
            pltpu.VMEM((HEAD_WIDTH, length), F32),
            pltpu.VMEM((HEAD_WIDTH, length), F32),
        ],
        compiler_params=params(60),
        cost_estimate=cost(),
        name="attend_back",
    )(qkv, o, do, lse, segments[:, None, :], segments[:, :, None], cos, sin, *before)


PIECES = ((0, 128), (128, OWN))


def weight_kernel(where_ref, h_ref, dqkv_ref, o_ref, da_ref, *out_refs):
    def store(block, grad):
        def put(x, keep, send):
            for i, (low, high) in enumerate(PIECES):
                at = block ^ block_here(where_ref)
                out_refs[2 * i][x, at] = keep[low:high]
                out_refs[2 * i + 1][x, at] = send[low:high]

        split_owners(grad, where_ref, put)

    grad = dot(h_ref[...], dqkv_ref[:PAIR, :], 1, 1)
    store(0, grad[:, :CUT])
    store(1, grad[:, CUT:])
    left = dot(h_ref[...], dqkv_ref[2 * CUT:, :], 1, 1)
    right = dot(o_ref[...], da_ref[:3 * CUT - WIDE, :], 1, 1)
    store(2, jnp.concatenate([left, right], axis=1))
    store(3, dot(o_ref[...], da_ref[3 * CUT - WIDE:, :], 1, 1))


def weight_grads(where, h, dqkv, o, da):
    rows = h.shape[1]
    shapes = [(2, 4, high - low, CUT) for low, high in PIECES for _ in range(2)]
    return pl.pallas_call(
        weight_kernel,
        grid=(1,),
        in_specs=[SMEM, fixed((D, rows)), fixed((WIDE, rows)), fixed((D, rows)), fixed((D, rows))],
        out_specs=[fixed(shape) for shape in shapes],
        out_shape=shaped(*((shape, BF16) for shape in shapes)),
        compiler_params=params(60),
        cost_estimate=cost(),
        name="weight_grads",
    )(where, h, dqkv, o, da)


def inputs_kernel(weights, where_ref, x_ref, dx_ref, dqkv_ref, *refs):
    out_ref, gain_grad, wq, q_sem, wk, k_sem = refs[8:]
    first = pl.program_id(0) == 0

    @pl.when(first)
    def _():
        weights[0].load(where_ref, refs[:4], wq, q_sem)
        weights[1].load(where_ref, refs[4:8], wk, k_sem)
        wait_for(wq, q_sem)
        wait_for(wk, k_sem)

    gain = wk[:, 2 * KEYS:2 * KEYS + 1].astype(F32)
    dh = dot(wq[...], dqkv_ref[:D], 1, 0) + dot(wk[:, :2 * KEYS], dqkv_ref[D:], 1, 0)
    normal, inverse = norm_columns(x_ref[...].astype(F32))
    back, part = norm_columns_back(dh, normal, inverse, gain)
    out_ref[...] = (dx_ref[...] + back).astype(BF16)

    @pl.when(first)
    def _():
        gain_grad[...] = part

    @pl.when(jnp.logical_not(first))
    def _():
        gain_grad[...] += part


def input_grads(where, x, dx, wq, wk, dqkv):
    rows = x.shape[1]
    return pl.pallas_call(
        functools.partial(inputs_kernel, (wq, wk)),
        grid=(rows // HALF_TILE,),
        in_specs=[SMEM, columns(D, HALF_TILE), columns(D, HALF_TILE), columns(WIDE, HALF_TILE)]
        + wq.specs() + wk.specs(),
        out_specs=[columns(D, HALF_TILE), pl.BlockSpec((D, 1), lambda i: (0, 0))],
        out_shape=shaped(((D, rows), BF16), ((D, 1), F32)),
        scratch_shapes=wq.scratch() + wk.scratch(),
        compiler_params=params(60),
        cost_estimate=cost(2 * rows * D * WIDE, rows * (D * 8 + WIDE * 2) + D * WIDE * 2),
        name="input_grads",
    )(where, x, dx, dqkv, *wq.arrays, *wk.arrays)


def tables(segments):
    length = segments.shape[1]
    index = jnp.arange(length, dtype=jnp.int32)
    same = segments[:, :, None] == segments[:, None, :]
    start = jnp.min(jnp.where(same, index[None, :, None], length), axis=1)
    position = (index[None, :] - start).astype(F32).reshape(1, -1)
    freq = THETA ** (-(jnp.arange(HALF, dtype=F32) * 2.0 / HEAD_WIDTH))
    angle = freq[:, None] * position
    return jnp.cos(angle), jnp.sin(angle)


def after(value, *others):
    return lax.optimization_barrier((value,) + others)[0]


class Cube:
    def __init__(self, count):
        self.count = count
        self.dims = count.bit_length() - 1
        replica, group = lax.axis_index("replica"), lax.axis_index("group")
        self.coordinate = {i: (replica >> i) & 1 for i in range(self.dims)}
        self.coordinate["x"] = group >> 1
        self.coordinate["core"] = group & 1
        self.me = group

    def swap(self, value, dim):
        if dim == "x":
            return lax.ppermute(value, "group", [(i, i ^ 2) for i in range(4)])
        if dim == "core":
            return lax.ppermute(value, "group", [(i, i ^ 1) for i in range(4)])
        return lax.ppermute(value, "replica", [(i, i ^ (1 << dim)) for i in range(self.count)])

    def ordered(self, dim, mine, other, axis):
        return jnp.where(
            self.coordinate[dim] == 0,
            jnp.concatenate([mine, other], axis=axis),
            jnp.concatenate([other, mine], axis=axis),
        )


def rows_of(own, sibling, across, diagonal):
    pieces = own, sibling, across, diagonal
    return Weight(0, [(array, flip, None) for flip, array in enumerate(pieces)])


class Relay:
    def __init__(self, cube, shard, axis, first, second):
        self.cube, self.shard, self.axis, self.first, self.second = cube, shard, axis, first, second
        self.cut = 1 - axis
        size = shard.shape[self.cut] // (2 if first is None else 4)
        at = cube.coordinate[second]
        if first is not None:
            at = 2 * at + cube.coordinate[first]
        self.part = lax.dynamic_slice_in_dim(shard, at * size, size, self.cut)

    def cross(self, *others):
        self.direct = self.cube.swap(after(self.part, *others), "x")
        return self.direct

    def hand_on(self, *others):
        self.direct = after(self.direct, *others)
        if self.first is None:
            self.half = self.direct
            self.rest = self.cube.swap(self.half, self.second)
            return self.rest
        self.handed = self.cube.swap(self.direct, self.first)
        return self.handed

    def finish(self, *others):
        cube = self.cube
        if self.first is not None:
            handed = after(self.handed, *others)
            self.half = cube.ordered(self.first, self.direct, handed, self.cut)
            self.rest = cube.swap(self.half, self.second)
        self.half_diagonal = cube.swap(self.half, "core")

    def weight(self, sibling, *others):
        rest = after(self.rest, *others)
        pieces = [
            (self.shard, 0, None), (sibling, 1, None), (self.half, 2, 0), (rest, 2, 1),
            (self.half_diagonal, 3, 0), (self.cube.swap(rest, "core"), 3, 1),
        ]
        return Weight(self.axis, pieces, self.second, 4)


class Reduce:
    def __init__(self, cube, keep, got, halves, gathers):
        rows, wide = keep.shape[2:]
        self.cube, self.shape = cube, (4, rows, wide)
        self.order = halves + tuple(range(2, cube.dims)) + gathers
        self.place = {"x": 0, 0: 1, 1: 2}
        self.terms = [t.reshape(2, 2, 2, rows, wide) for t in (keep, got)]
        self.index = 0
        self.done = False

    def sum(self, terms):
        if len(terms) == 1:
            return terms[0]
        return functools.reduce(jnp.add, [t.astype(F32) for t in terms]).astype(BF16)

    @staticmethod
    def land(pieces, other):
        got = lax.optimization_barrier((*(piece.terms[-1] for piece in pieces), other))
        for piece, value in zip(pieces, got):
            piece.terms[-1] = value

    def ready(self, *others):
        dim = self.order[self.index]
        if others:
            self.terms[-1] = after(self.terms[-1], *others)
        if self.index < 3:
            axis = self.place[dim]
            take = lambda i: [lax.slice_in_dim(t, i, i + 1, axis=axis) for t in self.terms]
            self.send, self.terms = self.sum(take(1)), take(0)
        else:
            self.send = self.sum(self.terms)
        return self.send

    def swap(self):
        dim = self.order[self.index]
        got = self.cube.swap(self.send, dim)
        self.index += 1
        if self.index <= 3:
            self.terms = self.terms + [got]
        elif self.index <= len(self.order) - 2:
            self.terms = [self.send, got]
        elif self.index < len(self.order):
            self.terms = [self.cube.ordered(dim, self.send, got, self.place[dim])]
        else:
            self.terms = [self.send, got]

    def finish(self, *others):
        self.done = True
        low, got = (after(value, *others) for value in self.terms)
        self.result = self.cube.ordered(self.order[-1], low, got, self.place[self.order[-1]])
        self.result = self.result.reshape(self.shape)
        return self.result


def per_device(
    tokens,
    segments,
    query_weight,
    key_weight,
    value_weight,
    output_weight,
    w_gate,
    w_up,
    w_down,
    attn_gain,
    ffn_gain,
    cotangent,
    replicas,
):
    cube = Cube(replicas)
    where = jnp.stack([cube.me] + [cube.coordinate[i] for i in range(3)]).astype(jnp.int32)
    x, dy = tokens.T, cotangent.T

    core = lambda value: cube.swap(value, "core")
    q_across = cube.swap(query_weight, "x")
    pad = jnp.zeros((OWN, GAINS - 2), BF16)
    kv = jnp.concatenate(
        [key_weight, value_weight, attn_gain[:, None], ffn_gain[:, None], pad], axis=1
    )
    kv_across = cube.swap(after(kv, q_across), "x")
    relays = [
        Relay(cube, w_gate, 0, 0, 1), Relay(cube, w_up, 0, 1, 0), Relay(cube, w_down.T, 1, None, 0)
    ]
    q_sibling, kv_sibling, wo_sibling = core(query_weight), core(kv), core(output_weight)
    siblings = [core(relay.shard) for relay in relays]
    cos, sin = tables(segments)
    early = [relay.part for relay in relays] + [cos, sin, where, q_sibling, kv_sibling, wo_sibling]
    q_across, kv_across = lax.optimization_barrier((q_across, kv_across, *early, *siblings))[:2]
    q_diagonal, kv_diagonal = core(q_across), core(kv_across)
    direct = [relay.cross(q_across, kv_across) for relay in relays]
    wq = rows_of(query_weight, q_sibling, q_across, q_diagonal)
    wk = rows_of(kv, kv_sibling, kv_across, kv_diagonal)
    qkv, h, gains = project(where, x, wq, wk, cos, sin)
    *first, done0 = attend(qkv, segments, 0)
    for relay in relays:
        relay.hand_on(done0)
    wo_across = cube.swap(after(output_weight, done0, *direct), "x")
    o, lse, done1 = attend(after(qkv, done0, *direct), segments, 1, first)
    for relay in relays:
        relay.finish(done1)
    wo_diagonal = core(after(wo_across, done1))
    wo = rows_of(output_weight, wo_sibling, wo_across, wo_diagonal)
    x1, h2 = middle(where, x, after(o, relays[0].half, relays[1].half), wo, gains)
    weights = [relay.weight(sibling, h2) for relay, sibling in zip(relays, siblings)]
    y, dh2, hid, dgate, dup = feed_forward(where, h2, dy, x1, weights)

    gd_keep, gd_send = ffn_grads(where, dy, hid, True)
    gd = Reduce(cube, gd_keep, core(gd_send), ("x", 0, 1), (1, 0))
    gg_keep, gg_send = ffn_grads(where, h2, after(dgate, gd_send), False)
    gg = Reduce(cube, gg_keep, core(gg_send), (0, "x", 1), (1, 0))
    gd.ready(gg_send)
    gu_keep, gu_send = ffn_grads(where, h2, after(dup, gd.send), False)
    gd.swap()
    gu = Reduce(cube, gu_keep, core(gu_send), (1, 0, "x"), (1, 0))
    gg.ready(gu_send)
    dx1, da, do, ffn_gain_grad = branch(where, after(dh2, gg.send), x1, dy, gains, wo)
    gg.swap()
    gu.ready(da)
    do0 = after(do, gu.send)
    gu.swap()
    *first, done0 = attend_back(qkv, o, do0, lse, segments, cos, sin, 0)
    Reduce.land((gd, gg), done0)
    do1 = after(do, done0, gd.ready(), gg.ready())
    gd.swap()
    gg.swap()
    dqkv, done1 = attend_back(qkv, o, do1, lse, segments, cos, sin, 1, first)
    swaps = [gd, gg, gu]
    Reduce.land(swaps, done1)
    dqkv = after(dqkv, *[piece.ready() for piece in swaps])
    for piece in swaps:
        piece.swap()
    parts = []
    weight_parts = weight_grads(where, h, dqkv, o, da)
    for i, halves in enumerate((("x", 0, 1), (0, "x", 1))):
        keep, send = weight_parts[2 * i:2 * i + 2]
        parts.append(Reduce(cube, keep, core(send), halves, (1, 0)))
    dqkv = after(dqkv, *[part.ready() for part in parts])
    for part in parts:
        part.swap()
    grad_x, attn_gain_grad = input_grads(where, x, dx1, wq, wk, dqkv)
    swaps = [gd, gg, gu] + parts
    Reduce.land(swaps, grad_x)
    both = jnp.concatenate([attn_gain_grad, ffn_gain_grad], axis=1).T.reshape(-1)
    ends = ["core", "x"] + list(range(cube.dims))
    token = grad_x
    for piece in swaps:
        token = piece.ready(token)
        piece.swap()
    swaps = parts + [gd, gg, gu]
    while any(piece.index < len(piece.order) for piece in swaps):
        active = [piece for piece in swaps if piece.index < len(piece.order)]
        for piece in active:
            token = piece.ready(token, both)
            piece.swap()
        for piece in swaps:
            if piece not in active and not piece.done:
                token = piece.finish(token)
        if ends:
            both = both + after(cube.swap(both, ends.pop(0)), token)
    for piece in swaps:
        if not piece.done:
            token = piece.finish(token)
    for dim in ends:
        both = both + cube.swap(both, dim)
    both = lax.dynamic_slice_in_dim(both.reshape(2, D), cube.me * OWN, OWN, 1)
    flat = lambda g: jnp.concatenate([g[i] for i in range(4)], axis=1)
    ga = jnp.concatenate([flat(part.result) for part in parts], axis=0).astype(F32)
    return (
        y.T,
        grad_x.T,
        ga[:, :D],
        ga[:, D:D + KEYS],
        ga[:, D + KEYS:WIDE],
        ga[:, WIDE:],
        flat(gg.result).astype(F32),
        flat(gu.result).astype(F32),
        gd.result.reshape(D, CUT).T.astype(F32),
        both[0],
        both[1],
    )


def solution(mesh):
    rows = P(("group", "replica"), None)
    weight, gain = P("group", None), P("group")
    replicas = mesh.shape["replica"]
    return jax.shard_map(
        lambda *args: per_device(*args, replicas),
        mesh=mesh,
        in_specs=(rows, rows) + (weight,) * 7 + (gain, gain, rows),
        out_specs=(rows, rows) + (weight,) * 7 + (gain, gain),
        check_vma=False,
    )
```
